32 devices in a mesh: grp: 4 (over z), dev: 8 (over y, x, core).
Axes of the slice: x: 2, y: 2, z: 4, core: 2. Of those that a mesh axis runs over, the one named last changes fastest.
Arguments:
- stored_tiles: float32 [32, 9, 128, 128], P(('grp', 'dev')), may hold values from -0.22097087 to 0.22097087, as said below
- tile_flags: int32 [32, 9], P(('grp', 'dev')), may hold values from 0 to 1, as said below
- orbitals: float32 [4096, 256], P(('grp', 'dev')), may hold values from -6 to 6
Outputs:
- product: float32 [4096, 256], P(('grp', 'dev'))
The draws below stay inside these ranges and needn't reach their ends.
Inputs may be any that keep to these rules, and one draw needn't show every extreme that they name: tile_flags[p, s] is 1 at s = p mod 8, 0 for s below that, and 0 at s = 8 in the last 8 block rows. `stored_tiles`: the tile at slot p mod 8 of block row p is symmetric.
All inputs are finite; a program needn't handle non-finite values.
Results may differ from the reference program's by a relative error of at most 0.000075.
Values sent between devices are 32-bit elements; how exact they have to be, the bound alone decides.
No kernel may reach another device: no remote copies, remote signals or barrier semaphores. Data moves between devices by JAX's collectives and lax.ppermute only.
A program may use at most 64 MiB of HBM per device.

```python
import math
import jax
import jax.numpy as jnp
from jax import lax

B = 128
K = 256
SLOTS = 9
NB = 32
ROWS = 4096


def draw_stored_tiles(key, part):
    spread = 0.25 / math.sqrt(B)
    full_shape = (NB, SLOTS, B, B)
    entries = jax.random.truncated_normal(key, -4.0, 4.0, full_shape, jnp.float32)
    row_index = lax.broadcasted_iota(jnp.int32, (NB, SLOTS, 1, 1), 0) % (SLOTS - 1)
    slot_index = lax.broadcasted_iota(jnp.int32, (NB, SLOTS, 1, 1), 1)
    mirrored = (entries + jnp.swapaxes(entries, 2, 3)) * 0.70710678
    return jnp.where(row_index == slot_index, mirrored, entries) * spread


def draw_tile_flags(key, part):
    group_width = SLOTS - 1
    coin_flips = jax.random.randint(key, (NB, SLOTS), 0, 2)
    row_index = lax.broadcasted_iota(jnp.int32, (NB, SLOTS), 0)
    slot_index = lax.broadcasted_iota(jnp.int32, (NB, SLOTS), 1)
    own_slot = row_index % group_width
    result = jnp.where(slot_index == own_slot, 1, jnp.where(slot_index < own_slot, 0, coin_flips))
    last_group = row_index >= NB - group_width
    result = jnp.where((slot_index == group_width) & last_group, 0, result)
    return result.astype(jnp.int32)


def steps_of(stream_key, dims, cuts, low, top_value):
    factor_of, own = 1.0, jax.random.fold_in(stream_key, 6)
    for axis_at, parts in cuts:
        heights = jnp.exp(jax.random.uniform(jax.random.fold_in(own, axis_at), (parts,), jnp.float32, low / len(cuts), top_value / len(cuts)))
        factor_of = factor_of * jnp.repeat(heights, dims[axis_at] // parts).reshape([-1 if axis == axis_at else 1 for axis in range(len(dims))])
    return factor_of


def scatter_about(own_key, shape, deviation, reach, cuts=(), kind=jnp.bfloat16):
    drawn = deviation * jax.random.normal(own_key, shape, jnp.float32)
    if cuts:
        drawn = drawn * steps_of(own_key, shape, cuts, -0.22, 0.18)
    return jnp.clip(drawn, -reach, reach).astype(kind)


def setup_inputs(seed: int = 0) -> dict:
    seeds = jax.random.split(jax.random.key(seed), 4)
    stored_tiles = draw_stored_tiles(jax.random.fold_in(seeds[3], 71), 0)
    tile_flags = draw_tile_flags(jax.random.fold_in(seeds[3], 71), 0)
    orbitals = scatter_about(seeds[2], (ROWS, K), 1.0, 6.0, ((0, 32),), jnp.float32)
    return {"stored_tiles": stored_tiles, "tile_flags": tile_flags, "orbitals": orbitals}


def reference(stored_tiles, tile_flags, orbitals):
    group_width = SLOTS - 1
    groups = NB // group_width
    highest = lax.Precision.HIGHEST
    tile_groups = stored_tiles.reshape(groups, group_width, SLOTS, B, B)
    flag_groups = tile_flags.reshape(groups, group_width, SLOTS)
    orbital_groups = orbitals.reshape(groups, group_width, B, K)
    following = jnp.concatenate([orbital_groups[1:], jnp.zeros((1, group_width, B, K), orbitals.dtype)], 0)
    offdiag = 1.0 - jnp.eye(group_width, dtype=orbitals.dtype)

    def one_group(inputs):
        group_tiles, group_flags, x_here, x_after = inputs
        blocks = group_tiles * group_flags.astype(group_tiles.dtype)[:, :, None, None]
        in_group = blocks[:, :group_width]
        next_tile = blocks[:, group_width]
        direct = jnp.einsum("dsij,sjk->dik", in_group, x_here, precision=highest)
        beside = in_group * offdiag[:, :, None, None]
        mirror = jnp.einsum("dsij,dik->sjk", beside, x_here, precision=highest)
        forward = jnp.einsum("dij,djk->dik", next_tile, x_after, precision=highest)
        upward = jnp.einsum("dij,dik->djk", next_tile, x_here, precision=highest)
        return direct + mirror + forward, upward

    in_sums, upward = lax.map(one_group, (tile_groups, flag_groups, orbital_groups, following))
    shifted = jnp.concatenate([jnp.zeros((1, group_width, B, K), orbitals.dtype), upward[:-1]], 0)
    return (in_sums + shifted).reshape(NB * B, K)
```

```python
import jax
import jax.numpy as jnp
from jax import lax
from jax.sharding import PartitionSpec as P


def shifted(shard, axis, by):
    count = lax.axis_size(axis)
    pairs = [(i, i + by) for i in range(count) if 0 <= i + by < count]
    return lax.ppermute(shard, axis, pairs)


def per_device(stored_tiles, tile_flags, orbitals):
    high = lax.Precision.HIGH
    group_width = lax.axis_size("dev")
    own_index = lax.axis_index("dev")
    slot_index = lax.broadcasted_iota(jnp.int32, (group_width, 1, 1), 0)
    flags_float = tile_flags[0].astype(jnp.float32)
    blocks = stored_tiles[0] * flags_float[:, None, None]
    in_group = blocks[:group_width]
    next_tile = blocks[group_width]

    following = shifted(orbitals, "grp", -1)
    upward = shifted(
        jnp.einsum("ji,jk->ik", next_tile, orbitals, precision=high), "grp", 1
    )
    terms = jnp.einsum("sji,jk->sik", in_group, orbitals, precision=high)
    outgoing = jnp.where(slot_index <= own_index, orbitals[None], terms)
    arrived = lax.all_to_all(outgoing, "dev", 0, 0)
    before = slot_index < own_index
    product = jnp.einsum("sij,sjk->ik", in_group, arrived, precision=high)
    product = product + jnp.sum(jnp.where(before, arrived, 0.0), axis=0)
    product = product + jnp.dot(next_tile, following, precision=high)
    return product + upward


def solution(mesh):
    in_specs = (
        P(("grp", "dev"), None, None, None),
        P(("grp", "dev"), None),
        P(("grp", "dev"), None),
    )
    out_specs = P(("grp", "dev"), None)
    return jax.shard_map(
        per_device, mesh=mesh, in_specs=in_specs, out_specs=out_specs, check_vma=False
    )
```

```python
import jax
import jax.numpy as jnp
from jax import lax
from jax.sharding import PartitionSpec as P

HIGH = lax.Precision.HIGH


def shifted(shard, axis, by):
    count = lax.axis_size(axis)
    pairs = [(i, i + by) for i in range(count) if 0 <= i + by < count]
    return lax.ppermute(shard, axis, pairs)


def partnered(shard):
    count = lax.axis_size("dev")
    return lax.ppermute(shard, "dev", [(i, i ^ 1) for i in range(count)])


def per_device(stored_tiles, tile_flags, orbitals):
    group_width = lax.axis_size("dev")
    pair_count = group_width // 2
    own_index = lax.axis_index("dev")
    own_pair, side = own_index // 2, own_index % 2
    order = stored_tiles.shape[2]
    columns = orbitals.shape[1]
    pair_index = lax.broadcasted_iota(jnp.int32, (pair_count, 1, 1), 0)
    flags_float = tile_flags[0].astype(jnp.float32)
    blocks = stored_tiles[0] * flags_float[:, None, None]
    next_tile = blocks[group_width]

    sided = blocks[:group_width].reshape(pair_count, 2, order, order)
    kept = lax.dynamic_index_in_dim(sided, side, 1, keepdims=False)
    given = lax.dynamic_index_in_dim(sided, 1 - side, 1, keepdims=False)
    halves = orbitals.reshape(order, 2, columns // 2).swapaxes(0, 1)
    taken = partnered(jnp.concatenate([given, halves], axis=0))
    other, other_halves = taken[:pair_count], taken[pair_count:]
    other_orbitals = other_halves.swapaxes(0, 1).reshape(order, columns)

    following = shifted(orbitals, "grp", -1)
    upward = shifted(
        jnp.einsum("ji,jk->ik", next_tile, orbitals, precision=HIGH), "grp", 1
    )

    terms = jnp.einsum("sji,jk->sik", kept, orbitals, precision=HIGH)
    terms += jnp.einsum("sji,jk->sik", other, other_orbitals, precision=HIGH)
    outgoing = jnp.where(pair_index <= own_pair, orbitals[None], terms)
    groups = [list(range(s, group_width, 2)) for s in range(2)]
    arrived = lax.all_to_all(outgoing, "dev", 0, 0, axis_index_groups=groups)

    own_given = lax.dynamic_index_in_dim(given, own_pair, 0, keepdims=False)
    own_other = lax.dynamic_index_in_dim(other, own_pair, 0, keepdims=False)
    product = jnp.dot(own_given, other_orbitals, precision=HIGH)
    product += jnp.einsum("ji,jk->ik", own_other, other_orbitals, precision=HIGH)

    beyond = jnp.where(pair_index > own_pair, other, 0.0)
    returned = partnered(jnp.einsum("sij,sjk->ik", beyond, arrived, precision=HIGH))
    product += jnp.einsum("sij,sjk->ik", kept, arrived, precision=HIGH)
    product += jnp.sum(jnp.where(pair_index < own_pair, arrived, 0.0), axis=0)
    product += jnp.dot(next_tile, following, precision=HIGH)
    return product + upward + returned


def solution(mesh):
    in_specs = (
        P(("grp", "dev"), None, None, None),
        P(("grp", "dev"), None),
        P(("grp", "dev"), None),
    )
    out_specs = P(("grp", "dev"), None)
    return jax.shard_map(
        per_device, mesh=mesh, in_specs=in_specs, out_specs=out_specs, check_vma=False
    )
```

```python
import functools

import jax
import jax.numpy as jnp
from jax import lax
from jax.experimental import pallas as pl
from jax.experimental.pallas import tpu as pltpu
from jax.sharding import PartitionSpec as P

VMEM = pl.BlockSpec(memory_space=pltpu.VMEM)
SMEM = pl.BlockSpec(memory_space=pltpu.SMEM)
F32 = jnp.float32


def parted(value):
    high = value.astype(jnp.bfloat16)
    return high, (value - high.astype(F32)).astype(jnp.bfloat16)


def product_of(left, right, contract):
    dims = ((contract, (0,)), ((), ()))
    dot = functools.partial(
        lax.dot_general, dimension_numbers=dims, preferred_element_type=F32
    )
    (left_high, left_low), (right_high, right_low) = left, right
    return (
        dot(left_high, right_high)
        + dot(left_high, right_low)
        + dot(left_low, right_high)
    )


def times(left, right):
    return product_of(parted(left), parted(right), (1,))


def transposed_times(left, right):
    return product_of(parted(left), parted(right), (0,))


class Layout:
    def __init__(self, group_width):
        self.pairs = group_width // 2
        self.rounds = (self.pairs - 1) // 2
        self.split_offset = self.pairs - 1
        self.given = 2 * self.rounds + 2

    def offset(self, round_index, side):
        return 2 * round_index + 1 + side


def place(group_width):
    index = lax.axis_index("dev")
    return index, index // 2, index % 2


def pack_kernel(layout, group_width, flags, tiles, orbitals, packed):
    index, pair, side = place(group_width)

    def masked(slot):
        return tiles[slot] * flags[0, slot].astype(F32)

    for r in range(layout.rounds):
        far = pair ^ layout.offset(r, 1 - side)
        packed[2 * r] = masked(2 * far)
        packed[2 * r + 1] = masked(2 * far + 1)
    far = pair ^ layout.split_offset
    packed[2 * layout.rounds] = masked(2 * far + 1 - side)
    packed[2 * layout.rounds + 1] = masked(group_width)
    half = orbitals.shape[1] // 2
    packed[layout.given] = orbitals[:, :half]
    packed[layout.given + 1] = orbitals[:, half:]


def send_kernel(layout, group_width, flags, tiles, orbitals, taken, *outs):
    index, pair, side = place(group_width)
    full_outs, group_out, split_out = outs[:-2], outs[-2], outs[-1]

    def masked(slot):
        return tiles[slot] * flags[0, slot].astype(F32)

    own = orbitals[...]
    other = jnp.concatenate(
        [taken[layout.given], taken[layout.given + 1]], axis=1
    )
    both = parted(jnp.concatenate([own, other], axis=0))

    def term(slot, taken_slot):
        stack = jnp.concatenate([masked(slot), taken[taken_slot]], axis=0)
        return product_of(parted(stack), both, (0,))

    first = jnp.where(side == 0, own, other)
    second = jnp.where(side == 0, other, own)
    for r in range(layout.rounds):
        far = pair ^ layout.offset(r, side)
        out = full_outs[r]

        @pl.when(far > pair)
        def _():
            out[0] = term(2 * far, 2 * r)
            out[1] = term(2 * far + 1, 2 * r + 1)

        @pl.when(far < pair)
        def _():
            out[0] = first
            out[1] = second

    far = pair ^ layout.split_offset

    @pl.when(far > pair)
    def _():
        split_out[...] = term(2 * far + side, 2 * layout.rounds)

    @pl.when(far < pair)
    def _():
        split_out[...] = own

    @pl.when(side == 0)
    def _():
        group_out[0] = transposed_times(masked(group_width), own)
        group_out[1] = transposed_times(taken[layout.given - 1], other)

    @pl.when(side == 1)
    def _():
        group_out[0] = other
        group_out[1] = own


def gather_kernel(layout, group_width, flags, tiles, orbitals, taken, *refs):
    index, pair, side = place(group_width)
    full_ins, group_in, sums = refs[: layout.rounds], refs[-2], refs[-1]

    def masked(slot):
        return tiles[slot] * flags[0, slot].astype(F32)

    own = orbitals[...]
    other = jnp.concatenate(
        [taken[layout.given], taken[layout.given + 1]], axis=1
    )
    beside = masked(index ^ 1)
    row = jnp.concatenate([masked(index), beside], axis=1)
    sums[0] = times(row, jnp.concatenate([own, other], axis=0))
    sums[1] = transposed_times(beside, own)

    for r in range(layout.rounds):
        far = pair ^ layout.offset(r, side)
        arrived = full_ins[r]

        @pl.when(far > pair)
        def _():
            mine = jnp.concatenate([masked(2 * far), masked(2 * far + 1)], axis=1)
            others = jnp.concatenate([taken[2 * r], taken[2 * r + 1]], axis=1)
            left = jnp.concatenate([mine, others], axis=0)
            right = jnp.concatenate([arrived[0], arrived[1]], axis=0)
            terms = times(left, right)
            order = own.shape[0]
            sums[0] += terms[:order]
            sums[1] += terms[order:]

        @pl.when(far < pair)
        def _():
            sums[0] += arrived[side]
            sums[1] += arrived[1 - side]

    @pl.when(side == 0)
    def _():
        sums[0] += group_in[0]
        sums[1] += group_in[1]

    @pl.when(side == 1)
    def _():
        sums[0] += times(masked(group_width), group_in[1])
        sums[1] += times(taken[layout.given - 1], group_in[0])


def split_kernel(layout, group_width, flags, tiles, taken, arrived, sums, own, back):
    index, pair, side = place(group_width)
    far = pair ^ layout.split_offset

    @pl.when(far > pair)
    def _():
        slot = 2 * far + side
        mine = tiles[slot] * flags[0, slot].astype(F32)
        left = jnp.concatenate([mine, taken[2 * layout.rounds]], axis=0)
        terms = times(left, arrived[...])
        order = mine.shape[0]
        own[...] = sums[0] + terms[:order]
        back[...] = sums[1] + terms[order:]

    @pl.when(far < pair)
    def _():
        own[...] = sums[0] + arrived[...]
        back[...] = sums[1]


def call(body, outs, *operands):
    return pl.pallas_call(
        body,
        out_shape=outs,
        in_specs=[SMEM] + [VMEM] * (len(operands) - 1),
        out_specs=jax.tree.map(lambda _: VMEM, outs),
        compiler_params=pltpu.CompilerParams(vmem_limit_bytes=32 * 1024 * 1024),
    )(*operands)


def per_device(stored_tiles, tile_flags, orbitals):
    group_width = lax.axis_size("dev")
    groups = lax.axis_size("grp")
    layout = Layout(group_width)
    tiles = stored_tiles[0]
    order, columns = orbitals.shape
    block = jax.ShapeDtypeStruct((order, columns), F32)
    two = jax.ShapeDtypeStruct((2, order, columns), F32)
    partners = [(i, i ^ 1) for i in range(group_width)]

    packed = call(
        functools.partial(pack_kernel, layout, group_width),
        jax.ShapeDtypeStruct((layout.given + 2, order, order), F32),
        tile_flags, tiles, orbitals,
    )
    taken = lax.ppermute(packed, "dev", partners)

    *full, upward, split = call(
        functools.partial(send_kernel, layout, group_width),
        [two] * layout.rounds + [two, block],
        tile_flags, tiles, orbitals, taken,
    )
    arrived = []
    for r in range(layout.rounds):
        swaps = [
            (i, i ^ (2 * layout.offset(r, i % 2))) for i in range(group_width)
        ]
        arrived.append(lax.ppermute(full[r], "dev", swaps))
    shifts = []
    for g in range(groups):
        for i in range(group_width):
            to = g + 1 - 2 * (i % 2)
            if 0 <= to < groups:
                shifts.append((g * group_width + i, to * group_width + i))
    group_arrived = lax.ppermute(upward, ("grp", "dev"), shifts)
    swaps = [(i, i ^ (2 * layout.split_offset)) for i in range(group_width)]
    split_arrived = lax.ppermute(split, "dev", swaps)

    sums = call(
        functools.partial(gather_kernel, layout, group_width),
        two,
        tile_flags, tiles, orbitals, taken, *arrived, group_arrived,
    )
    own, back = call(
        functools.partial(split_kernel, layout, group_width),
        [block, block],
        tile_flags, tiles, taken, split_arrived, sums,
    )
    return own + lax.ppermute(back, "dev", partners)


def solution(mesh):
    in_specs = (
        P(("grp", "dev"), None, None, None),
        P(("grp", "dev"), None),
        P(("grp", "dev"), None),
    )
    out_specs = P(("grp", "dev"), None)
    return jax.shard_map(
        per_device, mesh=mesh, in_specs=in_specs, out_specs=out_specs, check_vma=False
    )
```

```python
import functools

import jax
import jax.numpy as jnp
from jax import lax
from jax.experimental import pallas as pl
from jax.experimental.pallas import tpu as pltpu
from jax.sharding import PartitionSpec as P

HBM = pl.BlockSpec(memory_space=pltpu.HBM)
VMEM = pl.BlockSpec(memory_space=pltpu.VMEM)
F32 = jnp.float32


def parted(value):
    high = value.astype(jnp.bfloat16)
    return high, (value - high.astype(F32)).astype(jnp.bfloat16)


def product_of(left, right, contract):
    dims = ((contract, (0,)), ((), ()))
    dot = functools.partial(
        lax.dot_general, dimension_numbers=dims, preferred_element_type=F32
    )
    (left_high, left_low), (right_high, right_low) = left, right
    return (
        dot(left_high, right_high)
        + dot(left_high, right_low)
        + dot(left_low, right_high)
    )


def times(left, right):
    return product_of(parted(left), parted(right), (1,))


def transposed_times(left, right):
    return product_of(parted(left), parted(right), (0,))


class Layout:
    def __init__(self, group_width):
        self.width = group_width
        self.pairs = group_width // 2
        self.rounds = (self.pairs - 1) // 2
        self.last_offset = self.pairs - 1
        self.last = 2 * self.rounds
        self.given = self.last + 2

    def offset(self, round_index, side):
        return 2 * round_index + 1 + side


def place():
    index = lax.axis_index("dev")
    return index, index // 2, index % 2


def pack_kernel(
    layout, flags_in, tiles_in, orbitals_in, packed, tiles, orbitals,
    flags, flags_sem, given_sem, half_sem, tiles_sem, orbitals_sem,
):
    index, pair, side = place()
    half = orbitals.shape[1] // 2
    slots = []
    for r in range(layout.rounds):
        far = pair ^ layout.offset(r, 1 - side)
        slots += [2 * far, 2 * far + 1]
    far = pair ^ layout.last_offset
    slots += [jnp.where(side == 1, 2 * far, layout.width), 2 * far + 1]

    flags_copy = pltpu.make_async_copy(flags_in, flags, flags_sem)
    flags_copy.start()
    given_copies = []
    for k, slot in enumerate(slots):
        given_copies.append(
            pltpu.make_async_copy(tiles_in.at[slot], packed.at[k], given_sem.at[k])
        )
        given_copies[-1].start()
    half_copies = []
    for h in range(2):
        half_copies.append(
            pltpu.make_async_copy(
                orbitals_in.at[:, pl.ds(h * half, half)],
                packed.at[layout.given + h],
                half_sem.at[h],
            )
        )
        half_copies[-1].start()
    tiles_copy = pltpu.make_async_copy(tiles_in, tiles, tiles_sem)
    tiles_copy.start()
    orbitals_copy = pltpu.make_async_copy(orbitals_in, orbitals, orbitals_sem)
    orbitals_copy.start()

    flags_copy.wait()
    for k, slot in enumerate(slots):
        given_copies[k].wait()
        packed[k] = packed[k] * flags[0, slot].astype(F32)
    tiles_copy.wait()
    for slot in range(layout.width + 1):
        tiles[slot] = tiles[slot] * flags[0, slot].astype(F32)
    for copy in half_copies:
        copy.wait()
    orbitals_copy.wait()


def both_orbitals(layout, orbitals, taken):
    other = jnp.concatenate(
        [taken[layout.given], taken[layout.given + 1]], axis=1
    )
    return orbitals[...], other


def send_pair(layout, far, pair, side, at, tiles, taken, own, other, out):
    @pl.when(far > pair)
    def _():
        right = parted(jnp.concatenate([own, other], axis=0))
        for k in range(2):
            stack = jnp.concatenate([tiles[2 * far + k], taken[at + k]], axis=0)
            out[k] = product_of(parted(stack), right, (0,))

    @pl.when(far < pair)
    def _():
        out[0] = jnp.where(side == 0, own, other)
        out[1] = jnp.where(side == 0, other, own)


def send_full_kernel(layout, tiles, orbitals, taken, *outs):
    index, pair, side = place()
    own, other = both_orbitals(layout, orbitals, taken)
    for r in range(layout.rounds):
        far = pair ^ layout.offset(r, side)
        send_pair(layout, far, pair, side, 2 * r, tiles, taken, own, other, outs[r])


def send_last_kernel(layout, tiles, orbitals, taken, out):
    index, pair, side = place()
    own, other = both_orbitals(layout, orbitals, taken)

    @pl.when(side == 0)
    def _():
        far = pair ^ layout.last_offset
        send_pair(layout, far, pair, side, layout.last, tiles, taken, own, other, out)

    @pl.when(side == 1)
    def _():
        out[0] = transposed_times(taken[layout.last], other)
        out[1] = transposed_times(tiles[layout.width], own)


def take_pair(layout, far, pair, side, at, tiles, taken, arrived, mine_out, other_out):
    order = tiles.shape[1]

    @pl.when(far > pair)
    def _():
        mine = jnp.concatenate([tiles[2 * far], tiles[2 * far + 1]], axis=1)
        others = jnp.concatenate([taken[at], taken[at + 1]], axis=1)
        right = jnp.concatenate([arrived[0], arrived[1]], axis=0)
        terms = times(jnp.concatenate([mine, others], axis=0), right)
        mine_out[...] += terms[:order]
        other_out[...] += terms[order:]

    @pl.when(far < pair)
    def _():
        mine_out[...] += arrived[side]
        other_out[...] += arrived[1 - side]


def near_kernel(layout, tiles, orbitals, taken, following, mine_out, other_out):
    index, pair, side = place()
    own, other = both_orbitals(layout, orbitals, taken)
    beside = tiles[index ^ 1]
    row = jnp.concatenate([tiles[index], beside], axis=1)
    mine_out[...] = times(row, jnp.concatenate([own, other], axis=0)) + times(
        tiles[layout.width], following[...]
    )
    other_out[...] = transposed_times(beside, own)


def gather_kernel(layout, tiles, taken, mine_in, other_in, *refs):
    index, pair, side = place()
    arrived, mine_out, other_out = refs[:-2], refs[-2], refs[-1]
    mine_out[...] = mine_in[...]
    other_out[...] = other_in[...]
    for r in range(layout.rounds):
        far = pair ^ layout.offset(r, side)
        take_pair(
            layout, far, pair, side, 2 * r, tiles, taken, arrived[r], mine_out, other_out
        )


def last_kernel(layout, tiles, taken, mine_in, other_in, arrived, mine_out, other_out):
    index, pair, side = place()
    mine_out[...] = mine_in[...]
    other_out[...] = other_in[...]

    @pl.when(side == 0)
    def _():
        far = pair ^ layout.last_offset
        take_pair(
            layout, far, pair, side, layout.last, tiles, taken, arrived, mine_out, other_out
        )

    @pl.when(side == 1)
    def _():
        mine_out[...] += arrived[1]
        other_out[...] += arrived[0]


def call(body, outs, operands, specs=None, scratch=(), flops=0):
    return pl.pallas_call(
        body,
        out_shape=outs,
        in_specs=specs or [VMEM] * len(operands),
        out_specs=jax.tree.map(lambda _: VMEM, outs),
        scratch_shapes=scratch,
        cost_estimate=pl.CostEstimate(
            flops=flops, bytes_accessed=0, transcendentals=0
        ),
        compiler_params=pltpu.CompilerParams(vmem_limit_bytes=32 * 1024 * 1024),
    )(*operands)


def per_device(stored_tiles, tile_flags, orbitals):
    group_width = lax.axis_size("dev")
    groups = lax.axis_size("grp")
    layout = Layout(group_width)
    order, columns = orbitals.shape
    block = jax.ShapeDtypeStruct((order, columns), F32)
    two = jax.ShapeDtypeStruct((2, order, columns), F32)
    partners = [(i, i ^ 1) for i in range(group_width)]

    packed, tiles, held = call(
        functools.partial(pack_kernel, layout),
        [
            jax.ShapeDtypeStruct((layout.given + 2, order, order), F32),
            jax.ShapeDtypeStruct((group_width + 1, order, order), F32),
            block,
        ],
        [
            pltpu.with_memory_space_constraint(operand, pltpu.HBM)
            for operand in (tile_flags, stored_tiles[0], orbitals)
        ],
        [HBM, HBM, HBM],
        [
            pltpu.SMEM(tile_flags.shape, jnp.int32),
            pltpu.SemaphoreType.DMA,
            pltpu.SemaphoreType.DMA((layout.given,)),
            pltpu.SemaphoreType.DMA((2,)),
            pltpu.SemaphoreType.DMA,
            pltpu.SemaphoreType.DMA,
        ],
    )
    taken = lax.ppermute(packed, "dev", partners)
    downward = [(g, g - 1) for g in range(1, groups)]
    following = lax.ppermute(held, "grp", downward)

    full = call(
        functools.partial(send_full_kernel, layout),
        [two] * layout.rounds,
        [tiles, held, taken],
    )
    arrived = []
    for r in range(layout.rounds):
        swaps = [
            (i, i ^ (2 * layout.offset(r, i % 2))) for i in range(group_width)
        ]
        arrived.append(lax.ppermute(full[r], "dev", swaps))

    last = call(
        functools.partial(send_last_kernel, layout), two, [tiles, held, taken]
    )
    moves = []
    for g in range(groups):
        for i in range(group_width):
            if i % 2 == 0:
                moves.append((g, i, g, i ^ (2 * layout.last_offset)))
            elif g + 1 < groups:
                moves.append((g, i, g + 1, i))
    moves = [(g * group_width + i, h * group_width + j) for g, i, h, j in moves]
    last_arrived = lax.ppermute(last, ("grp", "dev"), moves)

    mine, other = call(
        functools.partial(near_kernel, layout),
        [block, block],
        [tiles, held, taken, following],
        flops=10**10,
    )
    mine, other = call(
        functools.partial(gather_kernel, layout),
        [block, block],
        [tiles, taken, mine, other, *arrived],
        flops=10**8,
    )
    mine, other = call(
        functools.partial(last_kernel, layout),
        [block, block],
        [tiles, taken, mine, other, last_arrived],
    )
    return mine + lax.ppermute(other, "dev", partners)


def solution(mesh):
    in_specs = (
        P(("grp", "dev"), None, None, None),
        P(("grp", "dev"), None),
        P(("grp", "dev"), None),
    )
    out_specs = P(("grp", "dev"), None)
    return jax.shard_map(
        per_device, mesh=mesh, in_specs=in_specs, out_specs=out_specs, check_vma=False
    )
```

```python
import functools

import jax
import jax.numpy as jnp
from jax import lax
from jax.experimental import pallas as pl
from jax.experimental.pallas import tpu as pltpu
from jax.sharding import PartitionSpec as P

HBM = pl.BlockSpec(memory_space=pltpu.HBM)
VMEM = pl.BlockSpec(memory_space=pltpu.VMEM)
F32 = jnp.float32


def parted(value):
    high = value.astype(jnp.bfloat16)
    return high, (value - high.astype(F32)).astype(jnp.bfloat16)


def product_of(left, right, contract):
    dims = ((contract, (0,)), ((), ()))
    dot = functools.partial(
        lax.dot_general, dimension_numbers=dims, preferred_element_type=F32
    )
    (left_high, left_low), (right_high, right_low) = left, right
    return (
        dot(left_high, right_high)
        + dot(left_high, right_low)
        + dot(left_low, right_high)
    )


def times(left, right):
    return product_of(parted(left), parted(right), (1,))


def transposed_times(left, right):
    return product_of(parted(left), parted(right), (0,))


class Layout:
    def __init__(self, group_width):
        self.width = group_width
        self.pairs = group_width // 2
        self.rounds = (self.pairs - 1) // 2
        self.split_offset = self.pairs - 1
        self.split = 2 * self.rounds
        self.group = self.split + 1
        self.given = self.group + 1

    def offset(self, round_index, side):
        return 2 * round_index + 1 + side


def place():
    index = lax.axis_index("dev")
    return index, index // 2, index % 2


def pack_kernel(layout, flags_in, tiles_in, orbitals_in, packed, flags, flags_sem, sems):
    index, pair, side = place()
    half = orbitals_in.shape[1] // 2
    slots = []
    for r in range(layout.rounds):
        far = pair ^ layout.offset(r, 1 - side)
        slots += [2 * far, 2 * far + 1]
    slots += [2 * (pair ^ layout.split_offset) + 1 - side, layout.width]
    sources = [tiles_in.at[slot] for slot in slots]
    sources += [orbitals_in.at[:, pl.ds(h * half, half)] for h in range(2)]
    copies = [pltpu.make_async_copy(flags_in, flags, flags_sem)]
    for k, source in enumerate(sources):
        copies.append(pltpu.make_async_copy(source, packed.at[k], sems.at[k]))
    for copy in copies:
        copy.start()
    for copy in copies:
        copy.wait()
    for k, slot in enumerate(slots):
        packed[k] = packed[k] * flags[0, slot].astype(F32)


def load_kernel(layout, flags_in, tiles_in, tiles, flags, flags_sem, sem):
    copies = [
        pltpu.make_async_copy(flags_in, flags, flags_sem),
        pltpu.make_async_copy(tiles_in, tiles, sem),
    ]
    for copy in copies:
        copy.start()
    for copy in copies:
        copy.wait()
    for slot in range(layout.width + 1):
        tiles[slot] = tiles[slot] * flags[0, slot].astype(F32)


def orbitals_of(layout, packed):
    return jnp.concatenate([packed[layout.given], packed[layout.given + 1]], axis=1)


def send_split_kernel(layout, tiles, packed, taken, out):
    index, pair, side = place()
    far = pair ^ layout.split_offset

    @pl.when(far > pair)
    def _():
        left = jnp.concatenate([tiles[2 * far + side], taken[layout.split]], axis=0)
        right = jnp.concatenate(
            [orbitals_of(layout, packed), orbitals_of(layout, taken)], axis=0
        )
        out[...] = transposed_times(left, right)

    @pl.when(far < pair)
    def _():
        out[...] = orbitals_of(layout, packed)


def send_group_kernel(layout, tiles, packed, taken, out):
    index, pair, side = place()

    @pl.when(side == 0)
    def _():
        out[0] = transposed_times(tiles[layout.width], orbitals_of(layout, packed))
        out[1] = transposed_times(taken[layout.group], orbitals_of(layout, taken))

    @pl.when(side == 1)
    def _():
        out[0] = orbitals_of(layout, taken)
        out[1] = orbitals_of(layout, packed)


def send_full_kernel(layout, tiles, packed, taken, *outs):
    index, pair, side = place()
    own, other = orbitals_of(layout, packed), orbitals_of(layout, taken)
    for r in range(layout.rounds):
        far = pair ^ layout.offset(r, side)
        out = outs[r]

        @pl.when(far > pair)
        def _():
            right = parted(jnp.concatenate([own, other], axis=0))
            for k in range(2):
                left = jnp.concatenate([tiles[2 * far + k], taken[2 * r + k]], axis=0)
                out[k] = product_of(parted(left), right, (0,))

        @pl.when(far < pair)
        def _():
            out[0] = jnp.where(side == 0, own, other)
            out[1] = jnp.where(side == 0, other, own)


def near_kernel(layout, tiles, packed, taken, arrived, mine, others):
    index, pair, side = place()
    own, other = orbitals_of(layout, packed), orbitals_of(layout, taken)
    beside = tiles[index ^ 1]
    row = jnp.concatenate([tiles[index], beside], axis=1)
    mine[...] = times(row, jnp.concatenate([own, other], axis=0))
    others[...] = transposed_times(beside, own)
    far = pair ^ layout.split_offset

    @pl.when(far > pair)
    def _():
        left = jnp.concatenate([tiles[2 * far + side], taken[layout.split]], axis=0)
        terms = times(left, arrived[...])
        order = beside.shape[0]
        mine[...] += terms[:order]
        others[...] += terms[order:]

    @pl.when(far < pair)
    def _():
        mine[...] += arrived[...]


def group_kernel(layout, tiles, taken, mine_in, others_in, arrived, mine, others):
    index, pair, side = place()

    @pl.when(side == 0)
    def _():
        mine[...] = mine_in[...] + arrived[0]
        others[...] = others_in[...] + arrived[1]

    @pl.when(side == 1)
    def _():
        mine[...] = mine_in[...] + times(tiles[layout.width], arrived[1])
        others[...] = others_in[...] + times(taken[layout.group], arrived[0])


def full_kernel(layout, tiles, taken, mine_in, others_in, *refs):
    index, pair, side = place()
    arrived, mine, others = refs[:-2], refs[-2], refs[-1]
    order = tiles.shape[1]
    mine[...] = mine_in[...]
    others[...] = others_in[...]
    for r in range(layout.rounds):
        far = pair ^ layout.offset(r, side)
        came = arrived[r]

        @pl.when(far > pair)
        def _():
            upper = jnp.concatenate([tiles[2 * far], tiles[2 * far + 1]], axis=1)
            lower = jnp.concatenate([taken[2 * r], taken[2 * r + 1]], axis=1)
            right = jnp.concatenate([came[0], came[1]], axis=0)
            terms = times(jnp.concatenate([upper, lower], axis=0), right)
            mine[...] += terms[:order]
            others[...] += terms[order:]

        @pl.when(far < pair)
        def _():
            mine[...] += came[side]
            others[...] += came[1 - side]


def call(body, outs, operands, specs=None, scratch=(), flops=0):
    return pl.pallas_call(
        body,
        out_shape=outs,
        in_specs=specs or [VMEM] * len(operands),
        out_specs=jax.tree.map(lambda _: VMEM, outs),
        scratch_shapes=scratch,
        cost_estimate=pl.CostEstimate(
            flops=flops, bytes_accessed=0, transcendentals=0
        ),
        compiler_params=pltpu.CompilerParams(vmem_limit_bytes=32 * 1024 * 1024),
    )(*operands)


def per_device(stored_tiles, tile_flags, orbitals):
    group_width = lax.axis_size("dev")
    groups = lax.axis_size("grp")
    layout = Layout(group_width)
    order, columns = orbitals.shape
    block = jax.ShapeDtypeStruct((order, columns), F32)
    two = jax.ShapeDtypeStruct((2, order, columns), F32)
    partners = [(i, i ^ 1) for i in range(group_width)]
    flags, stored, held = (
        pltpu.with_memory_space_constraint(operand, pltpu.HBM)
        for operand in (tile_flags, stored_tiles[0], orbitals)
    )
    flags_scratch = pltpu.SMEM(tile_flags.shape, jnp.int32)
    semaphore = pltpu.SemaphoreType.DMA

    packed = call(
        functools.partial(pack_kernel, layout),
        jax.ShapeDtypeStruct((layout.given + 2, order, order), F32),
        [flags, stored, held],
        [HBM] * 3,
        [flags_scratch, semaphore, semaphore((layout.given + 2,))],
    )
    taken = lax.ppermute(packed, "dev", partners)
    tiles = call(
        functools.partial(load_kernel, layout),
        jax.ShapeDtypeStruct(stored.shape, F32),
        [flags, stored],
        [HBM] * 2,
        [flags_scratch, semaphore, semaphore],
        flops=10**9,
    )

    split = call(
        functools.partial(send_split_kernel, layout), block, [tiles, packed, taken]
    )
    swaps = [(i, i ^ (2 * layout.split_offset)) for i in range(group_width)]
    split_arrived = lax.ppermute(split, "dev", swaps)

    across = call(
        functools.partial(send_group_kernel, layout), two, [tiles, packed, taken]
    )
    shifts = []
    for g in range(groups):
        for i in range(group_width):
            to = g + 1 - 2 * (i % 2)
            if 0 <= to < groups:
                shifts.append((g * group_width + i, to * group_width + i))
    group_arrived = lax.ppermute(across, ("grp", "dev"), shifts)

    full = call(
        functools.partial(send_full_kernel, layout),
        [two] * layout.rounds,
        [tiles, packed, taken],
    )
    full_arrived = []
    for r in range(layout.rounds):
        swaps = [
            (i, i ^ (2 * layout.offset(r, i % 2))) for i in range(group_width)
        ]
        full_arrived.append(lax.ppermute(full[r], "dev", swaps))

    mine, others = call(
        functools.partial(near_kernel, layout),
        [block, block],
        [tiles, packed, taken, split_arrived],
        flops=10**10,
    )
    mine, others = call(
        functools.partial(group_kernel, layout),
        [block, block],
        [tiles, taken, mine, others, group_arrived],
        flops=10**10,
    )
    mine, others = call(
        functools.partial(full_kernel, layout),
        [block, block],
        [tiles, taken, mine, others, *full_arrived],
    )
    return mine + lax.ppermute(others, "dev", partners)


def solution(mesh):
    in_specs = (
        P(("grp", "dev"), None, None, None),
        P(("grp", "dev"), None),
        P(("grp", "dev"), None),
    )
    out_specs = P(("grp", "dev"), None)
    return jax.shard_map(
        per_device, mesh=mesh, in_specs=in_specs, out_specs=out_specs, check_vma=False
    )
```

```python
import functools

import jax
import jax.numpy as jnp
from jax import lax
from jax.experimental import pallas as pl
from jax.experimental.pallas import tpu as pltpu
from jax.sharding import PartitionSpec as P

HBM = pl.BlockSpec(memory_space=pltpu.HBM)
VMEM = pl.BlockSpec(memory_space=pltpu.VMEM)
F32 = jnp.float32


def parted(value):
    high = value.astype(jnp.bfloat16)
    return high, (value - high.astype(F32)).astype(jnp.bfloat16)


def product_of(left, right, contract):
    dims = ((contract, (0,)), ((), ()))
    dot = functools.partial(
        lax.dot_general, dimension_numbers=dims, preferred_element_type=F32
    )
    (left_high, left_low), (right_high, right_low) = left, right
    return (
        dot(left_high, right_high)
        + dot(left_high, right_low)
        + dot(left_low, right_high)
    )


def times(left, right):
    return product_of(parted(left), parted(right), (1,))


def transposed_times(left, right):
    return product_of(parted(left), parted(right), (0,))


class Layout:
    def __init__(self, group_width):
        self.width = group_width
        self.pairs = group_width // 2
        self.rounds = (self.pairs - 1) // 2
        self.last_offset = self.pairs - 1
        self.last = 2 * self.rounds
        self.given = self.last + 2

    def offset(self, round_index, side):
        return 2 * round_index + 1 + side


def place():
    index = lax.axis_index("dev")
    return index, index // 2, index % 2


def pack_kernel(
    layout, flags_in, tiles_in, orbitals_in, packed, tiles, orbitals,
    flags, flags_sem, given_sem, half_sem, tiles_sem, orbitals_sem,
):
    index, pair, side = place()
    half = orbitals.shape[1] // 2
    slots = []
    for r in range(layout.rounds):
        far = pair ^ layout.offset(r, 1 - side)
        slots += [2 * far, 2 * far + 1]
    far = pair ^ layout.last_offset
    slots += [jnp.where(side == 1, 2 * far, layout.width), 2 * far + 1]

    flags_copy = pltpu.make_async_copy(flags_in, flags, flags_sem)
    flags_copy.start()
    given_copies = []
    for k, slot in enumerate(slots):
        given_copies.append(
            pltpu.make_async_copy(tiles_in.at[slot], packed.at[k], given_sem.at[k])
        )
        given_copies[-1].start()
    half_copies = []
    for h in range(2):
        half_copies.append(
            pltpu.make_async_copy(
                orbitals_in.at[:, pl.ds(h * half, half)],
                packed.at[layout.given + h],
                half_sem.at[h],
            )
        )
        half_copies[-1].start()
    tiles_copy = pltpu.make_async_copy(tiles_in, tiles, tiles_sem)
    tiles_copy.start()
    orbitals_copy = pltpu.make_async_copy(orbitals_in, orbitals, orbitals_sem)
    orbitals_copy.start()

    flags_copy.wait()
    for k, slot in enumerate(slots):
        given_copies[k].wait()
        packed[k] = packed[k] * flags[0, slot].astype(F32)
    tiles_copy.wait()
    for slot in range(layout.width + 1):
        tiles[slot] = tiles[slot] * flags[0, slot].astype(F32)
    for copy in half_copies:
        copy.wait()
    orbitals_copy.wait()


def both_orbitals(layout, orbitals, taken):
    other = jnp.concatenate(
        [taken[layout.given], taken[layout.given + 1]], axis=1
    )
    return orbitals[...], other


def send_pair(layout, far, pair, side, at, tiles, taken, own, other, out):
    @pl.when(far > pair)
    def _():
        right = parted(jnp.concatenate([own, other], axis=0))
        for k in range(2):
            stack = jnp.concatenate([tiles[2 * far + k], taken[at + k]], axis=0)
            out[k] = product_of(parted(stack), right, (0,))

    @pl.when(far < pair)
    def _():
        out[0] = jnp.where(side == 0, own, other)
        out[1] = jnp.where(side == 0, other, own)


def send_full_kernel(layout, tiles, orbitals, taken, *outs):
    index, pair, side = place()
    own, other = both_orbitals(layout, orbitals, taken)
    for r in range(layout.rounds):
        far = pair ^ layout.offset(r, side)
        send_pair(layout, far, pair, side, 2 * r, tiles, taken, own, other, outs[r])


def send_last_kernel(layout, tiles, orbitals, taken, out):
    index, pair, side = place()
    own, other = both_orbitals(layout, orbitals, taken)

    @pl.when(side == 0)
    def _():
        far = pair ^ layout.last_offset
        send_pair(layout, far, pair, side, layout.last, tiles, taken, own, other, out)

    @pl.when(side == 1)
    def _():
        out[0] = transposed_times(taken[layout.last], other)
        out[1] = transposed_times(tiles[layout.width], own)


def take_pair(layout, far, pair, side, at, tiles, taken, arrived, mine_out, other_out):
    order = tiles.shape[1]

    @pl.when(far > pair)
    def _():
        mine = jnp.concatenate([tiles[2 * far], tiles[2 * far + 1]], axis=1)
        others = jnp.concatenate([taken[at], taken[at + 1]], axis=1)
        right = jnp.concatenate([arrived[0], arrived[1]], axis=0)
        terms = times(jnp.concatenate([mine, others], axis=0), right)
        mine_out[...] += terms[:order]
        other_out[...] += terms[order:]

    @pl.when(far < pair)
    def _():
        mine_out[...] += arrived[side]
        other_out[...] += arrived[1 - side]


def near_kernel(layout, tiles, orbitals, taken, following, mine_out, other_out):
    index, pair, side = place()
    own, other = both_orbitals(layout, orbitals, taken)
    beside = tiles[index ^ 1]
    row = jnp.concatenate([tiles[index], beside], axis=1)
    mine_out[...] = times(row, jnp.concatenate([own, other], axis=0)) + times(
        tiles[layout.width], following[...]
    )
    other_out[...] = transposed_times(beside, own)


def gather_kernel(layout, tiles, taken, mine_in, other_in, *refs):
    index, pair, side = place()
    arrived, mine_out, other_out = refs[:-2], refs[-2], refs[-1]
    mine_out[...] = mine_in[...]
    other_out[...] = other_in[...]
    for r in range(layout.rounds):
        far = pair ^ layout.offset(r, side)
        take_pair(
            layout, far, pair, side, 2 * r, tiles, taken, arrived[r], mine_out, other_out
        )


def last_kernel(layout, tiles, taken, mine_in, other_in, arrived, mine_out, other_out):
    index, pair, side = place()
    mine_out[...] = mine_in[...]
    other_out[...] = other_in[...]

    @pl.when(side == 0)
    def _():
        far = pair ^ layout.last_offset
        take_pair(
            layout, far, pair, side, layout.last, tiles, taken, arrived, mine_out, other_out
        )

    @pl.when(side == 1)
    def _():
        mine_out[...] += arrived[1]
        other_out[...] += arrived[0]


def call(body, outs, operands, specs=None, scratch=(), flops=0):
    return pl.pallas_call(
        body,
        out_shape=outs,
        in_specs=specs or [VMEM] * len(operands),
        out_specs=jax.tree.map(lambda _: VMEM, outs),
        scratch_shapes=scratch,
        cost_estimate=pl.CostEstimate(
            flops=flops, bytes_accessed=0, transcendentals=0
        ),
        compiler_params=pltpu.CompilerParams(vmem_limit_bytes=32 * 1024 * 1024),
    )(*operands)


def per_device(stored_tiles, tile_flags, orbitals):
    group_width = lax.axis_size("dev")
    groups = lax.axis_size("grp")
    layout = Layout(group_width)
    order, columns = orbitals.shape
    block = jax.ShapeDtypeStruct((order, columns), F32)
    two = jax.ShapeDtypeStruct((2, order, columns), F32)
    partners = [(i, i ^ 1) for i in range(group_width)]

    packed, tiles, held = call(
        functools.partial(pack_kernel, layout),
        [
            jax.ShapeDtypeStruct((layout.given + 2, order, order), F32),
            jax.ShapeDtypeStruct((group_width + 1, order, order), F32),
            block,
        ],
        [
            pltpu.with_memory_space_constraint(operand, pltpu.HBM)
            for operand in (tile_flags, stored_tiles[0], orbitals)
        ],
        [HBM, HBM, HBM],
        [
            pltpu.SMEM(tile_flags.shape, jnp.int32),
            pltpu.SemaphoreType.DMA,
            pltpu.SemaphoreType.DMA((layout.given,)),
            pltpu.SemaphoreType.DMA((2,)),
            pltpu.SemaphoreType.DMA,
            pltpu.SemaphoreType.DMA,
        ],
    )
    taken = lax.ppermute(packed, "dev", partners)
    downward = [(g, (g - 1) % groups) for g in range(groups)]
    following = lax.ppermute(held, "grp", downward)

    full = call(
        functools.partial(send_full_kernel, layout),
        [two] * layout.rounds,
        [tiles, held, taken],
    )
    arrived = []
    for r in range(layout.rounds):
        swaps = [
            (i, i ^ (2 * layout.offset(r, i % 2))) for i in range(group_width)
        ]
        arrived.append(lax.ppermute(full[r], "dev", swaps))

    last = call(
        functools.partial(send_last_kernel, layout), two, [tiles, held, taken]
    )
    moves = []
    for g in range(groups):
        for i in range(group_width):
            if i % 2 == 0:
                moves.append((g, i, g, i ^ (2 * layout.last_offset)))
            else:
                moves.append((g, i, (g + 1) % groups, i))
    moves = [(g * group_width + i, h * group_width + j) for g, i, h, j in moves]
    last_arrived = lax.ppermute(last, ("grp", "dev"), moves)

    mine, other = call(
        functools.partial(near_kernel, layout),
        [block, block],
        [tiles, held, taken, following],
        flops=10**10,
    )
    mine, other = call(
        functools.partial(gather_kernel, layout),
        [block, block],
        [tiles, taken, mine, other, *arrived],
        flops=10**8,
    )
    mine, other = call(
        functools.partial(last_kernel, layout),
        [block, block],
        [tiles, taken, mine, other, last_arrived],
    )
    return mine + lax.ppermute(other, "dev", partners)


def solution(mesh):
    in_specs = (
        P(("grp", "dev"), None, None, None),
        P(("grp", "dev"), None),
        P(("grp", "dev"), None),
    )
    out_specs = P(("grp", "dev"), None)
    return jax.shard_map(
        per_device, mesh=mesh, in_specs=in_specs, out_specs=out_specs, check_vma=False
    )
```

```python
import functools

import jax
import jax.numpy as jnp
from jax import lax
from jax.experimental import pallas as pl
from jax.experimental.pallas import tpu as pltpu
from jax.sharding import PartitionSpec as P

HBM = pl.BlockSpec(memory_space=pltpu.HBM)
VMEM = pl.BlockSpec(memory_space=pltpu.VMEM)
F32 = jnp.float32


def parted(value):
    high = value.astype(jnp.bfloat16)
    return high, (value - high.astype(F32)).astype(jnp.bfloat16)


def product_of(left, right, contract):
    dims = ((contract, (0,)), ((), ()))
    dot = functools.partial(
        lax.dot_general, dimension_numbers=dims, preferred_element_type=F32
    )
    (left_high, left_low), (right_high, right_low) = left, right
    return (
        dot(left_high, right_high)
        + dot(left_high, right_low)
        + dot(left_low, right_high)
    )


def times(left, right):
    return product_of(parted(left), parted(right), (1,))


def transposed_times(left, right):
    return product_of(parted(left), parted(right), (0,))


class Layout:
    def __init__(self, group_width):
        self.width = group_width
        self.pairs = group_width // 2
        self.rounds = (self.pairs - 1) // 2
        self.split_offset = self.pairs - 1
        self.split = 2 * self.rounds
        self.given = self.split + 1

    def offset(self, round_index, side):
        return 2 * round_index + 1 + side


def place():
    index = lax.axis_index("dev")
    return index, index // 2, index % 2


def pack_kernel(layout, flags_in, tiles_in, orbitals_in, packed, flags, flags_sem, sems):
    index, pair, side = place()
    half = orbitals_in.shape[1] // 2
    slots = []
    for r in range(layout.rounds):
        far = pair ^ layout.offset(r, 1 - side)
        slots += [2 * far, 2 * far + 1]
    slots.append(2 * (pair ^ layout.split_offset) + 1 - side)
    sources = [tiles_in.at[slot] for slot in slots]
    sources += [orbitals_in.at[:, pl.ds(h * half, half)] for h in range(2)]
    copies = [pltpu.make_async_copy(flags_in, flags, flags_sem)]
    for k, source in enumerate(sources):
        copies.append(pltpu.make_async_copy(source, packed.at[k], sems.at[k]))
    for copy in copies:
        copy.start()
    for copy in copies:
        copy.wait()
    for k, slot in enumerate(slots):
        packed[k] = packed[k] * flags[0, slot].astype(F32)


def load_kernel(layout, flags_in, tiles_in, tiles, flags, flags_sem, sem):
    copies = [
        pltpu.make_async_copy(flags_in, flags, flags_sem),
        pltpu.make_async_copy(tiles_in, tiles, sem),
    ]
    for copy in copies:
        copy.start()
    for copy in copies:
        copy.wait()
    for slot in range(layout.width + 1):
        tiles[slot] = tiles[slot] * flags[0, slot].astype(F32)


def orbitals_of(layout, packed):
    return jnp.concatenate([packed[layout.given], packed[layout.given + 1]], axis=1)


def send_full_kernel(layout, tiles, packed, taken, *outs):
    index, pair, side = place()
    own, other = orbitals_of(layout, packed), orbitals_of(layout, taken)
    for r in range(layout.rounds):
        far = pair ^ layout.offset(r, side)
        out = outs[r]

        @pl.when(far > pair)
        def _():
            right = parted(jnp.concatenate([own, other], axis=0))
            for k in range(2):
                left = jnp.concatenate([tiles[2 * far + k], taken[2 * r + k]], axis=0)
                out[k] = product_of(parted(left), right, (0,))

        @pl.when(far < pair)
        def _():
            out[0] = jnp.where(side == 0, own, other)
            out[1] = jnp.where(side == 0, other, own)


def send_across_kernel(layout, tiles, packed, even_out, odd_out):
    upper = lax.axis_index("grp") % 2
    own = orbitals_of(layout, packed)
    term = transposed_times(tiles[layout.width], own)
    even_out[...] = jnp.where(upper == 0, term, own)
    odd_out[...] = jnp.where(upper == 1, term, own)


def send_split_kernel(layout, tiles, packed, taken, out):
    index, pair, side = place()
    far = pair ^ layout.split_offset

    @pl.when(far > pair)
    def _():
        left = jnp.concatenate([tiles[2 * far + side], taken[layout.split]], axis=0)
        right = jnp.concatenate(
            [orbitals_of(layout, packed), orbitals_of(layout, taken)], axis=0
        )
        out[...] = transposed_times(left, right)

    @pl.when(far < pair)
    def _():
        out[...] = orbitals_of(layout, packed)


def near_kernel(layout, tiles, packed, taken, mine, others):
    index, pair, side = place()
    own, other = orbitals_of(layout, packed), orbitals_of(layout, taken)
    beside = tiles[index ^ 1]
    row = jnp.concatenate([tiles[index], beside], axis=1)
    mine[...] = times(row, jnp.concatenate([own, other], axis=0))
    others[...] = transposed_times(beside, own)


def full_kernel(layout, tiles, taken, mine_in, others_in, *refs):
    index, pair, side = place()
    arrived, mine, others = refs[:-2], refs[-2], refs[-1]
    order = tiles.shape[1]
    mine[...] = mine_in[...]
    others[...] = others_in[...]
    for r in range(layout.rounds):
        far = pair ^ layout.offset(r, side)
        came = arrived[r]

        @pl.when(far > pair)
        def _():
            upper = jnp.concatenate([tiles[2 * far], tiles[2 * far + 1]], axis=1)
            lower = jnp.concatenate([taken[2 * r], taken[2 * r + 1]], axis=1)
            right = jnp.concatenate([came[0], came[1]], axis=0)
            terms = times(jnp.concatenate([upper, lower], axis=0), right)
            mine[...] += terms[:order]
            others[...] += terms[order:]

        @pl.when(far < pair)
        def _():
            mine[...] += came[side]
            others[...] += came[1 - side]


def split_kernel(layout, tiles, taken, mine_in, others_in, arrived, mine, others):
    index, pair, side = place()
    far = pair ^ layout.split_offset

    @pl.when(far > pair)
    def _():
        left = jnp.concatenate([tiles[2 * far + side], taken[layout.split]], axis=0)
        terms = times(left, arrived[...])
        order = tiles.shape[1]
        mine[...] = mine_in[...] + terms[:order]
        others[...] = others_in[...] + terms[order:]

    @pl.when(far < pair)
    def _():
        mine[...] = mine_in[...] + arrived[...]
        others[...] = others_in[...]


def across_kernel(layout, lower_parity, tiles, mine_in, arrived, mine):
    group = lax.axis_index("grp")

    @pl.when(group % 2 == lower_parity)
    def _():
        mine[...] = mine_in[...] + times(tiles[layout.width], arrived[...])

    @pl.when(group % 2 != lower_parity)
    def _():
        mine[...] = mine_in[...] + jnp.where(group > 0, arrived[...], 0.0)


def call(body, outs, operands, specs=None, scratch=(), flops=0):
    return pl.pallas_call(
        body,
        out_shape=outs,
        in_specs=specs or [VMEM] * len(operands),
        out_specs=jax.tree.map(lambda _: VMEM, outs),
        scratch_shapes=scratch,
        cost_estimate=pl.CostEstimate(
            flops=flops, bytes_accessed=0, transcendentals=0
        ),
        compiler_params=pltpu.CompilerParams(vmem_limit_bytes=32 * 1024 * 1024),
    )(*operands)


def exchange(block, group_width, groups, lower_parity):
    moves = []
    for g in range(groups):
        to = g + 1 if g % 2 == lower_parity else g - 1
        for i in range(group_width):
            if 0 <= to < groups:
                moves.append((g * group_width + i, to * group_width + i))
            else:
                moves.append((g * group_width + i, g * group_width + (i ^ 1)))
    return lax.ppermute(block, ("grp", "dev"), moves)


def per_device(stored_tiles, tile_flags, orbitals):
    group_width = lax.axis_size("dev")
    groups = lax.axis_size("grp")
    layout = Layout(group_width)
    order, columns = orbitals.shape
    block = jax.ShapeDtypeStruct((order, columns), F32)
    two = jax.ShapeDtypeStruct((2, order, columns), F32)
    partners = [(i, i ^ 1) for i in range(group_width)]
    flags, stored, held = (
        pltpu.with_memory_space_constraint(operand, pltpu.HBM)
        for operand in (tile_flags, stored_tiles[0], orbitals)
    )
    flags_scratch = pltpu.SMEM(tile_flags.shape, jnp.int32)
    semaphore = pltpu.SemaphoreType.DMA

    packed = call(
        functools.partial(pack_kernel, layout),
        jax.ShapeDtypeStruct((layout.given + 2, order, order), F32),
        [flags, stored, held],
        [HBM] * 3,
        [flags_scratch, semaphore, semaphore((layout.given + 2,))],
    )
    taken = lax.ppermute(packed, "dev", partners)
    tiles = call(
        functools.partial(load_kernel, layout),
        jax.ShapeDtypeStruct(stored.shape, F32),
        [flags, stored],
        [HBM] * 2,
        [flags_scratch, semaphore, semaphore],
        flops=10**9,
    )

    full = call(
        functools.partial(send_full_kernel, layout),
        [two] * layout.rounds,
        [tiles, packed, taken],
    )
    full_arrived = []
    for r in range(layout.rounds):
        swaps = [
            (i, i ^ (2 * layout.offset(r, i % 2))) for i in range(group_width)
        ]
        full_arrived.append(lax.ppermute(full[r], "dev", swaps))

    even, odd = call(
        functools.partial(send_across_kernel, layout), [block, block], [tiles, packed]
    )
    even_arrived = exchange(even, group_width, groups, 0)

    split = call(
        functools.partial(send_split_kernel, layout), block, [tiles, packed, taken]
    )
    swaps = [(i, i ^ (2 * layout.split_offset)) for i in range(group_width)]
    split_arrived = lax.ppermute(split, "dev", swaps)

    odd_arrived = exchange(odd, group_width, groups, 1)

    mine, others = call(
        functools.partial(near_kernel, layout), [block, block], [tiles, packed, taken]
    )
    mine, others = call(
        functools.partial(full_kernel, layout),
        [block, block],
        [tiles, taken, mine, others, *full_arrived],
    )
    mine = call(
        functools.partial(across_kernel, layout, 0),
        block,
        [tiles, mine, even_arrived],
    )
    mine, others = call(
        functools.partial(split_kernel, layout),
        [block, block],
        [tiles, taken, mine, others, split_arrived],
        flops=10**10,
    )
    returned = lax.ppermute(others, "dev", partners)
    mine = call(
        functools.partial(across_kernel, layout, 1),
        block,
        [tiles, mine, odd_arrived],
    )
    return mine + returned


def solution(mesh):
    in_specs = (
        P(("grp", "dev"), None, None, None),
        P(("grp", "dev"), None),
        P(("grp", "dev"), None),
    )
    out_specs = P(("grp", "dev"), None)
    return jax.shard_map(
        per_device, mesh=mesh, in_specs=in_specs, out_specs=out_specs, check_vma=False
    )
```

```python
import functools

import jax
import jax.numpy as jnp
from jax import lax
from jax.experimental import pallas as pl
from jax.experimental.pallas import tpu as pltpu
from jax.sharding import PartitionSpec as P

HBM = pl.BlockSpec(memory_space=pltpu.HBM)
VMEM = pl.BlockSpec(memory_space=pltpu.VMEM)
F32 = jnp.float32


def parted(value):
    high = value.astype(jnp.bfloat16)
    return high, (value - high.astype(F32)).astype(jnp.bfloat16)


def product_of(left, right, contract):
    dims = ((contract, (0,)), ((), ()))
    dot = functools.partial(
        lax.dot_general, dimension_numbers=dims, preferred_element_type=F32
    )
    (left_high, left_low), (right_high, right_low) = left, right
    return (
        dot(left_high, right_high)
        + dot(left_high, right_low)
        + dot(left_low, right_high)
    )


def times(left, right):
    return product_of(parted(left), parted(right), (1,))


def transposed_times(left, right):
    return product_of(parted(left), parted(right), (0,))


class Layout:
    def __init__(self, group_width):
        self.width = group_width
        self.pairs = group_width // 2
        self.rounds = (self.pairs - 1) // 2
        self.split_offset = self.pairs - 1
        self.split = 2 * self.rounds
        self.given = self.split + 1

    def offset(self, round_index, side):
        return 2 * round_index + 1 + side


def place():
    index = lax.axis_index("dev")
    return index, index // 2, index % 2


def pack_kernel(layout, flags_in, tiles_in, orbitals_in, packed, flags, flags_sem, sems):
    index, pair, side = place()
    half = orbitals_in.shape[1] // 2
    slots = []
    for r in range(layout.rounds):
        far = pair ^ layout.offset(r, 1 - side)
        slots += [2 * far, 2 * far + 1]
    slots.append(2 * (pair ^ layout.split_offset) + 1 - side)
    sources = [tiles_in.at[slot] for slot in slots]
    sources += [orbitals_in.at[:, pl.ds(h * half, half)] for h in range(2)]
    copies = [pltpu.make_async_copy(flags_in, flags, flags_sem)]
    for k, source in enumerate(sources):
        copies.append(pltpu.make_async_copy(source, packed.at[k], sems.at[k]))
    for copy in copies:
        copy.start()
    for copy in copies:
        copy.wait()
    for k, slot in enumerate(slots):
        packed[k] = packed[k] * flags[0, slot].astype(F32)


def load_kernel(layout, flags_in, tiles_in, tiles, flags, flags_sem, sem):
    copies = [
        pltpu.make_async_copy(flags_in, flags, flags_sem),
        pltpu.make_async_copy(tiles_in, tiles, sem),
    ]
    for copy in copies:
        copy.start()
    for copy in copies:
        copy.wait()
    for slot in range(layout.width + 1):
        tiles[slot] = tiles[slot] * flags[0, slot].astype(F32)


def orbitals_of(layout, packed):
    return jnp.concatenate([packed[layout.given], packed[layout.given + 1]], axis=1)


def send_full_kernel(layout, tiles, packed, taken, *outs):
    index, pair, side = place()
    own, other = orbitals_of(layout, packed), orbitals_of(layout, taken)
    for r in range(layout.rounds):
        far = pair ^ layout.offset(r, side)
        out = outs[r]

        @pl.when(far > pair)
        def _():
            right = parted(jnp.concatenate([own, other], axis=0))
            for k in range(2):
                left = jnp.concatenate([tiles[2 * far + k], taken[2 * r + k]], axis=0)
                out[k] = product_of(parted(left), right, (0,))

        @pl.when(far < pair)
        def _():
            out[0] = jnp.where(side == 0, own, other)
            out[1] = jnp.where(side == 0, other, own)


def send_across_kernel(layout, tiles, packed, even_out, odd_out):
    upper = lax.axis_index("grp") % 2
    own = orbitals_of(layout, packed)
    term = transposed_times(tiles[layout.width], own)
    even_out[...] = jnp.where(upper == 0, term, own)
    odd_out[...] = jnp.where(upper == 1, term, own)


def send_split_kernel(layout, tiles, packed, taken, out):
    index, pair, side = place()
    far = pair ^ layout.split_offset

    @pl.when(far > pair)
    def _():
        left = jnp.concatenate([tiles[2 * far + side], taken[layout.split]], axis=0)
        right = jnp.concatenate(
            [orbitals_of(layout, packed), orbitals_of(layout, taken)], axis=0
        )
        out[...] = transposed_times(left, right)

    @pl.when(far < pair)
    def _():
        out[...] = orbitals_of(layout, packed)


def near_kernel(layout, tiles, packed, taken, mine, others):
    index, pair, side = place()
    own, other = orbitals_of(layout, packed), orbitals_of(layout, taken)
    beside = tiles[index ^ 1]
    row = jnp.concatenate([tiles[index], beside], axis=1)
    mine[...] = times(row, jnp.concatenate([own, other], axis=0))
    others[...] = transposed_times(beside, own)


def full_kernel(layout, tiles, taken, mine_in, others_in, *refs):
    index, pair, side = place()
    arrived, mine, others = refs[:-2], refs[-2], refs[-1]
    order = tiles.shape[1]
    mine[...] = mine_in[...]
    others[...] = others_in[...]
    for r in range(layout.rounds):
        far = pair ^ layout.offset(r, side)
        came = arrived[r]

        @pl.when(far > pair)
        def _():
            upper = jnp.concatenate([tiles[2 * far], tiles[2 * far + 1]], axis=1)
            lower = jnp.concatenate([taken[2 * r], taken[2 * r + 1]], axis=1)
            right = jnp.concatenate([came[0], came[1]], axis=0)
            terms = times(jnp.concatenate([upper, lower], axis=0), right)
            mine[...] += terms[:order]
            others[...] += terms[order:]

        @pl.when(far < pair)
        def _():
            mine[...] += came[side]
            others[...] += came[1 - side]


def back_kernel(layout, taken, others_in, arrived, others):
    index, pair, side = place()
    far = pair ^ layout.split_offset

    @pl.when(far > pair)
    def _():
        others[...] = others_in[...] + times(taken[layout.split], arrived[...])

    @pl.when(far < pair)
    def _():
        others[...] = others_in[...]


def mine_kernel(layout, tiles, mine_in, arrived, even_in, odd_in, mine):
    index, pair, side = place()
    group = lax.axis_index("grp")
    far = pair ^ layout.split_offset
    even = group % 2 == 0
    following = jnp.where(even, even_in[...], odd_in[...])
    previous = jnp.where(even, odd_in[...], even_in[...])
    mine[...] = (
        mine_in[...]
        + times(tiles[layout.width], following)
        + jnp.where(group > 0, previous, 0.0)
    )

    @pl.when(far > pair)
    def _():
        mine[...] += times(tiles[2 * far + side], arrived[...])

    @pl.when(far < pair)
    def _():
        mine[...] += arrived[...]


def call(body, outs, operands, specs=None, scratch=(), flops=0):
    return pl.pallas_call(
        body,
        out_shape=outs,
        in_specs=specs or [VMEM] * len(operands),
        out_specs=jax.tree.map(lambda _: VMEM, outs),
        scratch_shapes=scratch,
        cost_estimate=pl.CostEstimate(
            flops=flops, bytes_accessed=0, transcendentals=0
        ),
        compiler_params=pltpu.CompilerParams(vmem_limit_bytes=32 * 1024 * 1024),
    )(*operands)


def exchange(block, group_width, groups, lower_parity):
    moves = []
    for g in range(groups):
        to = g + 1 if g % 2 == lower_parity else g - 1
        for i in range(group_width):
            if 0 <= to < groups:
                moves.append((g * group_width + i, to * group_width + i))
            else:
                moves.append((g * group_width + i, g * group_width + (i ^ 1)))
    return lax.ppermute(block, ("grp", "dev"), moves)


def per_device(stored_tiles, tile_flags, orbitals):
    group_width = lax.axis_size("dev")
    groups = lax.axis_size("grp")
    layout = Layout(group_width)
    order, columns = orbitals.shape
    block = jax.ShapeDtypeStruct((order, columns), F32)
    two = jax.ShapeDtypeStruct((2, order, columns), F32)
    partners = [(i, i ^ 1) for i in range(group_width)]
    flags, stored, held = (
        pltpu.with_memory_space_constraint(operand, pltpu.HBM)
        for operand in (tile_flags, stored_tiles[0], orbitals)
    )
    flags_scratch = pltpu.SMEM(tile_flags.shape, jnp.int32)
    semaphore = pltpu.SemaphoreType.DMA

    packed = call(
        functools.partial(pack_kernel, layout),
        jax.ShapeDtypeStruct((layout.given + 2, order, order), F32),
        [flags, stored, held],
        [HBM] * 3,
        [flags_scratch, semaphore, semaphore((layout.given + 2,))],
    )
    taken = lax.ppermute(packed, "dev", partners)
    tiles = call(
        functools.partial(load_kernel, layout),
        jax.ShapeDtypeStruct(stored.shape, F32),
        [flags, stored],
        [HBM] * 2,
        [flags_scratch, semaphore, semaphore],
        flops=10**9,
    )

    full = call(
        functools.partial(send_full_kernel, layout),
        [two] * layout.rounds,
        [tiles, packed, taken],
    )
    full_arrived = []
    for r in range(layout.rounds):
        swaps = [
            (i, i ^ (2 * layout.offset(r, i % 2))) for i in range(group_width)
        ]
        full_arrived.append(lax.ppermute(full[r], "dev", swaps))

    split = call(
        functools.partial(send_split_kernel, layout), block, [tiles, packed, taken]
    )
    swaps = [(i, i ^ (2 * layout.split_offset)) for i in range(group_width)]
    split_arrived = lax.ppermute(split, "dev", swaps)

    even, odd = call(
        functools.partial(send_across_kernel, layout), [block, block], [tiles, packed]
    )
    even_arrived = exchange(even, group_width, groups, 0)
    odd_arrived = exchange(odd, group_width, groups, 1)

    mine, others = call(
        functools.partial(near_kernel, layout), [block, block], [tiles, packed, taken]
    )
    mine, others = call(
        functools.partial(full_kernel, layout),
        [block, block],
        [tiles, taken, mine, others, *full_arrived],
    )
    others = call(
        functools.partial(back_kernel, layout),
        block,
        [taken, others, split_arrived],
    )
    returned = lax.ppermute(others, "dev", partners)
    mine = call(
        functools.partial(mine_kernel, layout),
        block,
        [tiles, mine, split_arrived, even_arrived, odd_arrived],
    )
    return mine + returned


def solution(mesh):
    in_specs = (
        P(("grp", "dev"), None, None, None),
        P(("grp", "dev"), None),
        P(("grp", "dev"), None),
    )
    out_specs = P(("grp", "dev"), None)
    return jax.shard_map(
        per_device, mesh=mesh, in_specs=in_specs, out_specs=out_specs, check_vma=False
    )
```

```python
import functools

import jax
import jax.numpy as jnp
from jax import lax
from jax.experimental import pallas as pl
from jax.experimental.pallas import tpu as pltpu
from jax.sharding import PartitionSpec as P

HBM = pl.BlockSpec(memory_space=pltpu.HBM)
VMEM = pl.BlockSpec(memory_space=pltpu.VMEM)
F32 = jnp.float32


def parted(value):
    high = value.astype(jnp.bfloat16)
    return high, (value - high.astype(F32)).astype(jnp.bfloat16)


def product_of(left, right, contract):
    dims = ((contract, (0,)), ((), ()))
    dot = functools.partial(
        lax.dot_general, dimension_numbers=dims, preferred_element_type=F32
    )
    (left_high, left_low), (right_high, right_low) = left, right
    return (
        dot(left_high, right_high)
        + dot(left_high, right_low)
        + dot(left_low, right_high)
    )


def times(left, right):
    return product_of(parted(left), parted(right), (1,))


def transposed_times(left, right):
    return product_of(parted(left), parted(right), (0,))


class Layout:
    def __init__(self, group_width):
        self.width = group_width
        self.pairs = group_width // 2
        self.rounds = (self.pairs - 1) // 2
        self.split_offset = self.pairs - 1
        self.split = 2 * self.rounds
        self.given = self.split + 1

    def offset(self, round_index, side):
        return 2 * round_index + 2 - side


def place():
    index = lax.axis_index("dev")
    return index, index // 2, index % 2


def pack_kernel(layout, flags_in, tiles_in, orbitals_in, packed, flags, flags_sem, sems):
    index, pair, side = place()
    half = orbitals_in.shape[1] // 2
    slots = []
    for r in range(layout.rounds):
        far = pair ^ layout.offset(r, 1 - side)
        slots += [2 * far, 2 * far + 1]
    slots.append(2 * (pair ^ layout.split_offset) + 1 - side)
    sources = [tiles_in.at[slot] for slot in slots]
    sources += [orbitals_in.at[:, pl.ds(h * half, half)] for h in range(2)]
    copies = [pltpu.make_async_copy(flags_in, flags, flags_sem)]
    for k, source in enumerate(sources):
        copies.append(pltpu.make_async_copy(source, packed.at[k], sems.at[k]))
    for copy in copies:
        copy.start()
    for copy in copies:
        copy.wait()
    for k, slot in enumerate(slots):
        packed[k] = packed[k] * flags[0, slot].astype(F32)


def load_kernel(layout, flags_in, tiles_in, tiles, flags, flags_sem, sem):
    copies = [
        pltpu.make_async_copy(flags_in, flags, flags_sem),
        pltpu.make_async_copy(tiles_in, tiles, sem),
    ]
    for copy in copies:
        copy.start()
    for copy in copies:
        copy.wait()
    for slot in range(layout.width + 1):
        tiles[slot] = tiles[slot] * flags[0, slot].astype(F32)


def orbitals_of(layout, packed):
    return jnp.concatenate([packed[layout.given], packed[layout.given + 1]], axis=1)


def send_full_kernel(layout, tiles, packed, taken, *outs):
    index, pair, side = place()
    own, other = orbitals_of(layout, packed), orbitals_of(layout, taken)
    for r in range(layout.rounds):
        far = pair ^ layout.offset(r, side)
        out = outs[r]

        @pl.when(far > pair)
        def _():
            right = parted(jnp.concatenate([own, other], axis=0))
            for k in range(2):
                left = jnp.concatenate([tiles[2 * far + k], taken[2 * r + k]], axis=0)
                out[k] = product_of(parted(left), right, (0,))

        @pl.when(far < pair)
        def _():
            out[0] = jnp.where(side == 0, own, other)
            out[1] = jnp.where(side == 0, other, own)


def send_across_kernel(layout, tiles, packed, even_out, odd_out):
    upper = lax.axis_index("grp") % 2
    own = orbitals_of(layout, packed)
    term = transposed_times(tiles[layout.width], own)
    even_out[...] = jnp.where(upper == 0, term, own)
    odd_out[...] = jnp.where(upper == 1, term, own)


def send_split_kernel(layout, tiles, packed, taken, out):
    index, pair, side = place()
    far = pair ^ layout.split_offset

    @pl.when(far > pair)
    def _():
        left = jnp.concatenate([tiles[2 * far + side], taken[layout.split]], axis=0)
        right = jnp.concatenate(
            [orbitals_of(layout, packed), orbitals_of(layout, taken)], axis=0
        )
        out[...] = transposed_times(left, right)

    @pl.when(far < pair)
    def _():
        out[...] = orbitals_of(layout, packed)


def near_kernel(layout, tiles, packed, taken, mine, others):
    index, pair, side = place()
    own, other = orbitals_of(layout, packed), orbitals_of(layout, taken)
    beside = tiles[index ^ 1]
    row = jnp.concatenate([tiles[index], beside], axis=1)
    mine[...] = times(row, jnp.concatenate([own, other], axis=0))
    others[...] = transposed_times(beside, own)


def full_kernel(layout, tiles, taken, mine_in, others_in, *refs):
    index, pair, side = place()
    arrived, mine, others = refs[:-2], refs[-2], refs[-1]
    order = tiles.shape[1]
    mine[...] = mine_in[...]
    others[...] = others_in[...]
    for r in range(layout.rounds):
        far = pair ^ layout.offset(r, side)
        came = arrived[r]

        @pl.when(far > pair)
        def _():
            upper = jnp.concatenate([tiles[2 * far], tiles[2 * far + 1]], axis=1)
            lower = jnp.concatenate([taken[2 * r], taken[2 * r + 1]], axis=1)
            right = jnp.concatenate([came[0], came[1]], axis=0)
            terms = times(jnp.concatenate([upper, lower], axis=0), right)
            mine[...] += terms[:order]
            others[...] += terms[order:]

        @pl.when(far < pair)
        def _():
            mine[...] += came[side]
            others[...] += came[1 - side]


def back_kernel(layout, taken, others_in, arrived, others):
    index, pair, side = place()
    far = pair ^ layout.split_offset

    @pl.when(far > pair)
    def _():
        others[...] = others_in[...] + times(taken[layout.split], arrived[...])

    @pl.when(far < pair)
    def _():
        others[...] = others_in[...]


def mine_kernel(layout, tiles, mine_in, arrived, even_in, odd_in, mine):
    index, pair, side = place()
    group = lax.axis_index("grp")
    far = pair ^ layout.split_offset
    even = group % 2 == 0
    following = jnp.where(even, even_in[...], odd_in[...])
    previous = jnp.where(even, odd_in[...], even_in[...])
    mine[...] = (
        mine_in[...]
        + times(tiles[layout.width], following)
        + jnp.where(group > 0, previous, 0.0)
    )

    @pl.when(far > pair)
    def _():
        mine[...] += times(tiles[2 * far + side], arrived[...])

    @pl.when(far < pair)
    def _():
        mine[...] += arrived[...]


def call(body, outs, operands, specs=None, scratch=(), flops=0):
    return pl.pallas_call(
        body,
        out_shape=outs,
        in_specs=specs or [VMEM] * len(operands),
        out_specs=jax.tree.map(lambda _: VMEM, outs),
        scratch_shapes=scratch,
        cost_estimate=pl.CostEstimate(
            flops=flops, bytes_accessed=0, transcendentals=0
        ),
        compiler_params=pltpu.CompilerParams(vmem_limit_bytes=32 * 1024 * 1024),
    )(*operands)


def exchange(block, group_width, groups, lower_parity):
    moves = []
    for g in range(groups):
        to = g + 1 if g % 2 == lower_parity else g - 1
        for i in range(group_width):
            if 0 <= to < groups:
                moves.append((g * group_width + i, to * group_width + i))
            else:
                moves.append((g * group_width + i, g * group_width + (i ^ 1)))
    return lax.ppermute(block, ("grp", "dev"), moves)


def per_device(stored_tiles, tile_flags, orbitals):
    group_width = lax.axis_size("dev")
    groups = lax.axis_size("grp")
    layout = Layout(group_width)
    order, columns = orbitals.shape
    block = jax.ShapeDtypeStruct((order, columns), F32)
    two = jax.ShapeDtypeStruct((2, order, columns), F32)
    partners = [(i, i ^ 1) for i in range(group_width)]
    flags, stored, held = (
        pltpu.with_memory_space_constraint(operand, pltpu.HBM)
        for operand in (tile_flags, stored_tiles[0], orbitals)
    )
    flags_scratch = pltpu.SMEM(tile_flags.shape, jnp.int32)
    semaphore = pltpu.SemaphoreType.DMA

    packed = call(
        functools.partial(pack_kernel, layout),
        jax.ShapeDtypeStruct((layout.given + 2, order, order), F32),
        [flags, stored, held],
        [HBM] * 3,
        [flags_scratch, semaphore, semaphore((layout.given + 2,))],
    )
    taken = lax.ppermute(packed, "dev", partners)
    tiles = call(
        functools.partial(load_kernel, layout),
        jax.ShapeDtypeStruct(stored.shape, F32),
        [flags, stored],
        [HBM] * 2,
        [flags_scratch, semaphore, semaphore],
        flops=10**9,
    )

    full = call(
        functools.partial(send_full_kernel, layout),
        [two] * layout.rounds,
        [tiles, packed, taken],
    )
    full_arrived = []
    for r in range(layout.rounds):
        swaps = [
            (i, i ^ (2 * layout.offset(r, i % 2))) for i in range(group_width)
        ]
        full_arrived.append(lax.ppermute(full[r], "dev", swaps))

    split = call(
        functools.partial(send_split_kernel, layout), block, [tiles, packed, taken]
    )
    swaps = [(i, i ^ (2 * layout.split_offset)) for i in range(group_width)]
    split_arrived = lax.ppermute(split, "dev", swaps)

    even, odd = call(
        functools.partial(send_across_kernel, layout), [block, block], [tiles, packed]
    )
    even_arrived = exchange(even, group_width, groups, 0)
    odd_arrived = exchange(odd, group_width, groups, 1)

    mine, others = call(
        functools.partial(near_kernel, layout), [block, block], [tiles, packed, taken]
    )
    mine, others = call(
        functools.partial(full_kernel, layout),
        [block, block],
        [tiles, taken, mine, others, *full_arrived],
    )
    others = call(
        functools.partial(back_kernel, layout),
        block,
        [taken, others, split_arrived],
    )
    returned = lax.ppermute(others, "dev", partners)
    mine = call(
        functools.partial(mine_kernel, layout),
        block,
        [tiles, mine, split_arrived, even_arrived, odd_arrived],
    )
    return mine + returned


def solution(mesh):
    in_specs = (
        P(("grp", "dev"), None, None, None),
        P(("grp", "dev"), None),
        P(("grp", "dev"), None),
    )
    out_specs = P(("grp", "dev"), None)
    return jax.shard_map(
        per_device, mesh=mesh, in_specs=in_specs, out_specs=out_specs, check_vma=False
    )
```

```python
import functools

import jax
import jax.numpy as jnp
from jax import lax
from jax.experimental import pallas as pl
from jax.experimental.pallas import tpu as pltpu
from jax.sharding import PartitionSpec as P

HBM = pl.BlockSpec(memory_space=pltpu.HBM)
VMEM = pl.BlockSpec(memory_space=pltpu.VMEM)
F32 = jnp.float32


def parted(value):
    high = value.astype(jnp.bfloat16)
    return high, (value - high.astype(F32)).astype(jnp.bfloat16)


def product_of(left, right, contract):
    dims = ((contract, (0,)), ((), ()))
    dot = functools.partial(
        lax.dot_general, dimension_numbers=dims, preferred_element_type=F32
    )
    (left_high, left_low), (right_high, right_low) = left, right
    return (
        dot(left_high, right_high)
        + dot(left_high, right_low)
        + dot(left_low, right_high)
    )


def times(left, right):
    return product_of(parted(left), parted(right), (1,))


def transposed_times(left, right):
    return product_of(parted(left), parted(right), (0,))


class Layout:
    def __init__(self, group_width):
        self.width = group_width
        self.pairs = group_width // 2
        self.rounds = (self.pairs - 1) // 2
        self.split_offset = self.pairs - 1

    def offset(self, round_index, side):
        return 2 * round_index + 2 - side


def place():
    index = lax.axis_index("dev")
    return index, index // 2, index % 2


def load_kernel(layout, flags_in, tiles_in, orbitals_in, tiles, orbitals, flags, sems):
    copies = [
        pltpu.make_async_copy(flags_in, flags, sems.at[0]),
        pltpu.make_async_copy(tiles_in, tiles, sems.at[1]),
        pltpu.make_async_copy(orbitals_in, orbitals, sems.at[2]),
    ]
    for copy in copies:
        copy.start()
    for copy in copies:
        copy.wait()
    for slot in range(layout.width + 1):
        tiles[slot] = tiles[slot] * flags[0, slot].astype(F32)


def mask_kernel(layout, flags, mask):
    row = flags[...].astype(F32)
    for slot in range(layout.width + 1):
        mask[slot : slot + 1] = jnp.broadcast_to(
            row[:, slot : slot + 1], (1, mask.shape[1])
        )


def taken_tile(taken, mask, slot):
    return taken[slot] * mask[pl.ds(slot, 1), :]


def send_full_kernel(layout, tiles, taken, mask, orbitals, taken_orbitals, *outs):
    index, pair, side = place()
    own, other = orbitals[...], taken_orbitals[...]
    for r in range(layout.rounds):
        far = pair ^ layout.offset(r, side)
        out = outs[r]

        @pl.when(far > pair)
        def _():
            right = parted(jnp.concatenate([own, other], axis=0))
            for k in range(2):
                slot = 2 * far + k
                left = jnp.concatenate(
                    [tiles[slot], taken_tile(taken, mask, slot)], axis=0
                )
                out[k] = product_of(parted(left), right, (0,))

        @pl.when(far < pair)
        def _():
            out[0] = jnp.where(side == 0, own, other)
            out[1] = jnp.where(side == 0, other, own)


def send_across_kernel(layout, tiles, orbitals, even_out, odd_out):
    upper = lax.axis_index("grp") % 2
    own = orbitals[...]
    term = transposed_times(tiles[layout.width], own)
    even_out[...] = jnp.where(upper == 0, term, own)
    odd_out[...] = jnp.where(upper == 1, term, own)


def send_split_kernel(layout, tiles, taken, mask, orbitals, taken_orbitals, out):
    index, pair, side = place()
    far = pair ^ layout.split_offset

    @pl.when(far > pair)
    def _():
        slot = 2 * far + side
        left = jnp.concatenate([tiles[slot], taken_tile(taken, mask, slot)], axis=0)
        right = jnp.concatenate([orbitals[...], taken_orbitals[...]], axis=0)
        out[...] = transposed_times(left, right)

    @pl.when(far < pair)
    def _():
        out[...] = orbitals[...]


def near_kernel(layout, tiles, orbitals, taken_orbitals, mine, others):
    index, pair, side = place()
    own, other = orbitals[...], taken_orbitals[...]
    beside = tiles[index ^ 1]
    row = jnp.concatenate([tiles[index], beside], axis=1)
    mine[...] = times(row, jnp.concatenate([own, other], axis=0))
    others[...] = transposed_times(beside, own)


def back_kernel(layout, taken, mask, others_in, split_arrived, *refs):
    index, pair, side = place()
    arrived, others = refs[:-1], refs[-1]
    others[...] = others_in[...]
    for r in range(layout.rounds):
        far = pair ^ layout.offset(r, side)
        came = arrived[r]

        @pl.when(far > pair)
        def _():
            left = jnp.concatenate(
                [taken_tile(taken, mask, 2 * far + k) for k in range(2)], axis=1
            )
            right = jnp.concatenate([came[0], came[1]], axis=0)
            others[...] += times(left, right)

        @pl.when(far < pair)
        def _():
            others[...] += came[1 - side]

    far = pair ^ layout.split_offset

    @pl.when(far > pair)
    def _():
        left = taken_tile(taken, mask, 2 * far + side)
        others[...] += times(left, split_arrived[...])


def mine_kernel(layout, tiles, mine_in, split_arrived, even_in, odd_in, *refs):
    index, pair, side = place()
    arrived, mine = refs[:-1], refs[-1]
    group = lax.axis_index("grp")
    even = group % 2 == 0
    following = jnp.where(even, even_in[...], odd_in[...])
    previous = jnp.where(even, odd_in[...], even_in[...])
    mine[...] = (
        mine_in[...]
        + times(tiles[layout.width], following)
        + jnp.where(group > 0, previous, 0.0)
    )
    for r in range(layout.rounds):
        far = pair ^ layout.offset(r, side)
        came = arrived[r]

        @pl.when(far > pair)
        def _():
            left = jnp.concatenate([tiles[2 * far], tiles[2 * far + 1]], axis=1)
            right = jnp.concatenate([came[0], came[1]], axis=0)
            mine[...] += times(left, right)

        @pl.when(far < pair)
        def _():
            mine[...] += came[side]

    far = pair ^ layout.split_offset

    @pl.when(far > pair)
    def _():
        mine[...] += times(tiles[2 * far + side], split_arrived[...])

    @pl.when(far < pair)
    def _():
        mine[...] += split_arrived[...]


def call(body, outs, operands, specs=None, scratch=(), flops=0):
    return pl.pallas_call(
        body,
        out_shape=outs,
        in_specs=specs or [VMEM] * len(operands),
        out_specs=jax.tree.map(lambda _: VMEM, outs),
        scratch_shapes=scratch,
        cost_estimate=pl.CostEstimate(
            flops=flops, bytes_accessed=0, transcendentals=0
        ),
        compiler_params=pltpu.CompilerParams(vmem_limit_bytes=32 * 1024 * 1024),
    )(*operands)


def exchange(block, group_width, groups, lower_parity):
    moves = []
    for g in range(groups):
        to = g + 1 if g % 2 == lower_parity else g - 1
        for i in range(group_width):
            if 0 <= to < groups:
                moves.append((g * group_width + i, to * group_width + i))
            else:
                moves.append((g * group_width + i, g * group_width + (i ^ 1)))
    return lax.ppermute(block, ("grp", "dev"), moves)


def per_device(stored_tiles, tile_flags, orbitals):
    group_width = lax.axis_size("dev")
    groups = lax.axis_size("grp")
    layout = Layout(group_width)
    order, columns = orbitals.shape
    block = jax.ShapeDtypeStruct((order, columns), F32)
    two = jax.ShapeDtypeStruct((2, order, columns), F32)
    partners = [(i, i ^ 1) for i in range(group_width)]
    semaphore = pltpu.SemaphoreType.DMA

    taken = lax.ppermute(stored_tiles, "dev", partners)[0]
    taken_orbitals = lax.ppermute(orbitals, "dev", partners)
    taken_flags = lax.ppermute(tile_flags, "dev", partners)
    tiles, held = call(
        functools.partial(load_kernel, layout),
        [jax.ShapeDtypeStruct(stored_tiles.shape[1:], F32), block],
        [
            pltpu.with_memory_space_constraint(operand, pltpu.HBM)
            for operand in (tile_flags, stored_tiles[0], orbitals)
        ],
        [HBM] * 3,
        [pltpu.SMEM(tile_flags.shape, jnp.int32), semaphore((3,))],
        flops=10**9,
    )
    mask = call(
        functools.partial(mask_kernel, layout),
        jax.ShapeDtypeStruct((group_width + 1, order), F32),
        [taken_flags],
    )

    full = call(
        functools.partial(send_full_kernel, layout),
        [two] * layout.rounds,
        [tiles, taken, mask, held, taken_orbitals],
    )
    full_arrived = []
    for r in range(layout.rounds):
        swaps = [
            (i, i ^ (2 * layout.offset(r, i % 2))) for i in range(group_width)
        ]
        full_arrived.append(lax.ppermute(full[r], "dev", swaps))

    split = call(
        functools.partial(send_split_kernel, layout),
        block,
        [tiles, taken, mask, held, taken_orbitals],
    )
    swaps = [(i, i ^ (2 * layout.split_offset)) for i in range(group_width)]
    split_arrived = lax.ppermute(split, "dev", swaps)

    even, odd = call(
        functools.partial(send_across_kernel, layout), [block, block], [tiles, held]
    )
    even_arrived = exchange(even, group_width, groups, 0)
    odd_arrived = exchange(odd, group_width, groups, 1)

    mine, others = call(
        functools.partial(near_kernel, layout),
        [block, block],
        [tiles, held, taken_orbitals],
    )
    others = call(
        functools.partial(back_kernel, layout),
        block,
        [taken, mask, others, split_arrived, *full_arrived],
    )
    returned = lax.ppermute(others, "dev", partners)
    mine = call(
        functools.partial(mine_kernel, layout),
        block,
        [tiles, mine, split_arrived, even_arrived, odd_arrived, *full_arrived],
    )
    return mine + returned


def solution(mesh):
    in_specs = (
        P(("grp", "dev"), None, None, None),
        P(("grp", "dev"), None),
        P(("grp", "dev"), None),
    )
    out_specs = P(("grp", "dev"), None)
    return jax.shard_map(
        per_device, mesh=mesh, in_specs=in_specs, out_specs=out_specs, check_vma=False
    )
```

```python
import functools

import jax
import jax.numpy as jnp
from jax import lax
from jax.experimental import pallas as pl
from jax.experimental.pallas import tpu as pltpu
from jax.sharding import PartitionSpec as P

HBM = pl.BlockSpec(memory_space=pltpu.HBM)
VMEM = pl.BlockSpec(memory_space=pltpu.VMEM)
F32 = jnp.float32


def parted(value):
    high = value.astype(jnp.bfloat16)
    return high, (value - high.astype(F32)).astype(jnp.bfloat16)


def product_of(left, right, contract):
    dims = ((contract, (0,)), ((), ()))
    dot = functools.partial(
        lax.dot_general, dimension_numbers=dims, preferred_element_type=F32
    )
    (left_high, left_low), (right_high, right_low) = left, right
    return (
        dot(left_high, right_high)
        + dot(left_high, right_low)
        + dot(left_low, right_high)
    )


def times(left, right):
    return product_of(parted(left), parted(right), (1,))


def transposed_times(left, right):
    return product_of(parted(left), parted(right), (0,))


class Layout:
    def __init__(self, group_width):
        self.width = group_width
        self.pairs = group_width // 2
        self.rounds = (self.pairs - 1) // 2
        self.split_offset = self.pairs - 1

    def offset(self, round_index, side):
        return 2 * round_index + 2 - side


def place():
    index = lax.axis_index("dev")
    return index, index // 2, index % 2


def load_kernel(layout, flags_in, tiles_in, orbitals_in, tiles, orbitals, flags, sems):
    copies = [
        pltpu.make_async_copy(flags_in, flags, sems.at[0]),
        pltpu.make_async_copy(tiles_in, tiles, sems.at[1]),
        pltpu.make_async_copy(orbitals_in, orbitals, sems.at[2]),
    ]
    for copy in copies:
        copy.start()
    for copy in copies:
        copy.wait()
    for slot in range(layout.width + 1):
        tiles[slot] = tiles[slot] * flags[0, slot].astype(F32)


def mask_kernel(layout, flags, mask):
    row = flags[...].astype(F32)
    for slot in range(layout.width + 1):
        mask[slot : slot + 1] = jnp.broadcast_to(
            row[:, slot : slot + 1], (1, mask.shape[1])
        )


def taken_tile(taken, mask, slot):
    return taken[slot] * mask[pl.ds(slot, 1), :]


def send_full_kernel(layout, tiles, taken, mask, orbitals, taken_orbitals, *outs):
    index, pair, side = place()
    own, other = orbitals[...], taken_orbitals[...]
    for r in range(layout.rounds):
        far = pair ^ layout.offset(r, side)
        out = outs[r]

        @pl.when(far > pair)
        def _():
            right = parted(jnp.concatenate([own, other], axis=0))
            for k in range(2):
                slot = 2 * far + k
                left = jnp.concatenate(
                    [tiles[slot], taken_tile(taken, mask, slot)], axis=0
                )
                out[k] = product_of(parted(left), right, (0,))

        @pl.when(far < pair)
        def _():
            out[0] = jnp.where(side == 0, own, other)
            out[1] = jnp.where(side == 0, other, own)


def send_across_kernel(layout, tiles, orbitals, even_out, odd_out):
    upper = lax.axis_index("grp") % 2
    own = orbitals[...]
    term = transposed_times(tiles[layout.width], own)
    even_out[...] = jnp.where(upper == 0, term, own)
    odd_out[...] = jnp.where(upper == 1, term, own)


def send_split_kernel(layout, tiles, taken, mask, orbitals, taken_orbitals, out):
    index, pair, side = place()
    far = pair ^ layout.split_offset

    @pl.when(far > pair)
    def _():
        slot = 2 * far + side
        left = jnp.concatenate([tiles[slot], taken_tile(taken, mask, slot)], axis=0)
        right = jnp.concatenate([orbitals[...], taken_orbitals[...]], axis=0)
        out[...] = transposed_times(left, right)

    @pl.when(far < pair)
    def _():
        out[...] = orbitals[...]


def near_kernel(layout, tiles, orbitals, taken_orbitals, mine, others):
    index, pair, side = place()
    own, other = orbitals[...], taken_orbitals[...]
    beside = tiles[index ^ 1]
    row = jnp.concatenate([tiles[index], beside], axis=1)
    mine[...] = times(row, jnp.concatenate([own, other], axis=0))
    others[...] = transposed_times(beside, own)


def back_full_kernel(layout, taken, mask, others_in, *refs):
    index, pair, side = place()
    arrived, others = refs[:-1], refs[-1]
    others[...] = others_in[...]
    for r in range(layout.rounds):
        far = pair ^ layout.offset(r, side)
        came = arrived[r]

        @pl.when(far > pair)
        def _():
            left = jnp.concatenate(
                [taken_tile(taken, mask, 2 * far + k) for k in range(2)], axis=1
            )
            right = jnp.concatenate([came[0], came[1]], axis=0)
            others[...] += times(left, right)

        @pl.when(far < pair)
        def _():
            others[...] += came[1 - side]


def back_split_kernel(layout, taken, mask, others_in, arrived, others):
    index, pair, side = place()
    far = pair ^ layout.split_offset

    @pl.when(far > pair)
    def _():
        left = taken_tile(taken, mask, 2 * far + side)
        others[...] = others_in[...] + times(left, arrived[...])

    @pl.when(far < pair)
    def _():
        others[...] = others_in[...]


def mine_kernel(layout, tiles, mine_in, split_arrived, even_in, odd_in, *refs):
    index, pair, side = place()
    arrived, mine = refs[:-1], refs[-1]
    group = lax.axis_index("grp")
    even = group % 2 == 0
    following = jnp.where(even, even_in[...], odd_in[...])
    previous = jnp.where(even, odd_in[...], even_in[...])
    mine[...] = (
        mine_in[...]
        + times(tiles[layout.width], following)
        + jnp.where(group > 0, previous, 0.0)
    )
    for r in range(layout.rounds):
        far = pair ^ layout.offset(r, side)
        came = arrived[r]

        @pl.when(far > pair)
        def _():
            left = jnp.concatenate([tiles[2 * far], tiles[2 * far + 1]], axis=1)
            right = jnp.concatenate([came[0], came[1]], axis=0)
            mine[...] += times(left, right)

        @pl.when(far < pair)
        def _():
            mine[...] += came[side]

    far = pair ^ layout.split_offset

    @pl.when(far > pair)
    def _():
        mine[...] += times(tiles[2 * far + side], split_arrived[...])

    @pl.when(far < pair)
    def _():
        mine[...] += split_arrived[...]


def call(body, outs, operands, specs=None, scratch=(), flops=0):
    return pl.pallas_call(
        body,
        out_shape=outs,
        in_specs=specs or [VMEM] * len(operands),
        out_specs=jax.tree.map(lambda _: VMEM, outs),
        scratch_shapes=scratch,
        cost_estimate=pl.CostEstimate(
            flops=flops, bytes_accessed=0, transcendentals=0
        ),
        compiler_params=pltpu.CompilerParams(vmem_limit_bytes=32 * 1024 * 1024),
    )(*operands)


def exchange(block, group_width, groups, lower_parity):
    moves = []
    for g in range(groups):
        to = g + 1 if g % 2 == lower_parity else g - 1
        for i in range(group_width):
            if 0 <= to < groups:
                moves.append((g * group_width + i, to * group_width + i))
            else:
                moves.append((g * group_width + i, g * group_width + (i ^ 1)))
    return lax.ppermute(block, ("grp", "dev"), moves)


def per_device(stored_tiles, tile_flags, orbitals):
    group_width = lax.axis_size("dev")
    groups = lax.axis_size("grp")
    layout = Layout(group_width)
    order, columns = orbitals.shape
    block = jax.ShapeDtypeStruct((order, columns), F32)
    two = jax.ShapeDtypeStruct((2, order, columns), F32)
    partners = [(i, i ^ 1) for i in range(group_width)]
    semaphore = pltpu.SemaphoreType.DMA

    taken = lax.ppermute(stored_tiles, "dev", partners)[0]
    taken_orbitals = lax.ppermute(orbitals, "dev", partners)
    taken_flags = lax.ppermute(tile_flags, "dev", partners)
    tiles, held = call(
        functools.partial(load_kernel, layout),
        [jax.ShapeDtypeStruct(stored_tiles.shape[1:], F32), block],
        [
            pltpu.with_memory_space_constraint(operand, pltpu.HBM)
            for operand in (tile_flags, stored_tiles[0], orbitals)
        ],
        [HBM] * 3,
        [pltpu.SMEM(tile_flags.shape, jnp.int32), semaphore((3,))],
        flops=10**9,
    )
    mask = call(
        functools.partial(mask_kernel, layout),
        jax.ShapeDtypeStruct((group_width + 1, order), F32),
        [taken_flags],
        flops=10**10,
    )

    full = call(
        functools.partial(send_full_kernel, layout),
        [two] * layout.rounds,
        [tiles, taken, mask, held, taken_orbitals],
    )
    full_arrived = []
    for r in range(layout.rounds):
        swaps = [
            (i, i ^ (2 * layout.offset(r, i % 2))) for i in range(group_width)
        ]
        full_arrived.append(lax.ppermute(full[r], "dev", swaps))

    split = call(
        functools.partial(send_split_kernel, layout),
        block,
        [tiles, taken, mask, held, taken_orbitals],
    )
    swaps = [(i, i ^ (2 * layout.split_offset)) for i in range(group_width)]
    split_arrived = lax.ppermute(split, "dev", swaps)

    even, odd = call(
        functools.partial(send_across_kernel, layout), [block, block], [tiles, held]
    )
    even_arrived = exchange(even, group_width, groups, 0)
    odd_arrived = exchange(odd, group_width, groups, 1)

    mine, others = call(
        functools.partial(near_kernel, layout),
        [block, block],
        [tiles, held, taken_orbitals],
    )
    others = call(
        functools.partial(back_full_kernel, layout),
        block,
        [taken, mask, others, *full_arrived],
    )
    others = call(
        functools.partial(back_split_kernel, layout),
        block,
        [taken, mask, others, split_arrived],
    )
    returned = lax.ppermute(others, "dev", partners)
    mine = call(
        functools.partial(mine_kernel, layout),
        block,
        [tiles, mine, split_arrived, even_arrived, odd_arrived, *full_arrived],
    )
    return mine + returned


def solution(mesh):
    in_specs = (
        P(("grp", "dev"), None, None, None),
        P(("grp", "dev"), None),
        P(("grp", "dev"), None),
    )
    out_specs = P(("grp", "dev"), None)
    return jax.shard_map(
        per_device, mesh=mesh, in_specs=in_specs, out_specs=out_specs, check_vma=False
    )
```

```python
import functools

import jax
import jax.numpy as jnp
from jax import lax
from jax.experimental import pallas as pl
from jax.experimental.pallas import tpu as pltpu
from jax.sharding import PartitionSpec as P

HBM = pl.BlockSpec(memory_space=pltpu.HBM)
VMEM = pl.BlockSpec(memory_space=pltpu.VMEM)
F32 = jnp.float32


def parted(value):
    high = value.astype(jnp.bfloat16)
    return high, (value - high.astype(F32)).astype(jnp.bfloat16)


def product_of(left, right, contract):
    dims = ((contract, (0,)), ((), ()))
    dot = functools.partial(
        lax.dot_general, dimension_numbers=dims, preferred_element_type=F32
    )
    (left_high, left_low), (right_high, right_low) = left, right
    return (
        dot(left_high, right_high)
        + dot(left_high, right_low)
        + dot(left_low, right_high)
    )


def times(left, right):
    return product_of(parted(left), parted(right), (1,))


def transposed_times(left, right):
    return product_of(parted(left), parted(right), (0,))


class Layout:
    def __init__(self, group_width):
        self.width = group_width
        self.pairs = group_width // 2
        self.rounds = (self.pairs - 1) // 2
        self.split_offset = self.pairs - 1

    def offset(self, round_index, side):
        return 2 * round_index + 2 - side


def place():
    index = lax.axis_index("dev")
    return index, index // 2, index % 2


def load_kernel(
    layout, flags_in, tiles_in, orbitals_in,
    tiles, orbitals, full_terms, split_term, even_out, odd_out, flags, sems,
):
    index, pair, side = place()
    copies = [
        pltpu.make_async_copy(flags_in, flags, sems.at[0]),
        pltpu.make_async_copy(orbitals_in, orbitals, sems.at[1]),
        pltpu.make_async_copy(tiles_in, tiles, sems.at[2]),
    ]
    for copy in copies:
        copy.start()
    for copy in copies:
        copy.wait()
    for slot in range(layout.width + 1):
        tiles[slot] = tiles[slot] * flags[0, slot].astype(F32)
    own = orbitals[...]
    right = parted(own)

    def term(slot):
        return product_of(parted(tiles[slot]), right, (0,))

    upper = lax.axis_index("grp") % 2
    upward = term(layout.width)
    even_out[...] = jnp.where(upper == 0, upward, own)
    odd_out[...] = jnp.where(upper == 1, upward, own)
    for r in range(layout.rounds):
        far = pair ^ layout.offset(r, side)

        @pl.when(far > pair)
        def _():
            full_terms[2 * r] = term(2 * far)
            full_terms[2 * r + 1] = term(2 * far + 1)

        @pl.when(far < pair)
        def _():
            full_terms[2 * r] = own
            full_terms[2 * r + 1] = own

    far = pair ^ layout.split_offset

    @pl.when(far > pair)
    def _():
        split_term[...] = term(2 * far + side)

    @pl.when(far < pair)
    def _():
        split_term[...] = own


def mask_kernel(layout, flags, mask):
    row = flags[...].astype(F32)
    for slot in range(layout.width + 1):
        mask[slot : slot + 1] = jnp.broadcast_to(
            row[:, slot : slot + 1], (1, mask.shape[1])
        )


def taken_tile(taken, mask, slot):
    return taken[slot] * mask[pl.ds(slot, 1), :]


def send_full_kernel(layout, taken, mask, full_terms, taken_orbitals, *outs):
    index, pair, side = place()
    other = taken_orbitals[...]
    for r in range(layout.rounds):
        far = pair ^ layout.offset(r, side)
        out = outs[r]

        @pl.when(far > pair)
        def _():
            right = parted(other)
            for k in range(2):
                left = parted(taken_tile(taken, mask, 2 * far + k))
                out[k] = full_terms[2 * r + k] + product_of(left, right, (0,))

        @pl.when(far < pair)
        def _():
            own = full_terms[2 * r]
            out[0] = jnp.where(side == 0, own, other)
            out[1] = jnp.where(side == 0, other, own)


def send_split_kernel(layout, taken, mask, split_term, taken_orbitals, out):
    index, pair, side = place()
    far = pair ^ layout.split_offset

    @pl.when(far > pair)
    def _():
        left = taken_tile(taken, mask, 2 * far + side)
        out[...] = split_term[...] + transposed_times(left, taken_orbitals[...])

    @pl.when(far < pair)
    def _():
        out[...] = split_term[...]


def near_kernel(layout, tiles, orbitals, taken_orbitals, mine, others):
    index, pair, side = place()
    own, other = orbitals[...], taken_orbitals[...]
    beside = tiles[index ^ 1]
    row = jnp.concatenate([tiles[index], beside], axis=1)
    mine[...] = times(row, jnp.concatenate([own, other], axis=0))
    others[...] = transposed_times(beside, own)


def full_kernel(layout, tiles, taken, mask, mine_in, others_in, *refs):
    index, pair, side = place()
    arrived, mine, others = refs[:-2], refs[-2], refs[-1]
    order = tiles.shape[1]
    mine[...] = mine_in[...]
    others[...] = others_in[...]
    for r in range(layout.rounds):
        far = pair ^ layout.offset(r, side)
        came = arrived[r]

        @pl.when(far > pair)
        def _():
            slots = [2 * far, 2 * far + 1]
            upper = jnp.concatenate([tiles[slot] for slot in slots], axis=1)
            lower = jnp.concatenate(
                [taken_tile(taken, mask, slot) for slot in slots], axis=1
            )
            right = jnp.concatenate([came[0], came[1]], axis=0)
            terms = times(jnp.concatenate([upper, lower], axis=0), right)
            mine[...] += terms[:order]
            others[...] += terms[order:]

        @pl.when(far < pair)
        def _():
            mine[...] += came[side]
            others[...] += came[1 - side]


def back_kernel(layout, taken, mask, others_in, arrived, others):
    index, pair, side = place()
    far = pair ^ layout.split_offset

    @pl.when(far > pair)
    def _():
        left = taken_tile(taken, mask, 2 * far + side)
        others[...] = others_in[...] + times(left, arrived[...])

    @pl.when(far < pair)
    def _():
        others[...] = others_in[...]


def mine_kernel(layout, tiles, mine_in, arrived, even_in, odd_in, mine):
    index, pair, side = place()
    group = lax.axis_index("grp")
    far = pair ^ layout.split_offset
    even = group % 2 == 0
    following = jnp.where(even, even_in[...], odd_in[...])
    previous = jnp.where(even, odd_in[...], even_in[...])
    total = mine_in[...] + jnp.where(group > 0, previous, 0.0)

    @pl.when(far > pair)
    def _():
        left = jnp.concatenate([tiles[layout.width], tiles[2 * far + side]], axis=1)
        right = jnp.concatenate([following, arrived[...]], axis=0)
        mine[...] = total + times(left, right)

    @pl.when(far < pair)
    def _():
        mine[...] = total + times(tiles[layout.width], following) + arrived[...]


def finish_kernel(mine, returned, product, total, sems):
    half = mine.shape[0] // 2
    copies = []
    for h in range(2):
        rows = pl.ds(h * half, half)
        total[rows] = mine[rows] + returned[rows]
        copies.append(
            pltpu.make_async_copy(total.at[rows], product.at[rows], sems.at[h])
        )
        copies[-1].start()
    for copy in copies:
        copy.wait()


def call(body, outs, operands, specs=None, scratch=(), flops=0, out_spec=VMEM):
    return pl.pallas_call(
        body,
        out_shape=outs,
        in_specs=specs or [VMEM] * len(operands),
        out_specs=jax.tree.map(lambda _: out_spec, outs),
        scratch_shapes=scratch,
        cost_estimate=pl.CostEstimate(
            flops=flops, bytes_accessed=0, transcendentals=0
        ),
        compiler_params=pltpu.CompilerParams(vmem_limit_bytes=32 * 1024 * 1024),
    )(*operands)


def exchange(block, group_width, groups, lower_parity):
    moves = []
    for g in range(groups):
        to = g + 1 if g % 2 == lower_parity else g - 1
        for i in range(group_width):
            if 0 <= to < groups:
                moves.append((g * group_width + i, to * group_width + i))
            else:
                moves.append((g * group_width + i, g * group_width + (i ^ 1)))
    return lax.ppermute(block, ("grp", "dev"), moves)


def per_device(stored_tiles, tile_flags, orbitals):
    group_width = lax.axis_size("dev")
    groups = lax.axis_size("grp")
    layout = Layout(group_width)
    order, columns = orbitals.shape
    block = jax.ShapeDtypeStruct((order, columns), F32)
    two = jax.ShapeDtypeStruct((2, order, columns), F32)
    partners = [(i, i ^ 1) for i in range(group_width)]
    semaphore = pltpu.SemaphoreType.DMA

    taken = lax.ppermute(stored_tiles, "dev", partners)[0]
    taken_orbitals = lax.ppermute(orbitals, "dev", partners)
    taken_flags = lax.ppermute(tile_flags, "dev", partners)
    terms = jax.ShapeDtypeStruct((2 * layout.rounds, order, columns), F32)
    tiles, held, full_terms, split_term, even, odd = call(
        functools.partial(load_kernel, layout),
        [
            jax.ShapeDtypeStruct(stored_tiles.shape[1:], F32),
            block, terms, block, block, block,
        ],
        [
            pltpu.with_memory_space_constraint(operand, pltpu.HBM)
            for operand in (tile_flags, stored_tiles[0], orbitals)
        ],
        [HBM] * 3,
        [pltpu.SMEM(tile_flags.shape, jnp.int32), semaphore((3,))],
        flops=10**9,
    )
    mask = call(
        functools.partial(mask_kernel, layout),
        jax.ShapeDtypeStruct((group_width + 1, order), F32),
        [taken_flags],
        flops=10**9,
    )

    full = call(
        functools.partial(send_full_kernel, layout),
        [two] * layout.rounds,
        [taken, mask, full_terms, taken_orbitals],
    )
    full_arrived = []
    for r in range(layout.rounds):
        swaps = [
            (i, i ^ (2 * layout.offset(r, i % 2))) for i in range(group_width)
        ]
        full_arrived.append(lax.ppermute(full[r], "dev", swaps))

    split = call(
        functools.partial(send_split_kernel, layout),
        block,
        [taken, mask, split_term, taken_orbitals],
    )
    swaps = [(i, i ^ (2 * layout.split_offset)) for i in range(group_width)]
    split_arrived = lax.ppermute(split, "dev", swaps)

    even_arrived = exchange(even, group_width, groups, 0)
    odd_arrived = exchange(odd, group_width, groups, 1)

    mine, others = call(
        functools.partial(near_kernel, layout),
        [block, block],
        [tiles, held, taken_orbitals],
    )
    mine, others = call(
        functools.partial(full_kernel, layout),
        [block, block],
        [tiles, taken, mask, mine, others, *full_arrived],
    )
    others = call(
        functools.partial(back_kernel, layout),
        block,
        [taken, mask, others, split_arrived],
    )
    returned = lax.ppermute(others, "dev", partners)
    mine = call(
        functools.partial(mine_kernel, layout),
        block,
        [tiles, mine, split_arrived, even_arrived, odd_arrived],
    )
    return call(
        finish_kernel,
        block,
        [mine, returned],
        scratch=[pltpu.VMEM((order, columns), F32), semaphore((2,))],
        out_spec=HBM,
    )


def solution(mesh):
    in_specs = (
        P(("grp", "dev"), None, None, None),
        P(("grp", "dev"), None),
        P(("grp", "dev"), None),
    )
    out_specs = P(("grp", "dev"), None)
    return jax.shard_map(
        per_device, mesh=mesh, in_specs=in_specs, out_specs=out_specs, check_vma=False
    )
```

```python
import functools

import jax
import jax.numpy as jnp
from jax import lax
from jax.experimental import pallas as pl
from jax.experimental.pallas import tpu as pltpu
from jax.sharding import PartitionSpec as P

HBM = pl.BlockSpec(memory_space=pltpu.HBM)
VMEM = pl.BlockSpec(memory_space=pltpu.VMEM)
F32 = jnp.float32


def parted(value):
    high = value.astype(jnp.bfloat16)
    return high, (value - high.astype(F32)).astype(jnp.bfloat16)


def product_of(left, right, contract):
    dims = ((contract, (0,)), ((), ()))
    dot = functools.partial(
        lax.dot_general, dimension_numbers=dims, preferred_element_type=F32
    )
    (left_high, left_low), (right_high, right_low) = left, right
    return (
        dot(left_high, right_high)
        + dot(left_high, right_low)
        + dot(left_low, right_high)
    )


def times(left, right):
    return product_of(parted(left), parted(right), (1,))


def transposed_times(left, right):
    return product_of(parted(left), parted(right), (0,))


class Layout:
    def __init__(self, group_width):
        self.width = group_width
        self.pairs = group_width // 2
        self.rounds = (self.pairs - 1) // 2
        self.split_offset = self.pairs - 1

    def offset(self, round_index, side):
        return 2 * round_index + 2 - side


def place():
    index = lax.axis_index("dev")
    return index, index // 2, index % 2


def first_kernel(
    layout, flags_in, tiles_in, orbitals_in, tiles, orbitals, flags, small_sems, sems
):
    index, pair, side = place()
    slots = []
    for r in range(layout.rounds):
        far = pair ^ layout.offset(r, side)
        slots += [2 * far, 2 * far + 1]
    slots += [2 * (pair ^ layout.split_offset) + side, layout.width]
    copies = [
        pltpu.make_async_copy(flags_in, flags, small_sems.at[0]),
        pltpu.make_async_copy(orbitals_in, orbitals, small_sems.at[1]),
    ]
    for k, slot in enumerate(slots):
        copies.append(
            pltpu.make_async_copy(tiles_in.at[slot], tiles.at[k], sems.at[k])
        )
    for copy in copies:
        copy.start()
    for copy in copies:
        copy.wait()
    for k, slot in enumerate(slots):
        tiles[k] = tiles[k] * flags[0, slot].astype(F32)


def load_kernel(layout, flags_in, tiles_in, _, tiles, flags, sems):
    copies = [
        pltpu.make_async_copy(flags_in, flags, sems.at[0]),
        pltpu.make_async_copy(tiles_in, tiles, sems.at[1]),
    ]
    for copy in copies:
        copy.start()
    for copy in copies:
        copy.wait()
    for slot in range(layout.width + 1):
        tiles[slot] = tiles[slot] * flags[0, slot].astype(F32)


def mask_kernel(layout, flags, mask):
    row = flags[...].astype(F32)
    for slot in range(layout.width + 1):
        mask[slot : slot + 1] = jnp.broadcast_to(
            row[:, slot : slot + 1], (1, mask.shape[1])
        )


def taken_tile(taken, mask, slot):
    return taken[slot] * mask[pl.ds(slot, 1), :]


def send_full_kernel(layout, first, taken, mask, orbitals, taken_orbitals, *outs):
    index, pair, side = place()
    own, other = orbitals[...], taken_orbitals[...]
    for r in range(layout.rounds):
        far = pair ^ layout.offset(r, side)
        out = outs[r]

        @pl.when(far > pair)
        def _():
            right = parted(jnp.concatenate([own, other], axis=0))
            for k in range(2):
                left = jnp.concatenate(
                    [first[2 * r + k], taken_tile(taken, mask, 2 * far + k)], axis=0
                )
                out[k] = product_of(parted(left), right, (0,))

        @pl.when(far < pair)
        def _():
            out[0] = jnp.where(side == 0, own, other)
            out[1] = jnp.where(side == 0, other, own)


def send_split_kernel(layout, first, taken, mask, orbitals, taken_orbitals, out):
    index, pair, side = place()
    far = pair ^ layout.split_offset

    @pl.when(far > pair)
    def _():
        left = jnp.concatenate(
            [first[2 * layout.rounds], taken_tile(taken, mask, 2 * far + side)], axis=0
        )
        right = jnp.concatenate([orbitals[...], taken_orbitals[...]], axis=0)
        out[...] = transposed_times(left, right)

    @pl.when(far < pair)
    def _():
        out[...] = orbitals[...]


def send_across_kernel(layout, first, orbitals, _, even_out, odd_out):
    upper = lax.axis_index("grp") % 2
    own = orbitals[...]
    term = transposed_times(first[2 * layout.rounds + 1], own)
    even_out[...] = jnp.where(upper == 0, term, own)
    odd_out[...] = jnp.where(upper == 1, term, own)


def near_kernel(
    layout, tiles, taken, mask, orbitals, taken_orbitals, split_orbitals, mine, others
):
    index, pair, side = place()
    own, other = orbitals[...], taken_orbitals[...]
    beside = tiles[index ^ 1]
    row = jnp.concatenate([tiles[index], beside], axis=1)
    mine[...] = times(row, jnp.concatenate([own, other], axis=0))
    others[...] = transposed_times(beside, own)
    far = pair ^ layout.split_offset

    @pl.when(far > pair)
    def _():
        slot = 2 * far + side
        left = jnp.concatenate([tiles[slot], taken_tile(taken, mask, slot)], axis=0)
        terms = times(left, split_orbitals[...])
        order = beside.shape[0]
        mine[...] += terms[:order]
        others[...] += terms[order:]


def full_kernel(layout, tiles, taken, mask, mine_in, others_in, *refs):
    index, pair, side = place()
    arrived, mine, others = refs[:-2], refs[-2], refs[-1]
    order = tiles.shape[1]
    mine[...] = mine_in[...]
    others[...] = others_in[...]
    for r in range(layout.rounds):
        far = pair ^ layout.offset(r, side)
        came = arrived[r]

        @pl.when(far > pair)
        def _():
            slots = [2 * far, 2 * far + 1]
            upper = jnp.concatenate([tiles[slot] for slot in slots], axis=1)
            lower = jnp.concatenate(
                [taken_tile(taken, mask, slot) for slot in slots], axis=1
            )
            right = jnp.concatenate([came[0], came[1]], axis=0)
            terms = times(jnp.concatenate([upper, lower], axis=0), right)
            mine[...] += terms[:order]
            others[...] += terms[order:]

        @pl.when(far < pair)
        def _():
            mine[...] += came[side]
            others[...] += came[1 - side]


def across_kernel(layout, first, mine_in, even_in, odd_in, mine):
    group = lax.axis_index("grp")
    even = group % 2 == 0
    following = jnp.where(even, even_in[...], odd_in[...])
    previous = jnp.where(even, odd_in[...], even_in[...])
    mine[...] = (
        mine_in[...]
        + jnp.where(group > 0, previous, 0.0)
        + times(first[2 * layout.rounds + 1], following)
    )


def split_kernel(layout, mine_in, terms, mine):
    index, pair, side = place()
    far = pair ^ layout.split_offset
    mine[...] = mine_in[...] + jnp.where(far < pair, terms[...], 0.0)


def call(body, outs, operands, specs=None, scratch=(), flops=0):
    return pl.pallas_call(
        body,
        out_shape=outs,
        in_specs=specs or [VMEM] * len(operands),
        out_specs=jax.tree.map(lambda _: VMEM, outs),
        scratch_shapes=scratch,
        cost_estimate=pl.CostEstimate(
            flops=flops, bytes_accessed=0, transcendentals=0
        ),
        compiler_params=pltpu.CompilerParams(vmem_limit_bytes=32 * 1024 * 1024),
    )(*operands)


def exchange(block, group_width, groups, lower_parity):
    moves = []
    for g in range(groups):
        to = g + 1 if g % 2 == lower_parity else g - 1
        for i in range(group_width):
            if 0 <= to < groups:
                moves.append((g * group_width + i, to * group_width + i))
            else:
                moves.append((g * group_width + i, g * group_width + (i ^ 1)))
    return lax.ppermute(block, ("grp", "dev"), moves)


def per_device(stored_tiles, tile_flags, orbitals):
    group_width = lax.axis_size("dev")
    groups = lax.axis_size("grp")
    layout = Layout(group_width)
    order, columns = orbitals.shape
    block = jax.ShapeDtypeStruct((order, columns), F32)
    two = jax.ShapeDtypeStruct((2, order, columns), F32)
    partners = [(i, i ^ 1) for i in range(group_width)]
    semaphore = pltpu.SemaphoreType.DMA

    taken = lax.ppermute(stored_tiles, "dev", partners)[0]
    taken_orbitals = lax.ppermute(orbitals, "dev", partners)
    taken_flags = lax.ppermute(tile_flags, "dev", partners)
    split_swaps = [(i, i ^ (2 * layout.split_offset)) for i in range(group_width)]
    split_orbitals = lax.ppermute(orbitals, "dev", split_swaps)
    arguments = [
        pltpu.with_memory_space_constraint(operand, pltpu.HBM)
        for operand in (tile_flags, stored_tiles[0], orbitals)
    ]
    flags_scratch = pltpu.SMEM(tile_flags.shape, jnp.int32)
    count = 2 * layout.rounds + 2
    first, held = call(
        functools.partial(first_kernel, layout),
        [jax.ShapeDtypeStruct((count, order, order), F32), block],
        arguments,
        [HBM] * 3,
        [flags_scratch, semaphore((2,)), semaphore((count,))],
        flops=10**9,
    )
    mask = call(
        functools.partial(mask_kernel, layout),
        jax.ShapeDtypeStruct((group_width + 1, order), F32),
        [taken_flags],
        flops=10**9,
    )

    full = call(
        functools.partial(send_full_kernel, layout),
        [two] * layout.rounds,
        [first, taken, mask, held, taken_orbitals],
    )
    full_arrived = []
    for r in range(layout.rounds):
        swaps = [
            (i, i ^ (2 * layout.offset(r, i % 2))) for i in range(group_width)
        ]
        full_arrived.append(lax.ppermute(full[r], "dev", swaps))

    split = call(
        functools.partial(send_split_kernel, layout),
        block,
        [first, taken, mask, held, taken_orbitals],
    )
    split_terms = lax.ppermute(split, "dev", split_swaps)

    even, odd = call(
        functools.partial(send_across_kernel, layout),
        [block, block],
        [first, held, split],
    )
    even_arrived = exchange(even, group_width, groups, 0)
    odd_arrived = exchange(odd, group_width, groups, 1)

    tiles = call(
        functools.partial(load_kernel, layout),
        jax.ShapeDtypeStruct(stored_tiles.shape[1:], F32),
        [arguments[0], arguments[1], odd],
        [HBM, HBM, VMEM],
        [flags_scratch, semaphore((2,))],
        flops=10**8,
    )
    mine, others = call(
        functools.partial(near_kernel, layout),
        [block, block],
        [tiles, taken, mask, held, taken_orbitals, split_orbitals],
        flops=2 * 10**9,
    )
    mine, others = call(
        functools.partial(full_kernel, layout),
        [block, block],
        [tiles, taken, mask, mine, others, *full_arrived],
    )
    returned = lax.ppermute(others, "dev", partners)
    mine = call(
        functools.partial(split_kernel, layout),
        block,
        [mine, split_terms],
    )
    mine = call(
        functools.partial(across_kernel, layout),
        block,
        [first, mine, even_arrived, odd_arrived],
    )
    return mine + returned


def solution(mesh):
    in_specs = (
        P(("grp", "dev"), None, None, None),
        P(("grp", "dev"), None),
        P(("grp", "dev"), None),
    )
    out_specs = P(("grp", "dev"), None)
    return jax.shard_map(
        per_device, mesh=mesh, in_specs=in_specs, out_specs=out_specs, check_vma=False
    )
```

```python
import functools

import jax
import jax.numpy as jnp
from jax import lax
from jax.experimental import pallas as pl
from jax.experimental.pallas import tpu as pltpu
from jax.sharding import PartitionSpec as P

HBM = pl.BlockSpec(memory_space=pltpu.HBM)
VMEM = pl.BlockSpec(memory_space=pltpu.VMEM)
F32 = jnp.float32


def parted(value):
    high = value.astype(jnp.bfloat16)
    return high, (value - high.astype(F32)).astype(jnp.bfloat16)


def product_of(left, right, contract):
    dims = ((contract, (0,)), ((), ()))
    dot = functools.partial(
        lax.dot_general, dimension_numbers=dims, preferred_element_type=F32
    )
    (left_high, left_low), (right_high, right_low) = left, right
    return (
        dot(left_high, right_high)
        + dot(left_high, right_low)
        + dot(left_low, right_high)
    )


def times(left, right):
    return product_of(parted(left), parted(right), (1,))


def transposed_times(left, right):
    return product_of(parted(left), parted(right), (0,))


class Layout:
    def __init__(self, group_width):
        self.width = group_width
        self.pairs = group_width // 2
        self.rounds = (self.pairs - 1) // 2
        self.last_offset = self.pairs - 1

    def offset(self, round_index, side):
        return 2 * round_index + 1 + side


def place():
    index = lax.axis_index("dev")
    return index, index // 2, index % 2


def load_kernel(layout, flags_in, tiles_in, orbitals_in, tiles, orbitals, flags, sems):
    copies = [
        pltpu.make_async_copy(flags_in, flags, sems.at[0]),
        pltpu.make_async_copy(tiles_in, tiles, sems.at[1]),
        pltpu.make_async_copy(orbitals_in, orbitals, sems.at[2]),
    ]
    for copy in copies:
        copy.start()
    for copy in copies:
        copy.wait()
    for slot in range(layout.width + 1):
        tiles[slot] = tiles[slot] * flags[0, slot].astype(F32)


def mask_kernel(layout, flags, mask):
    row = flags[...].astype(F32)
    for slot in range(layout.width + 1):
        mask[slot : slot + 1] = jnp.broadcast_to(
            row[:, slot : slot + 1], (1, mask.shape[1])
        )


def taken_tile(taken, mask, slot):
    return taken[slot] * mask[pl.ds(slot, 1), :]


def send_full_kernel(layout, tiles, taken, mask, orbitals, taken_orbitals, *outs):
    index, pair, side = place()
    own, other = orbitals[...], taken_orbitals[...]
    for r in range(layout.rounds):
        far = pair ^ layout.offset(r, side)
        out = outs[r]

        @pl.when(far > pair)
        def _():
            right = parted(jnp.concatenate([own, other], axis=0))
            for k in range(2):
                slot = 2 * far + k
                left = jnp.concatenate(
                    [tiles[slot], taken_tile(taken, mask, slot)], axis=0
                )
                out[k] = product_of(parted(left), right, (0,))

        @pl.when(far < pair)
        def _():
            out[0] = jnp.where(side == 0, own, other)
            out[1] = jnp.where(side == 0, other, own)


def send_last_kernel(layout, tiles, taken, mask, orbitals, taken_orbitals, out):
    index, pair, side = place()
    own, other = orbitals[...], taken_orbitals[...]
    far = pair ^ layout.last_offset
    lower = lax.axis_index("grp") % 2 == 0

    @pl.when((side == 1) & (far > pair))
    def _():
        right = parted(jnp.concatenate([own, other], axis=0))
        for k in range(2):
            slot = 2 * far + k
            left = jnp.concatenate(
                [tiles[slot], taken_tile(taken, mask, slot)], axis=0
            )
            out[k] = product_of(parted(left), right, (0,))

    @pl.when((side == 1) & (far < pair))
    def _():
        out[0] = other
        out[1] = own

    @pl.when((side == 0) & lower)
    def _():
        out[0] = transposed_times(tiles[layout.width], own)
        out[1] = transposed_times(taken_tile(taken, mask, layout.width), other)

    @pl.when((side == 0) & jnp.logical_not(lower))
    def _():
        out[0] = own
        out[1] = other


def send_odd_kernel(layout, tiles, orbitals, out):
    lower = lax.axis_index("grp") % 2 == 1

    @pl.when(lower)
    def _():
        out[...] = transposed_times(tiles[layout.width], orbitals[...])

    @pl.when(jnp.logical_not(lower))
    def _():
        out[...] = orbitals[...]


def near_kernel(layout, tiles, orbitals, taken_orbitals, mine, others):
    index, pair, side = place()
    own, other = orbitals[...], taken_orbitals[...]
    beside = tiles[index ^ 1]
    row = jnp.concatenate([tiles[index], beside], axis=1)
    mine[...] = times(row, jnp.concatenate([own, other], axis=0))
    others[...] = transposed_times(beside, own)


def full_kernel(layout, tiles, taken, mask, mine_in, others_in, *refs):
    index, pair, side = place()
    arrived, mine, others = refs[:-2], refs[-2], refs[-1]
    order = tiles.shape[1]
    mine[...] = mine_in[...]
    others[...] = others_in[...]
    for r in range(layout.rounds):
        far = pair ^ layout.offset(r, side)
        came = arrived[r]

        @pl.when(far > pair)
        def _():
            slots = [2 * far, 2 * far + 1]
            upper = jnp.concatenate([tiles[slot] for slot in slots], axis=1)
            lower = jnp.concatenate(
                [taken_tile(taken, mask, slot) for slot in slots], axis=1
            )
            right = jnp.concatenate([came[0], came[1]], axis=0)
            terms = times(jnp.concatenate([upper, lower], axis=0), right)
            mine[...] += terms[:order]
            others[...] += terms[order:]

        @pl.when(far < pair)
        def _():
            mine[...] += came[side]
            others[...] += came[1 - side]


def back_kernel(layout, taken, mask, others_in, came, others):
    index, pair, side = place()
    far = pair ^ layout.last_offset
    lower = lax.axis_index("grp") % 2 == 0

    @pl.when((side == 1) & (far > pair))
    def _():
        left = jnp.concatenate(
            [taken_tile(taken, mask, 2 * far + k) for k in range(2)], axis=1
        )
        right = jnp.concatenate([came[0], came[1]], axis=0)
        others[...] = others_in[...] + times(left, right)

    @pl.when((side == 1) & (far < pair))
    def _():
        others[...] = others_in[...] + came[0]

    @pl.when((side == 0) & lower)
    def _():
        left = taken_tile(taken, mask, layout.width)
        others[...] = others_in[...] + times(left, came[1])

    @pl.when((side == 0) & jnp.logical_not(lower))
    def _():
        others[...] = others_in[...] + came[1]


def mine_kernel(layout, tiles, mine_in, came, odd_in, mine):
    index, pair, side = place()
    far = pair ^ layout.last_offset
    group = lax.axis_index("grp")
    lower = group % 2 == 0

    @pl.when((side == 1) & (far > pair))
    def _():
        left = jnp.concatenate([tiles[2 * far], tiles[2 * far + 1]], axis=1)
        right = jnp.concatenate([came[0], came[1]], axis=0)
        mine[...] = mine_in[...] + times(left, right)

    @pl.when((side == 1) & (far < pair))
    def _():
        mine[...] = mine_in[...] + came[1]

    @pl.when((side == 0) & lower)
    def _():
        mine[...] = mine_in[...] + times(tiles[layout.width], came[0])

    @pl.when((side == 0) & jnp.logical_not(lower))
    def _():
        mine[...] = mine_in[...] + came[0]

    @pl.when(lower)
    def _():
        mine[...] += jnp.where(group > 0, odd_in[...], 0.0)

    @pl.when(jnp.logical_not(lower))
    def _():
        mine[...] += times(tiles[layout.width], odd_in[...])


def call(body, outs, operands, specs=None, scratch=(), flops=0):
    return pl.pallas_call(
        body,
        out_shape=outs,
        in_specs=specs or [VMEM] * len(operands),
        out_specs=jax.tree.map(lambda _: VMEM, outs),
        scratch_shapes=scratch,
        cost_estimate=pl.CostEstimate(
            flops=flops, bytes_accessed=0, transcendentals=0
        ),
        compiler_params=pltpu.CompilerParams(vmem_limit_bytes=32 * 1024 * 1024),
    )(*operands)


def last_moves(layout, groups):
    moves = []
    for g in range(groups):
        for i in range(layout.width):
            if i % 2 == 1:
                to, j = g, i ^ (2 * layout.last_offset)
            else:
                to, j = g ^ 1, i
                if to >= groups:
                    to = g
            moves.append((g * layout.width + i, to * layout.width + j))
    return moves


def odd_moves(layout, groups):
    moves = []
    for g in range(groups):
        to = g + 1 if g % 2 == 1 else g - 1
        for i in range(layout.width):
            if 0 <= to < groups:
                moves.append((g * layout.width + i, to * layout.width + i))
            else:
                moves.append((g * layout.width + i, g * layout.width + (i ^ 1)))
    return moves


def per_device(stored_tiles, tile_flags, orbitals):
    group_width = lax.axis_size("dev")
    groups = lax.axis_size("grp")
    layout = Layout(group_width)
    order, columns = orbitals.shape
    block = jax.ShapeDtypeStruct((order, columns), F32)
    two = jax.ShapeDtypeStruct((2, order, columns), F32)
    partners = [(i, i ^ 1) for i in range(group_width)]
    semaphore = pltpu.SemaphoreType.DMA

    taken = lax.ppermute(stored_tiles, "dev", partners)[0]
    taken_orbitals = lax.ppermute(orbitals, "dev", partners)
    taken_flags = lax.ppermute(tile_flags, "dev", partners)
    tiles, held = call(
        functools.partial(load_kernel, layout),
        [jax.ShapeDtypeStruct(stored_tiles.shape[1:], F32), block],
        [
            pltpu.with_memory_space_constraint(operand, pltpu.HBM)
            for operand in (tile_flags, stored_tiles[0], orbitals)
        ],
        [HBM] * 3,
        [pltpu.SMEM(tile_flags.shape, jnp.int32), semaphore((3,))],
        flops=10**9,
    )
    mask = call(
        functools.partial(mask_kernel, layout),
        jax.ShapeDtypeStruct((group_width + 1, order), F32),
        [taken_flags],
        flops=10**10,
    )

    full = call(
        functools.partial(send_full_kernel, layout),
        [two] * layout.rounds,
        [tiles, taken, mask, held, taken_orbitals],
    )
    full_arrived = []
    for r in range(layout.rounds):
        swaps = [
            (i, i ^ (2 * layout.offset(r, i % 2))) for i in range(group_width)
        ]
        full_arrived.append(lax.ppermute(full[r], "dev", swaps))

    last = call(
        functools.partial(send_last_kernel, layout),
        two,
        [tiles, taken, mask, held, taken_orbitals],
    )
    last_arrived = lax.ppermute(last, ("grp", "dev"), last_moves(layout, groups))

    odd = call(functools.partial(send_odd_kernel, layout), block, [tiles, held])
    odd_arrived = lax.ppermute(odd, ("grp", "dev"), odd_moves(layout, groups))

    mine, others = call(
        functools.partial(near_kernel, layout),
        [block, block],
        [tiles, held, taken_orbitals],
    )
    mine, others = call(
        functools.partial(full_kernel, layout),
        [block, block],
        [tiles, taken, mask, mine, others, *full_arrived],
    )
    others = call(
        functools.partial(back_kernel, layout),
        block,
        [taken, mask, others, last_arrived],
    )
    returned = lax.ppermute(others, "dev", partners)
    mine = call(
        functools.partial(mine_kernel, layout),
        block,
        [tiles, mine, last_arrived, odd_arrived],
    )
    return mine + returned


def solution(mesh):
    in_specs = (
        P(("grp", "dev"), None, None, None),
        P(("grp", "dev"), None),
        P(("grp", "dev"), None),
    )
    out_specs = P(("grp", "dev"), None)
    return jax.shard_map(
        per_device, mesh=mesh, in_specs=in_specs, out_specs=out_specs, check_vma=False
    )
```

```python
import functools

import jax
import jax.numpy as jnp
from jax import lax
from jax.experimental import pallas as pl
from jax.experimental.pallas import tpu as pltpu
from jax.sharding import PartitionSpec as P

HBM = pl.BlockSpec(memory_space=pltpu.HBM)
VMEM = pl.BlockSpec(memory_space=pltpu.VMEM)
F32 = jnp.float32


def parted(value):
    high = value.astype(jnp.bfloat16)
    return high, (value - high.astype(F32)).astype(jnp.bfloat16)


def product_of(left, right, contract):
    dims = ((contract, (0,)), ((), ()))
    dot = functools.partial(
        lax.dot_general, dimension_numbers=dims, preferred_element_type=F32
    )
    (left_high, left_low), (right_high, right_low) = left, right
    return (
        dot(left_high, right_high)
        + dot(left_high, right_low)
        + dot(left_low, right_high)
    )


def times(left, right):
    return product_of(parted(left), parted(right), (1,))


def transposed_times(left, right):
    return product_of(parted(left), parted(right), (0,))


class Layout:
    def __init__(self, group_width):
        self.width = group_width
        self.pairs = group_width // 2
        self.rounds = (self.pairs - 1) // 2
        self.last_offset = 1

    def offset(self, round_index, side):
        return 2 * round_index + 2 + side


def place():
    index = lax.axis_index("dev")
    return index, index // 2, index % 2


def load_kernel(layout, flags_in, tiles_in, orbitals_in, tiles, orbitals, flags, sems):
    copies = [
        pltpu.make_async_copy(flags_in, flags, sems.at[0]),
        pltpu.make_async_copy(tiles_in, tiles, sems.at[1]),
        pltpu.make_async_copy(orbitals_in, orbitals, sems.at[2]),
    ]
    for copy in copies:
        copy.start()
    for copy in copies:
        copy.wait()
    for slot in range(layout.width + 1):
        tiles[slot] = tiles[slot] * flags[0, slot].astype(F32)


def mask_kernel(layout, flags, mask):
    row = flags[...].astype(F32)
    for slot in range(layout.width + 1):
        mask[slot : slot + 1] = jnp.broadcast_to(
            row[:, slot : slot + 1], (1, mask.shape[1])
        )


def taken_tile(taken, mask, slot):
    return taken[slot] * mask[pl.ds(slot, 1), :]


def send_full_kernel(layout, tiles, taken, mask, orbitals, taken_orbitals, *outs):
    index, pair, side = place()
    own, other = orbitals[...], taken_orbitals[...]
    for r in range(layout.rounds):
        far = pair ^ layout.offset(r, side)
        out = outs[r]

        @pl.when(far > pair)
        def _():
            right = parted(jnp.concatenate([own, other], axis=0))
            for k in range(2):
                slot = 2 * far + k
                left = jnp.concatenate(
                    [tiles[slot], taken_tile(taken, mask, slot)], axis=0
                )
                out[k] = product_of(parted(left), right, (0,))

        @pl.when(far < pair)
        def _():
            out[0] = jnp.where(side == 0, own, other)
            out[1] = jnp.where(side == 0, other, own)


def send_last_kernel(layout, tiles, taken, mask, orbitals, taken_orbitals, out):
    index, pair, side = place()
    own, other = orbitals[...], taken_orbitals[...]
    far = pair ^ layout.last_offset
    lower = lax.axis_index("grp") % 2 == 0

    @pl.when((side == 1) & (far > pair))
    def _():
        right = parted(jnp.concatenate([own, other], axis=0))
        for k in range(2):
            slot = 2 * far + k
            left = jnp.concatenate(
                [tiles[slot], taken_tile(taken, mask, slot)], axis=0
            )
            out[k] = product_of(parted(left), right, (0,))

    @pl.when((side == 1) & (far < pair))
    def _():
        out[0] = other
        out[1] = own

    @pl.when((side == 0) & lower)
    def _():
        out[0] = transposed_times(tiles[layout.width], own)
        out[1] = transposed_times(taken_tile(taken, mask, layout.width), other)

    @pl.when((side == 0) & jnp.logical_not(lower))
    def _():
        out[0] = own
        out[1] = other


def send_odd_kernel(layout, tiles, orbitals, out):
    lower = lax.axis_index("grp") % 2 == 1

    @pl.when(lower)
    def _():
        out[...] = transposed_times(tiles[layout.width], orbitals[...])

    @pl.when(jnp.logical_not(lower))
    def _():
        out[...] = orbitals[...]


def near_kernel(layout, tiles, orbitals, taken_orbitals, mine, others):
    index, pair, side = place()
    own, other = orbitals[...], taken_orbitals[...]
    beside = tiles[index ^ 1]
    row = jnp.concatenate([tiles[index], beside], axis=1)
    mine[...] = times(row, jnp.concatenate([own, other], axis=0))
    others[...] = transposed_times(beside, own)


def full_kernel(layout, tiles, taken, mask, mine_in, others_in, *refs):
    index, pair, side = place()
    arrived, mine, others = refs[:-2], refs[-2], refs[-1]
    order = tiles.shape[1]
    mine[...] = mine_in[...]
    others[...] = others_in[...]
    for r in range(layout.rounds):
        far = pair ^ layout.offset(r, side)
        came = arrived[r]

        @pl.when(far > pair)
        def _():
            slots = [2 * far, 2 * far + 1]
            upper = jnp.concatenate([tiles[slot] for slot in slots], axis=1)
            lower = jnp.concatenate(
                [taken_tile(taken, mask, slot) for slot in slots], axis=1
            )
            right = jnp.concatenate([came[0], came[1]], axis=0)
            terms = times(jnp.concatenate([upper, lower], axis=0), right)
            mine[...] += terms[:order]
            others[...] += terms[order:]

        @pl.when(far < pair)
        def _():
            mine[...] += came[side]
            others[...] += came[1 - side]


def back_kernel(layout, taken, mask, others_in, came, others):
    index, pair, side = place()
    far = pair ^ layout.last_offset
    lower = lax.axis_index("grp") % 2 == 0

    @pl.when((side == 1) & (far > pair))
    def _():
        left = jnp.concatenate(
            [taken_tile(taken, mask, 2 * far + k) for k in range(2)], axis=1
        )
        right = jnp.concatenate([came[0], came[1]], axis=0)
        others[...] = others_in[...] + times(left, right)

    @pl.when((side == 1) & (far < pair))
    def _():
        others[...] = others_in[...] + came[0]

    @pl.when((side == 0) & lower)
    def _():
        left = taken_tile(taken, mask, layout.width)
        others[...] = others_in[...] + times(left, came[1])

    @pl.when((side == 0) & jnp.logical_not(lower))
    def _():
        others[...] = others_in[...] + came[1]


def mine_kernel(layout, tiles, mine_in, came, odd_in, mine):
    index, pair, side = place()
    far = pair ^ layout.last_offset
    group = lax.axis_index("grp")
    lower = group % 2 == 0

    @pl.when((side == 1) & (far > pair))
    def _():
        left = jnp.concatenate([tiles[2 * far], tiles[2 * far + 1]], axis=1)
        right = jnp.concatenate([came[0], came[1]], axis=0)
        mine[...] = mine_in[...] + times(left, right)

    @pl.when((side == 1) & (far < pair))
    def _():
        mine[...] = mine_in[...] + came[1]

    @pl.when((side == 0) & lower)
    def _():
        mine[...] = mine_in[...] + times(tiles[layout.width], came[0])

    @pl.when((side == 0) & jnp.logical_not(lower))
    def _():
        mine[...] = mine_in[...] + came[0]

    @pl.when(lower)
    def _():
        mine[...] += jnp.where(group > 0, odd_in[...], 0.0)

    @pl.when(jnp.logical_not(lower))
    def _():
        mine[...] += times(tiles[layout.width], odd_in[...])


def call(body, outs, operands, specs=None, scratch=(), flops=0):
    return pl.pallas_call(
        body,
        out_shape=outs,
        in_specs=specs or [VMEM] * len(operands),
        out_specs=jax.tree.map(lambda _: VMEM, outs),
        scratch_shapes=scratch,
        cost_estimate=pl.CostEstimate(
            flops=flops, bytes_accessed=0, transcendentals=0
        ),
        compiler_params=pltpu.CompilerParams(vmem_limit_bytes=32 * 1024 * 1024),
    )(*operands)


def last_moves(layout, groups):
    moves = []
    for g in range(groups):
        for i in range(layout.width):
            if i % 2 == 1:
                to, j = g, i ^ (2 * layout.last_offset)
            else:
                to, j = g ^ 1, i
                if to >= groups:
                    to = g
            moves.append((g * layout.width + i, to * layout.width + j))
    return moves


def odd_moves(layout, groups):
    moves = []
    for g in range(groups):
        to = g + 1 if g % 2 == 1 else g - 1
        for i in range(layout.width):
            if 0 <= to < groups:
                moves.append((g * layout.width + i, to * layout.width + i))
            else:
                moves.append((g * layout.width + i, g * layout.width + (i ^ 1)))
    return moves


def per_device(stored_tiles, tile_flags, orbitals):
    group_width = lax.axis_size("dev")
    groups = lax.axis_size("grp")
    layout = Layout(group_width)
    order, columns = orbitals.shape
    block = jax.ShapeDtypeStruct((order, columns), F32)
    two = jax.ShapeDtypeStruct((2, order, columns), F32)
    partners = [(i, i ^ 1) for i in range(group_width)]
    semaphore = pltpu.SemaphoreType.DMA

    taken = lax.ppermute(stored_tiles, "dev", partners)[0]
    taken_orbitals = lax.ppermute(orbitals, "dev", partners)
    taken_flags = lax.ppermute(tile_flags, "dev", partners)
    tiles, held = call(
        functools.partial(load_kernel, layout),
        [jax.ShapeDtypeStruct(stored_tiles.shape[1:], F32), block],
        [
            pltpu.with_memory_space_constraint(operand, pltpu.HBM)
            for operand in (tile_flags, stored_tiles[0], orbitals)
        ],
        [HBM] * 3,
        [pltpu.SMEM(tile_flags.shape, jnp.int32), semaphore((3,))],
        flops=10**9,
    )
    mask = call(
        functools.partial(mask_kernel, layout),
        jax.ShapeDtypeStruct((group_width + 1, order), F32),
        [taken_flags],
        flops=10**10,
    )

    full = call(
        functools.partial(send_full_kernel, layout),
        [two] * layout.rounds,
        [tiles, taken, mask, held, taken_orbitals],
    )
    full_arrived = []
    for r in range(layout.rounds):
        swaps = [
            (i, i ^ (2 * layout.offset(r, i % 2))) for i in range(group_width)
        ]
        full_arrived.append(lax.ppermute(full[r], "dev", swaps))

    last = call(
        functools.partial(send_last_kernel, layout),
        two,
        [tiles, taken, mask, held, taken_orbitals],
    )
    last_arrived = lax.ppermute(last, ("grp", "dev"), last_moves(layout, groups))

    odd = call(functools.partial(send_odd_kernel, layout), block, [tiles, held])
    odd_arrived = lax.ppermute(odd, ("grp", "dev"), odd_moves(layout, groups))

    mine, others = call(
        functools.partial(near_kernel, layout),
        [block, block],
        [tiles, held, taken_orbitals],
    )
    mine, others = call(
        functools.partial(full_kernel, layout),
        [block, block],
        [tiles, taken, mask, mine, others, *full_arrived],
    )
    others = call(
        functools.partial(back_kernel, layout),
        block,
        [taken, mask, others, last_arrived],
    )
    returned = lax.ppermute(others, "dev", partners)
    mine = call(
        functools.partial(mine_kernel, layout),
        block,
        [tiles, mine, last_arrived, odd_arrived],
    )
    return mine + returned


def solution(mesh):
    in_specs = (
        P(("grp", "dev"), None, None, None),
        P(("grp", "dev"), None),
        P(("grp", "dev"), None),
    )
    out_specs = P(("grp", "dev"), None)
    return jax.shard_map(
        per_device, mesh=mesh, in_specs=in_specs, out_specs=out_specs, check_vma=False
    )
```

```python
import functools

import jax
import jax.numpy as jnp
from jax import lax
from jax.experimental import pallas as pl
from jax.experimental.pallas import tpu as pltpu
from jax.sharding import PartitionSpec as P

HBM = pl.BlockSpec(memory_space=pltpu.HBM)
VMEM = pl.BlockSpec(memory_space=pltpu.VMEM)
F32 = jnp.float32


def parted(value):
    high = value.astype(jnp.bfloat16)
    return high, (value - high.astype(F32)).astype(jnp.bfloat16)


def product_of(left, right, contract):
    dims = ((contract, (0,)), ((), ()))
    dot = functools.partial(
        lax.dot_general, dimension_numbers=dims, preferred_element_type=F32
    )
    (left_high, left_low), (right_high, right_low) = left, right
    return (
        dot(left_high, right_high)
        + dot(left_high, right_low)
        + dot(left_low, right_high)
    )


def times(left, right):
    return product_of(parted(left), parted(right), (1,))


def transposed_times(left, right):
    return product_of(parted(left), parted(right), (0,))


class Layout:
    def __init__(self, group_width):
        self.width = group_width
        self.pairs = group_width // 2
        self.rounds = (self.pairs - 1) // 2
        self.last_offset = self.pairs - 1

    def offset(self, round_index, side):
        return 2 * round_index + 2 - side


def place():
    index = lax.axis_index("dev")
    return index, index // 2, index % 2


def load_kernel(layout, flags_in, tiles_in, orbitals_in, tiles, orbitals, flags, sems):
    copies = [
        pltpu.make_async_copy(flags_in, flags, sems.at[0]),
        pltpu.make_async_copy(tiles_in, tiles, sems.at[1]),
        pltpu.make_async_copy(orbitals_in, orbitals, sems.at[2]),
    ]
    for copy in copies:
        copy.start()
    for copy in copies:
        copy.wait()
    for slot in range(layout.width + 1):
        tiles[slot] = tiles[slot] * flags[0, slot].astype(F32)


def mask_kernel(layout, flags, mask):
    row = flags[...].astype(F32)
    for slot in range(layout.width + 1):
        mask[slot : slot + 1] = jnp.broadcast_to(
            row[:, slot : slot + 1], (1, mask.shape[1])
        )


def taken_tile(taken, mask, slot):
    return taken[slot] * mask[pl.ds(slot, 1), :]


def send_full_kernel(layout, tiles, taken, mask, orbitals, taken_orbitals, *outs):
    index, pair, side = place()
    own, other = orbitals[...], taken_orbitals[...]
    for r in range(layout.rounds):
        far = pair ^ layout.offset(r, side)
        out = outs[r]

        @pl.when(far > pair)
        def _():
            right = parted(jnp.concatenate([own, other], axis=0))
            for k in range(2):
                slot = 2 * far + k
                left = jnp.concatenate(
                    [tiles[slot], taken_tile(taken, mask, slot)], axis=0
                )
                out[k] = product_of(parted(left), right, (0,))

        @pl.when(far < pair)
        def _():
            out[0] = jnp.where(side == 0, own, other)
            out[1] = jnp.where(side == 0, other, own)


def send_last_kernel(layout, tiles, taken, mask, orbitals, taken_orbitals, out):
    index, pair, side = place()
    own, other = orbitals[...], taken_orbitals[...]
    far = pair ^ layout.last_offset
    lower = lax.axis_index("grp") % 2 == 0

    @pl.when((side == 1) & (far > pair))
    def _():
        right = parted(jnp.concatenate([own, other], axis=0))
        for k in range(2):
            slot = 2 * far + k
            left = jnp.concatenate(
                [tiles[slot], taken_tile(taken, mask, slot)], axis=0
            )
            out[k] = product_of(parted(left), right, (0,))

    @pl.when((side == 1) & (far < pair))
    def _():
        out[0] = other
        out[1] = own

    @pl.when((side == 0) & lower)
    def _():
        out[0] = transposed_times(tiles[layout.width], own)
        out[1] = transposed_times(taken_tile(taken, mask, layout.width), other)

    @pl.when((side == 0) & jnp.logical_not(lower))
    def _():
        out[0] = own
        out[1] = other


def send_odd_kernel(layout, tiles, orbitals, out):
    lower = lax.axis_index("grp") % 2 == 1

    @pl.when(lower)
    def _():
        out[...] = transposed_times(tiles[layout.width], orbitals[...])

    @pl.when(jnp.logical_not(lower))
    def _():
        out[...] = orbitals[...]


def near_kernel(layout, tiles, orbitals, taken_orbitals, mine, others):
    index, pair, side = place()
    own, other = orbitals[...], taken_orbitals[...]
    beside = tiles[index ^ 1]
    row = jnp.concatenate([tiles[index], beside], axis=1)
    mine[...] = times(row, jnp.concatenate([own, other], axis=0))
    others[...] = transposed_times(beside, own)


def full_kernel(layout, tiles, taken, mask, mine_in, others_in, *refs):
    index, pair, side = place()
    arrived, mine, others = refs[:-2], refs[-2], refs[-1]
    order = tiles.shape[1]
    mine[...] = mine_in[...]
    others[...] = others_in[...]
    for r in range(layout.rounds):
        far = pair ^ layout.offset(r, side)
        came = arrived[r]

        @pl.when(far > pair)
        def _():
            slots = [2 * far, 2 * far + 1]
            upper = jnp.concatenate([tiles[slot] for slot in slots], axis=1)
            lower = jnp.concatenate(
                [taken_tile(taken, mask, slot) for slot in slots], axis=1
            )
            right = jnp.concatenate([came[0], came[1]], axis=0)
            terms = times(jnp.concatenate([upper, lower], axis=0), right)
            mine[...] += terms[:order]
            others[...] += terms[order:]

        @pl.when(far < pair)
        def _():
            mine[...] += came[side]
            others[...] += came[1 - side]


def back_kernel(layout, taken, mask, others_in, came, others):
    index, pair, side = place()
    far = pair ^ layout.last_offset
    lower = lax.axis_index("grp") % 2 == 0

    @pl.when((side == 1) & (far > pair))
    def _():
        left = jnp.concatenate(
            [taken_tile(taken, mask, 2 * far + k) for k in range(2)], axis=1
        )
        right = jnp.concatenate([came[0], came[1]], axis=0)
        others[...] = others_in[...] + times(left, right)

    @pl.when((side == 1) & (far < pair))
    def _():
        others[...] = others_in[...] + came[0]

    @pl.when((side == 0) & lower)
    def _():
        left = taken_tile(taken, mask, layout.width)
        others[...] = others_in[...] + times(left, came[1])

    @pl.when((side == 0) & jnp.logical_not(lower))
    def _():
        others[...] = others_in[...] + came[1]


def mine_kernel(layout, tiles, mine_in, came, odd_in, mine):
    index, pair, side = place()
    far = pair ^ layout.last_offset
    group = lax.axis_index("grp")
    lower = group % 2 == 0

    @pl.when((side == 1) & (far > pair))
    def _():
        left = jnp.concatenate([tiles[2 * far], tiles[2 * far + 1]], axis=1)
        right = jnp.concatenate([came[0], came[1]], axis=0)
        mine[...] = mine_in[...] + times(left, right)

    @pl.when((side == 1) & (far < pair))
    def _():
        mine[...] = mine_in[...] + came[1]

    @pl.when((side == 0) & lower)
    def _():
        mine[...] = mine_in[...] + times(tiles[layout.width], came[0])

    @pl.when((side == 0) & jnp.logical_not(lower))
    def _():
        mine[...] = mine_in[...] + came[0]

    @pl.when(lower)
    def _():
        mine[...] += jnp.where(group > 0, odd_in[...], 0.0)

    @pl.when(jnp.logical_not(lower))
    def _():
        mine[...] += times(tiles[layout.width], odd_in[...])


def call(body, outs, operands, specs=None, scratch=(), flops=0):
    return pl.pallas_call(
        body,
        out_shape=outs,
        in_specs=specs or [VMEM] * len(operands),
        out_specs=jax.tree.map(lambda _: VMEM, outs),
        scratch_shapes=scratch,
        cost_estimate=pl.CostEstimate(
            flops=flops, bytes_accessed=0, transcendentals=0
        ),
        compiler_params=pltpu.CompilerParams(vmem_limit_bytes=32 * 1024 * 1024),
    )(*operands)


def last_moves(layout, groups):
    moves = []
    for g in range(groups):
        for i in range(layout.width):
            if i % 2 == 1:
                to, j = g, i ^ (2 * layout.last_offset)
            else:
                to, j = g ^ 1, i
                if to >= groups:
                    to = g
            moves.append((g * layout.width + i, to * layout.width + j))
    return moves


def odd_moves(layout, groups):
    moves = []
    for g in range(groups):
        to = g + 1 if g % 2 == 1 else g - 1
        for i in range(layout.width):
            if 0 <= to < groups:
                moves.append((g * layout.width + i, to * layout.width + i))
            else:
                moves.append((g * layout.width + i, g * layout.width + (i ^ 1)))
    return moves


def per_device(stored_tiles, tile_flags, orbitals):
    group_width = lax.axis_size("dev")
    groups = lax.axis_size("grp")
    layout = Layout(group_width)
    order, columns = orbitals.shape
    block = jax.ShapeDtypeStruct((order, columns), F32)
    two = jax.ShapeDtypeStruct((2, order, columns), F32)
    partners = [(i, i ^ 1) for i in range(group_width)]
    semaphore = pltpu.SemaphoreType.DMA

    taken = lax.ppermute(stored_tiles, "dev", partners)[0]
    taken_orbitals = lax.ppermute(orbitals, "dev", partners)
    taken_flags = lax.ppermute(tile_flags, "dev", partners)
    tiles, held = call(
        functools.partial(load_kernel, layout),
        [jax.ShapeDtypeStruct(stored_tiles.shape[1:], F32), block],
        [
            pltpu.with_memory_space_constraint(operand, pltpu.HBM)
            for operand in (tile_flags, stored_tiles[0], orbitals)
        ],
        [HBM] * 3,
        [pltpu.SMEM(tile_flags.shape, jnp.int32), semaphore((3,))],
        flops=10**9,
    )
    mask = call(
        functools.partial(mask_kernel, layout),
        jax.ShapeDtypeStruct((group_width + 1, order), F32),
        [taken_flags],
        flops=10**10,
    )

    full = call(
        functools.partial(send_full_kernel, layout),
        [two] * layout.rounds,
        [tiles, taken, mask, held, taken_orbitals],
    )
    full_arrived = []
    for r in range(layout.rounds):
        swaps = [
            (i, i ^ (2 * layout.offset(r, i % 2))) for i in range(group_width)
        ]
        full_arrived.append(lax.ppermute(full[r], "dev", swaps))

    last = call(
        functools.partial(send_last_kernel, layout),
        two,
        [tiles, taken, mask, held, taken_orbitals],
    )
    last_arrived = lax.ppermute(last, ("grp", "dev"), last_moves(layout, groups))

    odd = call(functools.partial(send_odd_kernel, layout), block, [tiles, held])
    odd_arrived = lax.ppermute(odd, ("grp", "dev"), odd_moves(layout, groups))

    mine, others = call(
        functools.partial(near_kernel, layout),
        [block, block],
        [tiles, held, taken_orbitals],
    )
    mine, others = call(
        functools.partial(full_kernel, layout),
        [block, block],
        [tiles, taken, mask, mine, others, *full_arrived],
    )
    others = call(
        functools.partial(back_kernel, layout),
        block,
        [taken, mask, others, last_arrived],
    )
    returned = lax.ppermute(others, "dev", partners)
    mine = call(
        functools.partial(mine_kernel, layout),
        block,
        [tiles, mine, last_arrived, odd_arrived],
    )
    return mine + returned


def solution(mesh):
    in_specs = (
        P(("grp", "dev"), None, None, None),
        P(("grp", "dev"), None),
        P(("grp", "dev"), None),
    )
    out_specs = P(("grp", "dev"), None)
    return jax.shard_map(
        per_device, mesh=mesh, in_specs=in_specs, out_specs=out_specs, check_vma=False
    )
```

```python
import functools

import jax
import jax.numpy as jnp
from jax import lax
from jax.experimental import pallas as pl
from jax.experimental.pallas import tpu as pltpu
from jax.sharding import PartitionSpec as P

HBM = pl.BlockSpec(memory_space=pltpu.HBM)
VMEM = pl.BlockSpec(memory_space=pltpu.VMEM)
F32 = jnp.float32


def parted(value):
    high = value.astype(jnp.bfloat16)
    return high, (value - high.astype(F32)).astype(jnp.bfloat16)


def product_of(left, right, contract):
    dims = ((contract, (0,)), ((), ()))
    dot = functools.partial(
        lax.dot_general, dimension_numbers=dims, preferred_element_type=F32
    )
    (left_high, left_low), (right_high, right_low) = left, right
    return (
        dot(left_high, right_high)
        + dot(left_high, right_low)
        + dot(left_low, right_high)
    )


def times(left, right):
    return product_of(parted(left), parted(right), (1,))


def transposed_times(left, right):
    return product_of(parted(left), parted(right), (0,))


class Layout:
    def __init__(self, group_width):
        self.width = group_width
        self.pairs = group_width // 2
        self.offsets = list(range(self.pairs - 1, 0, -1))

    def moves(self, round_index, groups):
        moves = []
        for g in range(groups):
            to = g + 1 if g % 2 == round_index else g - 1
            if round_index > 1 or not 0 <= to < groups:
                to = g
            for i in range(self.width):
                if i % 2 == 0:
                    target = to * self.width + i
                else:
                    far = i ^ (2 * self.offsets[round_index])
                    target = g * self.width + far
                moves.append((g * self.width + i, target))
        return moves


def place():
    index = lax.axis_index("dev")
    return index, index // 2, index % 2


def load_kernel(layout, flags_in, tiles_in, orbitals_in, tiles, orbitals, flags, sems):
    copies = [
        pltpu.make_async_copy(flags_in, flags, sems.at[0]),
        pltpu.make_async_copy(tiles_in, tiles, sems.at[1]),
        pltpu.make_async_copy(orbitals_in, orbitals, sems.at[2]),
    ]
    for copy in copies:
        copy.start()
    for copy in copies:
        copy.wait()
    for slot in range(layout.width + 1):
        tiles[slot] = tiles[slot] * flags[0, slot].astype(F32)


def mask_kernel(layout, flags, mask):
    row = flags[...].astype(F32)
    for slot in range(layout.width + 1):
        mask[slot : slot + 1] = jnp.broadcast_to(
            row[:, slot : slot + 1], (1, mask.shape[1])
        )


def taken_tile(taken, mask, slot):
    return taken[slot] * mask[pl.ds(slot, 1), :]


def send_kernel(layout, r, tiles, taken, mask, orbitals, taken_orbitals, out):
    index, pair, side = place()
    own, other = orbitals[...], taken_orbitals[...]
    far = pair ^ layout.offsets[r]
    lower = lax.axis_index("grp") % 2 == r

    @pl.when((side == 1) & (far > pair))
    def _():
        right = parted(jnp.concatenate([own, other], axis=0))
        for k in range(2):
            slot = 2 * far + k
            left = jnp.concatenate(
                [tiles[slot], taken_tile(taken, mask, slot)], axis=0
            )
            out[k] = product_of(parted(left), right, (0,))

    @pl.when((side == 1) & (far < pair))
    def _():
        out[0] = other
        out[1] = own

    @pl.when((side == 0) & lower)
    def _():
        out[0] = transposed_times(tiles[layout.width], own)
        out[1] = transposed_times(taken_tile(taken, mask, layout.width), other)

    @pl.when((side == 0) & jnp.logical_not(lower))
    def _():
        out[0] = own
        out[1] = other


def near_kernel(layout, tiles, orbitals, taken_orbitals, mine, others):
    index, pair, side = place()
    own, other = orbitals[...], taken_orbitals[...]
    beside = tiles[index ^ 1]
    row = jnp.concatenate([tiles[index], beside], axis=1)
    mine[...] = times(row, jnp.concatenate([own, other], axis=0))
    others[...] = transposed_times(beside, own)


def take(layout, r, came, row, tile_of, total):
    index, pair, side = place()
    far = pair ^ layout.offsets[r]
    group = lax.axis_index("grp")
    lower = group % 2 == r

    @pl.when((side == 1) & (far > pair))
    def _():
        left = jnp.concatenate([tile_of(2 * far), tile_of(2 * far + 1)], axis=1)
        right = jnp.concatenate([came[0], came[1]], axis=0)
        total[...] += times(left, right)

    @pl.when((side == 1) & (far < pair))
    def _():
        total[...] += came[1 - row]

    if r < 2:

        @pl.when((side == 0) & lower)
        def _():
            total[...] += times(tile_of(layout.width), came[row])

        @pl.when((side == 0) & jnp.logical_not(lower) & (group > 0))
        def _():
            total[...] += came[row]


def take_mine_kernel(layout, rounds, tiles, mine_in, *refs):
    arrived, mine = refs[:-1], refs[-1]
    mine[...] = mine_in[...]
    for r, came in zip(rounds, arrived):
        take(layout, r, came, 0, lambda slot: tiles[slot], mine)


def take_others_kernel(layout, r, taken, mask, others_in, came, others):
    others[...] = others_in[...]
    take(layout, r, came, 1, lambda slot: taken_tile(taken, mask, slot), others)


def call(body, outs, operands, specs=None, scratch=(), flops=0):
    return pl.pallas_call(
        body,
        out_shape=outs,
        in_specs=specs or [VMEM] * len(operands),
        out_specs=jax.tree.map(lambda _: VMEM, outs),
        scratch_shapes=scratch,
        cost_estimate=pl.CostEstimate(
            flops=flops, bytes_accessed=0, transcendentals=0
        ),
        compiler_params=pltpu.CompilerParams(vmem_limit_bytes=32 * 1024 * 1024),
    )(*operands)


def per_device(stored_tiles, tile_flags, orbitals):
    group_width = lax.axis_size("dev")
    groups = lax.axis_size("grp")
    layout = Layout(group_width)
    order, columns = orbitals.shape
    block = jax.ShapeDtypeStruct((order, columns), F32)
    two = jax.ShapeDtypeStruct((2, order, columns), F32)
    partners = [(i, i ^ 1) for i in range(group_width)]
    semaphore = pltpu.SemaphoreType.DMA

    taken = lax.ppermute(stored_tiles, "dev", partners)[0]
    taken_orbitals = lax.ppermute(orbitals, "dev", partners)
    taken_flags = lax.ppermute(tile_flags, "dev", partners)
    tiles, held = call(
        functools.partial(load_kernel, layout),
        [jax.ShapeDtypeStruct(stored_tiles.shape[1:], F32), block],
        [
            pltpu.with_memory_space_constraint(operand, pltpu.HBM)
            for operand in (tile_flags, stored_tiles[0], orbitals)
        ],
        [HBM] * 3,
        [pltpu.SMEM(tile_flags.shape, jnp.int32), semaphore((3,))],
        flops=10**9,
    )
    mask = call(
        functools.partial(mask_kernel, layout),
        jax.ShapeDtypeStruct((group_width + 1, order), F32),
        [taken_flags],
        flops=10**9,
    )

    arrived = []
    for r in range(len(layout.offsets)):
        sent = call(
            functools.partial(send_kernel, layout, r),
            two,
            [tiles, taken, mask, held, taken_orbitals],
        )
        moves = layout.moves(r, groups)
        arrived.append(lax.ppermute(sent, ("grp", "dev"), moves))

    mine, others = call(
        functools.partial(near_kernel, layout),
        [block, block],
        [tiles, held, taken_orbitals],
    )
    for r, came in enumerate(arrived):
        others = call(
            functools.partial(take_others_kernel, layout, r),
            block,
            [taken, mask, others, came],
        )
    returned = lax.ppermute(others, "dev", partners)
    rounds = list(range(len(arrived)))
    mine = call(
        functools.partial(take_mine_kernel, layout, rounds),
        block,
        [tiles, mine, *arrived],
    )
    return mine + returned


def solution(mesh):
    in_specs = (
        P(("grp", "dev"), None, None, None),
        P(("grp", "dev"), None),
        P(("grp", "dev"), None),
    )
    out_specs = P(("grp", "dev"), None)
    return jax.shard_map(
        per_device, mesh=mesh, in_specs=in_specs, out_specs=out_specs, check_vma=False
    )
```

```python
import functools

import jax
import jax.numpy as jnp
from jax import lax
from jax.experimental import pallas as pl
from jax.experimental.pallas import tpu as pltpu
from jax.sharding import PartitionSpec as P

HBM = pl.BlockSpec(memory_space=pltpu.HBM)
VMEM = pl.BlockSpec(memory_space=pltpu.VMEM)
F32 = jnp.float32


def parted(value):
    high = value.astype(jnp.bfloat16)
    return high, (value - high.astype(F32)).astype(jnp.bfloat16)


def product_of(left, right, contract):
    dims = ((contract, (0,)), ((), ()))
    dot = functools.partial(
        lax.dot_general, dimension_numbers=dims, preferred_element_type=F32
    )
    (left_high, left_low), (right_high, right_low) = left, right
    return (
        dot(left_high, right_high)
        + dot(left_high, right_low)
        + dot(left_low, right_high)
    )


def times(left, right):
    return product_of(parted(left), parted(right), (1,))


def transposed_times(left, right):
    return product_of(parted(left), parted(right), (0,))


class Layout:
    def __init__(self, group_width, groups):
        self.width = group_width
        self.groups = groups
        self.pairs = group_width // 2
        self.offsets = list(range(self.pairs - 1, 0, -1))

    def moves(self, r):
        moves = []
        for g in range(self.groups):
            to = g + 1 if g % 2 == r else g - 1
            idle = r > 1 or not 0 <= to < self.groups
            for i in range(self.width):
                far = i ^ (2 * self.offsets[r])
                if i % 2 == 1:
                    target = (g, far ^ 1 if idle else far)
                else:
                    target = (g, i ^ 1) if idle else (to, i)
                moves.append((g * self.width + i, target[0] * self.width + target[1]))
        return moves

    def role(self, r):
        side = lax.axis_index("dev") % 2
        if r > 1:
            return side == 0, None
        group = lax.axis_index("grp")
        to = jnp.where(group % 2 == r, group + 1, group - 1)
        swaps = (to >= 0) & (to < self.groups)
        return swaps == (side == 1), (side == 0) & swaps


def place():
    index = lax.axis_index("dev")
    return index, index // 2, index % 2


def load_kernel(layout, flags_in, tiles_in, orbitals_in, tiles, orbitals, flags, sems):
    copies = [
        pltpu.make_async_copy(flags_in, flags, sems.at[0]),
        pltpu.make_async_copy(tiles_in, tiles, sems.at[1]),
        pltpu.make_async_copy(orbitals_in, orbitals, sems.at[2]),
    ]
    for copy in copies:
        copy.start()
    for copy in copies:
        copy.wait()
    for slot in range(layout.width + 1):
        tiles[slot] = tiles[slot] * flags[0, slot].astype(F32)


def mask_kernel(layout, flags, mask):
    row = flags[...].astype(F32)
    for slot in range(layout.width + 1):
        mask[slot : slot + 1] = jnp.broadcast_to(
            row[:, slot : slot + 1], (1, mask.shape[1])
        )


def taken_tile(taken, mask, slot):
    return taken[slot] * mask[pl.ds(slot, 1), :]


def send_kernel(layout, r, tiles, taken, mask, orbitals, taken_orbitals, out):
    index, pair, side = place()
    own, other = orbitals[...], taken_orbitals[...]
    far = pair ^ layout.offsets[r]
    lower = lax.axis_index("grp") % 2 == r

    @pl.when((side == 1) & (far > pair))
    def _():
        right = parted(jnp.concatenate([own, other], axis=0))
        for k in range(2):
            slot = 2 * far + k
            left = jnp.concatenate(
                [tiles[slot], taken_tile(taken, mask, slot)], axis=0
            )
            out[k] = product_of(parted(left), right, (0,))

    @pl.when((side == 1) & (far < pair))
    def _():
        out[0] = other
        out[1] = own

    @pl.when((side == 0) & lower)
    def _():
        out[0] = transposed_times(tiles[layout.width], own)
        out[1] = transposed_times(taken_tile(taken, mask, layout.width), other)

    @pl.when((side == 0) & jnp.logical_not(lower))
    def _():
        out[0] = own
        out[1] = other


def near_kernel(layout, tiles, orbitals, taken_orbitals, mine, others):
    index, pair, side = place()
    own, other = orbitals[...], taken_orbitals[...]
    beside = tiles[index ^ 1]
    row = jnp.concatenate([tiles[index], beside], axis=1)
    mine[...] = times(row, jnp.concatenate([own, other], axis=0))
    others[...] = transposed_times(beside, own)


def take(layout, r, came, row, tile_of, total):
    index, pair, side = place()
    far = pair ^ layout.offsets[r]
    takes_pair, takes_group = layout.role(r)

    @pl.when(takes_pair & (far > pair))
    def _():
        left = jnp.concatenate([tile_of(2 * far), tile_of(2 * far + 1)], axis=1)
        right = jnp.concatenate([came[0], came[1]], axis=0)
        total[...] += times(left, right)

    @pl.when(takes_pair & (far < pair))
    def _():
        total[...] += came[side ^ row]

    if takes_group is not None:
        lower = lax.axis_index("grp") % 2 == r

        @pl.when(takes_group & lower)
        def _():
            total[...] += times(tile_of(layout.width), came[row])

        @pl.when(takes_group & jnp.logical_not(lower))
        def _():
            total[...] += came[row]


def take_mine_kernel(layout, rounds, tiles, mine_in, *refs):
    arrived, mine = refs[:-1], refs[-1]
    mine[...] = mine_in[...]
    for r, came in zip(rounds, arrived):
        take(layout, r, came, 0, lambda slot: tiles[slot], mine)


def take_others_kernel(layout, r, taken, mask, others_in, came, others):
    others[...] = others_in[...]
    take(layout, r, came, 1, lambda slot: taken_tile(taken, mask, slot), others)


def call(body, outs, operands, specs=None, scratch=(), flops=0):
    return pl.pallas_call(
        body,
        out_shape=outs,
        in_specs=specs or [VMEM] * len(operands),
        out_specs=jax.tree.map(lambda _: VMEM, outs),
        scratch_shapes=scratch,
        cost_estimate=pl.CostEstimate(
            flops=flops, bytes_accessed=0, transcendentals=0
        ),
        compiler_params=pltpu.CompilerParams(vmem_limit_bytes=32 * 1024 * 1024),
    )(*operands)


def per_device(stored_tiles, tile_flags, orbitals):
    group_width = lax.axis_size("dev")
    layout = Layout(group_width, lax.axis_size("grp"))
    order, columns = orbitals.shape
    block = jax.ShapeDtypeStruct((order, columns), F32)
    two = jax.ShapeDtypeStruct((2, order, columns), F32)
    partners = [(i, i ^ 1) for i in range(group_width)]
    semaphore = pltpu.SemaphoreType.DMA

    taken = lax.ppermute(stored_tiles, "dev", partners)[0]
    taken_orbitals = lax.ppermute(orbitals, "dev", partners)
    taken_flags = lax.ppermute(tile_flags, "dev", partners)
    tiles, held = call(
        functools.partial(load_kernel, layout),
        [jax.ShapeDtypeStruct(stored_tiles.shape[1:], F32), block],
        [
            pltpu.with_memory_space_constraint(operand, pltpu.HBM)
            for operand in (tile_flags, stored_tiles[0], orbitals)
        ],
        [HBM] * 3,
        [pltpu.SMEM(tile_flags.shape, jnp.int32), semaphore((3,))],
        flops=10**9,
    )
    mask = call(
        functools.partial(mask_kernel, layout),
        jax.ShapeDtypeStruct((group_width + 1, order), F32),
        [taken_flags],
        flops=10**9,
    )

    arrived = []
    for r in range(len(layout.offsets)):
        sent = call(
            functools.partial(send_kernel, layout, r),
            two,
            [tiles, taken, mask, held, taken_orbitals],
        )
        arrived.append(lax.ppermute(sent, ("grp", "dev"), layout.moves(r)))

    mine, others = call(
        functools.partial(near_kernel, layout),
        [block, block],
        [tiles, held, taken_orbitals],
    )
    for r, came in enumerate(arrived):
        others = call(
            functools.partial(take_others_kernel, layout, r),
            block,
            [taken, mask, others, came],
        )
    returned = lax.ppermute(others, "dev", partners)
    rounds = list(range(len(arrived)))
    mine = call(
        functools.partial(take_mine_kernel, layout, rounds),
        block,
        [tiles, mine, *arrived],
    )
    return mine + returned


def solution(mesh):
    in_specs = (
        P(("grp", "dev"), None, None, None),
        P(("grp", "dev"), None),
        P(("grp", "dev"), None),
    )
    out_specs = P(("grp", "dev"), None)
    return jax.shard_map(
        per_device, mesh=mesh, in_specs=in_specs, out_specs=out_specs, check_vma=False
    )
```

```python
import functools

import jax
import jax.numpy as jnp
from jax import lax
from jax.experimental import pallas as pl
from jax.experimental.pallas import tpu as pltpu
from jax.sharding import PartitionSpec as P

HBM = pl.BlockSpec(memory_space=pltpu.HBM)
VMEM = pl.BlockSpec(memory_space=pltpu.VMEM)
F32 = jnp.float32


def parted(value):
    high = value.astype(jnp.bfloat16)
    return high, (value - high.astype(F32)).astype(jnp.bfloat16)


def product_of(left, right, contract):
    dims = ((contract, (0,)), ((), ()))
    dot = functools.partial(
        lax.dot_general, dimension_numbers=dims, preferred_element_type=F32
    )
    (left_high, left_low), (right_high, right_low) = left, right
    return (
        dot(left_high, right_high)
        + dot(left_high, right_low)
        + dot(left_low, right_high)
    )


def times(left, right):
    return product_of(parted(left), parted(right), (1,))


def transposed_times(left, right):
    return product_of(parted(left), parted(right), (0,))


class Layout:
    def __init__(self, group_width):
        self.width = group_width
        self.pairs = group_width // 2
        self.rounds = (self.pairs - 1) // 2
        self.first_offset = self.pairs - 1

    def offset(self, round_index, side):
        return 2 * round_index + 2 - side


def place():
    index = lax.axis_index("dev")
    return index, index // 2, index % 2


def load_kernel(layout, flags_in, tiles_in, orbitals_in, tiles, orbitals, flags, sems):
    copies = [
        pltpu.make_async_copy(flags_in, flags, sems.at[0]),
        pltpu.make_async_copy(tiles_in, tiles, sems.at[1]),
        pltpu.make_async_copy(orbitals_in, orbitals, sems.at[2]),
    ]
    for copy in copies:
        copy.start()
    for copy in copies:
        copy.wait()
    for slot in range(layout.width + 1):
        tiles[slot] = tiles[slot] * flags[0, slot].astype(F32)


def mask_kernel(layout, flags, mask):
    row = flags[...].astype(F32)
    for slot in range(layout.width + 1):
        mask[slot : slot + 1] = jnp.broadcast_to(
            row[:, slot : slot + 1], (1, mask.shape[1])
        )


def taken_tile(taken, mask, slot):
    return taken[slot] * mask[pl.ds(slot, 1), :]


def send_full_kernel(layout, tiles, taken, mask, orbitals, taken_orbitals, *outs):
    index, pair, side = place()
    own, other = orbitals[...], taken_orbitals[...]
    for r in range(layout.rounds):
        far = pair ^ layout.offset(r, side)
        out = outs[r]

        @pl.when(far > pair)
        def _():
            right = parted(jnp.concatenate([own, other], axis=0))
            for k in range(2):
                slot = 2 * far + k
                left = jnp.concatenate(
                    [tiles[slot], taken_tile(taken, mask, slot)], axis=0
                )
                out[k] = product_of(parted(left), right, (0,))

        @pl.when(far < pair)
        def _():
            out[0] = jnp.where(side == 0, own, other)
            out[1] = jnp.where(side == 0, other, own)


def send_first_kernel(layout, tiles, taken, mask, orbitals, taken_orbitals, out):
    index, pair, side = place()
    own, other = orbitals[...], taken_orbitals[...]
    far = pair ^ layout.first_offset
    lower = lax.axis_index("grp") % 2 == 0

    @pl.when((side == 1) & (far > pair))
    def _():
        right = parted(jnp.concatenate([own, other], axis=0))
        for k in range(2):
            slot = 2 * far + k
            left = jnp.concatenate(
                [tiles[slot], taken_tile(taken, mask, slot)], axis=0
            )
            out[k] = product_of(parted(left), right, (0,))

    @pl.when((side == 1) & (far < pair))
    def _():
        out[0] = other
        out[1] = own

    @pl.when((side == 0) & lower)
    def _():
        out[0] = transposed_times(tiles[layout.width], own)
        out[1] = transposed_times(taken_tile(taken, mask, layout.width), other)

    @pl.when((side == 0) & jnp.logical_not(lower))
    def _():
        out[0] = own
        out[1] = other


def send_odd_kernel(layout, tiles, orbitals, out):
    lower = lax.axis_index("grp") % 2 == 1

    @pl.when(lower)
    def _():
        out[...] = transposed_times(tiles[layout.width], orbitals[...])

    @pl.when(jnp.logical_not(lower))
    def _():
        out[...] = orbitals[...]


def near_kernel(layout, tiles, orbitals, taken_orbitals, mine, others):
    index, pair, side = place()
    own, other = orbitals[...], taken_orbitals[...]
    beside = tiles[index ^ 1]
    row = jnp.concatenate([tiles[index], beside], axis=1)
    mine[...] = times(row, jnp.concatenate([own, other], axis=0))
    others[...] = transposed_times(beside, own)


def take_first(layout, came, row, tile_of, total):
    index, pair, side = place()
    far = pair ^ layout.first_offset
    lower = lax.axis_index("grp") % 2 == 0

    @pl.when((side == 1) & (far > pair))
    def _():
        left = jnp.concatenate([tile_of(2 * far), tile_of(2 * far + 1)], axis=1)
        right = jnp.concatenate([came[0], came[1]], axis=0)
        total[...] += times(left, right)

    @pl.when((side == 1) & (far < pair))
    def _():
        total[...] += came[1 - row]

    @pl.when((side == 0) & lower)
    def _():
        total[...] += times(tile_of(layout.width), came[row])

    @pl.when((side == 0) & jnp.logical_not(lower))
    def _():
        total[...] += came[row]


def take_full(layout, arrived, row, tile_of, total):
    index, pair, side = place()
    for r, came in enumerate(arrived):
        far = pair ^ layout.offset(r, side)

        @pl.when(far > pair)
        def _():
            left = jnp.concatenate([tile_of(2 * far), tile_of(2 * far + 1)], axis=1)
            right = jnp.concatenate([came[0], came[1]], axis=0)
            total[...] += times(left, right)

        @pl.when(far < pair)
        def _():
            total[...] += came[side ^ row]


def first_kernel(layout, tiles, taken, mask, mine_in, others_in, came, mine, others):
    mine[...] = mine_in[...]
    others[...] = others_in[...]
    take_first(layout, came, 0, lambda slot: tiles[slot], mine)
    take_first(layout, came, 1, lambda slot: taken_tile(taken, mask, slot), others)


def others_kernel(layout, taken, mask, others_in, *refs):
    arrived, others = refs[:-1], refs[-1]
    others[...] = others_in[...]
    take_full(layout, arrived, 1, lambda slot: taken_tile(taken, mask, slot), others)


def mine_kernel(layout, tiles, mine_in, odd_in, *refs):
    arrived, mine = refs[:-1], refs[-1]
    group = lax.axis_index("grp")
    lower = group % 2 == 1

    @pl.when(lower)
    def _():
        mine[...] = mine_in[...] + times(tiles[layout.width], odd_in[...])

    @pl.when(jnp.logical_not(lower))
    def _():
        mine[...] = mine_in[...] + jnp.where(group > 0, odd_in[...], 0.0)

    take_full(layout, arrived, 0, lambda slot: tiles[slot], mine)


def call(body, outs, operands, specs=None, scratch=(), flops=0):
    return pl.pallas_call(
        body,
        out_shape=outs,
        in_specs=specs or [VMEM] * len(operands),
        out_specs=jax.tree.map(lambda _: VMEM, outs),
        scratch_shapes=scratch,
        cost_estimate=pl.CostEstimate(
            flops=flops, bytes_accessed=0, transcendentals=0
        ),
        compiler_params=pltpu.CompilerParams(vmem_limit_bytes=32 * 1024 * 1024),
    )(*operands)


def first_moves(layout, groups):
    moves = []
    for g in range(groups):
        for i in range(layout.width):
            if i % 2 == 1:
                to, j = g, i ^ (2 * layout.first_offset)
            else:
                to, j = g ^ 1, i
                if to >= groups:
                    to = g
            moves.append((g * layout.width + i, to * layout.width + j))
    return moves


def odd_moves(layout, groups):
    moves = []
    for g in range(groups):
        to = g + 1 if g % 2 == 1 else g - 1
        for i in range(layout.width):
            if 0 <= to < groups:
                moves.append((g * layout.width + i, to * layout.width + i))
            else:
                moves.append((g * layout.width + i, g * layout.width + (i ^ 1)))
    return moves


def per_device(stored_tiles, tile_flags, orbitals):
    group_width = lax.axis_size("dev")
    groups = lax.axis_size("grp")
    layout = Layout(group_width)
    order, columns = orbitals.shape
    block = jax.ShapeDtypeStruct((order, columns), F32)
    two = jax.ShapeDtypeStruct((2, order, columns), F32)
    partners = [(i, i ^ 1) for i in range(group_width)]
    semaphore = pltpu.SemaphoreType.DMA

    taken = lax.ppermute(stored_tiles, "dev", partners)[0]
    taken_orbitals = lax.ppermute(orbitals, "dev", partners)
    taken_flags = lax.ppermute(tile_flags, "dev", partners)
    tiles, held = call(
        functools.partial(load_kernel, layout),
        [jax.ShapeDtypeStruct(stored_tiles.shape[1:], F32), block],
        [
            pltpu.with_memory_space_constraint(operand, pltpu.HBM)
            for operand in (tile_flags, stored_tiles[0], orbitals)
        ],
        [HBM] * 3,
        [pltpu.SMEM(tile_flags.shape, jnp.int32), semaphore((3,))],
        flops=10**9,
    )
    mask = call(
        functools.partial(mask_kernel, layout),
        jax.ShapeDtypeStruct((group_width + 1, order), F32),
        [taken_flags],
        flops=10**9,
    )

    first = call(
        functools.partial(send_first_kernel, layout),
        two,
        [tiles, taken, mask, held, taken_orbitals],
    )
    first_arrived = lax.ppermute(first, ("grp", "dev"), first_moves(layout, groups))

    full = call(
        functools.partial(send_full_kernel, layout),
        [two] * layout.rounds,
        [tiles, taken, mask, held, taken_orbitals],
    )
    full_arrived = []
    for r in range(layout.rounds):
        swaps = [
            (i, i ^ (2 * layout.offset(r, i % 2))) for i in range(group_width)
        ]
        full_arrived.append(lax.ppermute(full[r], "dev", swaps))

    odd = call(functools.partial(send_odd_kernel, layout), block, [tiles, held])
    odd_arrived = lax.ppermute(odd, ("grp", "dev"), odd_moves(layout, groups))

    mine, others = call(
        functools.partial(near_kernel, layout),
        [block, block],
        [tiles, held, taken_orbitals],
    )
    mine, others = call(
        functools.partial(first_kernel, layout),
        [block, block],
        [tiles, taken, mask, mine, others, first_arrived],
    )
    others = call(
        functools.partial(others_kernel, layout),
        block,
        [taken, mask, others, *full_arrived],
    )
    returned = lax.ppermute(others, "dev", partners)
    mine = call(
        functools.partial(mine_kernel, layout),
        block,
        [tiles, mine, odd_arrived, *full_arrived],
    )
    return mine + returned


def solution(mesh):
    in_specs = (
        P(("grp", "dev"), None, None, None),
        P(("grp", "dev"), None),
        P(("grp", "dev"), None),
    )
    out_specs = P(("grp", "dev"), None)
    return jax.shard_map(
        per_device, mesh=mesh, in_specs=in_specs, out_specs=out_specs, check_vma=False
    )
```

```python
import functools

import jax
import jax.numpy as jnp
from jax import lax
from jax.experimental import pallas as pl
from jax.experimental.pallas import tpu as pltpu
from jax.sharding import PartitionSpec as P

HBM = pl.BlockSpec(memory_space=pltpu.HBM)
VMEM = pl.BlockSpec(memory_space=pltpu.VMEM)
F32 = jnp.float32


def parted(value):
    high = value.astype(jnp.bfloat16)
    return high, (value - high.astype(F32)).astype(jnp.bfloat16)


def product_of(left, right, contract):
    dims = ((contract, (0,)), ((), ()))
    dot = functools.partial(
        lax.dot_general, dimension_numbers=dims, preferred_element_type=F32
    )
    (left_high, left_low), (right_high, right_low) = left, right
    return (
        dot(left_high, right_high)
        + dot(left_high, right_low)
        + dot(left_low, right_high)
    )


def times(left, right):
    return product_of(parted(left), parted(right), (1,))


def transposed_times(left, right):
    return product_of(parted(left), parted(right), (0,))


class Layout:
    def __init__(self, group_width):
        self.width = group_width
        self.pairs = group_width // 2
        self.rounds = (self.pairs - 1) // 2
        self.last_offset = 1

    def offset(self, round_index, side):
        return 2 * round_index + 2 + side


def place():
    index = lax.axis_index("dev")
    return index, index // 2, index % 2


def load_kernel(layout, flags_in, tiles_in, orbitals_in, tiles, orbitals, flags, sems):
    copies = [
        pltpu.make_async_copy(flags_in, flags, sems.at[0]),
        pltpu.make_async_copy(tiles_in, tiles, sems.at[1]),
        pltpu.make_async_copy(orbitals_in, orbitals, sems.at[2]),
    ]
    for copy in copies:
        copy.start()
    for copy in copies:
        copy.wait()
    for slot in range(layout.width + 1):
        tiles[slot] = tiles[slot] * flags[0, slot].astype(F32)


def mask_kernel(layout, flags, mask):
    row = flags[...].astype(F32)
    for slot in range(layout.width + 1):
        mask[slot : slot + 1] = jnp.broadcast_to(
            row[:, slot : slot + 1], (1, mask.shape[1])
        )


def taken_tile(taken, mask, slot):
    return taken[slot] * mask[pl.ds(slot, 1), :]


def send_full_kernel(layout, tiles, taken, mask, orbitals, taken_orbitals, *outs):
    index, pair, side = place()
    own, other = orbitals[...], taken_orbitals[...]
    for r in range(layout.rounds):
        far = pair ^ layout.offset(r, side)
        out = outs[r]

        @pl.when(far > pair)
        def _():
            right = parted(jnp.concatenate([own, other], axis=0))
            for k in range(2):
                slot = 2 * far + k
                left = jnp.concatenate(
                    [tiles[slot], taken_tile(taken, mask, slot)], axis=0
                )
                out[k] = product_of(parted(left), right, (0,))

        @pl.when(far < pair)
        def _():
            out[0] = jnp.where(side == 0, own, other)
            out[1] = jnp.where(side == 0, other, own)


def send_last_kernel(layout, tiles, taken, mask, orbitals, taken_orbitals, out):
    index, pair, side = place()
    own, other = orbitals[...], taken_orbitals[...]
    far = pair ^ layout.last_offset
    lower = lax.axis_index("grp") % 2 == 0

    @pl.when((side == 1) & (far > pair))
    def _():
        right = parted(jnp.concatenate([own, other], axis=0))
        for k in range(2):
            slot = 2 * far + k
            left = jnp.concatenate(
                [tiles[slot], taken_tile(taken, mask, slot)], axis=0
            )
            out[k] = product_of(parted(left), right, (0,))

    @pl.when((side == 1) & (far < pair))
    def _():
        out[0] = other
        out[1] = own

    @pl.when((side == 0) & lower)
    def _():
        out[0] = transposed_times(tiles[layout.width], own)
        out[1] = transposed_times(taken_tile(taken, mask, layout.width), other)

    @pl.when((side == 0) & jnp.logical_not(lower))
    def _():
        out[0] = own
        out[1] = other


def send_odd_kernel(layout, tiles, orbitals, out):
    lower = lax.axis_index("grp") % 2 == 1

    @pl.when(lower)
    def _():
        out[...] = transposed_times(tiles[layout.width], orbitals[...])

    @pl.when(jnp.logical_not(lower))
    def _():
        out[...] = orbitals[...]


def near_kernel(layout, tiles, orbitals, taken_orbitals, mine, others):
    index, pair, side = place()
    own, other = orbitals[...], taken_orbitals[...]
    beside = tiles[index ^ 1]
    row = jnp.concatenate([tiles[index], beside], axis=1)
    mine[...] = times(row, jnp.concatenate([own, other], axis=0))
    others[...] = transposed_times(beside, own)


def take_last(layout, came, row, tile_of, total):
    index, pair, side = place()
    far = pair ^ layout.last_offset
    lower = lax.axis_index("grp") % 2 == 0

    @pl.when((side == 1) & (far > pair))
    def _():
        left = jnp.concatenate([tile_of(2 * far), tile_of(2 * far + 1)], axis=1)
        right = jnp.concatenate([came[0], came[1]], axis=0)
        total[...] += times(left, right)

    @pl.when((side == 1) & (far < pair))
    def _():
        total[...] += came[1 - row]

    @pl.when((side == 0) & lower)
    def _():
        total[...] += times(tile_of(layout.width), came[row])

    @pl.when((side == 0) & jnp.logical_not(lower))
    def _():
        total[...] += came[row]


def take_full(layout, arrived, row, tile_of, total):
    index, pair, side = place()
    for r, came in enumerate(arrived):
        far = pair ^ layout.offset(r, side)

        @pl.when(far > pair)
        def _():
            left = jnp.concatenate([tile_of(2 * far), tile_of(2 * far + 1)], axis=1)
            right = jnp.concatenate([came[0], came[1]], axis=0)
            total[...] += times(left, right)

        @pl.when(far < pair)
        def _():
            total[...] += came[side ^ row]


def others_kernel(layout, taken, mask, others_in, last, *refs):
    arrived, others = refs[:-1], refs[-1]
    others[...] = others_in[...]

    def tile_of(slot):
        return taken_tile(taken, mask, slot)

    take_last(layout, last, 1, tile_of, others)
    take_full(layout, arrived, 1, tile_of, others)


def mine_kernel(layout, tiles, mine_in, odd_in, last, *refs):
    arrived, mine = refs[:-1], refs[-1]
    group = lax.axis_index("grp")
    lower = group % 2 == 1

    @pl.when(lower)
    def _():
        mine[...] = mine_in[...] + times(tiles[layout.width], odd_in[...])

    @pl.when(jnp.logical_not(lower))
    def _():
        mine[...] = mine_in[...] + jnp.where(group > 0, odd_in[...], 0.0)

    take_last(layout, last, 0, lambda slot: tiles[slot], mine)
    take_full(layout, arrived, 0, lambda slot: tiles[slot], mine)


def call(body, outs, operands, specs=None, scratch=(), flops=0):
    return pl.pallas_call(
        body,
        out_shape=outs,
        in_specs=specs or [VMEM] * len(operands),
        out_specs=jax.tree.map(lambda _: VMEM, outs),
        scratch_shapes=scratch,
        cost_estimate=pl.CostEstimate(
            flops=flops, bytes_accessed=0, transcendentals=0
        ),
        compiler_params=pltpu.CompilerParams(vmem_limit_bytes=32 * 1024 * 1024),
    )(*operands)


def last_moves(layout, groups):
    moves = []
    for g in range(groups):
        for i in range(layout.width):
            if i % 2 == 1:
                to, j = g, i ^ (2 * layout.last_offset)
            else:
                to, j = g ^ 1, i
                if to >= groups:
                    to = g
            moves.append((g * layout.width + i, to * layout.width + j))
    return moves


def odd_moves(layout, groups):
    moves = []
    for g in range(groups):
        to = g + 1 if g % 2 == 1 else g - 1
        for i in range(layout.width):
            if 0 <= to < groups:
                moves.append((g * layout.width + i, to * layout.width + i))
            else:
                moves.append((g * layout.width + i, g * layout.width + (i ^ 1)))
    return moves


def per_device(stored_tiles, tile_flags, orbitals):
    group_width = lax.axis_size("dev")
    groups = lax.axis_size("grp")
    layout = Layout(group_width)
    order, columns = orbitals.shape
    block = jax.ShapeDtypeStruct((order, columns), F32)
    two = jax.ShapeDtypeStruct((2, order, columns), F32)
    partners = [(i, i ^ 1) for i in range(group_width)]
    semaphore = pltpu.SemaphoreType.DMA

    taken_flags = lax.ppermute(tile_flags, "dev", partners)
    taken = lax.ppermute(stored_tiles, "dev", partners)[0]
    taken_orbitals = lax.ppermute(orbitals, "dev", partners)
    tiles, held = call(
        functools.partial(load_kernel, layout),
        [jax.ShapeDtypeStruct(stored_tiles.shape[1:], F32), block],
        [
            pltpu.with_memory_space_constraint(operand, pltpu.HBM)
            for operand in (tile_flags, stored_tiles[0], orbitals)
        ],
        [HBM] * 3,
        [pltpu.SMEM(tile_flags.shape, jnp.int32), semaphore((3,))],
        flops=10**9,
    )
    mask = call(
        functools.partial(mask_kernel, layout),
        jax.ShapeDtypeStruct((group_width + 1, order), F32),
        [taken_flags],
        flops=10**9,
    )

    full = call(
        functools.partial(send_full_kernel, layout),
        [two] * layout.rounds,
        [tiles, taken, mask, held, taken_orbitals],
    )
    full_arrived = []
    for r in range(layout.rounds):
        swaps = [
            (i, i ^ (2 * layout.offset(r, i % 2))) for i in range(group_width)
        ]
        full_arrived.append(lax.ppermute(full[r], "dev", swaps))

    last = call(
        functools.partial(send_last_kernel, layout),
        two,
        [tiles, taken, mask, held, taken_orbitals],
    )
    last_arrived = lax.ppermute(last, ("grp", "dev"), last_moves(layout, groups))

    odd = call(functools.partial(send_odd_kernel, layout), block, [tiles, held])
    odd_arrived = lax.ppermute(odd, ("grp", "dev"), odd_moves(layout, groups))

    mine, others = call(
        functools.partial(near_kernel, layout),
        [block, block],
        [tiles, held, taken_orbitals],
    )
    others = call(
        functools.partial(others_kernel, layout),
        block,
        [taken, mask, others, last_arrived, *full_arrived],
    )
    returned = lax.ppermute(others, "dev", partners)
    mine = call(
        functools.partial(mine_kernel, layout),
        block,
        [tiles, mine, odd_arrived, last_arrived, *full_arrived],
    )
    return mine + returned


def solution(mesh):
    in_specs = (
        P(("grp", "dev"), None, None, None),
        P(("grp", "dev"), None),
        P(("grp", "dev"), None),
    )
    out_specs = P(("grp", "dev"), None)
    return jax.shard_map(
        per_device, mesh=mesh, in_specs=in_specs, out_specs=out_specs, check_vma=False
    )
```

```python
import functools

import jax
import jax.numpy as jnp
from jax import lax
from jax.experimental import pallas as pl
from jax.experimental.pallas import tpu as pltpu
from jax.sharding import PartitionSpec as P

HBM = pl.BlockSpec(memory_space=pltpu.HBM)
VMEM = pl.BlockSpec(memory_space=pltpu.VMEM)
F32 = jnp.float32


def parted(value):
    high = value.astype(jnp.bfloat16)
    return high, (value - high.astype(F32)).astype(jnp.bfloat16)


def times(left, right):
    left_high, left_low = parted(left)
    right_high, right_low = parted(right)
    dot = functools.partial(jnp.dot, preferred_element_type=F32)
    rows = left.shape[0]
    both = dot(jnp.concatenate([left_high, left_low], axis=0), right_high)
    return both[:rows] + both[rows:] + dot(left_high, right_low)


def transposed_times(left, right):
    return times(left.T, right)


class Layout:
    def __init__(self, group_width):
        self.width = group_width
        self.pairs = group_width // 2
        self.rounds = (self.pairs - 1) // 2
        self.last_offset = self.pairs - 1

    def offset(self, round_index, side):
        return 2 * round_index + 2 - side


def place():
    index = lax.axis_index("dev")
    return index, index // 2, index % 2


def load_kernel(layout, flags_in, tiles_in, orbitals_in, tiles, orbitals, flags, sems):
    copies = [
        pltpu.make_async_copy(flags_in, flags, sems.at[0]),
        pltpu.make_async_copy(tiles_in, tiles, sems.at[1]),
        pltpu.make_async_copy(orbitals_in, orbitals, sems.at[2]),
    ]
    for copy in copies:
        copy.start()
    for copy in copies:
        copy.wait()
    for slot in range(layout.width + 1):
        tiles[slot] = tiles[slot] * flags[0, slot].astype(F32)


def mask_kernel(layout, flags, mask):
    row = flags[...].astype(F32)
    for slot in range(layout.width + 1):
        mask[slot : slot + 1] = jnp.broadcast_to(
            row[:, slot : slot + 1], (1, mask.shape[1])
        )


def taken_tile(taken, mask, slot):
    return taken[slot] * mask[pl.ds(slot, 1), :]


def pair_terms(far, tiles, taken, mask, own, other, out):
    lefts = []
    for k in range(2):
        slot = 2 * far + k
        stack = jnp.concatenate([tiles[slot], taken_tile(taken, mask, slot)], axis=0)
        lefts.append(stack.T)
    terms = times(
        jnp.concatenate(lefts, axis=0), jnp.concatenate([own, other], axis=0)
    )
    order = own.shape[0]
    out[0] = terms[:order]
    out[1] = terms[order:]


def send_full_kernel(layout, tiles, taken, mask, orbitals, taken_orbitals, *outs):
    index, pair, side = place()
    own, other = orbitals[...], taken_orbitals[...]
    for r in range(layout.rounds):
        far = pair ^ layout.offset(r, side)
        out = outs[r]

        @pl.when(far > pair)
        def _():
            pair_terms(far, tiles, taken, mask, own, other, out)

        @pl.when(far < pair)
        def _():
            out[0] = jnp.where(side == 0, own, other)
            out[1] = jnp.where(side == 0, other, own)


def send_last_kernel(layout, tiles, taken, mask, orbitals, taken_orbitals, out):
    index, pair, side = place()
    own, other = orbitals[...], taken_orbitals[...]
    far = pair ^ layout.last_offset
    lower = lax.axis_index("grp") % 2 == 0

    @pl.when((side == 1) & (far > pair))
    def _():
        pair_terms(far, tiles, taken, mask, own, other, out)

    @pl.when((side == 1) & (far < pair))
    def _():
        out[0] = other
        out[1] = own

    @pl.when((side == 0) & lower)
    def _():
        out[0] = transposed_times(tiles[layout.width], own)
        out[1] = transposed_times(taken_tile(taken, mask, layout.width), other)

    @pl.when((side == 0) & jnp.logical_not(lower))
    def _():
        out[0] = own
        out[1] = other


def send_odd_kernel(layout, tiles, orbitals, out):
    lower = lax.axis_index("grp") % 2 == 1

    @pl.when(lower)
    def _():
        out[...] = transposed_times(tiles[layout.width], orbitals[...])

    @pl.when(jnp.logical_not(lower))
    def _():
        out[...] = orbitals[...]


def near_kernel(layout, tiles, orbitals, taken_orbitals, mine, others):
    index, pair, side = place()
    own, other = orbitals[...], taken_orbitals[...]
    beside = tiles[index ^ 1]
    row = jnp.concatenate([tiles[index], beside], axis=1)
    mine[...] = times(row, jnp.concatenate([own, other], axis=0))
    others[...] = transposed_times(beside, own)


def full_kernel(layout, tiles, taken, mask, mine_in, others_in, *refs):
    index, pair, side = place()
    arrived, mine, others = refs[:-2], refs[-2], refs[-1]
    order = tiles.shape[1]
    mine[...] = mine_in[...]
    others[...] = others_in[...]
    for r in range(layout.rounds):
        far = pair ^ layout.offset(r, side)
        came = arrived[r]

        @pl.when(far > pair)
        def _():
            slots = [2 * far, 2 * far + 1]
            upper = jnp.concatenate([tiles[slot] for slot in slots], axis=1)
            lower = jnp.concatenate(
                [taken_tile(taken, mask, slot) for slot in slots], axis=1
            )
            right = jnp.concatenate([came[0], came[1]], axis=0)
            terms = times(jnp.concatenate([upper, lower], axis=0), right)
            mine[...] += terms[:order]
            others[...] += terms[order:]

        @pl.when(far < pair)
        def _():
            mine[...] += came[side]
            others[...] += came[1 - side]


def back_kernel(layout, taken, mask, others_in, came, others):
    index, pair, side = place()
    far = pair ^ layout.last_offset
    lower = lax.axis_index("grp") % 2 == 0

    @pl.when((side == 1) & (far > pair))
    def _():
        left = jnp.concatenate(
            [taken_tile(taken, mask, 2 * far + k) for k in range(2)], axis=1
        )
        right = jnp.concatenate([came[0], came[1]], axis=0)
        others[...] = others_in[...] + times(left, right)

    @pl.when((side == 1) & (far < pair))
    def _():
        others[...] = others_in[...] + came[0]

    @pl.when((side == 0) & lower)
    def _():
        left = taken_tile(taken, mask, layout.width)
        others[...] = others_in[...] + times(left, came[1])

    @pl.when((side == 0) & jnp.logical_not(lower))
    def _():
        others[...] = others_in[...] + came[1]


def mine_kernel(layout, tiles, mine_in, came, odd_in, mine):
    index, pair, side = place()
    far = pair ^ layout.last_offset
    group = lax.axis_index("grp")
    lower = group % 2 == 0

    @pl.when((side == 1) & (far > pair))
    def _():
        left = jnp.concatenate([tiles[2 * far], tiles[2 * far + 1]], axis=1)
        right = jnp.concatenate([came[0], came[1]], axis=0)
        mine[...] = mine_in[...] + times(left, right)

    @pl.when((side == 1) & (far < pair))
    def _():
        mine[...] = mine_in[...] + came[1]

    @pl.when((side == 0) & lower)
    def _():
        mine[...] = mine_in[...] + times(tiles[layout.width], came[0])

    @pl.when((side == 0) & jnp.logical_not(lower))
    def _():
        mine[...] = mine_in[...] + came[0]

    @pl.when(lower)
    def _():
        mine[...] += jnp.where(group > 0, odd_in[...], 0.0)

    @pl.when(jnp.logical_not(lower))
    def _():
        mine[...] += times(tiles[layout.width], odd_in[...])


def call(body, outs, operands, specs=None, scratch=(), flops=0):
    return pl.pallas_call(
        body,
        out_shape=outs,
        in_specs=specs or [VMEM] * len(operands),
        out_specs=jax.tree.map(lambda _: VMEM, outs),
        scratch_shapes=scratch,
        cost_estimate=pl.CostEstimate(
            flops=flops, bytes_accessed=0, transcendentals=0
        ),
        compiler_params=pltpu.CompilerParams(vmem_limit_bytes=32 * 1024 * 1024),
    )(*operands)


def last_moves(layout, groups):
    moves = []
    for g in range(groups):
        for i in range(layout.width):
            if i % 2 == 1:
                to, j = g, i ^ (2 * layout.last_offset)
            else:
                to, j = g ^ 1, i
                if to >= groups:
                    to = g
            moves.append((g * layout.width + i, to * layout.width + j))
    return moves


def odd_moves(layout, groups):
    moves = []
    for g in range(groups):
        to = g + 1 if g % 2 == 1 else g - 1
        for i in range(layout.width):
            if 0 <= to < groups:
                moves.append((g * layout.width + i, to * layout.width + i))
            else:
                moves.append((g * layout.width + i, g * layout.width + (i ^ 1)))
    return moves


def per_device(stored_tiles, tile_flags, orbitals):
    group_width = lax.axis_size("dev")
    groups = lax.axis_size("grp")
    layout = Layout(group_width)
    order, columns = orbitals.shape
    block = jax.ShapeDtypeStruct((order, columns), F32)
    two = jax.ShapeDtypeStruct((2, order, columns), F32)
    partners = [(i, i ^ 1) for i in range(group_width)]
    semaphore = pltpu.SemaphoreType.DMA

    taken = lax.ppermute(stored_tiles, "dev", partners)[0]
    taken_orbitals = lax.ppermute(orbitals, "dev", partners)
    taken_flags = lax.ppermute(tile_flags, "dev", partners)
    tiles, held = call(
        functools.partial(load_kernel, layout),
        [jax.ShapeDtypeStruct(stored_tiles.shape[1:], F32), block],
        [
            pltpu.with_memory_space_constraint(operand, pltpu.HBM)
            for operand in (tile_flags, stored_tiles[0], orbitals)
        ],
        [HBM] * 3,
        [pltpu.SMEM(tile_flags.shape, jnp.int32), semaphore((3,))],
        flops=10**9,
    )
    mask = call(
        functools.partial(mask_kernel, layout),
        jax.ShapeDtypeStruct((group_width + 1, order), F32),
        [taken_flags],
        flops=10**10,
    )

    full = call(
        functools.partial(send_full_kernel, layout),
        [two] * layout.rounds,
        [tiles, taken, mask, held, taken_orbitals],
    )
    full_arrived = []
    for r in range(layout.rounds):
        swaps = [
            (i, i ^ (2 * layout.offset(r, i % 2))) for i in range(group_width)
        ]
        full_arrived.append(lax.ppermute(full[r], "dev", swaps))

    last = call(
        functools.partial(send_last_kernel, layout),
        two,
        [tiles, taken, mask, held, taken_orbitals],
    )
    last_arrived = lax.ppermute(last, ("grp", "dev"), last_moves(layout, groups))

    odd = call(functools.partial(send_odd_kernel, layout), block, [tiles, held])
    odd_arrived = lax.ppermute(odd, ("grp", "dev"), odd_moves(layout, groups))

    mine, others = call(
        functools.partial(near_kernel, layout),
        [block, block],
        [tiles, held, taken_orbitals],
    )
    mine, others = call(
        functools.partial(full_kernel, layout),
        [block, block],
        [tiles, taken, mask, mine, others, *full_arrived],
    )
    others = call(
        functools.partial(back_kernel, layout),
        block,
        [taken, mask, others, last_arrived],
    )
    returned = lax.ppermute(others, "dev", partners)
    mine = call(
        functools.partial(mine_kernel, layout),
        block,
        [tiles, mine, last_arrived, odd_arrived],
    )
    return mine + returned


def solution(mesh):
    in_specs = (
        P(("grp", "dev"), None, None, None),
        P(("grp", "dev"), None),
        P(("grp", "dev"), None),
    )
    out_specs = P(("grp", "dev"), None)
    return jax.shard_map(
        per_device, mesh=mesh, in_specs=in_specs, out_specs=out_specs, check_vma=False
    )
```

```python
import functools

import jax
import jax.numpy as jnp
from jax import lax
from jax.experimental import pallas as pl
from jax.experimental.pallas import tpu as pltpu
from jax.sharding import PartitionSpec as P

HBM = pl.BlockSpec(memory_space=pltpu.HBM)
VMEM = pl.BlockSpec(memory_space=pltpu.VMEM)
F32 = jnp.float32


def parted(value):
    high = value.astype(jnp.bfloat16)
    return high, (value - high.astype(F32)).astype(jnp.bfloat16)


def times(left, right):
    left_high, left_low = parted(left)
    right_high, right_low = parted(right)
    dot = functools.partial(jnp.dot, preferred_element_type=F32)
    rows = left.shape[0]
    both = dot(jnp.concatenate([left_high, left_low], axis=0), right_high)
    return both[:rows] + both[rows:] + dot(left_high, right_low)


def transposed_times(left, right):
    return times(left.T, right)


class Layout:
    def __init__(self, group_width):
        self.width = group_width
        self.pairs = group_width // 2
        self.rounds = (self.pairs - 1) // 2
        self.last_offset = 2

    def offset(self, round_index, side):
        if round_index == 0:
            return 1 + 2 * side
        return 2 * round_index + 2 + side


def place():
    index = lax.axis_index("dev")
    return index, index // 2, index % 2


def load_kernel(layout, flags_in, tiles_in, orbitals_in, tiles, orbitals, flags, sems):
    copies = [
        pltpu.make_async_copy(flags_in, flags, sems.at[0]),
        pltpu.make_async_copy(tiles_in, tiles, sems.at[1]),
        pltpu.make_async_copy(orbitals_in, orbitals, sems.at[2]),
    ]
    for copy in copies:
        copy.start()
    for copy in copies:
        copy.wait()
    for slot in range(layout.width + 1):
        tiles[slot] = tiles[slot] * flags[0, slot].astype(F32)


def mask_kernel(layout, flags, mask):
    row = flags[...].astype(F32)
    for slot in range(layout.width + 1):
        mask[slot : slot + 1] = jnp.broadcast_to(
            row[:, slot : slot + 1], (1, mask.shape[1])
        )


def taken_tile(taken, mask, slot):
    return taken[slot] * mask[pl.ds(slot, 1), :]


def pair_terms(far, tiles, taken, mask, own, other, out):
    lefts = []
    for k in range(2):
        slot = 2 * far + k
        stack = jnp.concatenate([tiles[slot], taken_tile(taken, mask, slot)], axis=0)
        lefts.append(stack.T)
    terms = times(
        jnp.concatenate(lefts, axis=0), jnp.concatenate([own, other], axis=0)
    )
    order = own.shape[0]
    out[0] = terms[:order]
    out[1] = terms[order:]


def send_full_kernel(layout, tiles, taken, mask, orbitals, taken_orbitals, *outs):
    index, pair, side = place()
    own, other = orbitals[...], taken_orbitals[...]
    for r in range(layout.rounds):
        far = pair ^ layout.offset(r, side)
        out = outs[r]

        @pl.when(far > pair)
        def _():
            pair_terms(far, tiles, taken, mask, own, other, out)

        @pl.when(far < pair)
        def _():
            out[0] = jnp.where(side == 0, own, other)
            out[1] = jnp.where(side == 0, other, own)


def send_last_kernel(layout, tiles, taken, mask, orbitals, taken_orbitals, out):
    index, pair, side = place()
    own, other = orbitals[...], taken_orbitals[...]
    far = pair ^ layout.last_offset
    lower = lax.axis_index("grp") % 2 == 0

    @pl.when((side == 1) & (far > pair))
    def _():
        pair_terms(far, tiles, taken, mask, own, other, out)

    @pl.when((side == 1) & (far < pair))
    def _():
        out[0] = other
        out[1] = own

    @pl.when((side == 0) & lower)
    def _():
        out[0] = transposed_times(tiles[layout.width], own)
        out[1] = transposed_times(taken_tile(taken, mask, layout.width), other)

    @pl.when((side == 0) & jnp.logical_not(lower))
    def _():
        out[0] = own
        out[1] = other


def send_odd_kernel(layout, tiles, orbitals, out):
    lower = lax.axis_index("grp") % 2 == 1

    @pl.when(lower)
    def _():
        out[...] = transposed_times(tiles[layout.width], orbitals[...])

    @pl.when(jnp.logical_not(lower))
    def _():
        out[...] = orbitals[...]


def near_kernel(layout, tiles, orbitals, taken_orbitals, mine, others):
    index, pair, side = place()
    own, other = orbitals[...], taken_orbitals[...]
    beside = tiles[index ^ 1]
    row = jnp.concatenate([tiles[index], beside], axis=1)
    mine[...] = times(row, jnp.concatenate([own, other], axis=0))
    others[...] = transposed_times(beside, own)


def full_kernel(layout, tiles, taken, mask, mine_in, others_in, *refs):
    index, pair, side = place()
    arrived, mine, others = refs[:-2], refs[-2], refs[-1]
    order = tiles.shape[1]
    mine[...] = mine_in[...]
    others[...] = others_in[...]
    for r in range(layout.rounds):
        far = pair ^ layout.offset(r, side)
        came = arrived[r]

        @pl.when(far > pair)
        def _():
            slots = [2 * far, 2 * far + 1]
            upper = jnp.concatenate([tiles[slot] for slot in slots], axis=1)
            lower = jnp.concatenate(
                [taken_tile(taken, mask, slot) for slot in slots], axis=1
            )
            right = jnp.concatenate([came[0], came[1]], axis=0)
            terms = times(jnp.concatenate([upper, lower], axis=0), right)
            mine[...] += terms[:order]
            others[...] += terms[order:]

        @pl.when(far < pair)
        def _():
            mine[...] += came[side]
            others[...] += came[1 - side]


def back_kernel(layout, taken, mask, others_in, came, others):
    index, pair, side = place()
    far = pair ^ layout.last_offset
    lower = lax.axis_index("grp") % 2 == 0

    @pl.when((side == 1) & (far > pair))
    def _():
        left = jnp.concatenate(
            [taken_tile(taken, mask, 2 * far + k) for k in range(2)], axis=1
        )
        right = jnp.concatenate([came[0], came[1]], axis=0)
        others[...] = others_in[...] + times(left, right)

    @pl.when((side == 1) & (far < pair))
    def _():
        others[...] = others_in[...] + came[0]

    @pl.when((side == 0) & lower)
    def _():
        left = taken_tile(taken, mask, layout.width)
        others[...] = others_in[...] + times(left, came[1])

    @pl.when((side == 0) & jnp.logical_not(lower))
    def _():
        others[...] = others_in[...] + came[1]


def mine_kernel(layout, tiles, mine_in, came, odd_in, mine):
    index, pair, side = place()
    far = pair ^ layout.last_offset
    group = lax.axis_index("grp")
    lower = group % 2 == 0

    @pl.when((side == 1) & (far > pair))
    def _():
        left = jnp.concatenate([tiles[2 * far], tiles[2 * far + 1]], axis=1)
        right = jnp.concatenate([came[0], came[1]], axis=0)
        mine[...] = mine_in[...] + times(left, right)

    @pl.when((side == 1) & (far < pair))
    def _():
        mine[...] = mine_in[...] + came[1]

    @pl.when((side == 0) & lower)
    def _():
        mine[...] = mine_in[...] + times(tiles[layout.width], came[0])

    @pl.when((side == 0) & jnp.logical_not(lower))
    def _():
        mine[...] = mine_in[...] + came[0]

    @pl.when(lower)
    def _():
        mine[...] += jnp.where(group > 0, odd_in[...], 0.0)

    @pl.when(jnp.logical_not(lower))
    def _():
        mine[...] += times(tiles[layout.width], odd_in[...])


def call(body, outs, operands, specs=None, scratch=(), flops=0):
    return pl.pallas_call(
        body,
        out_shape=outs,
        in_specs=specs or [VMEM] * len(operands),
        out_specs=jax.tree.map(lambda _: VMEM, outs),
        scratch_shapes=scratch,
        cost_estimate=pl.CostEstimate(
            flops=flops, bytes_accessed=0, transcendentals=0
        ),
        compiler_params=pltpu.CompilerParams(vmem_limit_bytes=32 * 1024 * 1024),
    )(*operands)


def last_moves(layout, groups):
    moves = []
    for g in range(groups):
        for i in range(layout.width):
            if i % 2 == 1:
                to, j = g, i ^ (2 * layout.last_offset)
            else:
                to, j = g ^ 1, i
                if to >= groups:
                    to = g
            moves.append((g * layout.width + i, to * layout.width + j))
    return moves


def odd_moves(layout, groups):
    moves = []
    for g in range(groups):
        to = g + 1 if g % 2 == 1 else g - 1
        for i in range(layout.width):
            if 0 <= to < groups:
                moves.append((g * layout.width + i, to * layout.width + i))
            else:
                moves.append((g * layout.width + i, g * layout.width + (i ^ 1)))
    return moves


def per_device(stored_tiles, tile_flags, orbitals):
    group_width = lax.axis_size("dev")
    groups = lax.axis_size("grp")
    layout = Layout(group_width)
    order, columns = orbitals.shape
    block = jax.ShapeDtypeStruct((order, columns), F32)
    two = jax.ShapeDtypeStruct((2, order, columns), F32)
    partners = [(i, i ^ 1) for i in range(group_width)]
    semaphore = pltpu.SemaphoreType.DMA

    taken = lax.ppermute(stored_tiles, "dev", partners)[0]
    taken_orbitals = lax.ppermute(orbitals, "dev", partners)
    taken_flags = lax.ppermute(tile_flags, "dev", partners)
    tiles, held = call(
        functools.partial(load_kernel, layout),
        [jax.ShapeDtypeStruct(stored_tiles.shape[1:], F32), block],
        [
            pltpu.with_memory_space_constraint(operand, pltpu.HBM)
            for operand in (tile_flags, stored_tiles[0], orbitals)
        ],
        [HBM] * 3,
        [pltpu.SMEM(tile_flags.shape, jnp.int32), semaphore((3,))],
        flops=10**9,
    )
    mask = call(
        functools.partial(mask_kernel, layout),
        jax.ShapeDtypeStruct((group_width + 1, order), F32),
        [taken_flags],
        flops=10**10,
    )

    full = call(
        functools.partial(send_full_kernel, layout),
        [two] * layout.rounds,
        [tiles, taken, mask, held, taken_orbitals],
    )
    full_arrived = []
    for r in range(layout.rounds):
        swaps = [
            (i, i ^ (2 * layout.offset(r, i % 2))) for i in range(group_width)
        ]
        full_arrived.append(lax.ppermute(full[r], "dev", swaps))

    last = call(
        functools.partial(send_last_kernel, layout),
        two,
        [tiles, taken, mask, held, taken_orbitals],
    )
    last_arrived = lax.ppermute(last, ("grp", "dev"), last_moves(layout, groups))

    odd = call(functools.partial(send_odd_kernel, layout), block, [tiles, held])
    odd_arrived = lax.ppermute(odd, ("grp", "dev"), odd_moves(layout, groups))

    mine, others = call(
        functools.partial(near_kernel, layout),
        [block, block],
        [tiles, held, taken_orbitals],
    )
    mine, others = call(
        functools.partial(full_kernel, layout),
        [block, block],
        [tiles, taken, mask, mine, others, *full_arrived],
    )
    others = call(
        functools.partial(back_kernel, layout),
        block,
        [taken, mask, others, last_arrived],
    )
    returned = lax.ppermute(others, "dev", partners)
    mine = call(
        functools.partial(mine_kernel, layout),
        block,
        [tiles, mine, last_arrived, odd_arrived],
    )
    return mine + returned


def solution(mesh):
    in_specs = (
        P(("grp", "dev"), None, None, None),
        P(("grp", "dev"), None),
        P(("grp", "dev"), None),
    )
    out_specs = P(("grp", "dev"), None)
    return jax.shard_map(
        per_device, mesh=mesh, in_specs=in_specs, out_specs=out_specs, check_vma=False
    )
```

```python
import functools

import jax
import jax.numpy as jnp
from jax import lax
from jax.experimental import pallas as pl
from jax.experimental.pallas import tpu as pltpu
from jax.sharding import PartitionSpec as P

HBM = pl.BlockSpec(memory_space=pltpu.HBM)
VMEM = pl.BlockSpec(memory_space=pltpu.VMEM)
F32 = jnp.float32


def parted(value):
    high = value.astype(jnp.bfloat16)
    return high, (value - high.astype(F32)).astype(jnp.bfloat16)


def times(left, right):
    left_high, left_low = parted(left)
    right_high, right_low = parted(right)
    dot = functools.partial(jnp.dot, preferred_element_type=F32)
    rows = left.shape[0]
    both = dot(jnp.concatenate([left_high, left_low], axis=0), right_high)
    return both[:rows] + both[rows:] + dot(left_high, right_low)


def transposed_times(left, right):
    return times(left.T, right)


class Layout:
    def __init__(self, group_width):
        self.width = group_width
        self.pairs = group_width // 2
        self.rounds = (self.pairs - 1) // 2
        self.last_offset = 2

    def offset(self, round_index, side):
        if round_index == 0:
            return 1 + 2 * side
        return 2 * round_index + 2 + side


def place():
    index = lax.axis_index("dev")
    return index, index // 2, index % 2


def load_kernel(layout, flags_in, tiles_in, orbitals_in, tiles, orbitals, flags, sems):
    copies = [
        pltpu.make_async_copy(flags_in, flags, sems.at[0]),
        pltpu.make_async_copy(tiles_in, tiles, sems.at[1]),
        pltpu.make_async_copy(orbitals_in, orbitals, sems.at[2]),
    ]
    for copy in copies:
        copy.start()
    for copy in copies:
        copy.wait()
    for slot in range(layout.width + 1):
        tiles[slot] = tiles[slot] * flags[0, slot].astype(F32)


def mask_kernel(layout, flags, mask):
    row = flags[...].astype(F32)
    for slot in range(layout.width + 1):
        mask[slot : slot + 1] = jnp.broadcast_to(
            row[:, slot : slot + 1], (1, mask.shape[1])
        )


def taken_tile(taken, mask, slot):
    return taken[slot] * mask[pl.ds(slot, 1), :]


def pair_terms(far, tiles, taken, mask, own, other, out):
    lefts = []
    for k in range(2):
        slot = 2 * far + k
        stack = jnp.concatenate([tiles[slot], taken_tile(taken, mask, slot)], axis=0)
        lefts.append(stack.T)
    terms = times(
        jnp.concatenate(lefts, axis=0), jnp.concatenate([own, other], axis=0)
    )
    order = own.shape[0]
    out[0] = terms[:order]
    out[1] = terms[order:]


def send_full_kernel(layout, tiles, taken, mask, orbitals, taken_orbitals, *outs):
    index, pair, side = place()
    own, other = orbitals[...], taken_orbitals[...]
    for r in range(layout.rounds):
        far = pair ^ layout.offset(r, side)
        out = outs[r]

        @pl.when(far > pair)
        def _():
            pair_terms(far, tiles, taken, mask, own, other, out)

        @pl.when(far < pair)
        def _():
            out[0] = jnp.where(side == 0, own, other)
            out[1] = jnp.where(side == 0, other, own)

    far = pair ^ layout.last_offset
    last = outs[-1]

    @pl.when((side == 1) & (far > pair))
    def _():
        pair_terms(far, tiles, taken, mask, own, other, last)

    @pl.when((side == 1) & (far < pair))
    def _():
        last[0] = other
        last[1] = own


def send_last_kernel(layout, tiles, taken, mask, orbitals, taken_orbitals, made, out):
    index, pair, side = place()
    own, other = orbitals[...], taken_orbitals[...]
    lower = lax.axis_index("grp") % 2 == 0

    @pl.when(side == 1)
    def _():
        out[...] = made[...]

    @pl.when((side == 0) & lower)
    def _():
        out[0] = transposed_times(tiles[layout.width], own)
        out[1] = transposed_times(taken_tile(taken, mask, layout.width), other)

    @pl.when((side == 0) & jnp.logical_not(lower))
    def _():
        out[0] = own
        out[1] = other


def send_odd_kernel(layout, tiles, orbitals, out):
    lower = lax.axis_index("grp") % 2 == 1

    @pl.when(lower)
    def _():
        out[...] = transposed_times(tiles[layout.width], orbitals[...])

    @pl.when(jnp.logical_not(lower))
    def _():
        out[...] = orbitals[...]


def near_kernel(layout, tiles, orbitals, taken_orbitals, mine, others):
    index, pair, side = place()
    own, other = orbitals[...], taken_orbitals[...]
    beside = tiles[index ^ 1]
    row = jnp.concatenate([tiles[index], beside], axis=1)
    mine[...] = times(row, jnp.concatenate([own, other], axis=0))
    others[...] = transposed_times(beside, own)


def take_full(layout, arrived, row, tile_of, total):
    index, pair, side = place()
    for r, came in enumerate(arrived):
        far = pair ^ layout.offset(r, side)

        @pl.when(far > pair)
        def _():
            left = jnp.concatenate([tile_of(2 * far), tile_of(2 * far + 1)], axis=1)
            right = jnp.concatenate([came[0], came[1]], axis=0)
            total[...] += times(left, right)

        @pl.when(far < pair)
        def _():
            total[...] += came[side ^ row]


def full_kernel(layout, taken, mask, others_in, *refs):
    arrived, others = refs[:-1], refs[-1]
    others[...] = others_in[...]
    take_full(layout, arrived, 1, lambda slot: taken_tile(taken, mask, slot), others)


def back_kernel(layout, taken, mask, others_in, came, others):
    index, pair, side = place()
    far = pair ^ layout.last_offset
    lower = lax.axis_index("grp") % 2 == 0

    @pl.when((side == 1) & (far > pair))
    def _():
        left = jnp.concatenate(
            [taken_tile(taken, mask, 2 * far + k) for k in range(2)], axis=1
        )
        right = jnp.concatenate([came[0], came[1]], axis=0)
        others[...] = others_in[...] + times(left, right)

    @pl.when((side == 1) & (far < pair))
    def _():
        others[...] = others_in[...] + came[0]

    @pl.when((side == 0) & lower)
    def _():
        left = taken_tile(taken, mask, layout.width)
        others[...] = others_in[...] + times(left, came[1])

    @pl.when((side == 0) & jnp.logical_not(lower))
    def _():
        others[...] = others_in[...] + came[1]


def mine_kernel(layout, tiles, mine_in, came, odd_in, *refs):
    arrived, mine = refs[:-1], refs[-1]
    index, pair, side = place()
    far = pair ^ layout.last_offset
    group = lax.axis_index("grp")
    lower = group % 2 == 0

    @pl.when((side == 1) & (far > pair))
    def _():
        left = jnp.concatenate([tiles[2 * far], tiles[2 * far + 1]], axis=1)
        right = jnp.concatenate([came[0], came[1]], axis=0)
        mine[...] = mine_in[...] + times(left, right)

    @pl.when((side == 1) & (far < pair))
    def _():
        mine[...] = mine_in[...] + came[1]

    @pl.when((side == 0) & lower)
    def _():
        mine[...] = mine_in[...] + times(tiles[layout.width], came[0])

    @pl.when((side == 0) & jnp.logical_not(lower))
    def _():
        mine[...] = mine_in[...] + came[0]

    @pl.when(lower)
    def _():
        mine[...] += jnp.where(group > 0, odd_in[...], 0.0)

    @pl.when(jnp.logical_not(lower))
    def _():
        mine[...] += times(tiles[layout.width], odd_in[...])

    take_full(layout, arrived, 0, lambda slot: tiles[slot], mine)


def call(body, outs, operands, specs=None, scratch=(), flops=0):
    return pl.pallas_call(
        body,
        out_shape=outs,
        in_specs=specs or [VMEM] * len(operands),
        out_specs=jax.tree.map(lambda _: VMEM, outs),
        scratch_shapes=scratch,
        cost_estimate=pl.CostEstimate(
            flops=flops, bytes_accessed=0, transcendentals=0
        ),
        compiler_params=pltpu.CompilerParams(vmem_limit_bytes=32 * 1024 * 1024),
    )(*operands)


def last_moves(layout, groups):
    moves = []
    for g in range(groups):
        for i in range(layout.width):
            if i % 2 == 1:
                to, j = g, i ^ (2 * layout.last_offset)
            else:
                to, j = g ^ 1, i
                if to >= groups:
                    to = g
            moves.append((g * layout.width + i, to * layout.width + j))
    return moves


def odd_moves(layout, groups):
    moves = []
    for g in range(groups):
        to = g + 1 if g % 2 == 1 else g - 1
        for i in range(layout.width):
            if 0 <= to < groups:
                moves.append((g * layout.width + i, to * layout.width + i))
            else:
                moves.append((g * layout.width + i, g * layout.width + (i ^ 1)))
    return moves


def per_device(stored_tiles, tile_flags, orbitals):
    group_width = lax.axis_size("dev")
    groups = lax.axis_size("grp")
    layout = Layout(group_width)
    order, columns = orbitals.shape
    block = jax.ShapeDtypeStruct((order, columns), F32)
    two = jax.ShapeDtypeStruct((2, order, columns), F32)
    partners = [(i, i ^ 1) for i in range(group_width)]
    semaphore = pltpu.SemaphoreType.DMA

    taken = lax.ppermute(stored_tiles, "dev", partners)[0]
    taken_orbitals = lax.ppermute(orbitals, "dev", partners)
    taken_flags = lax.ppermute(tile_flags, "dev", partners)
    tiles, held = call(
        functools.partial(load_kernel, layout),
        [jax.ShapeDtypeStruct(stored_tiles.shape[1:], F32), block],
        [
            pltpu.with_memory_space_constraint(operand, pltpu.HBM)
            for operand in (tile_flags, stored_tiles[0], orbitals)
        ],
        [HBM] * 3,
        [pltpu.SMEM(tile_flags.shape, jnp.int32), semaphore((3,))],
        flops=10**9,
    )
    mask = call(
        functools.partial(mask_kernel, layout),
        jax.ShapeDtypeStruct((group_width + 1, order), F32),
        [taken_flags],
        flops=10**10,
    )

    *full, made = call(
        functools.partial(send_full_kernel, layout),
        [two] * (layout.rounds + 1),
        [tiles, taken, mask, held, taken_orbitals],
    )
    full_arrived = []
    for r in range(layout.rounds):
        swaps = [
            (i, i ^ (2 * layout.offset(r, i % 2))) for i in range(group_width)
        ]
        full_arrived.append(lax.ppermute(full[r], "dev", swaps))

    last = call(
        functools.partial(send_last_kernel, layout),
        two,
        [tiles, taken, mask, held, taken_orbitals, made],
    )
    last_arrived = lax.ppermute(last, ("grp", "dev"), last_moves(layout, groups))

    odd = call(functools.partial(send_odd_kernel, layout), block, [tiles, held])
    odd_arrived = lax.ppermute(odd, ("grp", "dev"), odd_moves(layout, groups))

    mine, others = call(
        functools.partial(near_kernel, layout),
        [block, block],
        [tiles, held, taken_orbitals],
    )
    others = call(
        functools.partial(full_kernel, layout),
        block,
        [taken, mask, others, *full_arrived],
    )
    others = call(
        functools.partial(back_kernel, layout),
        block,
        [taken, mask, others, last_arrived],
    )
    returned = lax.ppermute(others, "dev", partners)
    mine = call(
        functools.partial(mine_kernel, layout),
        block,
        [tiles, mine, last_arrived, odd_arrived, *full_arrived],
    )
    return mine + returned


def solution(mesh):
    in_specs = (
        P(("grp", "dev"), None, None, None),
        P(("grp", "dev"), None),
        P(("grp", "dev"), None),
    )
    out_specs = P(("grp", "dev"), None)
    return jax.shard_map(
        per_device, mesh=mesh, in_specs=in_specs, out_specs=out_specs, check_vma=False
    )
```

```python
import functools

import jax
import jax.numpy as jnp
from jax import lax
from jax.experimental import pallas as pl
from jax.experimental.pallas import tpu as pltpu
from jax.sharding import PartitionSpec as P

HBM = pl.BlockSpec(memory_space=pltpu.HBM)
VMEM = pl.BlockSpec(memory_space=pltpu.VMEM)
F32 = jnp.float32


def parted(value):
    high = value.astype(jnp.bfloat16)
    return high, (value - high.astype(F32)).astype(jnp.bfloat16)


def times(left, right):
    left_high, left_low = parted(left)
    right_high, right_low = parted(right)
    dot = functools.partial(jnp.dot, preferred_element_type=F32)
    rows = left.shape[0]
    both = dot(jnp.concatenate([left_high, left_low], axis=0), right_high)
    return both[:rows] + both[rows:] + dot(left_high, right_low)


def transposed_times(left, right):
    return times(left.T, right)


class Layout:
    def __init__(self, group_width):
        self.width = group_width
        self.pairs = group_width // 2
        self.rounds = (self.pairs - 1) // 2
        self.last_offset = 2

    def offset(self, round_index, side):
        if round_index == 0:
            return 1 + 2 * side
        return 2 * round_index + 2 + side


def place():
    index = lax.axis_index("dev")
    return index, index // 2, index % 2


def load_kernel(layout, flags_in, tiles_in, orbitals_in, tiles, orbitals, flags, sems):
    copies = [
        pltpu.make_async_copy(flags_in, flags, sems.at[0]),
        pltpu.make_async_copy(tiles_in, tiles, sems.at[1]),
        pltpu.make_async_copy(orbitals_in, orbitals, sems.at[2]),
    ]
    for copy in copies:
        copy.start()
    for copy in copies:
        copy.wait()
    for slot in range(layout.width + 1):
        tiles[slot] = tiles[slot] * flags[0, slot].astype(F32)


def mask_kernel(layout, flags, mask):
    row = flags[...].astype(F32)
    for slot in range(layout.width + 1):
        mask[slot : slot + 1] = jnp.broadcast_to(
            row[:, slot : slot + 1], (1, mask.shape[1])
        )


def taken_tile(taken, mask, slot):
    return taken[slot] * mask[pl.ds(slot, 1), :]


def pair_terms(far, tiles, taken, mask, own, other, out):
    lefts = []
    for k in range(2):
        slot = 2 * far + k
        stack = jnp.concatenate([tiles[slot], taken_tile(taken, mask, slot)], axis=0)
        lefts.append(stack.T)
    terms = times(
        jnp.concatenate(lefts, axis=0), jnp.concatenate([own, other], axis=0)
    )
    order = own.shape[0]
    out[0] = terms[:order]
    out[1] = terms[order:]


def send_full_kernel(layout, tiles, taken, mask, orbitals, taken_orbitals, *outs):
    index, pair, side = place()
    own, other = orbitals[...], taken_orbitals[...]
    for r in range(layout.rounds):
        far = pair ^ layout.offset(r, side)
        out = outs[r]

        @pl.when(far > pair)
        def _():
            pair_terms(far, tiles, taken, mask, own, other, out)

        @pl.when(far < pair)
        def _():
            out[0] = jnp.where(side == 0, own, other)
            out[1] = jnp.where(side == 0, other, own)


def send_last_kernel(layout, tiles, taken, mask, orbitals, taken_orbitals, out):
    index, pair, side = place()
    own, other = orbitals[...], taken_orbitals[...]
    far = pair ^ layout.last_offset
    lower = lax.axis_index("grp") % 2 == 0

    @pl.when((side == 1) & (far > pair))
    def _():
        pair_terms(far, tiles, taken, mask, own, other, out)

    @pl.when((side == 1) & (far < pair))
    def _():
        out[0] = other
        out[1] = own

    @pl.when((side == 0) & lower)
    def _():
        out[0] = transposed_times(tiles[layout.width], own)
        out[1] = transposed_times(taken_tile(taken, mask, layout.width), other)

    @pl.when((side == 0) & jnp.logical_not(lower))
    def _():
        out[0] = own
        out[1] = other


def send_odd_kernel(layout, tiles, orbitals, out):
    lower = lax.axis_index("grp") % 2 == 1

    @pl.when(lower)
    def _():
        out[...] = transposed_times(tiles[layout.width], orbitals[...])

    @pl.when(jnp.logical_not(lower))
    def _():
        out[...] = orbitals[...]


def near_kernel(layout, tiles, orbitals, taken_orbitals, mine, others):
    index, pair, side = place()
    own, other = orbitals[...], taken_orbitals[...]
    beside = tiles[index ^ 1]
    row = jnp.concatenate([tiles[index], beside], axis=1)
    mine[...] = times(row, jnp.concatenate([own, other], axis=0))
    others[...] = transposed_times(beside, own)


def take_full(layout, arrived, row, tile_of, total):
    index, pair, side = place()
    for r, came in enumerate(arrived):
        far = pair ^ layout.offset(r, side)

        @pl.when(far > pair)
        def _():
            left = jnp.concatenate([tile_of(2 * far), tile_of(2 * far + 1)], axis=1)
            right = jnp.concatenate([came[0], came[1]], axis=0)
            total[...] += times(left, right)

        @pl.when(far < pair)
        def _():
            total[...] += came[side ^ row]


def full_kernel(layout, taken, mask, others_in, *refs):
    arrived, others = refs[:-1], refs[-1]
    others[...] = others_in[...]
    take_full(layout, arrived, 1, lambda slot: taken_tile(taken, mask, slot), others)


def back_kernel(layout, taken, mask, others_in, came, others):
    index, pair, side = place()
    far = pair ^ layout.last_offset
    lower = lax.axis_index("grp") % 2 == 0

    @pl.when((side == 1) & (far > pair))
    def _():
        left = jnp.concatenate(
            [taken_tile(taken, mask, 2 * far + k) for k in range(2)], axis=1
        )
        right = jnp.concatenate([came[0], came[1]], axis=0)
        others[...] = others_in[...] + times(left, right)

    @pl.when((side == 1) & (far < pair))
    def _():
        others[...] = others_in[...] + came[0]

    @pl.when((side == 0) & lower)
    def _():
        left = taken_tile(taken, mask, layout.width)
        others[...] = others_in[...] + times(left, came[1])

    @pl.when((side == 0) & jnp.logical_not(lower))
    def _():
        others[...] = others_in[...] + came[1]


def mine_kernel(layout, tiles, mine_in, came, odd_in, *refs):
    arrived, mine = refs[:-1], refs[-1]
    index, pair, side = place()
    far = pair ^ layout.last_offset
    group = lax.axis_index("grp")
    lower = group % 2 == 0

    @pl.when((side == 1) & (far > pair))
    def _():
        left = jnp.concatenate([tiles[2 * far], tiles[2 * far + 1]], axis=1)
        right = jnp.concatenate([came[0], came[1]], axis=0)
        mine[...] = mine_in[...] + times(left, right)

    @pl.when((side == 1) & (far < pair))
    def _():
        mine[...] = mine_in[...] + came[1]

    @pl.when((side == 0) & lower)
    def _():
        mine[...] = mine_in[...] + times(tiles[layout.width], came[0])

    @pl.when((side == 0) & jnp.logical_not(lower))
    def _():
        mine[...] = mine_in[...] + came[0]

    @pl.when(lower)
    def _():
        mine[...] += jnp.where(group > 0, odd_in[...], 0.0)

    @pl.when(jnp.logical_not(lower))
    def _():
        mine[...] += times(tiles[layout.width], odd_in[...])

    take_full(layout, arrived, 0, lambda slot: tiles[slot], mine)


def call(body, outs, operands, specs=None, scratch=(), flops=0):
    return pl.pallas_call(
        body,
        out_shape=outs,
        in_specs=specs or [VMEM] * len(operands),
        out_specs=jax.tree.map(lambda _: VMEM, outs),
        scratch_shapes=scratch,
        cost_estimate=pl.CostEstimate(
            flops=flops, bytes_accessed=0, transcendentals=0
        ),
        compiler_params=pltpu.CompilerParams(vmem_limit_bytes=32 * 1024 * 1024),
    )(*operands)


def last_moves(layout, groups):
    moves = []
    for g in range(groups):
        for i in range(layout.width):
            if i % 2 == 1:
                to, j = g, i ^ (2 * layout.last_offset)
            else:
                to, j = g ^ 1, i
                if to >= groups:
                    to = g
            moves.append((g * layout.width + i, to * layout.width + j))
    return moves


def odd_moves(layout, groups):
    moves = []
    for g in range(groups):
        to = g + 1 if g % 2 == 1 else g - 1
        for i in range(layout.width):
            if 0 <= to < groups:
                moves.append((g * layout.width + i, to * layout.width + i))
            else:
                moves.append((g * layout.width + i, g * layout.width + (i ^ 1)))
    return moves


def per_device(stored_tiles, tile_flags, orbitals):
    group_width = lax.axis_size("dev")
    groups = lax.axis_size("grp")
    layout = Layout(group_width)
    order, columns = orbitals.shape
    block = jax.ShapeDtypeStruct((order, columns), F32)
    two = jax.ShapeDtypeStruct((2, order, columns), F32)
    partners = [(i, i ^ 1) for i in range(group_width)]
    semaphore = pltpu.SemaphoreType.DMA

    taken = lax.ppermute(stored_tiles, "dev", partners)[0]
    taken_orbitals = lax.ppermute(orbitals, "dev", partners)
    taken_flags = lax.ppermute(tile_flags, "dev", partners)
    tiles, held = call(
        functools.partial(load_kernel, layout),
        [jax.ShapeDtypeStruct(stored_tiles.shape[1:], F32), block],
        [
            pltpu.with_memory_space_constraint(operand, pltpu.HBM)
            for operand in (tile_flags, stored_tiles[0], orbitals)
        ],
        [HBM] * 3,
        [pltpu.SMEM(tile_flags.shape, jnp.int32), semaphore((3,))],
        flops=10**9,
    )
    mask = call(
        functools.partial(mask_kernel, layout),
        jax.ShapeDtypeStruct((group_width + 1, order), F32),
        [taken_flags],
        flops=10**10,
    )

    full = call(
        functools.partial(send_full_kernel, layout),
        [two] * layout.rounds,
        [tiles, taken, mask, held, taken_orbitals],
    )
    full_arrived = []
    for r in range(layout.rounds):
        swaps = [
            (i, i ^ (2 * layout.offset(r, i % 2))) for i in range(group_width)
        ]
        full_arrived.append(lax.ppermute(full[r], "dev", swaps))

    last = call(
        functools.partial(send_last_kernel, layout),
        two,
        [tiles, taken, mask, held, taken_orbitals],
    )
    last_arrived = lax.ppermute(last, ("grp", "dev"), last_moves(layout, groups))

    odd = call(functools.partial(send_odd_kernel, layout), block, [tiles, held])
    odd_arrived = lax.ppermute(odd, ("grp", "dev"), odd_moves(layout, groups))

    mine, others = call(
        functools.partial(near_kernel, layout),
        [block, block],
        [tiles, held, taken_orbitals],
    )
    others = call(
        functools.partial(full_kernel, layout),
        block,
        [taken, mask, others, *full_arrived],
    )
    others = call(
        functools.partial(back_kernel, layout),
        block,
        [taken, mask, others, last_arrived],
    )
    returned = lax.ppermute(others, "dev", partners)
    mine = call(
        functools.partial(mine_kernel, layout),
        block,
        [tiles, mine, last_arrived, odd_arrived, *full_arrived],
    )
    return mine + returned


def solution(mesh):
    in_specs = (
        P(("grp", "dev"), None, None, None),
        P(("grp", "dev"), None),
        P(("grp", "dev"), None),
    )
    out_specs = P(("grp", "dev"), None)
    return jax.shard_map(
        per_device, mesh=mesh, in_specs=in_specs, out_specs=out_specs, check_vma=False
    )
```

```python
import functools

import jax
import jax.numpy as jnp
from jax import lax
from jax.experimental import pallas as pl
from jax.experimental.pallas import tpu as pltpu
from jax.sharding import PartitionSpec as P

HBM = pl.BlockSpec(memory_space=pltpu.HBM)
VMEM = pl.BlockSpec(memory_space=pltpu.VMEM)
F32 = jnp.float32


def parted(value):
    high = value.astype(jnp.bfloat16)
    return high, (value - high.astype(F32)).astype(jnp.bfloat16)


def times(left, right):
    left_high, left_low = parted(left)
    right_high, right_low = parted(right)
    dot = functools.partial(jnp.dot, preferred_element_type=F32)
    rows = left.shape[0]
    both = dot(jnp.concatenate([left_high, left_low], axis=0), right_high)
    return both[:rows] + both[rows:] + dot(left_high, right_low)


def transposed_times(left, right):
    return times(left.T, right)


class Layout:
    def __init__(self, group_width):
        self.width = group_width
        self.pairs = group_width // 2
        self.rounds = (self.pairs - 1) // 2
        self.last_offset = 2

    def offset(self, round_index, side):
        if round_index == 0:
            return 1 + 2 * side
        return 2 * round_index + 2 + side


def place():
    index = lax.axis_index("dev")
    return index, index // 2, index % 2


def load_kernel(layout, flags_in, tiles_in, orbitals_in, tiles, orbitals, flags, sems):
    copies = [
        pltpu.make_async_copy(flags_in, flags, sems.at[0]),
        pltpu.make_async_copy(tiles_in, tiles, sems.at[1]),
        pltpu.make_async_copy(orbitals_in, orbitals, sems.at[2]),
    ]
    for copy in copies:
        copy.start()
    for copy in copies:
        copy.wait()
    for slot in range(layout.width + 1):
        tiles[slot] = tiles[slot] * flags[0, slot].astype(F32)


def mask_kernel(layout, flags, mask):
    row = flags[...].astype(F32)
    for slot in range(layout.width + 1):
        mask[slot : slot + 1] = jnp.broadcast_to(
            row[:, slot : slot + 1], (1, mask.shape[1])
        )


def taken_tile(taken, mask, slot):
    return taken[slot] * mask[pl.ds(slot, 1), :]


def pair_terms(far, tiles, taken, mask, own, other, out):
    lefts = []
    for k in range(2):
        slot = 2 * far + k
        stack = jnp.concatenate([tiles[slot], taken_tile(taken, mask, slot)], axis=0)
        lefts.append(stack.T)
    terms = times(
        jnp.concatenate(lefts, axis=0), jnp.concatenate([own, other], axis=0)
    )
    order = own.shape[0]
    out[0] = terms[:order]
    out[1] = terms[order:]


def send_full_kernel(layout, tiles, taken, mask, orbitals, taken_orbitals, *outs):
    index, pair, side = place()
    own, other = orbitals[...], taken_orbitals[...]
    for r in range(layout.rounds):
        far = pair ^ layout.offset(r, side)
        out = outs[r]

        @pl.when(far > pair)
        def _():
            pair_terms(far, tiles, taken, mask, own, other, out)

        @pl.when(far < pair)
        def _():
            out[0] = jnp.where(side == 0, own, other)
            out[1] = jnp.where(side == 0, other, own)


def send_last_kernel(layout, tiles, taken, mask, orbitals, taken_orbitals, out):
    index, pair, side = place()
    own, other = orbitals[...], taken_orbitals[...]
    far = pair ^ layout.last_offset
    lower = lax.axis_index("grp") % 2 == 0

    @pl.when((side == 1) & (far > pair))
    def _():
        pair_terms(far, tiles, taken, mask, own, other, out)

    @pl.when((side == 1) & (far < pair))
    def _():
        out[0] = other
        out[1] = own

    @pl.when((side == 0) & lower)
    def _():
        out[0] = transposed_times(tiles[layout.width], own)
        out[1] = transposed_times(taken_tile(taken, mask, layout.width), other)

    @pl.when((side == 0) & jnp.logical_not(lower))
    def _():
        out[0] = own
        out[1] = other


def send_odd_kernel(layout, tiles, orbitals, out):
    lower = lax.axis_index("grp") % 2 == 1

    @pl.when(lower)
    def _():
        out[...] = transposed_times(tiles[layout.width], orbitals[...])

    @pl.when(jnp.logical_not(lower))
    def _():
        out[...] = orbitals[...]


def near_kernel(layout, tiles, orbitals, taken_orbitals, mine, others):
    index, pair, side = place()
    own, other = orbitals[...], taken_orbitals[...]
    beside = tiles[index ^ 1]
    row = jnp.concatenate([tiles[index], beside], axis=1)
    mine[...] = times(row, jnp.concatenate([own, other], axis=0))
    others[...] = transposed_times(beside, own)


def take_full(layout, arrived, row, tile_of, total):
    index, pair, side = place()
    for r, came in enumerate(arrived):
        far = pair ^ layout.offset(r, side)

        @pl.when(far > pair)
        def _():
            left = jnp.concatenate([tile_of(2 * far), tile_of(2 * far + 1)], axis=1)
            right = jnp.concatenate([came[0], came[1]], axis=0)
            total[...] += times(left, right)

        @pl.when(far < pair)
        def _():
            total[...] += came[side ^ row]


def full_kernel(layout, taken, mask, others_in, *refs):
    arrived, others = refs[:-1], refs[-1]
    others[...] = others_in[...]
    take_full(layout, arrived, 1, lambda slot: taken_tile(taken, mask, slot), others)


def back_kernel(layout, taken, mask, others_in, came, others):
    index, pair, side = place()
    far = pair ^ layout.last_offset
    lower = lax.axis_index("grp") % 2 == 0

    @pl.when((side == 1) & (far > pair))
    def _():
        left = jnp.concatenate(
            [taken_tile(taken, mask, 2 * far + k) for k in range(2)], axis=1
        )
        right = jnp.concatenate([came[0], came[1]], axis=0)
        others[...] = others_in[...] + times(left, right)

    @pl.when((side == 1) & (far < pair))
    def _():
        others[...] = others_in[...] + came[0]

    @pl.when((side == 0) & lower)
    def _():
        left = taken_tile(taken, mask, layout.width)
        others[...] = others_in[...] + times(left, came[1])

    @pl.when((side == 0) & jnp.logical_not(lower))
    def _():
        others[...] = others_in[...] + came[1]


def mine_kernel(layout, tiles, mine_in, came, odd_in, *refs):
    arrived, mine = refs[:-1], refs[-1]
    index, pair, side = place()
    far = pair ^ layout.last_offset
    group = lax.axis_index("grp")
    lower = group % 2 == 0

    @pl.when((side == 1) & (far > pair))
    def _():
        left = jnp.concatenate([tiles[2 * far], tiles[2 * far + 1]], axis=1)
        right = jnp.concatenate([came[0], came[1]], axis=0)
        mine[...] = mine_in[...] + times(left, right)

    @pl.when((side == 1) & (far < pair))
    def _():
        mine[...] = mine_in[...] + came[1]

    @pl.when((side == 0) & lower)
    def _():
        mine[...] = mine_in[...] + times(tiles[layout.width], came[0])

    @pl.when((side == 0) & jnp.logical_not(lower))
    def _():
        mine[...] = mine_in[...] + came[0]

    @pl.when(lower)
    def _():
        mine[...] += jnp.where(group > 0, odd_in[...], 0.0)

    @pl.when(jnp.logical_not(lower))
    def _():
        mine[...] += times(tiles[layout.width], odd_in[...])

    take_full(layout, arrived, 0, lambda slot: tiles[slot], mine)


def call(body, outs, operands, specs=None, scratch=(), flops=0):
    return pl.pallas_call(
        body,
        out_shape=outs,
        in_specs=specs or [VMEM] * len(operands),
        out_specs=jax.tree.map(lambda _: VMEM, outs),
        scratch_shapes=scratch,
        cost_estimate=pl.CostEstimate(
            flops=flops, bytes_accessed=0, transcendentals=0
        ),
        compiler_params=pltpu.CompilerParams(vmem_limit_bytes=32 * 1024 * 1024),
    )(*operands)


def last_moves(layout, groups):
    moves = []
    for g in range(groups):
        for i in range(layout.width):
            if i % 2 == 1:
                to, j = g, i ^ (2 * layout.last_offset)
            else:
                to, j = g ^ 1, i
                if to >= groups:
                    to = g
            moves.append((g * layout.width + i, to * layout.width + j))
    return moves


def odd_moves(layout, groups):
    moves = []
    for g in range(groups):
        to = g + 1 if g % 2 == 1 else g - 1
        for i in range(layout.width):
            if 0 <= to < groups:
                moves.append((g * layout.width + i, to * layout.width + i))
            else:
                moves.append((g * layout.width + i, g * layout.width + (i ^ 1)))
    return moves


def per_device(stored_tiles, tile_flags, orbitals):
    group_width = lax.axis_size("dev")
    groups = lax.axis_size("grp")
    layout = Layout(group_width)
    order, columns = orbitals.shape
    block = jax.ShapeDtypeStruct((order, columns), F32)
    two = jax.ShapeDtypeStruct((2, order, columns), F32)
    partners = [(i, i ^ 1) for i in range(group_width)]
    semaphore = pltpu.SemaphoreType.DMA

    taken = lax.ppermute(stored_tiles, "dev", partners)[0]
    taken_orbitals = lax.ppermute(orbitals, "dev", partners)
    taken_flags = lax.ppermute(tile_flags, "dev", partners)
    tiles, held = call(
        functools.partial(load_kernel, layout),
        [jax.ShapeDtypeStruct(stored_tiles.shape[1:], F32), block],
        [
            pltpu.with_memory_space_constraint(operand, pltpu.HBM)
            for operand in (tile_flags, stored_tiles[0], orbitals)
        ],
        [HBM] * 3,
        [pltpu.SMEM(tile_flags.shape, jnp.int32), semaphore((3,))],
        flops=10**9,
    )
    mask = call(
        functools.partial(mask_kernel, layout),
        jax.ShapeDtypeStruct((group_width + 1, order), F32),
        [taken_flags],
        flops=10**9,
    )

    full = call(
        functools.partial(send_full_kernel, layout),
        [two] * layout.rounds,
        [tiles, taken, mask, held, taken_orbitals],
    )
    full_arrived = []
    for r in range(layout.rounds):
        swaps = [
            (i, i ^ (2 * layout.offset(r, i % 2))) for i in range(group_width)
        ]
        full_arrived.append(lax.ppermute(full[r], "dev", swaps))

    last = call(
        functools.partial(send_last_kernel, layout),
        two,
        [tiles, taken, mask, held, taken_orbitals],
    )
    last_arrived = lax.ppermute(last, ("grp", "dev"), last_moves(layout, groups))

    odd = call(functools.partial(send_odd_kernel, layout), block, [tiles, held])
    odd_arrived = lax.ppermute(odd, ("grp", "dev"), odd_moves(layout, groups))

    mine, others = call(
        functools.partial(near_kernel, layout),
        [block, block],
        [tiles, held, taken_orbitals],
    )
    others = call(
        functools.partial(full_kernel, layout),
        block,
        [taken, mask, others, *full_arrived],
    )
    others = call(
        functools.partial(back_kernel, layout),
        block,
        [taken, mask, others, last_arrived],
    )
    returned = lax.ppermute(others, "dev", partners)
    mine = call(
        functools.partial(mine_kernel, layout),
        block,
        [tiles, mine, last_arrived, odd_arrived, *full_arrived],
    )
    return mine + returned


def solution(mesh):
    in_specs = (
        P(("grp", "dev"), None, None, None),
        P(("grp", "dev"), None),
        P(("grp", "dev"), None),
    )
    out_specs = P(("grp", "dev"), None)
    return jax.shard_map(
        per_device, mesh=mesh, in_specs=in_specs, out_specs=out_specs, check_vma=False
    )
```

```python
import functools

import jax
import jax.numpy as jnp
from jax import lax
from jax.experimental import pallas as pl
from jax.experimental.pallas import tpu as pltpu
from jax.sharding import PartitionSpec as P

HBM = pl.BlockSpec(memory_space=pltpu.HBM)
VMEM = pl.BlockSpec(memory_space=pltpu.VMEM)
F32 = jnp.float32


def parted(value):
    high = value.astype(jnp.bfloat16)
    return high, (value - high.astype(F32)).astype(jnp.bfloat16)


def times(left, right):
    left_high, left_low = parted(left)
    right_high, right_low = parted(right)
    dot = functools.partial(jnp.dot, preferred_element_type=F32)
    rows = left.shape[0]
    both = dot(jnp.concatenate([left_high, left_low], axis=0), right_high)
    return both[:rows] + both[rows:] + dot(left_high, right_low)


def transposed_times(left, right):
    return times(left.T, right)


class Layout:
    def __init__(self, group_width):
        self.width = group_width
        self.pairs = group_width // 2
        self.rounds = (self.pairs - 1) // 2
        self.last_offset = 2

    def offset(self, round_index, side):
        if round_index == 0:
            return 1 + 2 * side
        return 2 * round_index + 2 + side


def place():
    index = lax.axis_index("dev")
    return index, index // 2, index % 2


def load_kernel(layout, flags_in, tiles_in, orbitals_in, tiles, orbitals, flags, sems):
    copies = [
        pltpu.make_async_copy(flags_in, flags, sems.at[0]),
        pltpu.make_async_copy(tiles_in, tiles, sems.at[1]),
        pltpu.make_async_copy(orbitals_in, orbitals, sems.at[2]),
    ]
    for copy in copies:
        copy.start()
    for copy in copies:
        copy.wait()
    for slot in range(layout.width + 1):
        tiles[slot] = tiles[slot] * flags[0, slot].astype(F32)


def mask_kernel(layout, flags, mask):
    row = flags[...].astype(F32)
    for slot in range(layout.width + 1):
        mask[slot : slot + 1] = jnp.broadcast_to(
            row[:, slot : slot + 1], (1, mask.shape[1])
        )


def taken_tile(taken, mask, slot):
    return taken[slot] * mask[pl.ds(slot, 1), :]


def pair_terms(far, tiles, taken, mask, own, other, out):
    lefts = []
    for k in range(2):
        slot = 2 * far + k
        stack = jnp.concatenate([tiles[slot], taken_tile(taken, mask, slot)], axis=0)
        lefts.append(stack.T)
    terms = times(
        jnp.concatenate(lefts, axis=0), jnp.concatenate([own, other], axis=0)
    )
    order = own.shape[0]
    out[0] = terms[:order]
    out[1] = terms[order:]


def send_full_kernel(layout, tiles, taken, mask, orbitals, taken_orbitals, *outs):
    index, pair, side = place()
    own, other = orbitals[...], taken_orbitals[...]
    for r in range(layout.rounds):
        far = pair ^ layout.offset(r, side)
        out = outs[r]

        @pl.when(far > pair)
        def _():
            pair_terms(far, tiles, taken, mask, own, other, out)

        @pl.when(far < pair)
        def _():
            out[0] = jnp.where(side == 0, own, other)
            out[1] = jnp.where(side == 0, other, own)

    far = pair ^ layout.last_offset

    @pl.when((side == 1) & (pair == 0))
    def _():
        pair_terms(far, tiles, taken, mask, own, other, outs[-1])


def send_last_kernel(layout, tiles, taken, mask, orbitals, taken_orbitals, made, out):
    index, pair, side = place()
    own, other = orbitals[...], taken_orbitals[...]
    far = pair ^ layout.last_offset
    lower = lax.axis_index("grp") % 2 == 0

    @pl.when((side == 1) & (pair == 0))
    def _():
        out[...] = made[...]

    @pl.when((side == 1) & (far > pair) & (pair > 0))
    def _():
        pair_terms(far, tiles, taken, mask, own, other, out)

    @pl.when((side == 1) & (far < pair))
    def _():
        out[0] = other
        out[1] = own

    @pl.when((side == 0) & lower)
    def _():
        out[0] = transposed_times(tiles[layout.width], own)
        out[1] = transposed_times(taken_tile(taken, mask, layout.width), other)

    @pl.when((side == 0) & jnp.logical_not(lower))
    def _():
        out[0] = own
        out[1] = other


def send_odd_kernel(layout, tiles, orbitals, out):
    lower = lax.axis_index("grp") % 2 == 1

    @pl.when(lower)
    def _():
        out[...] = transposed_times(tiles[layout.width], orbitals[...])

    @pl.when(jnp.logical_not(lower))
    def _():
        out[...] = orbitals[...]


def near_kernel(layout, tiles, orbitals, taken_orbitals, mine, others):
    index, pair, side = place()
    own, other = orbitals[...], taken_orbitals[...]
    beside = tiles[index ^ 1]
    row = jnp.concatenate([tiles[index], beside], axis=1)
    mine[...] = times(row, jnp.concatenate([own, other], axis=0))
    others[...] = transposed_times(beside, own)


def take_full(layout, arrived, row, tile_of, total):
    index, pair, side = place()
    for r, came in enumerate(arrived):
        far = pair ^ layout.offset(r, side)

        @pl.when(far > pair)
        def _():
            left = jnp.concatenate([tile_of(2 * far), tile_of(2 * far + 1)], axis=1)
            right = jnp.concatenate([came[0], came[1]], axis=0)
            total[...] += times(left, right)

        @pl.when(far < pair)
        def _():
            total[...] += came[side ^ row]


def full_kernel(layout, taken, mask, others_in, *refs):
    arrived, others = refs[:-1], refs[-1]
    others[...] = others_in[...]
    take_full(layout, arrived, 1, lambda slot: taken_tile(taken, mask, slot), others)


def back_kernel(layout, taken, mask, others_in, came, others):
    index, pair, side = place()
    far = pair ^ layout.last_offset
    lower = lax.axis_index("grp") % 2 == 0

    @pl.when((side == 1) & (far > pair))
    def _():
        left = jnp.concatenate(
            [taken_tile(taken, mask, 2 * far + k) for k in range(2)], axis=1
        )
        right = jnp.concatenate([came[0], came[1]], axis=0)
        others[...] = others_in[...] + times(left, right)

    @pl.when((side == 1) & (far < pair))
    def _():
        others[...] = others_in[...] + came[0]

    @pl.when((side == 0) & lower)
    def _():
        left = taken_tile(taken, mask, layout.width)
        others[...] = others_in[...] + times(left, came[1])

    @pl.when((side == 0) & jnp.logical_not(lower))
    def _():
        others[...] = others_in[...] + came[1]


def mine_kernel(layout, tiles, mine_in, came, odd_in, *refs):
    arrived, mine = refs[:-1], refs[-1]
    index, pair, side = place()
    far = pair ^ layout.last_offset
    group = lax.axis_index("grp")
    lower = group % 2 == 0

    @pl.when((side == 1) & (far > pair))
    def _():
        left = jnp.concatenate([tiles[2 * far], tiles[2 * far + 1]], axis=1)
        right = jnp.concatenate([came[0], came[1]], axis=0)
        mine[...] = mine_in[...] + times(left, right)

    @pl.when((side == 1) & (far < pair))
    def _():
        mine[...] = mine_in[...] + came[1]

    @pl.when((side == 0) & lower)
    def _():
        mine[...] = mine_in[...] + times(tiles[layout.width], came[0])

    @pl.when((side == 0) & jnp.logical_not(lower))
    def _():
        mine[...] = mine_in[...] + came[0]

    @pl.when(lower)
    def _():
        mine[...] += jnp.where(group > 0, odd_in[...], 0.0)

    @pl.when(jnp.logical_not(lower))
    def _():
        mine[...] += times(tiles[layout.width], odd_in[...])

    take_full(layout, arrived, 0, lambda slot: tiles[slot], mine)


def call(body, outs, operands, specs=None, scratch=(), flops=0):
    return pl.pallas_call(
        body,
        out_shape=outs,
        in_specs=specs or [VMEM] * len(operands),
        out_specs=jax.tree.map(lambda _: VMEM, outs),
        scratch_shapes=scratch,
        cost_estimate=pl.CostEstimate(
            flops=flops, bytes_accessed=0, transcendentals=0
        ),
        compiler_params=pltpu.CompilerParams(vmem_limit_bytes=32 * 1024 * 1024),
    )(*operands)


def last_moves(layout, groups):
    moves = []
    for g in range(groups):
        for i in range(layout.width):
            if i % 2 == 1:
                to, j = g, i ^ (2 * layout.last_offset)
            else:
                to, j = g ^ 1, i
                if to >= groups:
                    to = g
            moves.append((g * layout.width + i, to * layout.width + j))
    return moves


def odd_moves(layout, groups):
    moves = []
    for g in range(groups):
        to = g + 1 if g % 2 == 1 else g - 1
        for i in range(layout.width):
            if 0 <= to < groups:
                moves.append((g * layout.width + i, to * layout.width + i))
            else:
                moves.append((g * layout.width + i, g * layout.width + (i ^ 1)))
    return moves


def per_device(stored_tiles, tile_flags, orbitals):
    group_width = lax.axis_size("dev")
    groups = lax.axis_size("grp")
    layout = Layout(group_width)
    order, columns = orbitals.shape
    block = jax.ShapeDtypeStruct((order, columns), F32)
    two = jax.ShapeDtypeStruct((2, order, columns), F32)
    partners = [(i, i ^ 1) for i in range(group_width)]
    semaphore = pltpu.SemaphoreType.DMA

    taken = lax.ppermute(stored_tiles, "dev", partners)[0]
    taken_orbitals = lax.ppermute(orbitals, "dev", partners)
    taken_flags = lax.ppermute(tile_flags, "dev", partners)
    tiles, held = call(
        functools.partial(load_kernel, layout),
        [jax.ShapeDtypeStruct(stored_tiles.shape[1:], F32), block],
        [
            pltpu.with_memory_space_constraint(operand, pltpu.HBM)
            for operand in (tile_flags, stored_tiles[0], orbitals)
        ],
        [HBM] * 3,
        [pltpu.SMEM(tile_flags.shape, jnp.int32), semaphore((3,))],
        flops=10**9,
    )
    mask = call(
        functools.partial(mask_kernel, layout),
        jax.ShapeDtypeStruct((group_width + 1, order), F32),
        [taken_flags],
        flops=10**9,
    )

    *full, made = call(
        functools.partial(send_full_kernel, layout),
        [two] * (layout.rounds + 1),
        [tiles, taken, mask, held, taken_orbitals],
    )
    full_arrived = []
    for r in range(layout.rounds):
        swaps = [
            (i, i ^ (2 * layout.offset(r, i % 2))) for i in range(group_width)
        ]
        full_arrived.append(lax.ppermute(full[r], "dev", swaps))

    last = call(
        functools.partial(send_last_kernel, layout),
        two,
        [tiles, taken, mask, held, taken_orbitals, made],
    )
    last_arrived = lax.ppermute(last, ("grp", "dev"), last_moves(layout, groups))

    odd = call(functools.partial(send_odd_kernel, layout), block, [tiles, held])
    odd_arrived = lax.ppermute(odd, ("grp", "dev"), odd_moves(layout, groups))

    mine, others = call(
        functools.partial(near_kernel, layout),
        [block, block],
        [tiles, held, taken_orbitals],
    )
    others = call(
        functools.partial(full_kernel, layout),
        block,
        [taken, mask, others, *full_arrived],
    )
    others = call(
        functools.partial(back_kernel, layout),
        block,
        [taken, mask, others, last_arrived],
    )
    returned = lax.ppermute(others, "dev", partners)
    mine = call(
        functools.partial(mine_kernel, layout),
        block,
        [tiles, mine, last_arrived, odd_arrived, *full_arrived],
    )
    return mine + returned


def solution(mesh):
    in_specs = (
        P(("grp", "dev"), None, None, None),
        P(("grp", "dev"), None),
        P(("grp", "dev"), None),
    )
    out_specs = P(("grp", "dev"), None)
    return jax.shard_map(
        per_device, mesh=mesh, in_specs=in_specs, out_specs=out_specs, check_vma=False
    )
```

```python
import functools

import jax
import jax.numpy as jnp
from jax import lax
from jax.experimental import pallas as pl
from jax.experimental.pallas import tpu as pltpu
from jax.sharding import PartitionSpec as P

HBM = pl.BlockSpec(memory_space=pltpu.HBM)
VMEM = pl.BlockSpec(memory_space=pltpu.VMEM)
F32 = jnp.float32


def parted(value):
    high = value.astype(jnp.bfloat16)
    return high, (value - high.astype(F32)).astype(jnp.bfloat16)


def product_of(left, right, contract):
    dims = ((contract, (0,)), ((), ()))
    dot = functools.partial(
        lax.dot_general, dimension_numbers=dims, preferred_element_type=F32
    )
    (left_high, left_low), (right_high, right_low) = left, right
    return (
        dot(left_high, right_high)
        + dot(left_high, right_low)
        + dot(left_low, right_high)
    )


def times(left, right):
    return product_of(parted(left), parted(right), (1,))


def transposed_times(left, right):
    return product_of(parted(left), parted(right), (0,))


class Layout:
    def __init__(self, group_width):
        self.width = group_width
        self.pairs = group_width // 2
        self.rounds = (self.pairs - 1) // 2
        self.first_offset = self.pairs - 1

    def offset(self, round_index, side):
        return 2 * round_index + 1 + side


def place():
    index = lax.axis_index("dev")
    return index, index // 2, index % 2


def load_kernel(layout, flags_in, tiles_in, orbitals_in, tiles, orbitals, flags, sems):
    copies = [
        pltpu.make_async_copy(flags_in, flags, sems.at[0]),
        pltpu.make_async_copy(tiles_in, tiles, sems.at[1]),
        pltpu.make_async_copy(orbitals_in, orbitals, sems.at[2]),
    ]
    for copy in copies:
        copy.start()
    for copy in copies:
        copy.wait()
    for slot in range(layout.width + 1):
        tiles[slot] = tiles[slot] * flags[0, slot].astype(F32)


def mask_kernel(layout, flags, mask):
    row = flags[...].astype(F32)
    for slot in range(layout.width + 1):
        mask[slot : slot + 1] = jnp.broadcast_to(
            row[:, slot : slot + 1], (1, mask.shape[1])
        )


def taken_tile(taken, mask, slot):
    return taken[slot] * mask[pl.ds(slot, 1), :]


def send_full_kernel(layout, tiles, taken, mask, orbitals, taken_orbitals, *outs):
    index, pair, side = place()
    own, other = orbitals[...], taken_orbitals[...]
    for r in range(layout.rounds):
        far = pair ^ layout.offset(r, side)
        out = outs[r]

        @pl.when(far > pair)
        def _():
            right = parted(jnp.concatenate([own, other], axis=0))
            for k in range(2):
                slot = 2 * far + k
                left = jnp.concatenate(
                    [tiles[slot], taken_tile(taken, mask, slot)], axis=0
                )
                out[k] = product_of(parted(left), right, (0,))

        @pl.when(far < pair)
        def _():
            out[0] = jnp.where(side == 0, own, other)
            out[1] = jnp.where(side == 0, other, own)


def send_first_kernel(layout, tiles, taken, mask, orbitals, taken_orbitals, out):
    index, pair, side = place()
    own, other = orbitals[...], taken_orbitals[...]
    far = pair ^ layout.first_offset
    lower = lax.axis_index("grp") % 2 == 0

    @pl.when((side == 1) & (far > pair))
    def _():
        right = parted(jnp.concatenate([own, other], axis=0))
        for k in range(2):
            slot = 2 * far + k
            left = jnp.concatenate(
                [tiles[slot], taken_tile(taken, mask, slot)], axis=0
            )
            out[k] = product_of(parted(left), right, (0,))

    @pl.when((side == 1) & (far < pair))
    def _():
        out[0] = other
        out[1] = own

    @pl.when((side == 0) & lower)
    def _():
        out[0] = transposed_times(tiles[layout.width], own)
        out[1] = transposed_times(taken_tile(taken, mask, layout.width), other)

    @pl.when((side == 0) & jnp.logical_not(lower))
    def _():
        out[0] = own
        out[1] = other


def send_odd_kernel(layout, tiles, orbitals, out):
    lower = lax.axis_index("grp") % 2 == 1

    @pl.when(lower)
    def _():
        out[...] = transposed_times(tiles[layout.width], orbitals[...])

    @pl.when(jnp.logical_not(lower))
    def _():
        out[...] = orbitals[...]


def near_kernel(layout, tiles, orbitals, taken_orbitals, mine, others):
    index, pair, side = place()
    own, other = orbitals[...], taken_orbitals[...]
    beside = tiles[index ^ 1]
    row = jnp.concatenate([tiles[index], beside], axis=1)
    mine[...] = times(row, jnp.concatenate([own, other], axis=0))
    others[...] = transposed_times(beside, own)


def take_first(layout, came, row, tile_of, total):
    index, pair, side = place()
    far = pair ^ layout.first_offset
    lower = lax.axis_index("grp") % 2 == 0

    @pl.when((side == 1) & (far > pair))
    def _():
        left = jnp.concatenate([tile_of(2 * far), tile_of(2 * far + 1)], axis=1)
        right = jnp.concatenate([came[0], came[1]], axis=0)
        total[...] += times(left, right)

    @pl.when((side == 1) & (far < pair))
    def _():
        total[...] += came[1 - row]

    @pl.when((side == 0) & lower)
    def _():
        total[...] += times(tile_of(layout.width), came[row])

    @pl.when((side == 0) & jnp.logical_not(lower))
    def _():
        total[...] += came[row]


def take_full(layout, arrived, row, tile_of, total):
    index, pair, side = place()
    for r, came in enumerate(arrived):
        far = pair ^ layout.offset(r, side)

        @pl.when(far > pair)
        def _():
            left = jnp.concatenate([tile_of(2 * far), tile_of(2 * far + 1)], axis=1)
            right = jnp.concatenate([came[0], came[1]], axis=0)
            total[...] += times(left, right)

        @pl.when(far < pair)
        def _():
            total[...] += came[side ^ row]


def first_kernel(layout, tiles, taken, mask, mine_in, others_in, came, mine, others):
    mine[...] = mine_in[...]
    others[...] = others_in[...]
    take_first(layout, came, 0, lambda slot: tiles[slot], mine)
    take_first(layout, came, 1, lambda slot: taken_tile(taken, mask, slot), others)


def others_kernel(layout, taken, mask, others_in, *refs):
    arrived, others = refs[:-1], refs[-1]
    others[...] = others_in[...]
    take_full(layout, arrived, 1, lambda slot: taken_tile(taken, mask, slot), others)


def mine_kernel(layout, tiles, mine_in, odd_in, *refs):
    arrived, mine = refs[:-1], refs[-1]
    group = lax.axis_index("grp")
    lower = group % 2 == 1

    @pl.when(lower)
    def _():
        mine[...] = mine_in[...] + times(tiles[layout.width], odd_in[...])

    @pl.when(jnp.logical_not(lower))
    def _():
        mine[...] = mine_in[...] + jnp.where(group > 0, odd_in[...], 0.0)

    take_full(layout, arrived, 0, lambda slot: tiles[slot], mine)


def call(body, outs, operands, specs=None, scratch=(), flops=0):
    return pl.pallas_call(
        body,
        out_shape=outs,
        in_specs=specs or [VMEM] * len(operands),
        out_specs=jax.tree.map(lambda _: VMEM, outs),
        scratch_shapes=scratch,
        cost_estimate=pl.CostEstimate(
            flops=flops, bytes_accessed=0, transcendentals=0
        ),
        compiler_params=pltpu.CompilerParams(vmem_limit_bytes=32 * 1024 * 1024),
    )(*operands)


def first_moves(layout, groups):
    moves = []
    for g in range(groups):
        for i in range(layout.width):
            if i % 2 == 1:
                to, j = g, i ^ (2 * layout.first_offset)
            else:
                to, j = g ^ 1, i
                if to >= groups:
                    to = g
            moves.append((g * layout.width + i, to * layout.width + j))
    return moves


def odd_moves(layout, groups):
    moves = []
    for g in range(groups):
        to = g + 1 if g % 2 == 1 else g - 1
        for i in range(layout.width):
            if 0 <= to < groups:
                moves.append((g * layout.width + i, to * layout.width + i))
            else:
                moves.append((g * layout.width + i, g * layout.width + (i ^ 1)))
    return moves


def per_device(stored_tiles, tile_flags, orbitals):
    group_width = lax.axis_size("dev")
    groups = lax.axis_size("grp")
    layout = Layout(group_width)
    order, columns = orbitals.shape
    block = jax.ShapeDtypeStruct((order, columns), F32)
    two = jax.ShapeDtypeStruct((2, order, columns), F32)
    partners = [(i, i ^ 1) for i in range(group_width)]
    semaphore = pltpu.SemaphoreType.DMA

    taken = lax.ppermute(stored_tiles, "dev", partners)[0]
    taken_orbitals = lax.ppermute(orbitals, "dev", partners)
    taken_flags = lax.ppermute(tile_flags, "dev", partners)
    tiles, held = call(
        functools.partial(load_kernel, layout),
        [jax.ShapeDtypeStruct(stored_tiles.shape[1:], F32), block],
        [
            pltpu.with_memory_space_constraint(operand, pltpu.HBM)
            for operand in (tile_flags, stored_tiles[0], orbitals)
        ],
        [HBM] * 3,
        [pltpu.SMEM(tile_flags.shape, jnp.int32), semaphore((3,))],
        flops=10**9,
    )
    mask = call(
        functools.partial(mask_kernel, layout),
        jax.ShapeDtypeStruct((group_width + 1, order), F32),
        [taken_flags],
        flops=10**9,
    )

    first = call(
        functools.partial(send_first_kernel, layout),
        two,
        [tiles, taken, mask, held, taken_orbitals],
    )
    first_arrived = lax.ppermute(first, ("grp", "dev"), first_moves(layout, groups))

    full = call(
        functools.partial(send_full_kernel, layout),
        [two] * layout.rounds,
        [tiles, taken, mask, held, taken_orbitals],
    )
    full_arrived = []
    for r in range(layout.rounds):
        swaps = [
            (i, i ^ (2 * layout.offset(r, i % 2))) for i in range(group_width)
        ]
        full_arrived.append(lax.ppermute(full[r], "dev", swaps))

    odd = call(functools.partial(send_odd_kernel, layout), block, [tiles, held])
    odd_arrived = lax.ppermute(odd, ("grp", "dev"), odd_moves(layout, groups))

    mine, others = call(
        functools.partial(near_kernel, layout),
        [block, block],
        [tiles, held, taken_orbitals],
    )
    mine, others = call(
        functools.partial(first_kernel, layout),
        [block, block],
        [tiles, taken, mask, mine, others, first_arrived],
    )
    others = call(
        functools.partial(others_kernel, layout),
        block,
        [taken, mask, others, *full_arrived],
    )
    returned = lax.ppermute(others, "dev", partners)
    mine = call(
        functools.partial(mine_kernel, layout),
        block,
        [tiles, mine, odd_arrived, *full_arrived],
    )
    return mine + returned


def solution(mesh):
    in_specs = (
        P(("grp", "dev"), None, None, None),
        P(("grp", "dev"), None),
        P(("grp", "dev"), None),
    )
    out_specs = P(("grp", "dev"), None)
    return jax.shard_map(
        per_device, mesh=mesh, in_specs=in_specs, out_specs=out_specs, check_vma=False
    )
```

```python
import functools

import jax
import jax.numpy as jnp
from jax import lax
from jax.experimental import pallas as pl
from jax.experimental.pallas import tpu as pltpu
from jax.sharding import PartitionSpec as P

HBM = pl.BlockSpec(memory_space=pltpu.HBM)
VMEM = pl.BlockSpec(memory_space=pltpu.VMEM)
F32 = jnp.float32


def parted(value):
    high = value.astype(jnp.bfloat16)
    return high, (value - high.astype(F32)).astype(jnp.bfloat16)


def times(left, right):
    left_high, left_low = parted(left)
    right_high, right_low = parted(right)
    dot = functools.partial(jnp.dot, preferred_element_type=F32)
    rows = left.shape[0]
    both = dot(jnp.concatenate([left_high, left_low], axis=0), right_high)
    return both[:rows] + both[rows:] + dot(left_high, right_low)


def narrow_times(left, right):
    left_high, left_low = parted(left)
    right_high, right_low = parted(right)
    dot = functools.partial(jnp.dot, preferred_element_type=F32)
    wide = jnp.concatenate([left_high, left_low], axis=1)
    both = dot(wide, jnp.concatenate([right_high, right_high], axis=0))
    return both + dot(left_high, right_low)


def transposed_times(left, right):
    return times(left.T, right)


class Layout:
    def __init__(self, group_width):
        self.width = group_width
        self.pairs = group_width // 2
        self.rounds = (self.pairs - 1) // 2
        self.last_offset = 2

    def offset(self, round_index, side):
        if round_index == 0:
            return 1 + 2 * side
        return 2 * round_index + 2 + side


def place():
    index = lax.axis_index("dev")
    return index, index // 2, index % 2


def load_kernel(
    layout, flags_in, tiles_in, orbitals_in, tiles, orbitals, shares, flags, sems
):
    index, pair, side = place()
    copies = [
        pltpu.make_async_copy(flags_in, flags, sems.at[0]),
        pltpu.make_async_copy(tiles_in, tiles, sems.at[1]),
        pltpu.make_async_copy(orbitals_in, orbitals, sems.at[2]),
    ]
    for copy in copies:
        copy.start()
    for copy in copies:
        copy.wait()
    for slot in range(layout.width + 1):
        tiles[slot] = tiles[slot] * flags[0, slot].astype(F32)
    for r in range(layout.rounds):
        far = pair ^ layout.offset(r, side)

        @pl.when(far > pair)
        def _():
            left = jnp.concatenate([tiles[2 * far].T, tiles[2 * far + 1].T], axis=0)
            shares[r] = narrow_times(left, orbitals[...])


def mask_kernel(layout, flags, mask):
    row = flags[...].astype(F32)
    for slot in range(layout.width + 1):
        mask[slot : slot + 1] = jnp.broadcast_to(
            row[:, slot : slot + 1], (1, mask.shape[1])
        )


def taken_tile(taken, mask, slot):
    return taken[slot] * mask[pl.ds(slot, 1), :]


def pair_terms(far, tiles, taken, mask, own, other, out):
    lefts = []
    for k in range(2):
        slot = 2 * far + k
        stack = jnp.concatenate([tiles[slot], taken_tile(taken, mask, slot)], axis=0)
        lefts.append(stack.T)
    terms = times(
        jnp.concatenate(lefts, axis=0), jnp.concatenate([own, other], axis=0)
    )
    order = own.shape[0]
    out[0] = terms[:order]
    out[1] = terms[order:]


def send_full_kernel(
    layout, tiles, taken, mask, orbitals, taken_orbitals, shares, *outs
):
    index, pair, side = place()
    own, other = orbitals[...], taken_orbitals[...]
    for r in range(layout.rounds):
        far = pair ^ layout.offset(r, side)
        out = outs[r]

        @pl.when(far > pair)
        def _():
            lefts = [taken_tile(taken, mask, 2 * far + k).T for k in range(2)]
            terms = narrow_times(jnp.concatenate(lefts, axis=0), other) + shares[r]
            order = own.shape[0]
            out[0] = terms[:order]
            out[1] = terms[order:]

        @pl.when(far < pair)
        def _():
            out[0] = jnp.where(side == 0, own, other)
            out[1] = jnp.where(side == 0, other, own)

    far = pair ^ layout.last_offset

    @pl.when((side == 1) & (pair == 0))
    def _():
        pair_terms(far, tiles, taken, mask, own, other, outs[-1])


def send_last_kernel(layout, tiles, taken, mask, orbitals, taken_orbitals, made, out):
    index, pair, side = place()
    own, other = orbitals[...], taken_orbitals[...]
    far = pair ^ layout.last_offset
    lower = lax.axis_index("grp") % 2 == 0

    @pl.when((side == 1) & (pair == 0))
    def _():
        out[...] = made[...]

    @pl.when((side == 1) & (far > pair) & (pair > 0))
    def _():
        pair_terms(far, tiles, taken, mask, own, other, out)

    @pl.when((side == 1) & (far < pair))
    def _():
        out[0] = other
        out[1] = own

    @pl.when((side == 0) & lower)
    def _():
        out[0] = transposed_times(tiles[layout.width], own)
        out[1] = transposed_times(taken_tile(taken, mask, layout.width), other)

    @pl.when((side == 0) & jnp.logical_not(lower))
    def _():
        out[0] = own
        out[1] = other


def send_odd_kernel(layout, tiles, orbitals, out):
    lower = lax.axis_index("grp") % 2 == 1

    @pl.when(lower)
    def _():
        out[...] = transposed_times(tiles[layout.width], orbitals[...])

    @pl.when(jnp.logical_not(lower))
    def _():
        out[...] = orbitals[...]


def near_kernel(layout, tiles, orbitals, taken_orbitals, mine, others):
    index, pair, side = place()
    own, other = orbitals[...], taken_orbitals[...]
    beside = tiles[index ^ 1]
    row = jnp.concatenate([tiles[index], beside], axis=1)
    mine[...] = times(row, jnp.concatenate([own, other], axis=0))
    others[...] = transposed_times(beside, own)


def take_full(layout, arrived, row, tile_of, total):
    index, pair, side = place()
    for r, came in enumerate(arrived):
        far = pair ^ layout.offset(r, side)

        @pl.when(far > pair)
        def _():
            left = jnp.concatenate([tile_of(2 * far), tile_of(2 * far + 1)], axis=1)
            right = jnp.concatenate([came[0], came[1]], axis=0)
            total[...] += times(left, right)

        @pl.when(far < pair)
        def _():
            total[...] += came[side ^ row]


def full_kernel(layout, taken, mask, others_in, *refs):
    arrived, others = refs[:-1], refs[-1]
    others[...] = others_in[...]
    take_full(layout, arrived, 1, lambda slot: taken_tile(taken, mask, slot), others)


def back_kernel(layout, taken, mask, others_in, came, others):
    index, pair, side = place()
    far = pair ^ layout.last_offset
    lower = lax.axis_index("grp") % 2 == 0

    @pl.when((side == 1) & (far > pair))
    def _():
        left = jnp.concatenate(
            [taken_tile(taken, mask, 2 * far + k) for k in range(2)], axis=1
        )
        right = jnp.concatenate([came[0], came[1]], axis=0)
        others[...] = others_in[...] + times(left, right)

    @pl.when((side == 1) & (far < pair))
    def _():
        others[...] = others_in[...] + came[0]

    @pl.when((side == 0) & lower)
    def _():
        left = taken_tile(taken, mask, layout.width)
        others[...] = others_in[...] + times(left, came[1])

    @pl.when((side == 0) & jnp.logical_not(lower))
    def _():
        others[...] = others_in[...] + came[1]


def mine_kernel(layout, tiles, mine_in, came, odd_in, *refs):
    arrived, mine = refs[:-1], refs[-1]
    index, pair, side = place()
    far = pair ^ layout.last_offset
    group = lax.axis_index("grp")
    lower = group % 2 == 0

    @pl.when((side == 1) & (far > pair))
    def _():
        left = jnp.concatenate([tiles[2 * far], tiles[2 * far + 1]], axis=1)
        right = jnp.concatenate([came[0], came[1]], axis=0)
        mine[...] = mine_in[...] + times(left, right)

    @pl.when((side == 1) & (far < pair))
    def _():
        mine[...] = mine_in[...] + came[1]

    @pl.when((side == 0) & lower)
    def _():
        mine[...] = mine_in[...] + times(tiles[layout.width], came[0])

    @pl.when((side == 0) & jnp.logical_not(lower))
    def _():
        mine[...] = mine_in[...] + came[0]

    @pl.when(lower)
    def _():
        mine[...] += jnp.where(group > 0, odd_in[...], 0.0)

    @pl.when(jnp.logical_not(lower))
    def _():
        mine[...] += times(tiles[layout.width], odd_in[...])

    take_full(layout, arrived, 0, lambda slot: tiles[slot], mine)


def call(body, outs, operands, specs=None, scratch=(), flops=0):
    return pl.pallas_call(
        body,
        out_shape=outs,
        in_specs=specs or [VMEM] * len(operands),
        out_specs=jax.tree.map(lambda _: VMEM, outs),
        scratch_shapes=scratch,
        cost_estimate=pl.CostEstimate(
            flops=flops, bytes_accessed=0, transcendentals=0
        ),
        compiler_params=pltpu.CompilerParams(vmem_limit_bytes=32 * 1024 * 1024),
    )(*operands)


def last_moves(layout, groups):
    moves = []
    for g in range(groups):
        for i in range(layout.width):
            if i % 2 == 1:
                to, j = g, i ^ (2 * layout.last_offset)
            else:
                to, j = g ^ 1, i
                if to >= groups:
                    to = g
            moves.append((g * layout.width + i, to * layout.width + j))
    return moves


def odd_moves(layout, groups):
    moves = []
    for g in range(groups):
        to = g + 1 if g % 2 == 1 else g - 1
        for i in range(layout.width):
            if 0 <= to < groups:
                moves.append((g * layout.width + i, to * layout.width + i))
            else:
                moves.append((g * layout.width + i, g * layout.width + (i ^ 1)))
    return moves


def per_device(stored_tiles, tile_flags, orbitals):
    group_width = lax.axis_size("dev")
    groups = lax.axis_size("grp")
    layout = Layout(group_width)
    order, columns = orbitals.shape
    block = jax.ShapeDtypeStruct((order, columns), F32)
    two = jax.ShapeDtypeStruct((2, order, columns), F32)
    partners = [(i, i ^ 1) for i in range(group_width)]
    semaphore = pltpu.SemaphoreType.DMA

    taken = lax.ppermute(stored_tiles, "dev", partners)[0]
    taken_orbitals = lax.ppermute(orbitals, "dev", partners)
    taken_flags = lax.ppermute(tile_flags, "dev", partners)
    tiles, held, shares = call(
        functools.partial(load_kernel, layout),
        [
            jax.ShapeDtypeStruct(stored_tiles.shape[1:], F32),
            block,
            jax.ShapeDtypeStruct((layout.rounds, 2 * order, columns), F32),
        ],
        [
            pltpu.with_memory_space_constraint(operand, pltpu.HBM)
            for operand in (tile_flags, stored_tiles[0], orbitals)
        ],
        [HBM] * 3,
        [pltpu.SMEM(tile_flags.shape, jnp.int32), semaphore((3,))],
        flops=10**9,
    )
    mask = call(
        functools.partial(mask_kernel, layout),
        jax.ShapeDtypeStruct((group_width + 1, order), F32),
        [taken_flags],
        flops=10**9,
    )

    *full, made = call(
        functools.partial(send_full_kernel, layout),
        [two] * (layout.rounds + 1),
        [tiles, taken, mask, held, taken_orbitals, shares],
    )
    full_arrived = []
    for r in range(layout.rounds):
        swaps = [
            (i, i ^ (2 * layout.offset(r, i % 2))) for i in range(group_width)
        ]
        full_arrived.append(lax.ppermute(full[r], "dev", swaps))

    last = call(
        functools.partial(send_last_kernel, layout),
        two,
        [tiles, taken, mask, held, taken_orbitals, made],
    )
    last_arrived = lax.ppermute(last, ("grp", "dev"), last_moves(layout, groups))

    odd = call(functools.partial(send_odd_kernel, layout), block, [tiles, held])
    odd_arrived = lax.ppermute(odd, ("grp", "dev"), odd_moves(layout, groups))

    mine, others = call(
        functools.partial(near_kernel, layout),
        [block, block],
        [tiles, held, taken_orbitals],
    )
    others = call(
        functools.partial(full_kernel, layout),
        block,
        [taken, mask, others, *full_arrived],
    )
    others = call(
        functools.partial(back_kernel, layout),
        block,
        [taken, mask, others, last_arrived],
    )
    returned = lax.ppermute(others, "dev", partners)
    mine = call(
        functools.partial(mine_kernel, layout),
        block,
        [tiles, mine, last_arrived, odd_arrived, *full_arrived],
    )
    return mine + returned


def solution(mesh):
    in_specs = (
        P(("grp", "dev"), None, None, None),
        P(("grp", "dev"), None),
        P(("grp", "dev"), None),
    )
    out_specs = P(("grp", "dev"), None)
    return jax.shard_map(
        per_device, mesh=mesh, in_specs=in_specs, out_specs=out_specs, check_vma=False
    )
```

```python
import functools

import jax
import jax.numpy as jnp
from jax import lax
from jax.experimental import pallas as pl
from jax.experimental.pallas import tpu as pltpu
from jax.sharding import PartitionSpec as P

HBM = pl.BlockSpec(memory_space=pltpu.HBM)
VMEM = pl.BlockSpec(memory_space=pltpu.VMEM)
F32 = jnp.float32


def parted(value):
    high = value.astype(jnp.bfloat16)
    return high, (value - high.astype(F32)).astype(jnp.bfloat16)


def times(left, right):
    left_high, left_low = parted(left)
    right_high, right_low = parted(right)
    dot = functools.partial(jnp.dot, preferred_element_type=F32)
    rows = left.shape[0]
    both = dot(jnp.concatenate([left_high, left_low], axis=0), right_high)
    return both[:rows] + both[rows:] + dot(left_high, right_low)


def transposed_times(left, right):
    return times(left.T, right)


class Layout:
    def __init__(self, group_width):
        self.width = group_width
        self.pairs = group_width // 2
        self.rounds = (self.pairs - 1) // 2
        self.last_offset = 1

    def offset(self, round_index, side):
        if round_index == 0:
            return 3 - side
        return 2 * round_index + 2 + side


def place():
    index = lax.axis_index("dev")
    return index, index // 2, index % 2


def load_kernel(layout, flags_in, tiles_in, orbitals_in, tiles, orbitals, flags, sems):
    copies = [
        pltpu.make_async_copy(flags_in, flags, sems.at[0]),
        pltpu.make_async_copy(tiles_in, tiles, sems.at[1]),
        pltpu.make_async_copy(orbitals_in, orbitals, sems.at[2]),
    ]
    for copy in copies:
        copy.start()
    for copy in copies:
        copy.wait()
    for slot in range(layout.width + 1):
        tiles[slot] = tiles[slot] * flags[0, slot].astype(F32)


def mask_kernel(layout, flags, mask):
    row = flags[...].astype(F32)
    for slot in range(layout.width + 1):
        mask[slot : slot + 1] = jnp.broadcast_to(
            row[:, slot : slot + 1], (1, mask.shape[1])
        )


def taken_tile(taken, mask, slot):
    return taken[slot] * mask[pl.ds(slot, 1), :]


def pair_terms(far, tiles, taken, mask, own, other, out):
    lefts = []
    for k in range(2):
        slot = 2 * far + k
        stack = jnp.concatenate([tiles[slot], taken_tile(taken, mask, slot)], axis=0)
        lefts.append(stack.T)
    terms = times(
        jnp.concatenate(lefts, axis=0), jnp.concatenate([own, other], axis=0)
    )
    order = own.shape[0]
    out[0] = terms[:order]
    out[1] = terms[order:]


def send_full_kernel(layout, tiles, taken, mask, orbitals, taken_orbitals, *outs):
    index, pair, side = place()
    own, other = orbitals[...], taken_orbitals[...]
    for r in range(layout.rounds):
        far = pair ^ layout.offset(r, side)
        out = outs[r]

        @pl.when(far > pair)
        def _():
            pair_terms(far, tiles, taken, mask, own, other, out)

        @pl.when(far < pair)
        def _():
            out[0] = jnp.where(side == 0, own, other)
            out[1] = jnp.where(side == 0, other, own)


def send_last_kernel(layout, tiles, taken, mask, orbitals, taken_orbitals, out):
    index, pair, side = place()
    own, other = orbitals[...], taken_orbitals[...]
    far = pair ^ layout.last_offset
    lower = lax.axis_index("grp") % 2 == 0

    @pl.when((side == 1) & (far > pair))
    def _():
        pair_terms(far, tiles, taken, mask, own, other, out)

    @pl.when((side == 1) & (far < pair))
    def _():
        out[0] = other
        out[1] = own

    @pl.when((side == 0) & lower)
    def _():
        out[0] = transposed_times(tiles[layout.width], own)
        out[1] = transposed_times(taken_tile(taken, mask, layout.width), other)

    @pl.when((side == 0) & jnp.logical_not(lower))
    def _():
        out[0] = own
        out[1] = other


def send_odd_kernel(layout, tiles, orbitals, out):
    lower = lax.axis_index("grp") % 2 == 1

    @pl.when(lower)
    def _():
        out[...] = transposed_times(tiles[layout.width], orbitals[...])

    @pl.when(jnp.logical_not(lower))
    def _():
        out[...] = orbitals[...]


def near_kernel(layout, tiles, orbitals, taken_orbitals, mine, others):
    index, pair, side = place()
    own, other = orbitals[...], taken_orbitals[...]
    beside = tiles[index ^ 1]
    row = jnp.concatenate([tiles[index], beside], axis=1)
    mine[...] = times(row, jnp.concatenate([own, other], axis=0))
    others[...] = transposed_times(beside, own)


def take_full(layout, arrived, row, tile_of, total):
    index, pair, side = place()
    for r, came in enumerate(arrived):
        far = pair ^ layout.offset(r, side)

        @pl.when(far > pair)
        def _():
            left = jnp.concatenate([tile_of(2 * far), tile_of(2 * far + 1)], axis=1)
            right = jnp.concatenate([came[0], came[1]], axis=0)
            total[...] += times(left, right)

        @pl.when(far < pair)
        def _():
            total[...] += came[side ^ row]


def full_kernel(layout, taken, mask, others_in, *refs):
    arrived, others = refs[:-1], refs[-1]
    others[...] = others_in[...]
    take_full(layout, arrived, 1, lambda slot: taken_tile(taken, mask, slot), others)


def back_kernel(layout, taken, mask, others_in, came, others):
    index, pair, side = place()
    far = pair ^ layout.last_offset
    lower = lax.axis_index("grp") % 2 == 0

    @pl.when((side == 1) & (far > pair))
    def _():
        left = jnp.concatenate(
            [taken_tile(taken, mask, 2 * far + k) for k in range(2)], axis=1
        )
        right = jnp.concatenate([came[0], came[1]], axis=0)
        others[...] = others_in[...] + times(left, right)

    @pl.when((side == 1) & (far < pair))
    def _():
        others[...] = others_in[...] + came[0]

    @pl.when((side == 0) & lower)
    def _():
        left = taken_tile(taken, mask, layout.width)
        others[...] = others_in[...] + times(left, came[1])

    @pl.when((side == 0) & jnp.logical_not(lower))
    def _():
        others[...] = others_in[...] + came[1]


def mine_kernel(layout, tiles, mine_in, came, odd_in, *refs):
    arrived, mine = refs[:-1], refs[-1]
    index, pair, side = place()
    far = pair ^ layout.last_offset
    group = lax.axis_index("grp")
    lower = group % 2 == 0

    @pl.when((side == 1) & (far > pair))
    def _():
        left = jnp.concatenate([tiles[2 * far], tiles[2 * far + 1]], axis=1)
        right = jnp.concatenate([came[0], came[1]], axis=0)
        mine[...] = mine_in[...] + times(left, right)

    @pl.when((side == 1) & (far < pair))
    def _():
        mine[...] = mine_in[...] + came[1]

    @pl.when((side == 0) & lower)
    def _():
        mine[...] = mine_in[...] + times(tiles[layout.width], came[0])

    @pl.when((side == 0) & jnp.logical_not(lower))
    def _():
        mine[...] = mine_in[...] + came[0]

    @pl.when(lower)
    def _():
        mine[...] += jnp.where(group > 0, odd_in[...], 0.0)

    @pl.when(jnp.logical_not(lower))
    def _():
        mine[...] += times(tiles[layout.width], odd_in[...])

    take_full(layout, arrived, 0, lambda slot: tiles[slot], mine)


def call(body, outs, operands, specs=None, scratch=(), flops=0):
    return pl.pallas_call(
        body,
        out_shape=outs,
        in_specs=specs or [VMEM] * len(operands),
        out_specs=jax.tree.map(lambda _: VMEM, outs),
        scratch_shapes=scratch,
        cost_estimate=pl.CostEstimate(
            flops=flops, bytes_accessed=0, transcendentals=0
        ),
        compiler_params=pltpu.CompilerParams(vmem_limit_bytes=32 * 1024 * 1024),
    )(*operands)


def last_moves(layout, groups):
    moves = []
    for g in range(groups):
        for i in range(layout.width):
            if i % 2 == 1:
                to, j = g, i ^ (2 * layout.last_offset)
            else:
                to, j = g ^ 1, i
                if to >= groups:
                    to = g
            moves.append((g * layout.width + i, to * layout.width + j))
    return moves


def odd_moves(layout, groups):
    moves = []
    for g in range(groups):
        to = g + 1 if g % 2 == 1 else g - 1
        for i in range(layout.width):
            if 0 <= to < groups:
                moves.append((g * layout.width + i, to * layout.width + i))
            else:
                moves.append((g * layout.width + i, g * layout.width + (i ^ 1)))
    return moves


def per_device(stored_tiles, tile_flags, orbitals):
    group_width = lax.axis_size("dev")
    groups = lax.axis_size("grp")
    layout = Layout(group_width)
    order, columns = orbitals.shape
    block = jax.ShapeDtypeStruct((order, columns), F32)
    two = jax.ShapeDtypeStruct((2, order, columns), F32)
    partners = [(i, i ^ 1) for i in range(group_width)]
    semaphore = pltpu.SemaphoreType.DMA

    taken = lax.ppermute(stored_tiles, "dev", partners)[0]
    taken_orbitals = lax.ppermute(orbitals, "dev", partners)
    taken_flags = lax.ppermute(tile_flags, "dev", partners)
    tiles, held = call(
        functools.partial(load_kernel, layout),
        [jax.ShapeDtypeStruct(stored_tiles.shape[1:], F32), block],
        [
            pltpu.with_memory_space_constraint(operand, pltpu.HBM)
            for operand in (tile_flags, stored_tiles[0], orbitals)
        ],
        [HBM] * 3,
        [pltpu.SMEM(tile_flags.shape, jnp.int32), semaphore((3,))],
        flops=10**9,
    )
    mask = call(
        functools.partial(mask_kernel, layout),
        jax.ShapeDtypeStruct((group_width + 1, order), F32),
        [taken_flags],
        flops=10**9,
    )

    full = call(
        functools.partial(send_full_kernel, layout),
        [two] * layout.rounds,
        [tiles, taken, mask, held, taken_orbitals],
    )
    full_arrived = []
    for r in range(layout.rounds):
        swaps = [
            (i, i ^ (2 * layout.offset(r, i % 2))) for i in range(group_width)
        ]
        full_arrived.append(lax.ppermute(full[r], "dev", swaps))

    last = call(
        functools.partial(send_last_kernel, layout),
        two,
        [tiles, taken, mask, held, taken_orbitals],
    )
    last_arrived = lax.ppermute(last, ("grp", "dev"), last_moves(layout, groups))

    odd = call(functools.partial(send_odd_kernel, layout), block, [tiles, held])
    odd_arrived = lax.ppermute(odd, ("grp", "dev"), odd_moves(layout, groups))

    mine, others = call(
        functools.partial(near_kernel, layout),
        [block, block],
        [tiles, held, taken_orbitals],
    )
    others = call(
        functools.partial(full_kernel, layout),
        block,
        [taken, mask, others, *full_arrived],
    )
    others = call(
        functools.partial(back_kernel, layout),
        block,
        [taken, mask, others, last_arrived],
    )
    returned = lax.ppermute(others, "dev", partners)
    mine = call(
        functools.partial(mine_kernel, layout),
        block,
        [tiles, mine, last_arrived, odd_arrived, *full_arrived],
    )
    return mine + returned


def solution(mesh):
    in_specs = (
        P(("grp", "dev"), None, None, None),
        P(("grp", "dev"), None),
        P(("grp", "dev"), None),
    )
    out_specs = P(("grp", "dev"), None)
    return jax.shard_map(
        per_device, mesh=mesh, in_specs=in_specs, out_specs=out_specs, check_vma=False
    )
```

```python
import functools

import jax
import jax.numpy as jnp
from jax import lax
from jax.experimental import pallas as pl
from jax.experimental.pallas import tpu as pltpu
from jax.sharding import PartitionSpec as P

HBM = pl.BlockSpec(memory_space=pltpu.HBM)
VMEM = pl.BlockSpec(memory_space=pltpu.VMEM)
F32 = jnp.float32


def parted(value):
    high = value.astype(jnp.bfloat16)
    return high, (value - high.astype(F32)).astype(jnp.bfloat16)


def times(left, right):
    left_high, left_low = parted(left)
    right_high, right_low = parted(right)
    dot = functools.partial(jnp.dot, preferred_element_type=F32)
    rows = left.shape[0]
    both = dot(jnp.concatenate([left_high, left_low], axis=0), right_high)
    return both[:rows] + both[rows:] + dot(left_high, right_low)


def prepared_times(stack, right):
    rows = stack.shape[0] // 2
    right_high, right_low = parted(right)
    dot = functools.partial(jnp.dot, preferred_element_type=F32)
    both = dot(stack[...], right_high)
    return both[:rows] + both[rows:] + dot(stack[:rows], right_low)


def transposed_times(left, right):
    return times(left.T, right)


class Layout:
    def __init__(self, group_width):
        self.width = group_width
        self.pairs = group_width // 2
        self.rounds = (self.pairs - 1) // 2
        self.last_offset = 2

    def offset(self, round_index, side):
        if round_index == 0:
            return 1 + 2 * side
        return 2 * round_index + 2 + side


def place():
    index = lax.axis_index("dev")
    return index, index // 2, index % 2


def load_kernel(layout, flags_in, tiles_in, orbitals_in, tiles, orbitals, flags, sems):
    copies = [
        pltpu.make_async_copy(flags_in, flags, sems.at[0]),
        pltpu.make_async_copy(tiles_in, tiles, sems.at[1]),
        pltpu.make_async_copy(orbitals_in, orbitals, sems.at[2]),
    ]
    for copy in copies:
        copy.start()
    for copy in copies:
        copy.wait()
    for slot in range(layout.width + 1):
        tiles[slot] = tiles[slot] * flags[0, slot].astype(F32)


def mask_kernel(layout, flags, mask):
    row = flags[...].astype(F32)
    for slot in range(layout.width + 1):
        mask[slot : slot + 1] = jnp.broadcast_to(
            row[:, slot : slot + 1], (1, mask.shape[1])
        )


def taken_tile(taken, mask, slot):
    return taken[slot] * mask[pl.ds(slot, 1), :]


def pair_terms(far, tiles, taken, mask, own, other, out):
    lefts = []
    for k in range(2):
        slot = 2 * far + k
        stack = jnp.concatenate([tiles[slot], taken_tile(taken, mask, slot)], axis=0)
        lefts.append(stack.T)
    terms = times(
        jnp.concatenate(lefts, axis=0), jnp.concatenate([own, other], axis=0)
    )
    order = own.shape[0]
    out[0] = terms[:order]
    out[1] = terms[order:]


def send_full_kernel(layout, tiles, taken, mask, orbitals, taken_orbitals, *outs):
    index, pair, side = place()
    own, other = orbitals[...], taken_orbitals[...]
    for r in range(layout.rounds):
        far = pair ^ layout.offset(r, side)
        out = outs[r]

        @pl.when(far > pair)
        def _():
            pair_terms(far, tiles, taken, mask, own, other, out)

        @pl.when(far < pair)
        def _():
            out[0] = jnp.where(side == 0, own, other)
            out[1] = jnp.where(side == 0, other, own)

    far = pair ^ layout.last_offset

    @pl.when((side == 1) & (pair == 0))
    def _():
        pair_terms(far, tiles, taken, mask, own, other, outs[-1])


def send_last_kernel(layout, tiles, taken, mask, orbitals, taken_orbitals, made, out):
    index, pair, side = place()
    own, other = orbitals[...], taken_orbitals[...]
    far = pair ^ layout.last_offset
    lower = lax.axis_index("grp") % 2 == 0

    @pl.when((side == 1) & (pair == 0))
    def _():
        out[...] = made[...]

    @pl.when((side == 1) & (far > pair) & (pair > 0))
    def _():
        pair_terms(far, tiles, taken, mask, own, other, out)

    @pl.when((side == 1) & (far < pair))
    def _():
        out[0] = other
        out[1] = own

    @pl.when((side == 0) & lower)
    def _():
        out[0] = transposed_times(tiles[layout.width], own)
        out[1] = transposed_times(taken_tile(taken, mask, layout.width), other)

    @pl.when((side == 0) & jnp.logical_not(lower))
    def _():
        out[0] = own
        out[1] = other


def send_odd_kernel(layout, tiles, orbitals, out):
    lower = lax.axis_index("grp") % 2 == 1

    @pl.when(lower)
    def _():
        out[...] = transposed_times(tiles[layout.width], orbitals[...])

    @pl.when(jnp.logical_not(lower))
    def _():
        out[...] = orbitals[...]


def near_kernel(layout, tiles, orbitals, taken_orbitals, mine, others):
    index, pair, side = place()
    own, other = orbitals[...], taken_orbitals[...]
    beside = tiles[index ^ 1]
    row = jnp.concatenate([tiles[index], beside], axis=1)
    mine[...] = times(row, jnp.concatenate([own, other], axis=0))
    others[...] = transposed_times(beside, own)


def take_full(layout, arrived, row, tile_of, total):
    index, pair, side = place()
    for r, came in enumerate(arrived):
        far = pair ^ layout.offset(r, side)

        @pl.when(far > pair)
        def _():
            left = jnp.concatenate([tile_of(2 * far), tile_of(2 * far + 1)], axis=1)
            right = jnp.concatenate([came[0], came[1]], axis=0)
            total[...] += times(left, right)

        @pl.when(far < pair)
        def _():
            total[...] += came[side ^ row]


def prepare_kernel(layout, taken, mask, *outs):
    index, pair, side = place()

    def put(out, left):
        out[...] = jnp.concatenate(parted(left), axis=0)

    def pair_row(far):
        return jnp.concatenate(
            [taken_tile(taken, mask, 2 * far + k) for k in range(2)], axis=1
        )

    for r in range(layout.rounds):
        put(outs[r], pair_row(pair ^ layout.offset(r, side)))

    @pl.when(side == 1)
    def _():
        put(outs[-1], pair_row(pair ^ layout.last_offset))

    @pl.when(side == 0)
    def _():
        tile = taken_tile(taken, mask, layout.width)
        put(outs[-1], jnp.concatenate([tile, jnp.zeros_like(tile)], axis=1))


def full_kernel(layout, others_in, *refs):
    index, pair, side = place()
    count = layout.rounds
    stacks, arrived, others = refs[:count], refs[count:-1], refs[-1]
    for r in range(count):
        far = pair ^ layout.offset(r, side)
        stack, came = stacks[r], arrived[r]
        so_far = others_in if r == 0 else others

        @pl.when(far > pair)
        def _():
            right = jnp.concatenate([came[0], came[1]], axis=0)
            others[...] = so_far[...] + prepared_times(stack, right)

        @pl.when(far < pair)
        def _():
            others[...] = so_far[...] + came[1 - side]


def back_kernel(layout, stack, others_in, came, others):
    index, pair, side = place()
    far = pair ^ layout.last_offset
    lower = lax.axis_index("grp") % 2 == 0
    gives = jnp.where(side == 1, far > pair, lower)

    @pl.when(gives)
    def _():
        right = jnp.concatenate([came[1 - side], came[side]], axis=0)
        others[...] = others_in[...] + prepared_times(stack, right)

    @pl.when(jnp.logical_not(gives))
    def _():
        others[...] = others_in[...] + came[1 - side]


def mine_kernel(layout, tiles, mine_in, came, odd_in, *refs):
    arrived, mine = refs[:-1], refs[-1]
    index, pair, side = place()
    far = pair ^ layout.last_offset
    group = lax.axis_index("grp")
    lower = group % 2 == 0

    @pl.when((side == 1) & (far > pair))
    def _():
        left = jnp.concatenate([tiles[2 * far], tiles[2 * far + 1]], axis=1)
        right = jnp.concatenate([came[0], came[1]], axis=0)
        mine[...] = mine_in[...] + times(left, right)

    @pl.when((side == 1) & (far < pair))
    def _():
        mine[...] = mine_in[...] + came[1]

    @pl.when((side == 0) & lower)
    def _():
        mine[...] = mine_in[...] + times(tiles[layout.width], came[0])

    @pl.when((side == 0) & jnp.logical_not(lower))
    def _():
        mine[...] = mine_in[...] + came[0]

    @pl.when(lower)
    def _():
        mine[...] += jnp.where(group > 0, odd_in[...], 0.0)

    @pl.when(jnp.logical_not(lower))
    def _():
        mine[...] += times(tiles[layout.width], odd_in[...])

    take_full(layout, arrived, 0, lambda slot: tiles[slot], mine)


def call(body, outs, operands, specs=None, scratch=(), flops=0):
    return pl.pallas_call(
        body,
        out_shape=outs,
        in_specs=specs or [VMEM] * len(operands),
        out_specs=jax.tree.map(lambda _: VMEM, outs),
        scratch_shapes=scratch,
        cost_estimate=pl.CostEstimate(
            flops=flops, bytes_accessed=0, transcendentals=0
        ),
        compiler_params=pltpu.CompilerParams(vmem_limit_bytes=32 * 1024 * 1024),
    )(*operands)


def last_moves(layout, groups):
    moves = []
    for g in range(groups):
        for i in range(layout.width):
            if i % 2 == 1:
                to, j = g, i ^ (2 * layout.last_offset)
            else:
                to, j = g ^ 1, i
                if to >= groups:
                    to = g
            moves.append((g * layout.width + i, to * layout.width + j))
    return moves


def odd_moves(layout, groups):
    moves = []
    for g in range(groups):
        to = g + 1 if g % 2 == 1 else g - 1
        for i in range(layout.width):
            if 0 <= to < groups:
                moves.append((g * layout.width + i, to * layout.width + i))
            else:
                moves.append((g * layout.width + i, g * layout.width + (i ^ 1)))
    return moves


def per_device(stored_tiles, tile_flags, orbitals):
    group_width = lax.axis_size("dev")
    groups = lax.axis_size("grp")
    layout = Layout(group_width)
    order, columns = orbitals.shape
    block = jax.ShapeDtypeStruct((order, columns), F32)
    two = jax.ShapeDtypeStruct((2, order, columns), F32)
    partners = [(i, i ^ 1) for i in range(group_width)]
    semaphore = pltpu.SemaphoreType.DMA

    taken = lax.ppermute(stored_tiles, "dev", partners)[0]
    taken_orbitals = lax.ppermute(orbitals, "dev", partners)
    taken_flags = lax.ppermute(tile_flags, "dev", partners)
    tiles, held = call(
        functools.partial(load_kernel, layout),
        [jax.ShapeDtypeStruct(stored_tiles.shape[1:], F32), block],
        [
            pltpu.with_memory_space_constraint(operand, pltpu.HBM)
            for operand in (tile_flags, stored_tiles[0], orbitals)
        ],
        [HBM] * 3,
        [pltpu.SMEM(tile_flags.shape, jnp.int32), semaphore((3,))],
        flops=10**9,
    )
    mask = call(
        functools.partial(mask_kernel, layout),
        jax.ShapeDtypeStruct((group_width + 1, order), F32),
        [taken_flags],
        flops=10**9,
    )

    *full, made = call(
        functools.partial(send_full_kernel, layout),
        [two] * (layout.rounds + 1),
        [tiles, taken, mask, held, taken_orbitals],
    )
    full_arrived = []
    for r in range(layout.rounds):
        swaps = [
            (i, i ^ (2 * layout.offset(r, i % 2))) for i in range(group_width)
        ]
        full_arrived.append(lax.ppermute(full[r], "dev", swaps))

    last = call(
        functools.partial(send_last_kernel, layout),
        two,
        [tiles, taken, mask, held, taken_orbitals, made],
    )
    last_arrived = lax.ppermute(last, ("grp", "dev"), last_moves(layout, groups))

    odd = call(functools.partial(send_odd_kernel, layout), block, [tiles, held])
    odd_arrived = lax.ppermute(odd, ("grp", "dev"), odd_moves(layout, groups))

    mine, others = call(
        functools.partial(near_kernel, layout),
        [block, block],
        [tiles, held, taken_orbitals],
    )
    stack = jax.ShapeDtypeStruct((2 * order, 2 * order), jnp.bfloat16)
    *full_stacks, last_stack = call(
        functools.partial(prepare_kernel, layout),
        [stack] * (layout.rounds + 1),
        [taken, mask],
    )
    others = call(
        functools.partial(full_kernel, layout),
        block,
        [others, *full_stacks, *full_arrived],
    )
    others = call(
        functools.partial(back_kernel, layout),
        block,
        [last_stack, others, last_arrived],
    )
    returned = lax.ppermute(others, "dev", partners)
    mine = call(
        functools.partial(mine_kernel, layout),
        block,
        [tiles, mine, last_arrived, odd_arrived, *full_arrived],
    )
    return mine + returned


def solution(mesh):
    in_specs = (
        P(("grp", "dev"), None, None, None),
        P(("grp", "dev"), None),
        P(("grp", "dev"), None),
    )
    out_specs = P(("grp", "dev"), None)
    return jax.shard_map(
        per_device, mesh=mesh, in_specs=in_specs, out_specs=out_specs, check_vma=False
    )
```

```python
import functools

import jax
import jax.numpy as jnp
from jax import lax
from jax.experimental import pallas as pl
from jax.experimental.pallas import tpu as pltpu
from jax.sharding import PartitionSpec as P

HBM = pl.BlockSpec(memory_space=pltpu.HBM)
VMEM = pl.BlockSpec(memory_space=pltpu.VMEM)
F32 = jnp.float32


def parted(value):
    high = value.astype(jnp.bfloat16)
    return high, (value - high.astype(F32)).astype(jnp.bfloat16)


def times(left, right):
    left_high, left_low = parted(left)
    right_high, right_low = parted(right)
    dot = functools.partial(jnp.dot, preferred_element_type=F32)
    rows = left.shape[0]
    both = dot(jnp.concatenate([left_high, left_low], axis=0), right_high)
    return both[:rows] + both[rows:] + dot(left_high, right_low)


def transposed_times(left, right):
    return times(left.T, right)


class Layout:
    def __init__(self, group_width):
        self.width = group_width
        self.pairs = group_width // 2
        self.rounds = (self.pairs - 1) // 2
        self.last_offset = 2

    def offset(self, round_index, side):
        if round_index == 0:
            return 1 + 2 * side
        return 2 * round_index + 2 + side


def place():
    index = lax.axis_index("dev")
    return index, index // 2, index % 2


def load_kernel(layout, flags_in, tiles_in, orbitals_in, tiles, orbitals, flags, sems):
    copies = [
        pltpu.make_async_copy(flags_in, flags, sems.at[0]),
        pltpu.make_async_copy(tiles_in, tiles, sems.at[1]),
        pltpu.make_async_copy(orbitals_in, orbitals, sems.at[2]),
    ]
    for copy in copies:
        copy.start()
    for copy in copies:
        copy.wait()
    for slot in range(layout.width + 1):
        tiles[slot] = tiles[slot] * flags[0, slot].astype(F32)


def mask_kernel(layout, flags, mask):
    row = flags[...].astype(F32)
    for slot in range(layout.width + 1):
        mask[slot : slot + 1] = jnp.broadcast_to(
            row[:, slot : slot + 1], (1, mask.shape[1])
        )


def taken_tile(taken, mask, slot):
    return taken[slot] * mask[pl.ds(slot, 1), :]


def pair_terms(far, tiles, taken, mask, own, other, out):
    lefts = []
    for k in range(2):
        slot = 2 * far + k
        stack = jnp.concatenate([tiles[slot], taken_tile(taken, mask, slot)], axis=0)
        lefts.append(stack.T)
    terms = times(
        jnp.concatenate(lefts, axis=0), jnp.concatenate([own, other], axis=0)
    )
    order = own.shape[0]
    out[0] = terms[:order]
    out[1] = terms[order:]


def send_full_kernel(layout, tiles, taken, mask, orbitals, taken_orbitals, *outs):
    index, pair, side = place()
    own, other = orbitals[...], taken_orbitals[...]
    for r in range(layout.rounds):
        far = pair ^ layout.offset(r, side)
        out = outs[r]

        @pl.when(far > pair)
        def _():
            pair_terms(far, tiles, taken, mask, own, other, out)

        @pl.when(far < pair)
        def _():
            out[0] = jnp.where(side == 0, own, other)
            out[1] = jnp.where(side == 0, other, own)

    far = pair ^ layout.last_offset

    made, odd = outs[-2], outs[-1]

    @pl.when((side == 1) & (pair == 0))
    def _():
        pair_terms(far, tiles, taken, mask, own, other, made)

    lower = lax.axis_index("grp") % 2 == 0

    @pl.when((side == 0) & lower)
    def _():
        made[0] = transposed_times(tiles[layout.width], own)
        made[1] = transposed_times(taken_tile(taken, mask, layout.width), other)

    @pl.when((side == 0) & jnp.logical_not(lower))
    def _():
        made[0] = own
        made[1] = other
        odd[...] = transposed_times(tiles[layout.width], own)


def send_last_kernel(layout, tiles, taken, mask, orbitals, taken_orbitals, made, out):
    index, pair, side = place()
    own, other = orbitals[...], taken_orbitals[...]
    far = pair ^ layout.last_offset
    ready = (side == 0) | (pair == 0)

    @pl.when(ready)
    def _():
        out[...] = made[...]

    @pl.when(jnp.logical_not(ready) & (far > pair))
    def _():
        pair_terms(far, tiles, taken, mask, own, other, out)

    @pl.when(jnp.logical_not(ready) & (far < pair))
    def _():
        out[0] = other
        out[1] = own


def send_odd_kernel(layout, tiles, orbitals, made, out):
    side = lax.axis_index("dev") % 2
    lower = lax.axis_index("grp") % 2 == 1

    @pl.when(lower & (side == 0))
    def _():
        out[...] = made[...]

    @pl.when(lower & (side == 1))
    def _():
        out[...] = transposed_times(tiles[layout.width], orbitals[...])

    @pl.when(jnp.logical_not(lower))
    def _():
        out[...] = orbitals[...]


def near_kernel(layout, tiles, orbitals, taken_orbitals, mine, others):
    index, pair, side = place()
    own, other = orbitals[...], taken_orbitals[...]
    beside = tiles[index ^ 1]
    row = jnp.concatenate([tiles[index], beside], axis=1)
    mine[...] = times(row, jnp.concatenate([own, other], axis=0))
    others[...] = transposed_times(beside, own)


def take_full(layout, arrived, row, tile_of, total):
    index, pair, side = place()
    for r, came in enumerate(arrived):
        far = pair ^ layout.offset(r, side)

        @pl.when(far > pair)
        def _():
            left = jnp.concatenate([tile_of(2 * far), tile_of(2 * far + 1)], axis=1)
            right = jnp.concatenate([came[0], came[1]], axis=0)
            total[...] += times(left, right)

        @pl.when(far < pair)
        def _():
            total[...] += came[side ^ row]


def full_kernel(layout, taken, mask, others_in, *refs):
    arrived, others = refs[:-1], refs[-1]
    others[...] = others_in[...]
    take_full(layout, arrived, 1, lambda slot: taken_tile(taken, mask, slot), others)


def back_kernel(layout, taken, mask, others_in, came, others):
    index, pair, side = place()
    far = pair ^ layout.last_offset
    lower = lax.axis_index("grp") % 2 == 0

    @pl.when((side == 1) & (far > pair))
    def _():
        left = jnp.concatenate(
            [taken_tile(taken, mask, 2 * far + k) for k in range(2)], axis=1
        )
        right = jnp.concatenate([came[0], came[1]], axis=0)
        others[...] = others_in[...] + times(left, right)

    @pl.when((side == 1) & (far < pair))
    def _():
        others[...] = others_in[...] + came[0]

    @pl.when((side == 0) & lower)
    def _():
        left = taken_tile(taken, mask, layout.width)
        others[...] = others_in[...] + times(left, came[1])

    @pl.when((side == 0) & jnp.logical_not(lower))
    def _():
        others[...] = others_in[...] + came[1]


def mine_kernel(layout, tiles, mine_in, came, odd_in, *refs):
    arrived, mine = refs[:-1], refs[-1]
    index, pair, side = place()
    far = pair ^ layout.last_offset
    group = lax.axis_index("grp")
    lower = group % 2 == 0

    @pl.when((side == 1) & (far > pair))
    def _():
        left = jnp.concatenate([tiles[2 * far], tiles[2 * far + 1]], axis=1)
        right = jnp.concatenate([came[0], came[1]], axis=0)
        mine[...] = mine_in[...] + times(left, right)

    @pl.when((side == 1) & (far < pair))
    def _():
        mine[...] = mine_in[...] + came[1]

    @pl.when((side == 0) & lower)
    def _():
        mine[...] = mine_in[...] + times(tiles[layout.width], came[0])

    @pl.when((side == 0) & jnp.logical_not(lower))
    def _():
        mine[...] = mine_in[...] + came[0]

    @pl.when(lower)
    def _():
        mine[...] += jnp.where(group > 0, odd_in[...], 0.0)

    @pl.when(jnp.logical_not(lower))
    def _():
        mine[...] += times(tiles[layout.width], odd_in[...])

    take_full(layout, arrived, 0, lambda slot: tiles[slot], mine)


def call(body, outs, operands, specs=None, scratch=(), flops=0):
    return pl.pallas_call(
        body,
        out_shape=outs,
        in_specs=specs or [VMEM] * len(operands),
        out_specs=jax.tree.map(lambda _: VMEM, outs),
        scratch_shapes=scratch,
        cost_estimate=pl.CostEstimate(
            flops=flops, bytes_accessed=0, transcendentals=0
        ),
        compiler_params=pltpu.CompilerParams(vmem_limit_bytes=32 * 1024 * 1024),
    )(*operands)


def last_moves(layout, groups):
    moves = []
    for g in range(groups):
        for i in range(layout.width):
            if i % 2 == 1:
                to, j = g, i ^ (2 * layout.last_offset)
            else:
                to, j = g ^ 1, i
                if to >= groups:
                    to = g
            moves.append((g * layout.width + i, to * layout.width + j))
    return moves


def odd_moves(layout, groups):
    moves = []
    for g in range(groups):
        to = g + 1 if g % 2 == 1 else g - 1
        for i in range(layout.width):
            if 0 <= to < groups:
                moves.append((g * layout.width + i, to * layout.width + i))
            else:
                moves.append((g * layout.width + i, g * layout.width + (i ^ 1)))
    return moves


def per_device(stored_tiles, tile_flags, orbitals):
    group_width = lax.axis_size("dev")
    groups = lax.axis_size("grp")
    layout = Layout(group_width)
    order, columns = orbitals.shape
    block = jax.ShapeDtypeStruct((order, columns), F32)
    two = jax.ShapeDtypeStruct((2, order, columns), F32)
    partners = [(i, i ^ 1) for i in range(group_width)]
    semaphore = pltpu.SemaphoreType.DMA

    taken = lax.ppermute(stored_tiles, "dev", partners)[0]
    taken_orbitals = lax.ppermute(orbitals, "dev", partners)
    taken_flags = lax.ppermute(tile_flags, "dev", partners)
    tiles, held = call(
        functools.partial(load_kernel, layout),
        [jax.ShapeDtypeStruct(stored_tiles.shape[1:], F32), block],
        [
            pltpu.with_memory_space_constraint(operand, pltpu.HBM)
            for operand in (tile_flags, stored_tiles[0], orbitals)
        ],
        [HBM] * 3,
        [pltpu.SMEM(tile_flags.shape, jnp.int32), semaphore((3,))],
        flops=10**9,
    )
    mask = call(
        functools.partial(mask_kernel, layout),
        jax.ShapeDtypeStruct((group_width + 1, order), F32),
        [taken_flags],
        flops=10**9,
    )

    *full, made, odd_made = call(
        functools.partial(send_full_kernel, layout),
        [two] * (layout.rounds + 1) + [block],
        [tiles, taken, mask, held, taken_orbitals],
    )
    full_arrived = []
    for r in range(layout.rounds):
        swaps = [
            (i, i ^ (2 * layout.offset(r, i % 2))) for i in range(group_width)
        ]
        full_arrived.append(lax.ppermute(full[r], "dev", swaps))

    last = call(
        functools.partial(send_last_kernel, layout),
        two,
        [tiles, taken, mask, held, taken_orbitals, made],
    )
    last_arrived = lax.ppermute(last, ("grp", "dev"), last_moves(layout, groups))

    odd = call(functools.partial(send_odd_kernel, layout), block, [tiles, held, odd_made])
    odd_arrived = lax.ppermute(odd, ("grp", "dev"), odd_moves(layout, groups))

    mine, others = call(
        functools.partial(near_kernel, layout),
        [block, block],
        [tiles, held, taken_orbitals],
    )
    others = call(
        functools.partial(full_kernel, layout),
        block,
        [taken, mask, others, *full_arrived],
    )
    others = call(
        functools.partial(back_kernel, layout),
        block,
        [taken, mask, others, last_arrived],
    )
    returned = lax.ppermute(others, "dev", partners)
    mine = call(
        functools.partial(mine_kernel, layout),
        block,
        [tiles, mine, last_arrived, odd_arrived, *full_arrived],
    )
    return mine + returned


def solution(mesh):
    in_specs = (
        P(("grp", "dev"), None, None, None),
        P(("grp", "dev"), None),
        P(("grp", "dev"), None),
    )
    out_specs = P(("grp", "dev"), None)
    return jax.shard_map(
        per_device, mesh=mesh, in_specs=in_specs, out_specs=out_specs, check_vma=False
    )
```

```python
import functools

import jax
import jax.numpy as jnp
from jax import lax
from jax.experimental import pallas as pl
from jax.experimental.pallas import tpu as pltpu
from jax.sharding import PartitionSpec as P

HBM = pl.BlockSpec(memory_space=pltpu.HBM)
VMEM = pl.BlockSpec(memory_space=pltpu.VMEM)
F32 = jnp.float32


def parted(value):
    high = value.astype(jnp.bfloat16)
    return high, (value - high.astype(F32)).astype(jnp.bfloat16)


def times(left, right):
    left_high, left_low = parted(left)
    right_high, right_low = parted(right)
    dot = functools.partial(jnp.dot, preferred_element_type=F32)
    rows = left.shape[0]
    both = dot(jnp.concatenate([left_high, left_low], axis=0), right_high)
    return both[:rows] + both[rows:] + dot(left_high, right_low)


def transposed_times(left, right):
    return times(left.T, right)


class Layout:
    def __init__(self, group_width, groups):
        self.width = group_width
        self.groups = groups
        self.pairs = group_width // 2
        self.rounds = (self.pairs - 1) // 2
        self.last_offset = 2

    def offset(self, round_index, side):
        if round_index == 0:
            return 1 + 2 * side
        return 2 * round_index + 2 + side


def late(layout):
    return lax.axis_index("grp") >= layout.groups // 2


def full_role(layout, r):
    index, pair, side = place()
    far = pair ^ layout.offset(r, side)
    return far, (side == 1) | jnp.logical_not(late(layout)) if r == 0 else side >= 0


def last_role(layout):
    index, pair, side = place()
    far = pair ^ jnp.where(side == 1, layout.last_offset, layout.offset(0, 0))
    return far, (side == 1) | late(layout)


def place():
    index = lax.axis_index("dev")
    return index, index // 2, index % 2


def load_kernel(layout, flags_in, tiles_in, orbitals_in, tiles, orbitals, flags, sems):
    copies = [
        pltpu.make_async_copy(flags_in, flags, sems.at[0]),
        pltpu.make_async_copy(tiles_in, tiles, sems.at[1]),
        pltpu.make_async_copy(orbitals_in, orbitals, sems.at[2]),
    ]
    for copy in copies:
        copy.start()
    for copy in copies:
        copy.wait()
    for slot in range(layout.width + 1):
        tiles[slot] = tiles[slot] * flags[0, slot].astype(F32)


def mask_kernel(layout, flags, mask):
    row = flags[...].astype(F32)
    for slot in range(layout.width + 1):
        mask[slot : slot + 1] = jnp.broadcast_to(
            row[:, slot : slot + 1], (1, mask.shape[1])
        )


def taken_tile(taken, mask, slot):
    return taken[slot] * mask[pl.ds(slot, 1), :]


def pair_terms(far, tiles, taken, mask, own, other, out):
    lefts = []
    for k in range(2):
        slot = 2 * far + k
        stack = jnp.concatenate([tiles[slot], taken_tile(taken, mask, slot)], axis=0)
        lefts.append(stack.T)
    terms = times(
        jnp.concatenate(lefts, axis=0), jnp.concatenate([own, other], axis=0)
    )
    order = own.shape[0]
    out[0] = terms[:order]
    out[1] = terms[order:]


def role_blocks(layout, role, tiles, taken, mask, own, other, out):
    index, pair, side = place()
    far, trades = role
    lower = lax.axis_index("grp") % 2 == 0

    @pl.when(trades & (far > pair))
    def _():
        pair_terms(far, tiles, taken, mask, own, other, out)

    @pl.when(jnp.logical_not(trades) & lower)
    def _():
        out[0] = transposed_times(tiles[layout.width], own)
        out[1] = transposed_times(taken_tile(taken, mask, layout.width), other)

    @pl.when(jnp.where(trades, far < pair, jnp.logical_not(lower)))
    def _():
        out[0] = jnp.where(side == 0, own, other)
        out[1] = jnp.where(side == 0, other, own)


def send_full_kernel(layout, tiles, taken, mask, orbitals, taken_orbitals, *outs):
    index, pair, side = place()
    own, other = orbitals[...], taken_orbitals[...]
    for r in range(layout.rounds):
        role = full_role(layout, r)
        role_blocks(layout, role, tiles, taken, mask, own, other, outs[r])

    @pl.when((side == 1) & (pair == 0))
    def _():
        far = pair ^ layout.last_offset
        pair_terms(far, tiles, taken, mask, own, other, outs[-1])


def send_last_kernel(layout, tiles, taken, mask, orbitals, taken_orbitals, made, out):
    index, pair, side = place()

    @pl.when((side == 1) & (pair == 0))
    def _():
        out[...] = made[...]

    @pl.when((side == 0) | (pair > 0))
    def _():
        own, other = orbitals[...], taken_orbitals[...]
        role_blocks(layout, last_role(layout), tiles, taken, mask, own, other, out)


def send_odd_kernel(layout, tiles, orbitals, out):
    lower = lax.axis_index("grp") % 2 == 1

    @pl.when(lower)
    def _():
        out[...] = transposed_times(tiles[layout.width], orbitals[...])

    @pl.when(jnp.logical_not(lower))
    def _():
        out[...] = orbitals[...]


def near_kernel(layout, tiles, orbitals, taken_orbitals, mine, others):
    index, pair, side = place()
    own, other = orbitals[...], taken_orbitals[...]
    beside = tiles[index ^ 1]
    row = jnp.concatenate([tiles[index], beside], axis=1)
    mine[...] = times(row, jnp.concatenate([own, other], axis=0))
    others[...] = transposed_times(beside, own)


def take(layout, role, came, row, tile_of, total):
    index, pair, side = place()
    far, trades = role
    lower = lax.axis_index("grp") % 2 == 0

    @pl.when(trades & (far > pair))
    def _():
        left = jnp.concatenate([tile_of(2 * far), tile_of(2 * far + 1)], axis=1)
        right = jnp.concatenate([came[0], came[1]], axis=0)
        total[...] += times(left, right)

    @pl.when(jnp.logical_not(trades) & lower)
    def _():
        total[...] += times(tile_of(layout.width), came[row])

    @pl.when(jnp.where(trades, far < pair, jnp.logical_not(lower)))
    def _():
        total[...] += came[side ^ row]


def full_kernel(layout, taken, mask, others_in, *refs):
    arrived, others = refs[:-1], refs[-1]
    others[...] = others_in[...]
    for r, came in enumerate(arrived):
        tile_of = functools.partial(taken_tile, taken, mask)
        take(layout, full_role(layout, r), came, 1, tile_of, others)


def back_kernel(layout, taken, mask, others_in, came, others):
    others[...] = others_in[...]
    tile_of = functools.partial(taken_tile, taken, mask)
    take(layout, last_role(layout), came, 1, tile_of, others)


def mine_kernel(layout, tiles, mine_in, last, odd_in, *refs):
    arrived, mine = refs[:-1], refs[-1]
    group = lax.axis_index("grp")

    @pl.when(group % 2 == 0)
    def _():
        mine[...] = mine_in[...] + jnp.where(group > 0, odd_in[...], 0.0)

    @pl.when(group % 2 == 1)
    def _():
        mine[...] = mine_in[...] + times(tiles[layout.width], odd_in[...])

    def tile_of(slot):
        return tiles[slot]

    take(layout, last_role(layout), last, 0, tile_of, mine)
    for r, came in enumerate(arrived):
        take(layout, full_role(layout, r), came, 0, tile_of, mine)


def call(body, outs, operands, specs=None, scratch=(), flops=0):
    return pl.pallas_call(
        body,
        out_shape=outs,
        in_specs=specs or [VMEM] * len(operands),
        out_specs=jax.tree.map(lambda _: VMEM, outs),
        scratch_shapes=scratch,
        cost_estimate=pl.CostEstimate(
            flops=flops, bytes_accessed=0, transcendentals=0
        ),
        compiler_params=pltpu.CompilerParams(vmem_limit_bytes=32 * 1024 * 1024),
    )(*operands)


def moves_of(layout, r):
    moves = []
    for g in range(layout.groups):
        upper_half = g >= layout.groups // 2
        for i in range(layout.width):
            side = i % 2
            if r is None:
                offset = layout.last_offset if side else layout.offset(0, 0)
                trades = side == 1 or upper_half
            else:
                offset = layout.offset(r, side)
                trades = side == 1 or r > 0 or not upper_half
            to, j = (g, i ^ (2 * offset)) if trades else (g ^ 1, i)
            moves.append((g * layout.width + i, to * layout.width + j))
    return moves


def odd_moves(layout, groups):
    moves = []
    for g in range(groups):
        to = g + 1 if g % 2 == 1 else g - 1
        for i in range(layout.width):
            if 0 <= to < groups:
                moves.append((g * layout.width + i, to * layout.width + i))
            else:
                moves.append((g * layout.width + i, g * layout.width + (i ^ 1)))
    return moves


def per_device(stored_tiles, tile_flags, orbitals):
    group_width = lax.axis_size("dev")
    groups = lax.axis_size("grp")
    layout = Layout(group_width, groups)
    order, columns = orbitals.shape
    block = jax.ShapeDtypeStruct((order, columns), F32)
    two = jax.ShapeDtypeStruct((2, order, columns), F32)
    partners = [(i, i ^ 1) for i in range(group_width)]
    semaphore = pltpu.SemaphoreType.DMA

    taken = lax.ppermute(stored_tiles, "dev", partners)[0]
    taken_orbitals = lax.ppermute(orbitals, "dev", partners)
    taken_flags = lax.ppermute(tile_flags, "dev", partners)
    tiles, held = call(
        functools.partial(load_kernel, layout),
        [jax.ShapeDtypeStruct(stored_tiles.shape[1:], F32), block],
        [
            pltpu.with_memory_space_constraint(operand, pltpu.HBM)
            for operand in (tile_flags, stored_tiles[0], orbitals)
        ],
        [HBM] * 3,
        [pltpu.SMEM(tile_flags.shape, jnp.int32), semaphore((3,))],
        flops=10**9,
    )
    mask = call(
        functools.partial(mask_kernel, layout),
        jax.ShapeDtypeStruct((group_width + 1, order), F32),
        [taken_flags],
        flops=10**9,
    )

    *full, made = call(
        functools.partial(send_full_kernel, layout),
        [two] * (layout.rounds + 1),
        [tiles, taken, mask, held, taken_orbitals],
    )
    full_arrived = []
    for r in range(layout.rounds):
        arrived = lax.ppermute(full[r], ("grp", "dev"), moves_of(layout, r))
        full_arrived.append(arrived)

    last = call(
        functools.partial(send_last_kernel, layout),
        two,
        [tiles, taken, mask, held, taken_orbitals, made],
    )
    last_arrived = lax.ppermute(last, ("grp", "dev"), moves_of(layout, None))

    odd = call(functools.partial(send_odd_kernel, layout), block, [tiles, held])
    odd_arrived = lax.ppermute(odd, ("grp", "dev"), odd_moves(layout, groups))

    mine, others = call(
        functools.partial(near_kernel, layout),
        [block, block],
        [tiles, held, taken_orbitals],
    )
    others = call(
        functools.partial(full_kernel, layout),
        block,
        [taken, mask, others, *full_arrived],
    )
    others = call(
        functools.partial(back_kernel, layout),
        block,
        [taken, mask, others, last_arrived],
    )
    returned = lax.ppermute(others, "dev", partners)
    mine = call(
        functools.partial(mine_kernel, layout),
        block,
        [tiles, mine, last_arrived, odd_arrived, *full_arrived],
    )
    return mine + returned


def solution(mesh):
    in_specs = (
        P(("grp", "dev"), None, None, None),
        P(("grp", "dev"), None),
        P(("grp", "dev"), None),
    )
    out_specs = P(("grp", "dev"), None)
    return jax.shard_map(
        per_device, mesh=mesh, in_specs=in_specs, out_specs=out_specs, check_vma=False
    )
```

```python
import functools

import jax
import jax.numpy as jnp
from jax import lax
from jax.experimental import pallas as pl
from jax.experimental.pallas import tpu as pltpu
from jax.sharding import PartitionSpec as P

HBM = pl.BlockSpec(memory_space=pltpu.HBM)
VMEM = pl.BlockSpec(memory_space=pltpu.VMEM)
F32 = jnp.float32


def parted(value):
    high = value.astype(jnp.bfloat16)
    return high, (value - high.astype(F32)).astype(jnp.bfloat16)


def times(left, right):
    left_high, left_low = parted(left)
    right_high, right_low = parted(right)
    dot = functools.partial(jnp.dot, preferred_element_type=F32)
    rows = left.shape[0]
    both = dot(jnp.concatenate([left_high, left_low], axis=0), right_high)
    return both[:rows] + both[rows:] + dot(left_high, right_low)


def transposed_times(left, right):
    return times(left.T, right)


class Layout:
    def __init__(self, group_width):
        self.width = group_width
        self.pairs = group_width // 2
        self.rounds = (self.pairs - 1) // 2
        self.last_offset = 2

    def offset(self, round_index, side):
        if round_index == 0:
            return 1 + 2 * side
        return 2 * round_index + 2 + side


def place():
    index = lax.axis_index("dev")
    return index, index // 2, index % 2


def load_kernel(layout, flags_in, tiles_in, orbitals_in, tiles, orbitals, flags, sems):
    copies = [
        pltpu.make_async_copy(flags_in, flags, sems.at[0]),
        pltpu.make_async_copy(tiles_in, tiles, sems.at[1]),
        pltpu.make_async_copy(orbitals_in, orbitals, sems.at[2]),
    ]
    for copy in copies:
        copy.start()
    for copy in copies:
        copy.wait()
    for slot in range(layout.width + 1):
        tiles[slot] = tiles[slot] * flags[0, slot].astype(F32)


def mask_kernel(layout, flags, mask):
    row = flags[...].astype(F32)
    for slot in range(layout.width + 1):
        mask[slot : slot + 1] = jnp.broadcast_to(
            row[:, slot : slot + 1], (1, mask.shape[1])
        )


def taken_tile(taken, mask, slot):
    return taken[slot] * mask[pl.ds(slot, 1), :]


def pair_terms(far, tiles, taken, mask, own, other, out):
    dot = functools.partial(
        lax.dot_general,
        dimension_numbers=(((0,), (0,)), ((), ())),
        preferred_element_type=F32,
    )
    right_high, right_low = parted(jnp.concatenate([own, other], axis=0))
    for k in range(2):
        slot = 2 * far + k
        stack = jnp.concatenate([tiles[slot], taken_tile(taken, mask, slot)], axis=0)
        high, low = parted(stack)
        out[k] = dot(high, right_high) + dot(high, right_low) + dot(low, right_high)


def send_full_kernel(layout, tiles, taken, mask, orbitals, taken_orbitals, *outs):
    index, pair, side = place()
    own, other = orbitals[...], taken_orbitals[...]
    for r in range(layout.rounds):
        far = pair ^ layout.offset(r, side)
        out = outs[r]

        @pl.when(far > pair)
        def _():
            pair_terms(far, tiles, taken, mask, own, other, out)

        @pl.when(far < pair)
        def _():
            out[0] = jnp.where(side == 0, own, other)
            out[1] = jnp.where(side == 0, other, own)

    far = pair ^ layout.last_offset

    @pl.when((side == 1) & (pair == 0))
    def _():
        pair_terms(far, tiles, taken, mask, own, other, outs[-1])


def send_last_kernel(layout, tiles, taken, mask, orbitals, taken_orbitals, made, out):
    index, pair, side = place()
    own, other = orbitals[...], taken_orbitals[...]
    far = pair ^ layout.last_offset
    lower = lax.axis_index("grp") % 2 == 0

    @pl.when((side == 1) & (pair == 0))
    def _():
        out[...] = made[...]

    @pl.when((side == 1) & (far > pair) & (pair > 0))
    def _():
        pair_terms(far, tiles, taken, mask, own, other, out)

    @pl.when((side == 1) & (far < pair))
    def _():
        out[0] = other
        out[1] = own

    @pl.when((side == 0) & lower)
    def _():
        out[0] = transposed_times(tiles[layout.width], own)
        out[1] = transposed_times(taken_tile(taken, mask, layout.width), other)

    @pl.when((side == 0) & jnp.logical_not(lower))
    def _():
        out[0] = own
        out[1] = other


def send_odd_kernel(layout, tiles, orbitals, out):
    lower = lax.axis_index("grp") % 2 == 1

    @pl.when(lower)
    def _():
        out[...] = transposed_times(tiles[layout.width], orbitals[...])

    @pl.when(jnp.logical_not(lower))
    def _():
        out[...] = orbitals[...]


def near_kernel(layout, tiles, orbitals, taken_orbitals, mine, others):
    index, pair, side = place()
    own, other = orbitals[...], taken_orbitals[...]
    beside = tiles[index ^ 1]
    row = jnp.concatenate([tiles[index], beside], axis=1)
    mine[...] = times(row, jnp.concatenate([own, other], axis=0))
    others[...] = transposed_times(beside, own)


def take_full(layout, arrived, row, tile_of, total):
    index, pair, side = place()
    for r, came in enumerate(arrived):
        far = pair ^ layout.offset(r, side)

        @pl.when(far > pair)
        def _():
            left = jnp.concatenate([tile_of(2 * far), tile_of(2 * far + 1)], axis=1)
            right = jnp.concatenate([came[0], came[1]], axis=0)
            total[...] += times(left, right)

        @pl.when(far < pair)
        def _():
            total[...] += came[side ^ row]


def full_kernel(layout, taken, mask, others_in, *refs):
    arrived, others = refs[:-1], refs[-1]
    others[...] = others_in[...]
    take_full(layout, arrived, 1, lambda slot: taken_tile(taken, mask, slot), others)


def back_kernel(layout, taken, mask, others_in, came, others):
    index, pair, side = place()
    far = pair ^ layout.last_offset
    lower = lax.axis_index("grp") % 2 == 0

    @pl.when((side == 1) & (far > pair))
    def _():
        left = jnp.concatenate(
            [taken_tile(taken, mask, 2 * far + k) for k in range(2)], axis=1
        )
        right = jnp.concatenate([came[0], came[1]], axis=0)
        others[...] = others_in[...] + times(left, right)

    @pl.when((side == 1) & (far < pair))
    def _():
        others[...] = others_in[...] + came[0]

    @pl.when((side == 0) & lower)
    def _():
        left = taken_tile(taken, mask, layout.width)
        others[...] = others_in[...] + times(left, came[1])

    @pl.when((side == 0) & jnp.logical_not(lower))
    def _():
        others[...] = others_in[...] + came[1]


def mine_kernel(layout, tiles, mine_in, came, odd_in, *refs):
    arrived, mine = refs[:-1], refs[-1]
    index, pair, side = place()
    far = pair ^ layout.last_offset
    group = lax.axis_index("grp")
    lower = group % 2 == 0

    @pl.when((side == 1) & (far > pair))
    def _():
        left = jnp.concatenate([tiles[2 * far], tiles[2 * far + 1]], axis=1)
        right = jnp.concatenate([came[0], came[1]], axis=0)
        mine[...] = mine_in[...] + times(left, right)

    @pl.when((side == 1) & (far < pair))
    def _():
        mine[...] = mine_in[...] + came[1]

    @pl.when((side == 0) & lower)
    def _():
        mine[...] = mine_in[...] + times(tiles[layout.width], came[0])

    @pl.when((side == 0) & jnp.logical_not(lower))
    def _():
        mine[...] = mine_in[...] + came[0]

    @pl.when(lower)
    def _():
        mine[...] += jnp.where(group > 0, odd_in[...], 0.0)

    @pl.when(jnp.logical_not(lower))
    def _():
        mine[...] += times(tiles[layout.width], odd_in[...])

    take_full(layout, arrived, 0, lambda slot: tiles[slot], mine)


def call(body, outs, operands, specs=None, scratch=(), flops=0):
    return pl.pallas_call(
        body,
        out_shape=outs,
        in_specs=specs or [VMEM] * len(operands),
        out_specs=jax.tree.map(lambda _: VMEM, outs),
        scratch_shapes=scratch,
        cost_estimate=pl.CostEstimate(
            flops=flops, bytes_accessed=0, transcendentals=0
        ),
        compiler_params=pltpu.CompilerParams(vmem_limit_bytes=32 * 1024 * 1024),
    )(*operands)


def last_moves(layout, groups):
    moves = []
    for g in range(groups):
        for i in range(layout.width):
            if i % 2 == 1:
                to, j = g, i ^ (2 * layout.last_offset)
            else:
                to, j = g ^ 1, i
                if to >= groups:
                    to = g
            moves.append((g * layout.width + i, to * layout.width + j))
    return moves


def odd_moves(layout, groups):
    moves = []
    for g in range(groups):
        to = g + 1 if g % 2 == 1 else g - 1
        for i in range(layout.width):
            if 0 <= to < groups:
                moves.append((g * layout.width + i, to * layout.width + i))
            else:
                moves.append((g * layout.width + i, g * layout.width + (i ^ 1)))
    return moves


def per_device(stored_tiles, tile_flags, orbitals):
    group_width = lax.axis_size("dev")
    groups = lax.axis_size("grp")
    layout = Layout(group_width)
    order, columns = orbitals.shape
    block = jax.ShapeDtypeStruct((order, columns), F32)
    two = jax.ShapeDtypeStruct((2, order, columns), F32)
    partners = [(i, i ^ 1) for i in range(group_width)]
    semaphore = pltpu.SemaphoreType.DMA

    taken = lax.ppermute(stored_tiles, "dev", partners)[0]
    taken_orbitals = lax.ppermute(orbitals, "dev", partners)
    taken_flags = lax.ppermute(tile_flags, "dev", partners)
    tiles, held = call(
        functools.partial(load_kernel, layout),
        [jax.ShapeDtypeStruct(stored_tiles.shape[1:], F32), block],
        [
            pltpu.with_memory_space_constraint(operand, pltpu.HBM)
            for operand in (tile_flags, stored_tiles[0], orbitals)
        ],
        [HBM] * 3,
        [pltpu.SMEM(tile_flags.shape, jnp.int32), semaphore((3,))],
        flops=10**9,
    )
    mask = call(
        functools.partial(mask_kernel, layout),
        jax.ShapeDtypeStruct((group_width + 1, order), F32),
        [taken_flags],
        flops=10**9,
    )

    *full, made = call(
        functools.partial(send_full_kernel, layout),
        [two] * (layout.rounds + 1),
        [tiles, taken, mask, held, taken_orbitals],
    )
    full_arrived = []
    for r in range(layout.rounds):
        swaps = [
            (i, i ^ (2 * layout.offset(r, i % 2))) for i in range(group_width)
        ]
        full_arrived.append(lax.ppermute(full[r], "dev", swaps))

    last = call(
        functools.partial(send_last_kernel, layout),
        two,
        [tiles, taken, mask, held, taken_orbitals, made],
    )
    last_arrived = lax.ppermute(last, ("grp", "dev"), last_moves(layout, groups))

    odd = call(functools.partial(send_odd_kernel, layout), block, [tiles, held])
    odd_arrived = lax.ppermute(odd, ("grp", "dev"), odd_moves(layout, groups))

    mine, others = call(
        functools.partial(near_kernel, layout),
        [block, block],
        [tiles, held, taken_orbitals],
    )
    others = call(
        functools.partial(full_kernel, layout),
        block,
        [taken, mask, others, *full_arrived],
    )
    others = call(
        functools.partial(back_kernel, layout),
        block,
        [taken, mask, others, last_arrived],
    )
    returned = lax.ppermute(others, "dev", partners)
    mine = call(
        functools.partial(mine_kernel, layout),
        block,
        [tiles, mine, last_arrived, odd_arrived, *full_arrived],
    )
    return mine + returned


def solution(mesh):
    in_specs = (
        P(("grp", "dev"), None, None, None),
        P(("grp", "dev"), None),
        P(("grp", "dev"), None),
    )
    out_specs = P(("grp", "dev"), None)
    return jax.shard_map(
        per_device, mesh=mesh, in_specs=in_specs, out_specs=out_specs, check_vma=False
    )
```

```python
import functools

import jax
import jax.numpy as jnp
from jax import lax
from jax.experimental import pallas as pl
from jax.experimental.pallas import tpu as pltpu
from jax.sharding import PartitionSpec as P

HBM = pl.BlockSpec(memory_space=pltpu.HBM)
VMEM = pl.BlockSpec(memory_space=pltpu.VMEM)
F32 = jnp.float32


def parted(value):
    high = value.astype(jnp.bfloat16)
    return high, (value - high.astype(F32)).astype(jnp.bfloat16)


def times(left, right):
    left_high, left_low = parted(left)
    right_high, right_low = parted(right)
    dot = functools.partial(jnp.dot, preferred_element_type=F32)
    rows = left.shape[0]
    both = dot(jnp.concatenate([left_high, left_low], axis=0), right_high)
    return both[:rows] + both[rows:] + dot(left_high, right_low)


def transposed_times(left, right):
    return times(left.T, right)


class Layout:
    def __init__(self, group_width, groups):
        self.width = group_width
        self.groups = groups
        self.pairs = group_width // 2
        self.rounds = (self.pairs - 1) // 2
        self.last_offset = 2

    def offset(self, round_index, side):
        if round_index == 0:
            return 1 + 2 * side
        return 2 * round_index + 2 + side


def late(layout):
    return lax.axis_index("grp") >= layout.groups // 2


def full_role(layout, r):
    index, pair, side = place()
    far = pair ^ layout.offset(r, side)
    return far, (side == 1) | jnp.logical_not(late(layout)) if r == 0 else side >= 0


def last_role(layout):
    index, pair, side = place()
    far = pair ^ jnp.where(side == 1, layout.last_offset, layout.offset(0, 0))
    return far, (side == 1) | late(layout)


def place():
    index = lax.axis_index("dev")
    return index, index // 2, index % 2


def load_kernel(layout, flags_in, tiles_in, orbitals_in, tiles, orbitals, flags, sems):
    copies = [
        pltpu.make_async_copy(flags_in, flags, sems.at[0]),
        pltpu.make_async_copy(tiles_in, tiles, sems.at[1]),
        pltpu.make_async_copy(orbitals_in, orbitals, sems.at[2]),
    ]
    for copy in copies:
        copy.start()
    for copy in copies:
        copy.wait()
    for slot in range(layout.width + 1):
        tiles[slot] = tiles[slot] * flags[0, slot].astype(F32)


def mask_kernel(layout, flags, mask):
    row = flags[...].astype(F32)
    for slot in range(layout.width + 1):
        mask[slot : slot + 1] = jnp.broadcast_to(
            row[:, slot : slot + 1], (1, mask.shape[1])
        )


def taken_tile(taken, mask, slot):
    return taken[slot] * mask[pl.ds(slot, 1), :]


def pair_terms(far, tiles, taken, mask, own, other, out):
    dot = functools.partial(
        lax.dot_general,
        dimension_numbers=(((0,), (0,)), ((), ())),
        preferred_element_type=F32,
    )
    right_high, right_low = parted(jnp.concatenate([own, other], axis=0))
    for k in range(2):
        slot = 2 * far + k
        stack = jnp.concatenate([tiles[slot], taken_tile(taken, mask, slot)], axis=0)
        high, low = parted(stack)
        out[k] = dot(high, right_high) + dot(high, right_low) + dot(low, right_high)


def role_blocks(layout, role, tiles, taken, mask, own, other, out):
    index, pair, side = place()
    far, trades = role
    lower = lax.axis_index("grp") % 2 == 0

    @pl.when(trades & (far > pair))
    def _():
        pair_terms(far, tiles, taken, mask, own, other, out)

    @pl.when(jnp.logical_not(trades) & lower)
    def _():
        out[0] = transposed_times(tiles[layout.width], own)
        out[1] = transposed_times(taken_tile(taken, mask, layout.width), other)

    @pl.when(jnp.where(trades, far < pair, jnp.logical_not(lower)))
    def _():
        out[0] = jnp.where(side == 0, own, other)
        out[1] = jnp.where(side == 0, other, own)


def send_full_kernel(layout, tiles, taken, mask, orbitals, taken_orbitals, *outs):
    index, pair, side = place()
    own, other = orbitals[...], taken_orbitals[...]
    for r in range(layout.rounds):
        role = full_role(layout, r)
        role_blocks(layout, role, tiles, taken, mask, own, other, outs[r])

    @pl.when((side == 1) & (pair == 0))
    def _():
        far = pair ^ layout.last_offset
        pair_terms(far, tiles, taken, mask, own, other, outs[-1])


def send_last_kernel(layout, tiles, taken, mask, orbitals, taken_orbitals, made, out):
    index, pair, side = place()

    @pl.when((side == 1) & (pair == 0))
    def _():
        out[...] = made[...]

    @pl.when((side == 0) | (pair > 0))
    def _():
        own, other = orbitals[...], taken_orbitals[...]
        role_blocks(layout, last_role(layout), tiles, taken, mask, own, other, out)


def send_odd_kernel(layout, tiles, orbitals, out):
    lower = lax.axis_index("grp") % 2 == 1

    @pl.when(lower)
    def _():
        out[...] = transposed_times(tiles[layout.width], orbitals[...])

    @pl.when(jnp.logical_not(lower))
    def _():
        out[...] = orbitals[...]


def near_kernel(layout, tiles, orbitals, taken_orbitals, mine, others):
    index, pair, side = place()
    own, other = orbitals[...], taken_orbitals[...]
    beside = tiles[index ^ 1]
    row = jnp.concatenate([tiles[index], beside], axis=1)
    mine[...] = times(row, jnp.concatenate([own, other], axis=0))
    others[...] = transposed_times(beside, own)


def take(layout, role, came, row, tile_of, total):
    index, pair, side = place()
    far, trades = role
    lower = lax.axis_index("grp") % 2 == 0

    @pl.when(trades & (far > pair))
    def _():
        left = jnp.concatenate([tile_of(2 * far), tile_of(2 * far + 1)], axis=1)
        right = jnp.concatenate([came[0], came[1]], axis=0)
        total[...] += times(left, right)

    @pl.when(jnp.logical_not(trades) & lower)
    def _():
        total[...] += times(tile_of(layout.width), came[row])

    @pl.when(jnp.where(trades, far < pair, jnp.logical_not(lower)))
    def _():
        total[...] += came[side ^ row]


def full_kernel(layout, taken, mask, others_in, *refs):
    arrived, others = refs[:-1], refs[-1]
    others[...] = others_in[...]
    for r, came in enumerate(arrived):
        tile_of = functools.partial(taken_tile, taken, mask)
        take(layout, full_role(layout, r), came, 1, tile_of, others)


def back_kernel(layout, taken, mask, others_in, came, others):
    others[...] = others_in[...]
    tile_of = functools.partial(taken_tile, taken, mask)
    take(layout, last_role(layout), came, 1, tile_of, others)


def mine_kernel(layout, tiles, mine_in, last, odd_in, *refs):
    arrived, mine = refs[:-1], refs[-1]
    group = lax.axis_index("grp")

    @pl.when(group % 2 == 0)
    def _():
        mine[...] = mine_in[...] + jnp.where(group > 0, odd_in[...], 0.0)

    @pl.when(group % 2 == 1)
    def _():
        mine[...] = mine_in[...] + times(tiles[layout.width], odd_in[...])

    def tile_of(slot):
        return tiles[slot]

    take(layout, last_role(layout), last, 0, tile_of, mine)
    for r, came in enumerate(arrived):
        take(layout, full_role(layout, r), came, 0, tile_of, mine)


def call(body, outs, operands, specs=None, scratch=(), flops=0):
    return pl.pallas_call(
        body,
        out_shape=outs,
        in_specs=specs or [VMEM] * len(operands),
        out_specs=jax.tree.map(lambda _: VMEM, outs),
        scratch_shapes=scratch,
        cost_estimate=pl.CostEstimate(
            flops=flops, bytes_accessed=0, transcendentals=0
        ),
        compiler_params=pltpu.CompilerParams(vmem_limit_bytes=32 * 1024 * 1024),
    )(*operands)


def moves_of(layout, r):
    moves = []
    for g in range(layout.groups):
        upper_half = g >= layout.groups // 2
        for i in range(layout.width):
            side = i % 2
            if r is None:
                offset = layout.last_offset if side else layout.offset(0, 0)
                trades = side == 1 or upper_half
            else:
                offset = layout.offset(r, side)
                trades = side == 1 or r > 0 or not upper_half
            to, j = (g, i ^ (2 * offset)) if trades else (g ^ 1, i)
            moves.append((g * layout.width + i, to * layout.width + j))
    return moves


def odd_moves(layout, groups):
    moves = []
    for g in range(groups):
        to = g + 1 if g % 2 == 1 else g - 1
        for i in range(layout.width):
            if 0 <= to < groups:
                moves.append((g * layout.width + i, to * layout.width + i))
            else:
                moves.append((g * layout.width + i, g * layout.width + (i ^ 1)))
    return moves


def per_device(stored_tiles, tile_flags, orbitals):
    group_width = lax.axis_size("dev")
    groups = lax.axis_size("grp")
    layout = Layout(group_width, groups)
    order, columns = orbitals.shape
    block = jax.ShapeDtypeStruct((order, columns), F32)
    two = jax.ShapeDtypeStruct((2, order, columns), F32)
    partners = [(i, i ^ 1) for i in range(group_width)]
    semaphore = pltpu.SemaphoreType.DMA

    taken = lax.ppermute(stored_tiles, "dev", partners)[0]
    taken_orbitals = lax.ppermute(orbitals, "dev", partners)
    taken_flags = lax.ppermute(tile_flags, "dev", partners)
    tiles, held = call(
        functools.partial(load_kernel, layout),
        [jax.ShapeDtypeStruct(stored_tiles.shape[1:], F32), block],
        [
            pltpu.with_memory_space_constraint(operand, pltpu.HBM)
            for operand in (tile_flags, stored_tiles[0], orbitals)
        ],
        [HBM] * 3,
        [pltpu.SMEM(tile_flags.shape, jnp.int32), semaphore((3,))],
        flops=10**9,
    )
    mask = call(
        functools.partial(mask_kernel, layout),
        jax.ShapeDtypeStruct((group_width + 1, order), F32),
        [taken_flags],
        flops=10**9,
    )

    *full, made = call(
        functools.partial(send_full_kernel, layout),
        [two] * (layout.rounds + 1),
        [tiles, taken, mask, held, taken_orbitals],
    )
    full_arrived = []
    for r in range(layout.rounds):
        arrived = lax.ppermute(full[r], ("grp", "dev"), moves_of(layout, r))
        full_arrived.append(arrived)

    last = call(
        functools.partial(send_last_kernel, layout),
        two,
        [tiles, taken, mask, held, taken_orbitals, made],
    )
    last_arrived = lax.ppermute(last, ("grp", "dev"), moves_of(layout, None))

    odd = call(functools.partial(send_odd_kernel, layout), block, [tiles, held])
    odd_arrived = lax.ppermute(odd, ("grp", "dev"), odd_moves(layout, groups))

    mine, others = call(
        functools.partial(near_kernel, layout),
        [block, block],
        [tiles, held, taken_orbitals],
    )
    others = call(
        functools.partial(full_kernel, layout),
        block,
        [taken, mask, others, *full_arrived],
    )
    others = call(
        functools.partial(back_kernel, layout),
        block,
        [taken, mask, others, last_arrived],
    )
    returned = lax.ppermute(others, "dev", partners)
    mine = call(
        functools.partial(mine_kernel, layout),
        block,
        [tiles, mine, last_arrived, odd_arrived, *full_arrived],
    )
    return mine + returned


def solution(mesh):
    in_specs = (
        P(("grp", "dev"), None, None, None),
        P(("grp", "dev"), None),
        P(("grp", "dev"), None),
    )
    out_specs = P(("grp", "dev"), None)
    return jax.shard_map(
        per_device, mesh=mesh, in_specs=in_specs, out_specs=out_specs, check_vma=False
    )
```

```python
import functools

import jax
import jax.numpy as jnp
from jax import lax
from jax.experimental import pallas as pl
from jax.experimental.pallas import tpu as pltpu
from jax.sharding import PartitionSpec as P

HBM = pl.BlockSpec(memory_space=pltpu.HBM)
VMEM = pl.BlockSpec(memory_space=pltpu.VMEM)
F32 = jnp.float32


def parted(value):
    high = value.astype(jnp.bfloat16)
    return high, (value - high.astype(F32)).astype(jnp.bfloat16)


def times(left, right):
    left_high, left_low = parted(left)
    right_high, right_low = parted(right)
    dot = functools.partial(jnp.dot, preferred_element_type=F32)
    rows = left.shape[0]
    both = dot(jnp.concatenate([left_high, left_low], axis=0), right_high)
    return both[:rows] + both[rows:] + dot(left_high, right_low)


def transposed_times(left, right):
    return times(left.T, right)


class Layout:
    def __init__(self, group_width, groups):
        self.width = group_width
        self.groups = groups
        self.pairs = group_width // 2
        self.rounds = (self.pairs - 1) // 2
        self.last_offset = 2

    def offset(self, round_index, side):
        if round_index == 0:
            return 1 + 2 * side
        return 2 * round_index + 2 + side


def late(layout):
    return lax.axis_index("grp") >= layout.groups // 2


def full_role(layout, r):
    index, pair, side = place()
    far = pair ^ layout.offset(r, side)
    return far, (side == 1) | jnp.logical_not(late(layout)) if r == 0 else side >= 0


def last_role(layout):
    index, pair, side = place()
    far = pair ^ jnp.where(side == 1, layout.last_offset, layout.offset(0, 0))
    return far, (side == 1) | late(layout)


def place():
    index = lax.axis_index("dev")
    return index, index // 2, index % 2


def load_kernel(layout, flags_in, tiles_in, orbitals_in, tiles, orbitals, flags, sems):
    copies = [
        pltpu.make_async_copy(flags_in, flags, sems.at[0]),
        pltpu.make_async_copy(tiles_in, tiles, sems.at[1]),
        pltpu.make_async_copy(orbitals_in, orbitals, sems.at[2]),
    ]
    for copy in copies:
        copy.start()
    for copy in copies:
        copy.wait()
    for slot in range(layout.width + 1):
        tiles[slot] = tiles[slot] * flags[0, slot].astype(F32)


def mask_kernel(layout, flags, mask):
    row = flags[...].astype(F32)
    for slot in range(layout.width + 1):
        mask[slot : slot + 1] = jnp.broadcast_to(
            row[:, slot : slot + 1], (1, mask.shape[1])
        )


def taken_tile(taken, mask, slot):
    return taken[slot] * mask[pl.ds(slot, 1), :]


def pair_terms(far, tiles, taken, mask, own, other, out):
    dot = functools.partial(
        lax.dot_general,
        dimension_numbers=(((0,), (0,)), ((), ())),
        preferred_element_type=F32,
    )
    right_high, right_low = parted(jnp.concatenate([own, other], axis=0))
    for k in range(2):
        slot = 2 * far + k
        stack = jnp.concatenate([tiles[slot], taken_tile(taken, mask, slot)], axis=0)
        high, low = parted(stack)
        out[k] = dot(high, right_high) + dot(high, right_low) + dot(low, right_high)


def role_blocks(layout, role, tiles, taken, mask, own, other, out):
    index, pair, side = place()
    far, trades = role
    lower = lax.axis_index("grp") % 2 == 0

    @pl.when(trades & (far > pair))
    def _():
        pair_terms(far, tiles, taken, mask, own, other, out)

    @pl.when(jnp.logical_not(trades) & lower)
    def _():
        out[0] = transposed_times(tiles[layout.width], own)
        out[1] = transposed_times(taken_tile(taken, mask, layout.width), other)

    @pl.when(jnp.where(trades, far < pair, jnp.logical_not(lower)))
    def _():
        out[0] = jnp.where(side == 0, own, other)
        out[1] = jnp.where(side == 0, other, own)


def send_full_kernel(layout, tiles, taken, mask, orbitals, taken_orbitals, *outs):
    index, pair, side = place()
    own, other = orbitals[...], taken_orbitals[...]
    for r in range(layout.rounds):
        role = full_role(layout, r)
        role_blocks(layout, role, tiles, taken, mask, own, other, outs[r])

    @pl.when((side == 1) & (pair == 0))
    def _():
        far = pair ^ layout.last_offset
        pair_terms(far, tiles, taken, mask, own, other, outs[-1])


def send_last_kernel(layout, tiles, taken, mask, orbitals, taken_orbitals, made, out):
    index, pair, side = place()

    @pl.when((side == 1) & (pair == 0))
    def _():
        out[...] = made[...]

    @pl.when((side == 0) | (pair > 0))
    def _():
        own, other = orbitals[...], taken_orbitals[...]
        role_blocks(layout, last_role(layout), tiles, taken, mask, own, other, out)


def send_odd_kernel(layout, tiles, orbitals, out):
    lower = lax.axis_index("grp") % 2 == 1

    @pl.when(lower)
    def _():
        out[...] = transposed_times(tiles[layout.width], orbitals[...])

    @pl.when(jnp.logical_not(lower))
    def _():
        out[...] = orbitals[...]


def near_kernel(layout, tiles, orbitals, taken_orbitals, mine, others):
    index, pair, side = place()
    own, other = orbitals[...], taken_orbitals[...]
    beside = tiles[index ^ 1]
    row = jnp.concatenate([tiles[index], beside], axis=1)
    mine[...] = times(row, jnp.concatenate([own, other], axis=0))
    others[...] = transposed_times(beside, own)


def take(layout, role, came, row, tile_of, base, total):
    index, pair, side = place()
    far, trades = role
    lower = lax.axis_index("grp") % 2 == 0

    @pl.when(trades & (far > pair))
    def _():
        left = jnp.concatenate([tile_of(2 * far), tile_of(2 * far + 1)], axis=1)
        right = jnp.concatenate([came[0], came[1]], axis=0)
        total[...] = base[...] + times(left, right)

    @pl.when(jnp.logical_not(trades) & lower)
    def _():
        total[...] = base[...] + times(tile_of(layout.width), came[row])

    @pl.when(jnp.where(trades, far < pair, jnp.logical_not(lower)))
    def _():
        total[...] = base[...] + came[side ^ row]


def full_kernel(layout, taken, mask, others_in, *refs):
    arrived, others = refs[:-1], refs[-1]
    tile_of = functools.partial(taken_tile, taken, mask)
    for r, came in enumerate(arrived):
        base = others_in if r == 0 else others
        take(layout, full_role(layout, r), came, 1, tile_of, base, others)


def back_kernel(layout, taken, mask, others_in, came, others):
    tile_of = functools.partial(taken_tile, taken, mask)
    take(layout, last_role(layout), came, 1, tile_of, others_in, others)


def mine_kernel(layout, tiles, mine_in, last, odd_in, *refs):
    arrived, mine = refs[:-1], refs[-1]
    group = lax.axis_index("grp")

    @pl.when(group % 2 == 0)
    def _():
        mine[...] = mine_in[...] + jnp.where(group > 0, odd_in[...], 0.0)

    @pl.when(group % 2 == 1)
    def _():
        mine[...] = mine_in[...] + times(tiles[layout.width], odd_in[...])

    def tile_of(slot):
        return tiles[slot]

    take(layout, last_role(layout), last, 0, tile_of, mine, mine)
    for r, came in enumerate(arrived):
        take(layout, full_role(layout, r), came, 0, tile_of, mine, mine)


def call(body, outs, operands, specs=None, scratch=(), flops=0):
    return pl.pallas_call(
        body,
        out_shape=outs,
        in_specs=specs or [VMEM] * len(operands),
        out_specs=jax.tree.map(lambda _: VMEM, outs),
        scratch_shapes=scratch,
        cost_estimate=pl.CostEstimate(
            flops=flops, bytes_accessed=0, transcendentals=0
        ),
        compiler_params=pltpu.CompilerParams(vmem_limit_bytes=32 * 1024 * 1024),
    )(*operands)


def moves_of(layout, r):
    moves = []
    for g in range(layout.groups):
        upper_half = g >= layout.groups // 2
        for i in range(layout.width):
            side = i % 2
            if r is None:
                offset = layout.last_offset if side else layout.offset(0, 0)
                trades = side == 1 or upper_half
            else:
                offset = layout.offset(r, side)
                trades = side == 1 or r > 0 or not upper_half
            to, j = (g, i ^ (2 * offset)) if trades else (g ^ 1, i)
            moves.append((g * layout.width + i, to * layout.width + j))
    return moves


def odd_moves(layout, groups):
    moves = []
    for g in range(groups):
        to = g + 1 if g % 2 == 1 else g - 1
        for i in range(layout.width):
            if 0 <= to < groups:
                moves.append((g * layout.width + i, to * layout.width + i))
            else:
                moves.append((g * layout.width + i, g * layout.width + (i ^ 1)))
    return moves


def per_device(stored_tiles, tile_flags, orbitals):
    group_width = lax.axis_size("dev")
    groups = lax.axis_size("grp")
    layout = Layout(group_width, groups)
    order, columns = orbitals.shape
    block = jax.ShapeDtypeStruct((order, columns), F32)
    two = jax.ShapeDtypeStruct((2, order, columns), F32)
    partners = [(i, i ^ 1) for i in range(group_width)]
    semaphore = pltpu.SemaphoreType.DMA

    taken = lax.ppermute(stored_tiles, "dev", partners)[0]
    taken_orbitals = lax.ppermute(orbitals, "dev", partners)
    taken_flags = lax.ppermute(tile_flags, "dev", partners)
    tiles, held = call(
        functools.partial(load_kernel, layout),
        [jax.ShapeDtypeStruct(stored_tiles.shape[1:], F32), block],
        [
            pltpu.with_memory_space_constraint(operand, pltpu.HBM)
            for operand in (tile_flags, stored_tiles[0], orbitals)
        ],
        [HBM] * 3,
        [pltpu.SMEM(tile_flags.shape, jnp.int32), semaphore((3,))],
        flops=10**9,
    )
    mask = call(
        functools.partial(mask_kernel, layout),
        jax.ShapeDtypeStruct((group_width + 1, order), F32),
        [taken_flags],
        flops=10**9,
    )

    *full, made = call(
        functools.partial(send_full_kernel, layout),
        [two] * (layout.rounds + 1),
        [tiles, taken, mask, held, taken_orbitals],
    )
    full_arrived = []
    for r in range(layout.rounds):
        arrived = lax.ppermute(full[r], ("grp", "dev"), moves_of(layout, r))
        full_arrived.append(arrived)

    last = call(
        functools.partial(send_last_kernel, layout),
        two,
        [tiles, taken, mask, held, taken_orbitals, made],
    )
    last_arrived = lax.ppermute(last, ("grp", "dev"), moves_of(layout, None))

    odd = call(functools.partial(send_odd_kernel, layout), block, [tiles, held])
    odd_arrived = lax.ppermute(odd, ("grp", "dev"), odd_moves(layout, groups))

    mine, others = call(
        functools.partial(near_kernel, layout),
        [block, block],
        [tiles, held, taken_orbitals],
    )
    others = call(
        functools.partial(full_kernel, layout),
        block,
        [taken, mask, others, *full_arrived],
    )
    others = call(
        functools.partial(back_kernel, layout),
        block,
        [taken, mask, others, last_arrived],
    )
    returned = lax.ppermute(others, "dev", partners)
    mine = call(
        functools.partial(mine_kernel, layout),
        block,
        [tiles, mine, last_arrived, odd_arrived, *full_arrived],
    )
    return mine + returned


def solution(mesh):
    in_specs = (
        P(("grp", "dev"), None, None, None),
        P(("grp", "dev"), None),
        P(("grp", "dev"), None),
    )
    out_specs = P(("grp", "dev"), None)
    return jax.shard_map(
        per_device, mesh=mesh, in_specs=in_specs, out_specs=out_specs, check_vma=False
    )
```

```python
import functools

import jax
import jax.numpy as jnp
from jax import lax
from jax.experimental import pallas as pl
from jax.experimental.pallas import tpu as pltpu
from jax.sharding import PartitionSpec as P

HBM = pl.BlockSpec(memory_space=pltpu.HBM)
VMEM = pl.BlockSpec(memory_space=pltpu.VMEM)
F32 = jnp.float32


def parted(value):
    high = value.astype(jnp.bfloat16)
    return high, (value - high.astype(F32)).astype(jnp.bfloat16)


def times(left, right):
    left_high, left_low = parted(left)
    right_high, right_low = parted(right)
    dot = functools.partial(jnp.dot, preferred_element_type=F32)
    return (
        dot(left_high, right_high)
        + dot(left_high, right_low)
        + dot(left_low, right_high)
    )


def transposed_times(left, right):
    return times(left.T, right)


class Layout:
    def __init__(self, group_width):
        self.width = group_width
        self.pairs = group_width // 2
        self.rounds = (self.pairs - 1) // 2
        self.last_offset = 2

    def offset(self, round_index, side):
        if round_index == 0:
            return 1 + 2 * side
        return 2 * round_index + 2 + side


def place():
    index = lax.axis_index("dev")
    return index, index // 2, index % 2


def load_kernel(layout, flags_in, tiles_in, orbitals_in, tiles, orbitals, flags, sems):
    copies = [
        pltpu.make_async_copy(flags_in, flags, sems.at[0]),
        pltpu.make_async_copy(tiles_in, tiles, sems.at[1]),
        pltpu.make_async_copy(orbitals_in, orbitals, sems.at[2]),
    ]
    for copy in copies:
        copy.start()
    for copy in copies:
        copy.wait()
    for slot in range(layout.width + 1):
        tiles[slot] = tiles[slot] * flags[0, slot].astype(F32)


def mask_kernel(layout, flags, mask):
    row = flags[...].astype(F32)
    for slot in range(layout.width + 1):
        mask[slot : slot + 1] = jnp.broadcast_to(
            row[:, slot : slot + 1], (1, mask.shape[1])
        )


def taken_tile(taken, mask, slot):
    return taken[slot] * mask[pl.ds(slot, 1), :]


def pair_terms(far, tiles, taken, mask, own, other, out):
    dot = functools.partial(
        lax.dot_general,
        dimension_numbers=(((0,), (0,)), ((), ())),
        preferred_element_type=F32,
    )
    right_high, right_low = parted(jnp.concatenate([own, other], axis=0))
    for k in range(2):
        slot = 2 * far + k
        stack = jnp.concatenate([tiles[slot], taken_tile(taken, mask, slot)], axis=0)
        high, low = parted(stack)
        out[k] = dot(high, right_high) + dot(high, right_low) + dot(low, right_high)


def send_full_kernel(layout, tiles, taken, mask, orbitals, taken_orbitals, *outs):
    index, pair, side = place()
    own, other = orbitals[...], taken_orbitals[...]
    for r in range(layout.rounds):
        far = pair ^ layout.offset(r, side)
        out = outs[r]

        @pl.when(far > pair)
        def _():
            pair_terms(far, tiles, taken, mask, own, other, out)

        @pl.when(far < pair)
        def _():
            out[0] = jnp.where(side == 0, own, other)
            out[1] = jnp.where(side == 0, other, own)

    far = pair ^ layout.last_offset

    @pl.when((side == 1) & (pair == 0))
    def _():
        pair_terms(far, tiles, taken, mask, own, other, outs[-1])


def send_last_kernel(layout, tiles, taken, mask, orbitals, taken_orbitals, made, out):
    index, pair, side = place()
    own, other = orbitals[...], taken_orbitals[...]
    far = pair ^ layout.last_offset
    lower = lax.axis_index("grp") % 2 == 0

    @pl.when((side == 1) & (pair == 0))
    def _():
        out[...] = made[...]

    @pl.when((side == 1) & (far > pair) & (pair > 0))
    def _():
        pair_terms(far, tiles, taken, mask, own, other, out)

    @pl.when((side == 1) & (far < pair))
    def _():
        out[0] = other
        out[1] = own

    @pl.when((side == 0) & lower)
    def _():
        out[0] = transposed_times(tiles[layout.width], own)
        out[1] = transposed_times(taken_tile(taken, mask, layout.width), other)

    @pl.when((side == 0) & jnp.logical_not(lower))
    def _():
        out[0] = own
        out[1] = other


def send_odd_kernel(layout, tiles, orbitals, out):
    lower = lax.axis_index("grp") % 2 == 1

    @pl.when(lower)
    def _():
        out[...] = transposed_times(tiles[layout.width], orbitals[...])

    @pl.when(jnp.logical_not(lower))
    def _():
        out[...] = orbitals[...]


def near_kernel(layout, tiles, orbitals, taken_orbitals, mine, others):
    index, pair, side = place()
    own, other = orbitals[...], taken_orbitals[...]
    beside = tiles[index ^ 1]
    row = jnp.concatenate([tiles[index], beside], axis=1)
    mine[...] = times(row, jnp.concatenate([own, other], axis=0))
    others[...] = transposed_times(beside, own)


def take_full(layout, arrived, row, tile_of, total):
    index, pair, side = place()
    for r, came in enumerate(arrived):
        far = pair ^ layout.offset(r, side)

        @pl.when(far > pair)
        def _():
            left = jnp.concatenate([tile_of(2 * far), tile_of(2 * far + 1)], axis=1)
            right = jnp.concatenate([came[0], came[1]], axis=0)
            total[...] += times(left, right)

        @pl.when(far < pair)
        def _():
            total[...] += came[side ^ row]


def full_kernel(layout, taken, mask, others_in, *refs):
    arrived, others = refs[:-1], refs[-1]
    others[...] = others_in[...]
    take_full(layout, arrived, 1, lambda slot: taken_tile(taken, mask, slot), others)


def back_kernel(layout, taken, mask, others_in, came, others):
    index, pair, side = place()
    far = pair ^ layout.last_offset
    lower = lax.axis_index("grp") % 2 == 0

    @pl.when((side == 1) & (far > pair))
    def _():
        left = jnp.concatenate(
            [taken_tile(taken, mask, 2 * far + k) for k in range(2)], axis=1
        )
        right = jnp.concatenate([came[0], came[1]], axis=0)
        others[...] = others_in[...] + times(left, right)

    @pl.when((side == 1) & (far < pair))
    def _():
        others[...] = others_in[...] + came[0]

    @pl.when((side == 0) & lower)
    def _():
        left = taken_tile(taken, mask, layout.width)
        others[...] = others_in[...] + times(left, came[1])

    @pl.when((side == 0) & jnp.logical_not(lower))
    def _():
        others[...] = others_in[...] + came[1]


def mine_kernel(layout, tiles, mine_in, came, odd_in, *refs):
    arrived, mine = refs[:-1], refs[-1]
    index, pair, side = place()
    far = pair ^ layout.last_offset
    group = lax.axis_index("grp")
    lower = group % 2 == 0

    @pl.when((side == 1) & (far > pair))
    def _():
        left = jnp.concatenate([tiles[2 * far], tiles[2 * far + 1]], axis=1)
        right = jnp.concatenate([came[0], came[1]], axis=0)
        mine[...] = mine_in[...] + times(left, right)

    @pl.when((side == 1) & (far < pair))
    def _():
        mine[...] = mine_in[...] + came[1]

    @pl.when((side == 0) & lower)
    def _():
        mine[...] = mine_in[...] + times(tiles[layout.width], came[0])

    @pl.when((side == 0) & jnp.logical_not(lower))
    def _():
        mine[...] = mine_in[...] + came[0]

    @pl.when(lower)
    def _():
        mine[...] += jnp.where(group > 0, odd_in[...], 0.0)

    @pl.when(jnp.logical_not(lower))
    def _():
        mine[...] += times(tiles[layout.width], odd_in[...])

    take_full(layout, arrived, 0, lambda slot: tiles[slot], mine)


def call(body, outs, operands, specs=None, scratch=(), flops=0):
    return pl.pallas_call(
        body,
        out_shape=outs,
        in_specs=specs or [VMEM] * len(operands),
        out_specs=jax.tree.map(lambda _: VMEM, outs),
        scratch_shapes=scratch,
        cost_estimate=pl.CostEstimate(
            flops=flops, bytes_accessed=0, transcendentals=0
        ),
        compiler_params=pltpu.CompilerParams(vmem_limit_bytes=32 * 1024 * 1024),
    )(*operands)


def last_moves(layout, groups):
    moves = []
    for g in range(groups):
        for i in range(layout.width):
            if i % 2 == 1:
                to, j = g, i ^ (2 * layout.last_offset)
            else:
                to, j = g ^ 1, i
                if to >= groups:
                    to = g
            moves.append((g * layout.width + i, to * layout.width + j))
    return moves


def odd_moves(layout, groups):
    moves = []
    for g in range(groups):
        to = g + 1 if g % 2 == 1 else g - 1
        for i in range(layout.width):
            if 0 <= to < groups:
                moves.append((g * layout.width + i, to * layout.width + i))
            else:
                moves.append((g * layout.width + i, g * layout.width + (i ^ 1)))
    return moves


def per_device(stored_tiles, tile_flags, orbitals):
    group_width = lax.axis_size("dev")
    groups = lax.axis_size("grp")
    layout = Layout(group_width)
    order, columns = orbitals.shape
    block = jax.ShapeDtypeStruct((order, columns), F32)
    two = jax.ShapeDtypeStruct((2, order, columns), F32)
    partners = [(i, i ^ 1) for i in range(group_width)]
    semaphore = pltpu.SemaphoreType.DMA

    taken = lax.ppermute(stored_tiles, "dev", partners)[0]
    taken_orbitals = lax.ppermute(orbitals, "dev", partners)
    taken_flags = lax.ppermute(tile_flags, "dev", partners)
    tiles, held = call(
        functools.partial(load_kernel, layout),
        [jax.ShapeDtypeStruct(stored_tiles.shape[1:], F32), block],
        [
            pltpu.with_memory_space_constraint(operand, pltpu.HBM)
            for operand in (tile_flags, stored_tiles[0], orbitals)
        ],
        [HBM] * 3,
        [pltpu.SMEM(tile_flags.shape, jnp.int32), semaphore((3,))],
        flops=10**9,
    )
    mask = call(
        functools.partial(mask_kernel, layout),
        jax.ShapeDtypeStruct((group_width + 1, order), F32),
        [taken_flags],
        flops=10**9,
    )

    *full, made = call(
        functools.partial(send_full_kernel, layout),
        [two] * (layout.rounds + 1),
        [tiles, taken, mask, held, taken_orbitals],
    )
    full_arrived = []
    for r in range(layout.rounds):
        swaps = [
            (i, i ^ (2 * layout.offset(r, i % 2))) for i in range(group_width)
        ]
        full_arrived.append(lax.ppermute(full[r], "dev", swaps))

    last = call(
        functools.partial(send_last_kernel, layout),
        two,
        [tiles, taken, mask, held, taken_orbitals, made],
    )
    last_arrived = lax.ppermute(last, ("grp", "dev"), last_moves(layout, groups))

    odd = call(functools.partial(send_odd_kernel, layout), block, [tiles, held])
    odd_arrived = lax.ppermute(odd, ("grp", "dev"), odd_moves(layout, groups))

    mine, others = call(
        functools.partial(near_kernel, layout),
        [block, block],
        [tiles, held, taken_orbitals],
    )
    others = call(
        functools.partial(full_kernel, layout),
        block,
        [taken, mask, others, *full_arrived],
    )
    others = call(
        functools.partial(back_kernel, layout),
        block,
        [taken, mask, others, last_arrived],
    )
    returned = lax.ppermute(others, "dev", partners)
    mine = call(
        functools.partial(mine_kernel, layout),
        block,
        [tiles, mine, last_arrived, odd_arrived, *full_arrived],
    )
    return mine + returned


def solution(mesh):
    in_specs = (
        P(("grp", "dev"), None, None, None),
        P(("grp", "dev"), None),
        P(("grp", "dev"), None),
    )
    out_specs = P(("grp", "dev"), None)
    return jax.shard_map(
        per_device, mesh=mesh, in_specs=in_specs, out_specs=out_specs, check_vma=False
    )
```

```python
import functools

import jax
import jax.numpy as jnp
from jax import lax
from jax.experimental import pallas as pl
from jax.experimental.pallas import tpu as pltpu
from jax.sharding import PartitionSpec as P

HBM = pl.BlockSpec(memory_space=pltpu.HBM)
VMEM = pl.BlockSpec(memory_space=pltpu.VMEM)
F32 = jnp.float32


def parted(value):
    high = value.astype(jnp.bfloat16)
    return high, (value - high.astype(F32)).astype(jnp.bfloat16)


def times(left, right):
    left_high, left_low = parted(left)
    right_high, right_low = parted(right)
    dot = functools.partial(jnp.dot, preferred_element_type=F32)
    return (
        dot(left_high, right_high)
        + dot(left_high, right_low)
        + dot(left_low, right_high)
    )


def transposed_times(left, right):
    return times(left.T, right)


class Layout:
    def __init__(self, group_width, groups):
        self.width = group_width
        self.groups = groups
        self.pairs = group_width // 2
        self.rounds = (self.pairs - 1) // 2
        self.last_offset = 2

    def offset(self, round_index, side):
        if round_index == 0:
            return 1 + 2 * side
        return 2 * round_index + 2 + side


def late(layout):
    return lax.axis_index("grp") >= layout.groups // 2


def full_role(layout, r):
    index, pair, side = place()
    far = pair ^ layout.offset(r, side)
    return far, (side == 1) | jnp.logical_not(late(layout)) if r == 0 else side >= 0


def last_role(layout):
    index, pair, side = place()
    far = pair ^ jnp.where(side == 1, layout.last_offset, layout.offset(0, 0))
    return far, (side == 1) | late(layout)


def place():
    index = lax.axis_index("dev")
    return index, index // 2, index % 2


def load_kernel(layout, flags_in, tiles_in, orbitals_in, tiles, orbitals, flags, sems):
    copies = [
        pltpu.make_async_copy(flags_in, flags, sems.at[0]),
        pltpu.make_async_copy(tiles_in, tiles, sems.at[1]),
        pltpu.make_async_copy(orbitals_in, orbitals, sems.at[2]),
    ]
    for copy in copies:
        copy.start()
    for copy in copies:
        copy.wait()
    for slot in range(layout.width + 1):
        tiles[slot] = tiles[slot] * flags[0, slot].astype(F32)


def mask_kernel(layout, flags, mask):
    row = flags[...].astype(F32)
    for slot in range(layout.width + 1):
        mask[slot : slot + 1] = jnp.broadcast_to(
            row[:, slot : slot + 1], (1, mask.shape[1])
        )


def taken_tile(taken, mask, slot):
    return taken[slot] * mask[pl.ds(slot, 1), :]


def pair_terms(far, tiles, taken, mask, own, other, out):
    dot = functools.partial(
        lax.dot_general,
        dimension_numbers=(((0,), (0,)), ((), ())),
        preferred_element_type=F32,
    )
    right_high, right_low = parted(jnp.concatenate([own, other], axis=0))
    for k in range(2):
        slot = 2 * far + k
        stack = jnp.concatenate([tiles[slot], taken_tile(taken, mask, slot)], axis=0)
        high, low = parted(stack)
        out[k] = dot(high, right_high) + dot(high, right_low) + dot(low, right_high)


def role_blocks(layout, role, tiles, taken, mask, own, other, out):
    index, pair, side = place()
    far, trades = role
    lower = lax.axis_index("grp") % 2 == 0

    @pl.when(trades & (far > pair))
    def _():
        pair_terms(far, tiles, taken, mask, own, other, out)

    @pl.when(jnp.logical_not(trades) & lower)
    def _():
        out[0] = transposed_times(tiles[layout.width], own)
        out[1] = transposed_times(taken_tile(taken, mask, layout.width), other)

    @pl.when(jnp.where(trades, far < pair, jnp.logical_not(lower)))
    def _():
        out[0] = jnp.where(side == 0, own, other)
        out[1] = jnp.where(side == 0, other, own)


def send_full_kernel(layout, tiles, taken, mask, orbitals, taken_orbitals, *outs):
    index, pair, side = place()
    own, other = orbitals[...], taken_orbitals[...]
    for r in range(layout.rounds):
        role = full_role(layout, r)
        role_blocks(layout, role, tiles, taken, mask, own, other, outs[r])

    @pl.when((side == 1) & (pair == 0))
    def _():
        far = pair ^ layout.last_offset
        pair_terms(far, tiles, taken, mask, own, other, outs[-1])


def send_last_kernel(layout, tiles, taken, mask, orbitals, taken_orbitals, made, out):
    index, pair, side = place()

    @pl.when((side == 1) & (pair == 0))
    def _():
        out[...] = made[...]

    @pl.when((side == 0) | (pair > 0))
    def _():
        own, other = orbitals[...], taken_orbitals[...]
        role_blocks(layout, last_role(layout), tiles, taken, mask, own, other, out)


def send_odd_kernel(layout, tiles, orbitals, out):
    lower = lax.axis_index("grp") % 2 == 1

    @pl.when(lower)
    def _():
        out[...] = transposed_times(tiles[layout.width], orbitals[...])

    @pl.when(jnp.logical_not(lower))
    def _():
        out[...] = orbitals[...]


def near_kernel(layout, tiles, orbitals, taken_orbitals, mine, others):
    index, pair, side = place()
    own, other = orbitals[...], taken_orbitals[...]
    beside = tiles[index ^ 1]
    row = jnp.concatenate([tiles[index], beside], axis=1)
    mine[...] = times(row, jnp.concatenate([own, other], axis=0))
    others[...] = transposed_times(beside, own)


def take(layout, role, came, row, tile_of, base, total):
    index, pair, side = place()
    far, trades = role
    lower = lax.axis_index("grp") % 2 == 0

    @pl.when(trades & (far > pair))
    def _():
        left = jnp.concatenate([tile_of(2 * far), tile_of(2 * far + 1)], axis=1)
        right = jnp.concatenate([came[0], came[1]], axis=0)
        total[...] = base[...] + times(left, right)

    @pl.when(jnp.logical_not(trades) & lower)
    def _():
        total[...] = base[...] + times(tile_of(layout.width), came[row])

    @pl.when(jnp.where(trades, far < pair, jnp.logical_not(lower)))
    def _():
        total[...] = base[...] + came[side ^ row]


def full_kernel(layout, taken, mask, others_in, *refs):
    arrived, others = refs[:-1], refs[-1]
    tile_of = functools.partial(taken_tile, taken, mask)
    for r, came in enumerate(arrived):
        base = others_in if r == 0 else others
        take(layout, full_role(layout, r), came, 1, tile_of, base, others)


def back_kernel(layout, taken, mask, others_in, came, others):
    tile_of = functools.partial(taken_tile, taken, mask)
    take(layout, last_role(layout), came, 1, tile_of, others_in, others)


def mine_kernel(layout, tiles, mine_in, last, odd_in, *refs):
    arrived, mine = refs[:-1], refs[-1]
    group = lax.axis_index("grp")

    @pl.when(group % 2 == 0)
    def _():
        mine[...] = mine_in[...] + jnp.where(group > 0, odd_in[...], 0.0)

    @pl.when(group % 2 == 1)
    def _():
        mine[...] = mine_in[...] + times(tiles[layout.width], odd_in[...])

    def tile_of(slot):
        return tiles[slot]

    take(layout, last_role(layout), last, 0, tile_of, mine, mine)
    for r, came in enumerate(arrived):
        take(layout, full_role(layout, r), came, 0, tile_of, mine, mine)


def call(body, outs, operands, specs=None, scratch=(), flops=0):
    return pl.pallas_call(
        body,
        out_shape=outs,
        in_specs=specs or [VMEM] * len(operands),
        out_specs=jax.tree.map(lambda _: VMEM, outs),
        scratch_shapes=scratch,
        cost_estimate=pl.CostEstimate(
            flops=flops, bytes_accessed=0, transcendentals=0
        ),
        compiler_params=pltpu.CompilerParams(vmem_limit_bytes=32 * 1024 * 1024),
    )(*operands)


def moves_of(layout, r):
    moves = []
    for g in range(layout.groups):
        upper_half = g >= layout.groups // 2
        for i in range(layout.width):
            side = i % 2
            if r is None:
                offset = layout.last_offset if side else layout.offset(0, 0)
                trades = side == 1 or upper_half
            else:
                offset = layout.offset(r, side)
                trades = side == 1 or r > 0 or not upper_half
            to, j = (g, i ^ (2 * offset)) if trades else (g ^ 1, i)
            moves.append((g * layout.width + i, to * layout.width + j))
    return moves


def odd_moves(layout, groups):
    moves = []
    for g in range(groups):
        to = g + 1 if g % 2 == 1 else g - 1
        for i in range(layout.width):
            if 0 <= to < groups:
                moves.append((g * layout.width + i, to * layout.width + i))
            else:
                moves.append((g * layout.width + i, g * layout.width + (i ^ 1)))
    return moves


def per_device(stored_tiles, tile_flags, orbitals):
    group_width = lax.axis_size("dev")
    groups = lax.axis_size("grp")
    layout = Layout(group_width, groups)
    order, columns = orbitals.shape
    block = jax.ShapeDtypeStruct((order, columns), F32)
    two = jax.ShapeDtypeStruct((2, order, columns), F32)
    partners = [(i, i ^ 1) for i in range(group_width)]
    semaphore = pltpu.SemaphoreType.DMA

    taken = lax.ppermute(stored_tiles, "dev", partners)[0]
    taken_orbitals = lax.ppermute(orbitals, "dev", partners)
    taken_flags = lax.ppermute(tile_flags, "dev", partners)
    tiles, held = call(
        functools.partial(load_kernel, layout),
        [jax.ShapeDtypeStruct(stored_tiles.shape[1:], F32), block],
        [
            pltpu.with_memory_space_constraint(operand, pltpu.HBM)
            for operand in (tile_flags, stored_tiles[0], orbitals)
        ],
        [HBM] * 3,
        [pltpu.SMEM(tile_flags.shape, jnp.int32), semaphore((3,))],
        flops=10**9,
    )
    mask = call(
        functools.partial(mask_kernel, layout),
        jax.ShapeDtypeStruct((group_width + 1, order), F32),
        [taken_flags],
        flops=10**9,
    )

    *full, made = call(
        functools.partial(send_full_kernel, layout),
        [two] * (layout.rounds + 1),
        [tiles, taken, mask, held, taken_orbitals],
    )
    full_arrived = []
    for r in range(layout.rounds):
        arrived = lax.ppermute(full[r], ("grp", "dev"), moves_of(layout, r))
        full_arrived.append(arrived)

    last = call(
        functools.partial(send_last_kernel, layout),
        two,
        [tiles, taken, mask, held, taken_orbitals, made],
    )
    last_arrived = lax.ppermute(last, ("grp", "dev"), moves_of(layout, None))

    odd = call(functools.partial(send_odd_kernel, layout), block, [tiles, held])
    odd_arrived = lax.ppermute(odd, ("grp", "dev"), odd_moves(layout, groups))

    mine, others = call(
        functools.partial(near_kernel, layout),
        [block, block],
        [tiles, held, taken_orbitals],
    )
    others = call(
        functools.partial(full_kernel, layout),
        block,
        [taken, mask, others, *full_arrived],
    )
    others = call(
        functools.partial(back_kernel, layout),
        block,
        [taken, mask, others, last_arrived],
    )
    returned = lax.ppermute(others, "dev", partners)
    mine = call(
        functools.partial(mine_kernel, layout),
        block,
        [tiles, mine, last_arrived, odd_arrived, *full_arrived],
    )
    return mine + returned


def solution(mesh):
    in_specs = (
        P(("grp", "dev"), None, None, None),
        P(("grp", "dev"), None),
        P(("grp", "dev"), None),
    )
    out_specs = P(("grp", "dev"), None)
    return jax.shard_map(
        per_device, mesh=mesh, in_specs=in_specs, out_specs=out_specs, check_vma=False
    )
```

```python
import functools

import jax
import jax.numpy as jnp
from jax import lax
from jax.experimental import pallas as pl
from jax.experimental.pallas import tpu as pltpu
from jax.sharding import PartitionSpec as P

HBM = pl.BlockSpec(memory_space=pltpu.HBM)
VMEM = pl.BlockSpec(memory_space=pltpu.VMEM)
F32 = jnp.float32


def parted(value):
    high = value.astype(jnp.bfloat16)
    return high, (value - high.astype(F32)).astype(jnp.bfloat16)


def times(left, right):
    left_high, left_low = parted(left)
    right_high, right_low = parted(right)
    dot = functools.partial(jnp.dot, preferred_element_type=F32)
    return (
        dot(left_high, right_high)
        + dot(left_high, right_low)
        + dot(left_low, right_high)
    )


def transposed_times(left, right):
    return times(left.T, right)


class Layout:
    def __init__(self, group_width, groups):
        self.width = group_width
        self.groups = groups
        self.pairs = group_width // 2
        self.rounds = (self.pairs - 1) // 2
        self.last_offset = 2

    def offset(self, round_index, side):
        if round_index == 0:
            return 1 + 2 * side
        return 2 * round_index + 2 + side


def late(layout):
    return lax.axis_index("grp") >= layout.groups // 2


def full_role(layout, r):
    index, pair, side = place()
    far = pair ^ layout.offset(r, side)
    return far, (side == 1) | jnp.logical_not(late(layout)) if r == 0 else side >= 0


def last_role(layout):
    index, pair, side = place()
    far = pair ^ jnp.where(side == 1, layout.last_offset, layout.offset(0, 0))
    return far, (side == 1) | late(layout)


def place():
    index = lax.axis_index("dev")
    return index, index // 2, index % 2


def load_kernel(layout, flags_in, tiles_in, orbitals_in, tiles, orbitals, flags, sems):
    copies = [
        pltpu.make_async_copy(tiles_in, tiles, sems.at[1]),
        pltpu.make_async_copy(orbitals_in, orbitals, sems.at[2]),
        pltpu.make_async_copy(flags_in, flags, sems.at[0]),
    ]
    for copy in copies:
        copy.start()
    for copy in copies:
        copy.wait()
    for slot in range(layout.width + 1):
        tiles[slot] = tiles[slot] * flags[0, slot].astype(F32)


def mask_kernel(layout, flags, mask):
    row = flags[...].astype(F32)
    for slot in range(layout.width + 1):
        mask[slot : slot + 1] = jnp.broadcast_to(
            row[:, slot : slot + 1], (1, mask.shape[1])
        )


def taken_tile(taken, mask, slot):
    return taken[slot] * mask[pl.ds(slot, 1), :]


def pair_terms(far, tiles, taken, mask, own, other, out):
    dot = functools.partial(
        lax.dot_general,
        dimension_numbers=(((0,), (0,)), ((), ())),
        preferred_element_type=F32,
    )
    right_high, right_low = parted(jnp.concatenate([own, other], axis=0))
    for k in range(2):
        slot = 2 * far + k
        stack = jnp.concatenate([tiles[slot], taken_tile(taken, mask, slot)], axis=0)
        high, low = parted(stack)
        out[k] = dot(high, right_high) + dot(high, right_low) + dot(low, right_high)


def role_blocks(layout, role, tiles, taken, mask, own, other, out):
    index, pair, side = place()
    far, trades = role
    lower = lax.axis_index("grp") % 2 == 0

    @pl.when(trades & (far > pair))
    def _():
        pair_terms(far, tiles, taken, mask, own, other, out)

    @pl.when(jnp.logical_not(trades) & lower)
    def _():
        out[0] = transposed_times(tiles[layout.width], own)
        out[1] = transposed_times(taken_tile(taken, mask, layout.width), other)

    @pl.when(jnp.where(trades, far < pair, jnp.logical_not(lower)))
    def _():
        out[0] = jnp.where(side == 0, own, other)
        out[1] = jnp.where(side == 0, other, own)


def send_full_kernel(layout, tiles, taken, mask, orbitals, taken_orbitals, *outs):
    index, pair, side = place()
    own, other = orbitals[...], taken_orbitals[...]
    for r in range(layout.rounds):
        role = full_role(layout, r)
        role_blocks(layout, role, tiles, taken, mask, own, other, outs[r])

    @pl.when((side == 1) & (pair == 0))
    def _():
        far = pair ^ layout.last_offset
        pair_terms(far, tiles, taken, mask, own, other, outs[-1])


def send_last_kernel(layout, tiles, taken, mask, orbitals, taken_orbitals, made, out):
    index, pair, side = place()

    @pl.when((side == 1) & (pair == 0))
    def _():
        out[...] = made[...]

    @pl.when((side == 0) | (pair > 0))
    def _():
        own, other = orbitals[...], taken_orbitals[...]
        role_blocks(layout, last_role(layout), tiles, taken, mask, own, other, out)


def send_odd_kernel(layout, tiles, orbitals, out):
    lower = lax.axis_index("grp") % 2 == 1

    @pl.when(lower)
    def _():
        out[...] = transposed_times(tiles[layout.width], orbitals[...])

    @pl.when(jnp.logical_not(lower))
    def _():
        out[...] = orbitals[...]


def near_kernel(layout, tiles, orbitals, taken_orbitals, mine, others):
    index, pair, side = place()
    own, other = orbitals[...], taken_orbitals[...]
    beside = tiles[index ^ 1]
    row = jnp.concatenate([tiles[index], beside], axis=1)
    mine[...] = times(row, jnp.concatenate([own, other], axis=0))
    others[...] = transposed_times(beside, own)


def take(layout, role, came, row, tile_of, base, total):
    index, pair, side = place()
    far, trades = role
    lower = lax.axis_index("grp") % 2 == 0

    @pl.when(trades & (far > pair))
    def _():
        left = jnp.concatenate([tile_of(2 * far), tile_of(2 * far + 1)], axis=1)
        right = jnp.concatenate([came[0], came[1]], axis=0)
        total[...] = base[...] + times(left, right)

    @pl.when(jnp.logical_not(trades) & lower)
    def _():
        total[...] = base[...] + times(tile_of(layout.width), came[row])

    @pl.when(jnp.where(trades, far < pair, jnp.logical_not(lower)))
    def _():
        total[...] = base[...] + came[side ^ row]


def full_kernel(layout, taken, mask, others_in, *refs):
    arrived, others = refs[:-1], refs[-1]
    tile_of = functools.partial(taken_tile, taken, mask)
    for r, came in enumerate(arrived):
        base = others_in if r == 0 else others
        take(layout, full_role(layout, r), came, 1, tile_of, base, others)


def back_kernel(layout, taken, mask, others_in, came, others):
    tile_of = functools.partial(taken_tile, taken, mask)
    take(layout, last_role(layout), came, 1, tile_of, others_in, others)


def mine_kernel(layout, tiles, mine_in, last, odd_in, *refs):
    arrived, mine = refs[:-1], refs[-1]
    group = lax.axis_index("grp")

    @pl.when(group % 2 == 0)
    def _():
        mine[...] = mine_in[...] + jnp.where(group > 0, odd_in[...], 0.0)

    @pl.when(group % 2 == 1)
    def _():
        mine[...] = mine_in[...] + times(tiles[layout.width], odd_in[...])

    def tile_of(slot):
        return tiles[slot]

    take(layout, last_role(layout), last, 0, tile_of, mine, mine)
    for r, came in enumerate(arrived):
        take(layout, full_role(layout, r), came, 0, tile_of, mine, mine)


def call(body, outs, operands, specs=None, scratch=(), flops=0):
    return pl.pallas_call(
        body,
        out_shape=outs,
        in_specs=specs or [VMEM] * len(operands),
        out_specs=jax.tree.map(lambda _: VMEM, outs),
        scratch_shapes=scratch,
        cost_estimate=pl.CostEstimate(
            flops=flops, bytes_accessed=0, transcendentals=0
        ),
        compiler_params=pltpu.CompilerParams(vmem_limit_bytes=32 * 1024 * 1024),
    )(*operands)


def moves_of(layout, r):
    moves = []
    for g in range(layout.groups):
        upper_half = g >= layout.groups // 2
        for i in range(layout.width):
            side = i % 2
            if r is None:
                offset = layout.last_offset if side else layout.offset(0, 0)
                trades = side == 1 or upper_half
            else:
                offset = layout.offset(r, side)
                trades = side == 1 or r > 0 or not upper_half
            to, j = (g, i ^ (2 * offset)) if trades else (g ^ 1, i)
            moves.append((g * layout.width + i, to * layout.width + j))
    return moves


def odd_moves(layout, groups):
    moves = []
    for g in range(groups):
        to = g + 1 if g % 2 == 1 else g - 1
        for i in range(layout.width):
            if 0 <= to < groups:
                moves.append((g * layout.width + i, to * layout.width + i))
            else:
                moves.append((g * layout.width + i, g * layout.width + (i ^ 1)))
    return moves


def per_device(stored_tiles, tile_flags, orbitals):
    group_width = lax.axis_size("dev")
    groups = lax.axis_size("grp")
    layout = Layout(group_width, groups)
    order, columns = orbitals.shape
    block = jax.ShapeDtypeStruct((order, columns), F32)
    two = jax.ShapeDtypeStruct((2, order, columns), F32)
    partners = [(i, i ^ 1) for i in range(group_width)]
    semaphore = pltpu.SemaphoreType.DMA

    taken = lax.ppermute(stored_tiles, "dev", partners)[0]
    taken_orbitals = lax.ppermute(orbitals, "dev", partners)
    taken_flags = lax.ppermute(tile_flags, "dev", partners)
    tiles, held = call(
        functools.partial(load_kernel, layout),
        [jax.ShapeDtypeStruct(stored_tiles.shape[1:], F32), block],
        [
            pltpu.with_memory_space_constraint(operand, pltpu.HBM)
            for operand in (tile_flags, stored_tiles[0], orbitals)
        ],
        [HBM] * 3,
        [pltpu.SMEM(tile_flags.shape, jnp.int32), semaphore((3,))],
        flops=10**9,
    )
    mask = call(
        functools.partial(mask_kernel, layout),
        jax.ShapeDtypeStruct((group_width + 1, order), F32),
        [taken_flags],
        flops=10**9,
    )

    *full, made = call(
        functools.partial(send_full_kernel, layout),
        [two] * (layout.rounds + 1),
        [tiles, taken, mask, held, taken_orbitals],
    )
    full_arrived = []
    for r in range(layout.rounds):
        arrived = lax.ppermute(full[r], ("grp", "dev"), moves_of(layout, r))
        full_arrived.append(arrived)

    last = call(
        functools.partial(send_last_kernel, layout),
        two,
        [tiles, taken, mask, held, taken_orbitals, made],
    )
    last_arrived = lax.ppermute(last, ("grp", "dev"), moves_of(layout, None))

    odd = call(functools.partial(send_odd_kernel, layout), block, [tiles, held])
    odd_arrived = lax.ppermute(odd, ("grp", "dev"), odd_moves(layout, groups))

    mine, others = call(
        functools.partial(near_kernel, layout),
        [block, block],
        [tiles, held, taken_orbitals],
    )
    others = call(
        functools.partial(full_kernel, layout),
        block,
        [taken, mask, others, *full_arrived],
    )
    others = call(
        functools.partial(back_kernel, layout),
        block,
        [taken, mask, others, last_arrived],
    )
    returned = lax.ppermute(others, "dev", partners)
    mine = call(
        functools.partial(mine_kernel, layout),
        block,
        [tiles, mine, last_arrived, odd_arrived, *full_arrived],
    )
    return mine + returned


def solution(mesh):
    in_specs = (
        P(("grp", "dev"), None, None, None),
        P(("grp", "dev"), None),
        P(("grp", "dev"), None),
    )
    out_specs = P(("grp", "dev"), None)
    return jax.shard_map(
        per_device, mesh=mesh, in_specs=in_specs, out_specs=out_specs, check_vma=False
    )
```
